32 devices in a mesh: gx: 4 (over z), gy: 4 (over x, core), role: 2 (over y).
Axes of the slice: x: 2, y: 2, z: 4, core: 2. Of those that a mesh axis runs over, the one named last changes fastest.
Arguments:
- velocity: float32 [3, 64, 64, 256], P(None, 'gx', 'gy', 'role'), may hold values from -6 to 6
- target_visc: bfloat16 [32, 32, 128], P('gx', 'gy', 'role'), may hold values from 0.049804688 to 1
- w_first: bfloat16 [64, 81], replicated, may hold values from -2 to 2
- w_hidden: bfloat16 [64, 1728], replicated, may hold values from -0.3125 to 0.3125
- w_last: bfloat16 [64], replicated, may hold values from -1.5 to 1.5
- sample_owner: int32 [4, 2, 32, 1], P('gy', 'role'), may hold values from 0 to 3; in each aligned block of 8 rows (0 to 7, 8 to 15, ..., all dimensions but the last counted through in order) at most 4 rows name the same one
- sample_block: int32 [4, 2, 32, 1], P('gy', 'role'), may hold values from 0 to 7
Outputs:
- u_next: float32 [3, 64, 64, 256], P(None, 'gx', 'gy', 'role')
- slot_loss: float32 [4, 2, 32], P('gy', 'role', 'gx')
- grad_first: float32 [64, 81], replicated
- grad_hidden: float32 [64, 1728], replicated
- grad_last: float32 [64], replicated
The draws below stay inside these ranges and needn't reach their ends.
Inputs may be any that keep to these rules, and one draw needn't show every extreme that they name: `sample_owner`: within one trainer's 8 rows (aligned blocks of rows) no gx index is named more than 4 times.
All inputs are finite; a program needn't handle non-finite values.
Results may differ from the reference program's by a relative error of at most 0.002.
The reference program's roundings to bfloat16 on the way (of `filtered`, `act_first`, `act_hidden`, `d_logit`, `d_hidden` and `d_first`) count: a program that leaves them out, or rounds other values in their place, can miss the bound.
Values may be sent and summed in bfloat16 or wider, within the bound.
No kernel may reach another device: no remote copies, remote signals or barrier semaphores. Data moves between devices by JAX's collectives and lax.ppermute only.
A program may use at most 128 MiB of HBM per device.

```python
import math
import jax
import jax.numpy as jnp
import numpy as np
from jax import lax

CX = 16
CY = 16
CZ = 128
BSIDE = 8
CH = 64
SLOTS = 8
NX = 64
NY = 64
NZ = 256
NXC = 32
NYC = 32
NZC = 128
BLK = 8
CAP = 4
TRAINERS = 32
YSLABS = 4
ZSLABS = 2
LISTLEN = 32
N_GX = 4
N_GY = 4
N_ROLE = 2


def plant(array, stream_key, smallest, top_value):
    dims = array.shape
    index_at = [jax.random.randint(jax.random.fold_in(stream_key, axis), (), 0, dims[axis]) for axis in range(len(dims))]
    array = array.at[tuple(index_at)].set(smallest)
    longest = dims.index(max(dims))
    index_at[longest] = (index_at[longest] + 1) % dims[longest]
    return array.at[tuple(index_at)].set(top_value)


def shard_levels(rng, shape, shards, least, largest):
    gain = 1.0
    for axis_at, shards_of in shards:
        draws = jax.random.uniform(jax.random.fold_in(jax.random.fold_in(rng, 6), axis_at), (shards_of,), jnp.float32, least / len(shards), largest / len(shards))
        gain = gain * jnp.repeat(jnp.exp(draws), shape[axis_at] // shards_of).reshape((-1,) + (1,) * (len(shape) - 1 - axis_at))
    return gain


def routed_block(stream_key, own, number, rows, amount, top, most, lean):
    order = jax.random.permutation(stream_key, amount)
    packed, ordinary = shares(amount, rows * top, most, lean, True), shares(amount, rows * top, most, lean, False)
    places = jnp.arange(amount)

    def named(lengths, offset_by):
        used = int((lengths > 0).sum())
        fixed = max(1, used // 4)
        moved = fixed + (places - fixed + offset_by * (used - fixed)) % max(1, amount - fixed)
        return jnp.zeros((amount,), jnp.int32).at[order[jnp.where(places < fixed, places, moved)]].set(jnp.asarray(lengths, jnp.int32))

    lengths = jnp.where(number % 4 == 0, named(packed, number // 4), named(ordinary, number - number // 4 - 1))
    mixed = jax.random.permutation(jax.random.fold_in(own, 3), amount)
    donor, sink = mixed[0:amount // 2 * 2:2], mixed[1:amount // 2 * 2:2]
    margin = jnp.minimum(lengths[donor] - 1, most - lengths[sink]) // 2
    margin = jnp.where((donor == order[0]) | (sink == order[0]) | (lengths[sink] == 0), 0, jnp.maximum(margin, 0))
    moved = jax.random.randint(jax.random.fold_in(own, 4), (amount // 2,), 0, 1 << 20) % (margin + 1)
    lengths = lengths.at[donor].add(-moved).at[sink].add(moved)
    labels = jnp.searchsorted(jnp.cumsum(lengths), jnp.arange(rows * top), side="right").astype(jnp.int32)
    grid = labels.reshape(top, rows).T
    grid = grid[jax.random.permutation(jax.random.fold_in(own, 1), rows)]
    offset_by = jax.random.randint(jax.random.fold_in(own, 2), (rows, 1), 0, top)
    return jnp.take_along_axis(grid, (jnp.arange(top)[None, :] + offset_by) % top, axis=1)


def shares(number_of, total, most, lean, full):
    loads = [(1 << 20) // math.isqrt(rank ** lean) + 1 for rank in range(1, number_of + 1)]
    largest = most if full else min(most, max(-(-total // number_of), total * loads[0] // sum(loads)))
    least = 1 if total - largest >= number_of - 1 else 0
    given, spare = [largest] + [least] * (number_of - 1), total - largest - least * (number_of - 1)
    while spare > 0:
        candidates = [i for i in range(1, number_of) if given[i] < largest] or [i for i in range(1, number_of) if given[i] < most]
        mass, remaining = sum([loads[i] for i in candidates]), spare
        for i in candidates:
            extra = min(most - given[i], max(1, remaining * loads[i] // mass), spare)
            given[i] = given[i] + extra
            spare = spare - extra
    return np.array(given)


def normal_values(key, extent, scale, most, pieces=(), held_as=jnp.bfloat16):
    values = jax.random.normal(key, extent, jnp.float32) * scale
    if len(pieces) > 0:
        values = shard_levels(key, extent, pieces, -0.22, 0.18) * values
    return jnp.clip(values, min=-most, max=most).astype(held_as)


def setup_inputs(seed: int = 0) -> dict:
    seeds = jax.random.split(jax.random.key(seed), 8)
    velocity = normal_values(seeds[0], (3, NX, NY, NZ), 1.0, 6.0, ((1, 4), (2, 4), (3, 2)), jnp.float32)
    target_visc = jnp.clip(jnp.exp(math.log(1.0) - 2.9996462 * jax.random.uniform(seeds[1], (NXC, NYC, NZC), jnp.float32) ** shard_levels(seeds[1], (NXC, NYC, NZC), ((0, 4), (1, 4), (2, 2)), -0.2, 0.2)), 0.049804688, 1.0).astype(jnp.bfloat16)
    w_first = normal_values(seeds[2], (CH, 81), 9 ** -0.5, 2.0)
    w_hidden = normal_values(seeds[3], (CH, 27 * CH), (27 * CH // 4) ** -0.5, 0.3125)
    w_last = normal_values(seeds[4], (CH,), (CH // 4) ** -0.5, 1.5)
    sample_owner_keys = jax.random.split(jax.random.fold_in(seeds[5], 1), YSLABS * ZSLABS * LISTLEN // SLOTS)
    sample_owner_turns = jax.random.permutation(jax.random.fold_in(seeds[5], 3), YSLABS * ZSLABS * LISTLEN // SLOTS)
    sample_owner = jax.vmap(lambda own, number: routed_block(jax.random.fold_in(seeds[5], 2), own, number, SLOTS, N_GX, 1, CAP, 2))(sample_owner_keys, sample_owner_turns).reshape((YSLABS, ZSLABS, LISTLEN, 1))
    sample_block = plant(jax.random.randint(seeds[6], (YSLABS, ZSLABS, LISTLEN, 1), 0, BLK), jax.random.fold_in(seeds[6], 1), 0, BLK - 1).astype(jnp.int32)
    return {"velocity": velocity, "target_visc": target_visc, "w_first": w_first, "w_hidden": w_hidden, "w_last": w_last, "sample_owner": sample_owner, "sample_block": sample_block}


base_visc = 0.02
time_step = 0.2


def cell_masks(side):
    count = side ** 3
    flat = jnp.arange(count, dtype=jnp.int32)
    first = flat // (side * side)
    second = (flat // side) % side
    third = flat % side
    rows = []
    for k in range(27):
        shift_x = k // 9 - 1
        shift_y = (k // 3) % 3 - 1
        shift_z = k % 3 - 1
        inside = (first + shift_x >= 0) & (first + shift_x < side)
        inside = inside & (second + shift_y >= 0) & (second + shift_y < side)
        inside = inside & (third + shift_z >= 0) & (third + shift_z < side)
        rows.append(inside)
    return jnp.stack(rows).astype(jnp.float32)


def pad_cells(field, side):
    reach = side * side + side + 1
    return jnp.pad(field, ((0, 0), (0, 0), (reach, reach)))


def shifted(padded, masks, side, k, count):
    reach = side * side + side + 1
    offset = (k // 9 - 1) * side * side + ((k // 3) % 3 - 1) * side + (k % 3 - 1)
    return lax.slice_in_dim(padded, reach + offset, reach + offset + count, axis=2) * masks[k]


def convolve(weight, field, masks, side):
    inner = field.shape[1]
    count = field.shape[2]
    padded = pad_cells(field.astype(jnp.float32), side)
    wide = weight.astype(jnp.float32)
    summed = None
    for k in range(27):
        term = jnp.einsum("oc,bcn->bon", wide[:, k * inner:(k + 1) * inner], shifted(padded, masks, side, k, count))
        summed = term if summed is None else summed + term
    return summed


def silu_slope(value):
    sig = jax.nn.sigmoid(value)
    return sig * (1.0 + value * (1.0 - sig))


def network(w_first, w_hidden, w_last, inputs, masks, side):
    pre_first = convolve(w_first, inputs, masks, side)
    act_first = jax.nn.silu(pre_first).astype(jnp.bfloat16)
    pre_hidden = convolve(w_hidden, act_first, masks, side)
    act_hidden = jax.nn.silu(pre_hidden).astype(jnp.bfloat16)
    logits = jnp.einsum("c,bcn->bn", w_last.astype(jnp.float32), act_hidden.astype(jnp.float32))
    eddy = 0.5 * jax.nn.softplus(logits)
    return pre_first, act_first, pre_hidden, act_hidden, logits, eddy


def fit_blocks(w_first, w_hidden, w_last, blocks, masks, side):
    count = blocks.shape[2]
    width = w_hidden.shape[0]
    inputs = blocks[:, :3]
    target = blocks[:, 3].astype(jnp.float32)
    pre_first, act_first, pre_hidden, act_hidden, logits, eddy = network(w_first, w_hidden, w_last, inputs, masks, side)
    error = eddy - target
    losses = jnp.mean(error * error, axis=1)
    d_logit = (error * jax.nn.sigmoid(logits) / (TRAINERS * count)).astype(jnp.bfloat16)
    grad_last = jnp.einsum("bn,bcn->c", d_logit.astype(jnp.float32), act_hidden.astype(jnp.float32))
    d_hidden = (w_last.astype(jnp.float32)[None, :, None] * d_logit.astype(jnp.float32)[:, None, :] * silu_slope(pre_hidden)).astype(jnp.bfloat16)
    wide_delta = d_hidden.astype(jnp.float32)
    padded_act = pad_cells(act_first.astype(jnp.float32), side)
    grad_hidden = jnp.concatenate([jnp.einsum("bon,bcn->oc", wide_delta, shifted(padded_act, masks, side, k, count)) for k in range(27)], axis=1)
    padded_delta = pad_cells(wide_delta, side)
    wide_hidden = w_hidden.astype(jnp.float32)
    d_act = None
    for k in range(27):
        term = jnp.einsum("oc,bon->bcn", wide_hidden[:, k * width:(k + 1) * width], shifted(padded_delta, masks, side, 26 - k, count))
        d_act = term if d_act is None else d_act + term
    d_first = (d_act * silu_slope(pre_first)).astype(jnp.bfloat16)
    wide_first = d_first.astype(jnp.float32)
    padded_in = pad_cells(inputs.astype(jnp.float32), side)
    grad_first = jnp.concatenate([jnp.einsum("bon,bcn->oc", wide_first, shifted(padded_in, masks, side, k, count)) for k in range(27)], axis=1)
    return losses, grad_first, grad_hidden, grad_last


def reference(velocity, target_visc, w_first, w_hidden, w_last, sample_owner, sample_block):
    side = BSIDE
    count = side ** 3
    masks = cell_masks(side)
    filtered = velocity.reshape(3, NXC, 2, NYC, 2, NZC, 2).mean(axis=(2, 4, 6)).astype(jnp.bfloat16)
    count_x = NXC // side
    count_y = NYC // side
    count_z = NZC // side
    joined = jnp.concatenate([filtered, target_visc[None]], axis=0)
    blocks = joined.reshape(4, count_x, side, count_y, side, count_z, side).transpose(1, 3, 5, 0, 2, 4, 6)
    blocks = blocks.reshape(count_x, count_y, count_z, 4, count)

    def infer_row(row_blocks):
        return network(w_first, w_hidden, w_last, row_blocks[:, :3], masks, side)[5]

    eddy_rows = lax.map(infer_row, blocks.reshape(count_x, count_y * count_z, 4, count))
    eddy_field = eddy_rows.reshape(count_x, count_y, count_z, side, side, side).transpose(0, 3, 1, 4, 2, 5).reshape(NXC, NYC, NZC)
    visc = base_visc + jnp.repeat(jnp.repeat(jnp.repeat(eddy_field, 2, 0), 2, 1), 2, 2)

    advect = jnp.zeros_like(velocity)
    diffuse = jnp.zeros_like(velocity)
    for axis in range(3):
        dim = axis + 1
        ahead_one = jnp.roll(velocity, -1, dim)
        behind_one = jnp.roll(velocity, 1, dim)
        ahead_two = jnp.roll(velocity, -2, dim)
        behind_two = jnp.roll(velocity, 2, dim)
        slope = (8.0 * (ahead_one - behind_one) - (ahead_two - behind_two)) / 12.0
        advect = advect + velocity[axis][None] * slope
        visc_ahead = 0.5 * (visc + jnp.roll(visc, -1, axis))
        visc_behind = 0.5 * (visc + jnp.roll(visc, 1, axis))
        diffuse = diffuse + visc_ahead[None] * (ahead_one - velocity) - visc_behind[None] * (velocity - behind_one)
    u_next = velocity + time_step * (diffuse - advect)

    per_x = CX // (2 * side)
    per_y = CY // (2 * side)
    per_z = CZ // (2 * side)
    owners = sample_owner[..., 0].reshape(N_GY, N_ROLE, N_GX, SLOTS)
    picks = sample_block[..., 0].reshape(N_GY, N_ROLE, N_GX, SLOTS)
    local_x = picks // (per_y * per_z)
    local_y = (picks // per_z) % per_y
    local_z = picks % per_z
    block_x = owners * per_x + local_x
    block_y = jnp.arange(N_GY, dtype=jnp.int32)[:, None, None, None] * per_y + local_y
    block_z = jnp.arange(N_ROLE, dtype=jnp.int32)[None, :, None, None] * per_z + local_z
    index_x = block_x.reshape(TRAINERS, SLOTS)
    index_y = block_y.reshape(TRAINERS, SLOTS)
    index_z = block_z.reshape(TRAINERS, SLOTS)

    def train_step(carry, indices):
        picked = blocks[indices[0], indices[1], indices[2]]
        losses, grad_first, grad_hidden, grad_last = fit_blocks(w_first, w_hidden, w_last, picked, masks, side)
        return (carry[0] + grad_first, carry[1] + grad_hidden, carry[2] + grad_last), losses

    start = (jnp.zeros(w_first.shape, jnp.float32), jnp.zeros(w_hidden.shape, jnp.float32), jnp.zeros(w_last.shape, jnp.float32))
    grads, losses = lax.scan(train_step, start, (index_x, index_y, index_z))
    slot_loss = losses.reshape(N_GY, N_ROLE, N_GX * SLOTS)
    return u_next, slot_loss, grads[0], grads[1], grads[2]
```

```python
import jax
import jax.numpy as jnp
from jax import lax
from jax.experimental import pallas as pl
from jax.experimental.pallas import tpu as pltpu
from jax.sharding import PartitionSpec as P

F32 = jnp.float32
BF16 = jnp.bfloat16
HIGH = lax.Precision.HIGHEST

SIDE = 8
CELLS = SIDE**3
CH = 64
BLK = 8
ROWS = SIDE * SIDE * BLK
WIDE = SIDE * CH
SLAB = SIDE * BLK
GRAD_AT = 128
PAY = 1920
LAST_COL = 81
LOSS_COL = 82

base_visc = 0.02
time_step = 0.2


def iota(shape, dim):
    return lax.broadcasted_iota(jnp.int32, shape, dim)


def onehot(cond, dtype=BF16):
    return jnp.where(cond, 1.0, 0.0).astype(dtype)


def nt(a, b, precision=None):
    return lax.dot_general(a, b, (((1,), (1,)), ((), ())), preferred_element_type=F32, precision=precision)


def tn(a, b, precision=None):
    return lax.dot_general(a, b, (((0,), (0,)), ((), ())), preferred_element_type=F32, precision=precision)


def nn(a, b, precision=None):
    return lax.dot_general(a, b, (((1,), (0,)), ((), ())), preferred_element_type=F32, precision=precision)


def net_kernel(
    scal, vel, tgt, w1, w2, w3, own, blk,
    keep, send, eddy_out, hx_a, hx_b, hy_a, hy_b, hz,
    pool_s, fp_s, i1_s, a_s, d_s, tt_s, tb_s, pre_s, slope1_s, ah_s, slope2_s, dw_s, big_s, gh_s,
):
    trainers = scal[0, 0]
    gx_at = scal[0, 1]
    gy_at = scal[0, 2]
    half = scal[0, 3]
    dev = scal[0, 4]
    gx_odd = gx_at % 2 == 1
    gy_odd = gy_at % 2 == 1

    for c in range(3):
        for x in range(SIDE):
            both = vel[c, 2 * x] + vel[c, 2 * x + 1]
            pool_s[c, x] = both
    rows = []
    for c in range(3):
        cols = []
        for x in range(SIDE):
            cols.append(pool_s[c, x, pl.ds(0, 8, stride=2), :] + pool_s[c, x, pl.ds(1, 8, stride=2), :])
        rows.append(jnp.concatenate(cols, axis=0))
    pooled = jnp.concatenate(rows, axis=0)
    zpool = jnp.where(iota((128, 64), 0) // 2 == iota((128, 64), 1), 0.125, 0.0).astype(F32)
    filt = nn(pooled, zpool, HIGH).astype(BF16)
    tgt_rows = tgt[...].reshape(64, 64)
    zsel = jnp.concatenate([filt[0:64], filt[64:128], filt[128:192], tgt_rows], axis=1)
    spread = onehot(iota((ROWS, 64), 0) // BLK == iota((ROWS, 64), 1))
    by_block = nn(spread, zsel)
    mine = (iota((ROWS, 256), 1) % 64) // SIDE == iota((ROWS, 256), 0) % BLK
    by_block = jnp.where(mine, by_block, 0.0).astype(BF16)
    src_c = iota((256, 256), 0) // 64
    src_z = iota((256, 256), 0) % SIDE
    dst = iota((256, 256), 1)
    pick = onehot((dst < 216) & ((dst % 24) // SIDE == src_c) & (dst % SIDE == src_z))
    cells = nn(by_block, pick)
    dst8 = iota((256, SIDE), 1)
    pick_t = onehot((iota((256, SIDE), 0) // 64 == 3) & (iota((256, SIDE), 0) % SIDE == dst8))
    target = nn(by_block, pick_t)

    fp_s[...] = jnp.zeros(fp_s.shape, F32)
    fp_s[1:9, 1:9] = cells.reshape(SIDE, SIDE, BLK, 256)
    group = iota((1, 1, 1, 256), 3) // 24
    for x in range(SIDE):
        acc = jnp.zeros((1, SIDE, BLK, 256), F32)
        for k in range(9):
            part = fp_s[x + k // 3 : x + k // 3 + 1, k % 3 : k % 3 + SIDE]
            acc = jnp.where(group == k, part, acc)
        i1_s[x * SLAB : (x + 1) * SLAB, :] = acc.reshape(SLAB, 256).astype(BF16)

    j_at = iota((81, 256), 0)
    l_at = iota((81, 256), 1)
    same = (l_at < 216) & (j_at // 9 == l_at // 24) & (j_at % 3 == (l_at % 24) // SIDE)
    delta = l_at % SIDE - ((j_at // 3) % 3 - 1)
    w1v = w1[...]
    t1 = jnp.concatenate([nn(w1v, onehot(same & (delta == z))).astype(BF16) for z in range(SIDE)], axis=0)
    pre_s[...] = nt(i1_s[...], t1)

    src = iota((256, 512), 0)
    dst = iota((256, 512), 1)
    d_of = dst // 128 - 2
    half_of = (dst % 128) // 64
    zero_tile = jnp.zeros((64, 128), BF16)
    for k in range(9):
        base = (192 * k) // 128 * 128
        off = 192 * k - base
        width = min(256, 1728 - base)
        rel = src - off
        chooser = onehot((rel >= 0) & (rel < 192) & (rel // 64 - 1 == d_of + half_of) & (rel % 64 == dst % 64))
        tiles = nn(w2[:, base : base + width], chooser[:width]).astype(BF16)
        ks, js = k // 3, k % 3
        kb, jb = (8 - k) // 3, (8 - k) % 3
        for z in range(SIDE):
            for m in range(4):
                d = 2 * m - z
                tile = tiles[:, (d + 2) * 128 : (d + 3) * 128] if -2 <= d <= 1 else zero_tile
                tt_s[ks, z * 64 : (z + 1) * 64, js * 512 + m * 128 : js * 512 + (m + 1) * 128] = tile
                tb_s[kb, jb * 512 + z * 64 : jb * 512 + (z + 1) * 64, m * 128 : (m + 1) * 128] = tile

    def shifted_store(dst_ref, x, val):
        zero = jnp.zeros((1, BLK, WIDE), F32)
        lo, hi = (x + 1) * SLAB, (x + 2) * SLAB
        dst_ref[lo:hi, 0:512] = jnp.concatenate([zero, val[:-1]], axis=0).reshape(SLAB, WIDE).astype(BF16)
        dst_ref[lo:hi, 512:1024] = val.reshape(SLAB, WIDE).astype(BF16)
        dst_ref[lo:hi, 1024:1536] = jnp.concatenate([val[1:], zero], axis=0).reshape(SLAB, WIDE).astype(BF16)

    for ref in (a_s, d_s):
        ref[0:SLAB, :] = jnp.zeros((SLAB, 1536), BF16)
        ref[9 * SLAB :, :] = jnp.zeros((SLAB, 1536), BF16)

    for x in range(SIDE):
        pre = pre_s[x * SLAB : (x + 1) * SLAB, :]
        sig = jax.nn.sigmoid(pre)
        slope1_s[x * SLAB : (x + 1) * SLAB, :] = sig * (1.0 + pre * (1.0 - sig))
        shifted_store(a_s, x, (pre * sig).reshape(SIDE, BLK, WIDE))

    acc = nt(a_s[0:ROWS, :], tt_s[0])
    acc = acc + nt(a_s[SLAB : SLAB + ROWS, :], tt_s[1])
    pre_s[...] = acc + nt(a_s[2 * SLAB : 2 * SLAB + ROWS, :], tt_s[2])
    for x in range(SIDE):
        pre = pre_s[x * SLAB : (x + 1) * SLAB, :]
        sig = jax.nn.sigmoid(pre)
        slope2_s[x * SLAB : (x + 1) * SLAB, :] = sig * (1.0 + pre * (1.0 - sig))
        ah_s[x * SLAB : (x + 1) * SLAB, :] = (pre * sig).astype(BF16)

    tile8 = onehot(iota((64, WIDE), 0) == iota((64, WIDE), 1) % 64)
    w3_wide = nn(w3[...], tile8)
    last = jnp.where(iota((SIDE, WIDE), 1) // 64 == iota((SIDE, WIDE), 0), w3_wide, 0.0).astype(BF16)
    logits = nt(ah_s[...], last)
    eddy = 0.5 * (jnp.maximum(logits, 0.0) + jnp.log1p(jnp.exp(-jnp.abs(logits))))
    error = eddy - target
    losses = jnp.sum(jnp.sum((error * error).reshape(64, BLK, SIDE), axis=0), axis=1, keepdims=True) / CELLS
    d_logit = (error * jax.nn.sigmoid(logits) / (trainers.astype(F32) * CELLS)).astype(BF16)

    zrep = onehot(iota((SIDE, 128), 0) == (iota((SIDE, 128), 1) % 16) // 2, F32)
    fine = nn(eddy, zrep, HIGH)
    fine = jnp.where(iota((ROWS, 128), 1) // 16 == iota((ROWS, 128), 0) % BLK, fine, 0.0)
    fine = jnp.sum(fine.reshape(64, BLK, 128), axis=1)
    eddy_out[...] = fine

    for c in range(3):
        for i in range(2):
            lo, hi = vel[c, i], vel[c, 14 + i]
            at = (c * 2 + i) * 16
            hx_a[at : at + 16, :] = jnp.where(gx_odd, lo, hi)
            hx_b[at : at + 16, :] = jnp.where(gx_odd, hi, lo)
    hx_a[96:104, :] = jnp.where(gx_odd, fine[0:8], fine[56:64])
    hx_b[96:104, :] = jnp.where(gx_odd, fine[56:64], fine[0:8])
    for c in range(3):
        for i in range(2):
            lo = jnp.concatenate([vel[c, x, i : i + 1, :] for x in range(16)], axis=0)
            hi = jnp.concatenate([vel[c, x, 14 + i : 15 + i, :] for x in range(16)], axis=0)
            at = (c * 2 + i) * 16
            hy_a[at : at + 16, :] = jnp.where(gy_odd, lo, hi)
            hy_b[at : at + 16, :] = jnp.where(gy_odd, hi, lo)
    lo = eddy_out[pl.ds(0, 8, stride=8), :]
    hi = eddy_out[pl.ds(7, 8, stride=8), :]
    hy_a[96:104, :] = jnp.where(gy_odd, lo, hi)
    hy_b[96:104, :] = jnp.where(gy_odd, hi, lo)
    vt = jnp.transpose(vel[...].reshape(768, 128))
    hz[...] = jnp.zeros(hz.shape, F32)
    hz[0:2, 0:768] = vt[0:2]
    hz[2:4, 0:768] = vt[126:128]
    et = jnp.transpose(jnp.concatenate([fine, jnp.zeros((64, 128), F32)], axis=0))
    hz[0:1, 768:896] = et[0:1]
    hz[1:2, 768:896] = et[127:128]

    code = own[...] * BLK + blk[...]
    listed = code.shape[1]
    wanted = gx_at * BLK + iota((BLK, listed), 0)
    count = jnp.sum(jnp.where(code == wanted, 1.0, 0.0), axis=1, keepdims=True)
    count_rows = jnp.broadcast_to(count.reshape(1, BLK, 1), (64, BLK, 1)).reshape(ROWS, 1)

    big_s[:, 0:512] = nn(d_logit, last)
    for x in range(SIDE):
        d_hid = big_s[x * SLAB : (x + 1) * SLAB, 0:512] * slope2_s[x * SLAB : (x + 1) * SLAB, :]
        d_hid = d_hid.astype(BF16).astype(F32).reshape(SIDE, BLK, WIDE)
        shifted_store(d_s, x, d_hid)
        dw_s[x * SLAB : (x + 1) * SLAB, :] = (d_hid * count[None]).reshape(SLAB, WIDE)
    dwt = jnp.transpose(dw_s[...]).astype(BF16)

    gh_s[...] = jnp.zeros(gh_s.shape, F32)
    low_half = iota((64, 128), 1) < 64
    for k in range(9):
        dx, j = k // 3, k % 3
        big_s[:, 0:512] = nn(dwt, a_s[dx * SLAB : dx * SLAB + ROWS, j * 512 : (j + 1) * 512])
        sums = []
        for m in (-1, 0, 1, 2):
            tot = None
            for p in range(4):
                z = 2 * p + m
                if 0 <= z < SIDE:
                    part = big_s[z * 64 : (z + 1) * 64, p * 128 : (p + 1) * 128]
                    tot = part if tot is None else tot + part
            sums.append(tot)
        for dz in (-1, 0, 1):
            low, high = sums[1 - dz], sums[2 - dz]
            at = (k * 3 + dz + 1) * 64
            tile, odd = at // 128 * 128, at % 128 != 0
            if odd:
                val = high + pltpu.roll(low, 64, 1)
                gh_s[:, tile : tile + 128] += jnp.where(low_half, 0.0, val)
            else:
                val = low + pltpu.roll(high, 64, 1)
                gh_s[:, tile : tile + 128] += jnp.where(low_half, val, 0.0)

    acc = nn(d_s[0:ROWS, :], tb_s[0])
    acc = acc + nn(d_s[SLAB : SLAB + ROWS, :], tb_s[1])
    acc = acc + nn(d_s[2 * SLAB : 2 * SLAB + ROWS, :], tb_s[2])
    d_first = (acc * slope1_s[...]).astype(BF16).astype(F32)
    dw_s[...] = (d_first.reshape(64, BLK, WIDE) * count[None]).reshape(ROWS, WIDE)
    d1t = jnp.transpose(dw_s[...])
    d1_hi = d1t.astype(BF16)
    d1_lo = (d1t - d1_hi.astype(F32)).astype(BF16)
    i1 = i1_s[...]
    g1 = nn(d1_hi, i1) + nn(d1_lo, i1)
    z_in = iota((64, 256), 1) % SIDE
    parts = []
    for dz in (-1, 0, 1):
        tot = jnp.zeros((64, 256), F32)
        for z in range(SIDE):
            if 0 <= z + dz < SIDE:
                tot = tot + jnp.where(z_in == z + dz, g1[z * 64 : (z + 1) * 64], 0.0)
        parts.append(tot)
    r_at = iota((768, 128), 0)
    c_at = iota((768, 128), 1)
    l_at = r_at % 256
    fold = onehot(
        (l_at < 216) & (c_at // 9 == l_at // 24) & ((c_at // 3) % 3 == r_at // 256) & (c_at % 3 == (l_at % 24) // SIDE)
        & (c_at < 81),
        F32,
    )
    g_first = nn(jnp.concatenate(parts, axis=1), fold, HIGH)

    dlw = d_logit.astype(F32) * count_rows
    dl_hi = dlw.astype(BF16)
    dl_lo = (dlw - dl_hi.astype(F32)).astype(BF16)
    ah = ah_s[...]
    gl = tn(dl_hi, ah) + tn(dl_lo, ah)
    gl = jnp.where(iota((SIDE, WIDE), 1) // 64 == iota((SIDE, WIDE), 0), gl, 0.0)
    fold_o = onehot(iota((64, WIDE), 1) % 64 == iota((64, WIDE), 0), F32)
    g_last = jnp.sum(nt(fold_o, gl, HIGH), axis=1, keepdims=True)

    lane8 = iota((BLK, 128), 1)
    loss_row = jnp.where(lane8 - (LOSS_COL + BLK * (dev // 64)) == iota((BLK, 128), 0), losses, 0.0)
    loss_row = jnp.sum(loss_row, axis=0, keepdims=True)
    lane = iota((64, 128), 1)
    extra = jnp.where(lane == LAST_COL, g_last, g_first)
    extra = extra + jnp.where(iota((64, 128), 0) == dev % 64, loss_row, 0.0)

    second = half == 1
    keep[:, 0:128] = jnp.where(second, extra[32:64], extra[0:32])
    send[:, 0:128] = jnp.where(second, extra[0:32], extra[32:64])
    top, bottom = gh_s[0:32, :], gh_s[32:64, :]
    keep[:, 128:PAY] = jnp.where(second, bottom, top)
    send[:, 128:PAY] = jnp.where(second, top, bottom)


def vmem_spec():
    return pl.BlockSpec(memory_space=pltpu.VMEM)


def run_net(scal, velocity, target, w1, w2, w3, own, blk):
    f = lambda *s: jax.ShapeDtypeStruct(s, F32)
    return pl.pallas_call(
        net_kernel,
        out_shape=(f(32, PAY), f(32, PAY), f(64, 128), f(104, 128), f(104, 128), f(104, 128), f(104, 128), f(8, 896)),
        in_specs=[pl.BlockSpec(memory_space=pltpu.SMEM)] + [vmem_spec()] * 7,
        out_specs=tuple(vmem_spec() for _ in range(8)),
        scratch_shapes=[
            pltpu.VMEM((3, SIDE, 16, 128), F32),
            pltpu.VMEM((10, 10, BLK, 256), F32),
            pltpu.VMEM((ROWS, 256), BF16),
            pltpu.VMEM((ROWS + 2 * SLAB, 1536), BF16),
            pltpu.VMEM((ROWS + 2 * SLAB, 1536), BF16),
            pltpu.VMEM((3, 512, 1536), BF16),
            pltpu.VMEM((3, 1536, 512), BF16),
            pltpu.VMEM((ROWS, WIDE), F32),
            pltpu.VMEM((ROWS, WIDE), F32),
            pltpu.VMEM((ROWS, WIDE), BF16),
            pltpu.VMEM((ROWS, WIDE), F32),
            pltpu.VMEM((ROWS, WIDE), F32),
            pltpu.VMEM((ROWS, WIDE), F32),
            pltpu.VMEM((64, PAY - 128), F32),
        ],
        compiler_params=pltpu.CompilerParams(vmem_limit_bytes=56 * 1024 * 1024),
        name="net",
    )(scal, velocity, target, w1, w2, w3, own, blk)


def flow_kernel(scal, vel, eddy, rx_a, rx_b, ry_a, ry_b, rz, out, vx_s, vy_s, visc_s, ez_s, fine_s):
    gx_odd = scal[0, 1] % 2 == 1
    gy_odd = scal[0, 2] % 2 == 1
    lane = iota((1, 128), 1)

    def sides(odd, a, b, at, rows):
        one, two = a[at : at + rows, :], b[at : at + rows, :]
        return jnp.where(odd, one, two), jnp.where(odd, two, one)

    for c in range(3):
        for x in range(16):
            vy_s[(c * 16 + x) * 32 + 8 : (c * 16 + x) * 32 + 24, :] = vel[c, x]
        for i in range(2):
            below, above = sides(gy_odd, ry_a, ry_b, (c * 2 + i) * 16, 16)
            vy_s[pl.ds(c * 512 + 6 + i, 16, stride=32), :] = below
            vy_s[pl.ds(c * 512 + 24 + i, 16, stride=32), :] = above
            below, above = sides(gx_odd, rx_a, rx_b, (c * 2 + i) * 16, 16)
            vx_s[c, i] = below
            vx_s[c, 2 + i] = above

    zcols = jnp.transpose(rz[...])
    coarse = eddy[...]
    e_first, e_last = zcols[768:832, 0:1], zcols[768:832, 1:2]
    ahead = jnp.where(lane == 127, e_first, pltpu.roll(coarse, 127, 1))
    behind = jnp.where(lane == 0, e_last, pltpu.roll(coarse, 1, 1))
    below_x, above_x = sides(gx_odd, rx_a, rx_b, 96, 8)
    below_y, above_y = sides(gy_odd, ry_a, ry_b, 96, 8)

    def put(dst, plane, val):
        dst[pl.ds(plane * 32 + 8, 8, stride=2), :] = val
        dst[pl.ds(plane * 32 + 9, 8, stride=2), :] = val

    put(visc_s, 0, base_visc + below_x)
    put(visc_s, 17, base_visc + above_x)
    for x in range(8):
        for r in range(2):
            plane = 2 * x + 1 + r
            put(visc_s, plane, base_visc + coarse[x * 8 : x * 8 + 8])
            visc_s[plane * 32 + 7 : plane * 32 + 8, :] = base_visc + below_y[x : x + 1]
            visc_s[plane * 32 + 24 : plane * 32 + 25, :] = base_visc + above_y[x : x + 1]
        put(ez_s, 2 * x, base_visc + ahead[x * 8 : x * 8 + 8])
        put(ez_s, 2 * x + 1, base_visc + behind[x * 8 : x * 8 + 8])

    def plane_of(c, x):
        if x < 0:
            return vx_s[c, x + 2]
        if x > 15:
            return vx_s[c, x - 14]
        return vel[c, x]

    for x in range(16):
        vat = (x + 1) * 32
        visc = visc_s[vat + 8 : vat + 24, :]
        faces = (
            (visc_s[vat + 40 : vat + 56, :], visc_s[vat - 24 : vat - 8, :]),
            (visc_s[vat + 9 : vat + 25, :], visc_s[vat + 7 : vat + 23, :]),
            (
                ez_s[(x // 2 * 2) * 32 + 8 : (x // 2 * 2) * 32 + 24, :],
                ez_s[(x // 2 * 2 + 1) * 32 + 8 : (x // 2 * 2 + 1) * 32 + 24, :],
            ),
        )
        faces = [(0.5 * (visc + a), 0.5 * (visc + b)) for a, b in faces]
        wind = [vel[a, x] for a in range(3)]
        for c in range(3):
            u = vel[c, x]
            at = (c * 16 + x) * 32
            zat = (c * 16 + x) * 16
            zc = zcols[zat : zat + 16]
            p1 = jnp.where(lane == 127, zc[:, 0:1], pltpu.roll(u, 127, 1))
            p2 = jnp.where(lane == 127, zc[:, 1:2], jnp.where(lane == 126, zc[:, 0:1], pltpu.roll(u, 126, 1)))
            m1 = jnp.where(lane == 0, zc[:, 3:4], pltpu.roll(u, 1, 1))
            m2 = jnp.where(lane == 0, zc[:, 2:3], jnp.where(lane == 1, zc[:, 3:4], pltpu.roll(u, 2, 1)))
            near = (
                (plane_of(c, x + 1), plane_of(c, x - 1), plane_of(c, x + 2), plane_of(c, x - 2)),
                (
                    vy_s[at + 9 : at + 25, :], vy_s[at + 7 : at + 23, :],
                    vy_s[at + 10 : at + 26, :], vy_s[at + 6 : at + 22, :],
                ),
                (p1, m1, p2, m2),
            )
            advect = None
            diffuse = None
            for a in range(3):
                q1, b1, q2, b2 = near[a]
                slope = (8.0 * (q1 - b1) - (q2 - b2)) * (1.0 / 12.0)
                term = wind[a] * slope
                advect = term if advect is None else advect + term
                flux = faces[a][0] * (q1 - u) - faces[a][1] * (u - b1)
                diffuse = flux if diffuse is None else diffuse + flux
            out[c, x] = u + time_step * (diffuse - advect)


def run_flow(scal, velocity, eddy, rx_a, rx_b, ry_a, ry_b, rz):
    return pl.pallas_call(
        flow_kernel,
        out_shape=jax.ShapeDtypeStruct(velocity.shape, F32),
        in_specs=[pl.BlockSpec(memory_space=pltpu.SMEM)] + [vmem_spec()] * 7,
        out_specs=vmem_spec(),
        scratch_shapes=[
            pltpu.VMEM((3, 4, 16, 128), F32),
            pltpu.VMEM((3 * 16 * 32, 128), F32),
            pltpu.VMEM((18 * 32, 128), F32),
            pltpu.VMEM((16 * 32, 128), F32),
            pltpu.VMEM((8, 128), F32),
        ],
        compiler_params=pltpu.CompilerParams(vmem_limit_bytes=32 * 1024 * 1024),
        name="flow",
    )(scal, velocity, eddy, rx_a, rx_b, ry_a, ry_b, rz)


def finish_kernel(scal, own, blk, mine, other, loss_out, first_out, hidden_out, last_out, ext_s):
    second = scal[0, 3] == 1
    one, two = mine[...], other[...]
    top = jnp.where(second, two, one)
    bottom = jnp.where(second, one, two)
    hidden_out[0:32, :] = top[:, GRAD_AT : GRAD_AT + 27 * CH]
    hidden_out[32:64, :] = bottom[:, GRAD_AT : GRAD_AT + 27 * CH]
    ext_s[0:32, :] = top[:, 0:128]
    ext_s[32:64, :] = bottom[:, 0:128]
    extra = ext_s[...]
    first_out[...] = extra[:, 0:81]
    turned = jnp.transpose(jnp.concatenate([extra, jnp.zeros((64, 128), F32)], axis=0))
    last_out[...] = turned[LAST_COL : LAST_COL + 1, 0:64]
    slots = loss_out.shape[1]
    lane = iota((1, 128), 1)
    slot_lane = iota((1, slots), 1)
    picked = jnp.zeros((1, slots), F32)
    for s in range(slots):
        at = scal[0, 1] * slots + s
        dev = own[0, at] * scal[0, 5] + scal[0, 6]
        row = ext_s[pl.ds(dev % 64, 1), :]
        col = LOSS_COL + BLK * (dev // 64) + blk[0, at]
        value = jnp.sum(jnp.where(lane == col, row, 0.0), axis=1, keepdims=True)
        picked = jnp.where(slot_lane == s, value, picked)
    loss_out[...] = picked


def run_finish(scal, own, blk, mine, other, slots):
    smem = pl.BlockSpec(memory_space=pltpu.SMEM)
    f = lambda *s: jax.ShapeDtypeStruct(s, F32)
    return pl.pallas_call(
        finish_kernel,
        out_shape=(f(1, slots), f(64, 81), f(64, 27 * CH), f(1, 64)),
        in_specs=[smem] * 3 + [vmem_spec()] * 2,
        out_specs=tuple(vmem_spec() for _ in range(4)),
        scratch_shapes=[pltpu.VMEM((64, 128), F32)],
        name="finish",
    )(scal, own, blk, mine, other)


def on_device(velocity, target_visc, w_first, w_hidden, w_last, sample_owner, sample_block):
    n_x, n_y, n_z = lax.axis_size("gx"), lax.axis_size("gy"), lax.axis_size("role")
    trainers = n_x * n_y * n_z
    at_x, at_y, at_z = lax.axis_index("gx"), lax.axis_index("gy"), lax.axis_index("role")
    group = at_y * n_z + at_z
    half = (at_y ^ (at_y >> 1)) & 1
    scal = jnp.stack(
        [jnp.int32(trainers), at_x, at_y, half, at_x * (n_y * n_z) + group, jnp.int32(n_y * n_z), group, jnp.int32(0)]
    ).astype(jnp.int32)[None]
    own = sample_owner.reshape(1, -1)
    blk = sample_block.reshape(1, -1)
    slots = own.shape[1] // n_x

    def pairs_a(count):
        return [(i, i ^ 1) for i in range(count)]

    def pairs_b(count):
        return [(i, (i - 1) % count if i % 2 == 0 else (i + 1) % count) for i in range(count)]

    keep, send, eddy, hx_a, hx_b, hy_a, hy_b, hz = run_net(
        scal, velocity, target_visc, w_first, w_hidden, w_last.reshape(1, CH), own, blk
    )
    rx_a = lax.ppermute(hx_a, "gx", pairs_a(n_x))
    rx_b = lax.ppermute(hx_b, "gx", pairs_b(n_x))
    ry_a = lax.ppermute(hy_a, "gy", pairs_a(n_y))
    ry_b = lax.ppermute(hy_b, "gy", pairs_b(n_y))
    rz = lax.ppermute(hz, "role", pairs_a(n_z))

    total = keep + lax.ppermute(send, "gy", pairs_a(n_y))
    total = total + lax.ppermute(total, "gy", pairs_b(n_y))
    total = total + lax.ppermute(total, "role", pairs_a(n_z))
    if n_x == 4:
        steps = [pairs_a(n_x), pairs_b(n_x)]
    else:
        steps = [[(i, i ^ (1 << s)) for i in range(n_x)] for s in range(n_x.bit_length() - 1)]
    for step in steps:
        total = total + lax.ppermute(total, "gx", step)
    other = lax.ppermute(total, "gy", pairs_a(n_y))

    u_next = run_flow(scal, velocity, eddy, rx_a, rx_b, ry_a, ry_b, rz)
    losses, first, hidden, last = run_finish(scal, own, blk, total, other, slots)
    return (u_next, losses.reshape(1, 1, slots), first, hidden, last.reshape(CH))


def solution(mesh):
    return jax.shard_map(
        on_device,
        mesh=mesh,
        in_specs=(
            P(None, "gx", "gy", "role"),
            P("gx", "gy", "role"),
            P(),
            P(),
            P(),
            P("gy", "role", None, None),
            P("gy", "role", None, None),
        ),
        out_specs=(P(None, "gx", "gy", "role"), P("gy", "role", "gx"), P(), P(), P()),
        check_vma=False,
    )
```

```python
import jax
import jax.numpy as jnp
from jax import lax
from jax.experimental import pallas as pl
from jax.experimental.pallas import tpu as pltpu
from jax.sharding import PartitionSpec as P

F32 = jnp.float32
BF16 = jnp.bfloat16
HIGH = lax.Precision.HIGHEST

SIDE = 8
CELLS = SIDE**3
CH = 64
BLK = 8
ROWS = SIDE * SIDE * BLK
WIDE = SIDE * CH
SLAB = SIDE * BLK
PAY = 1920
LAST_COL = 81
LOSS_COL = 82

base_visc = 0.02
time_step = 0.2


def iota(shape, dim):
    return lax.broadcasted_iota(jnp.int32, shape, dim)


def onehot(cond, dtype=BF16):
    return jnp.where(cond, 1.0, 0.0).astype(dtype)


def nt(a, b, precision=None):
    return lax.dot_general(a, b, (((1,), (1,)), ((), ())), preferred_element_type=F32, precision=precision)


def tn(a, b, precision=None):
    return lax.dot_general(a, b, (((0,), (0,)), ((), ())), preferred_element_type=F32, precision=precision)


def nn(a, b, precision=None):
    return lax.dot_general(a, b, (((1,), (0,)), ((), ())), preferred_element_type=F32, precision=precision)


def net_kernel(
    scal, vel, tgt, w1, w2, w3, own, blk,
    keep, send, eddy_out, halo1, halo2, halo3, halo4,
    hx_a, hx_b, hy_b, hz, pool_s, fp_s, i1_s, a_s, d_s, tt_s, tb_s, pre_s, slope1_s, ah_s, slope2_s, dw_s, big_s, gh_s,
):
    trainers = scal[0, 0]
    gx_at = scal[0, 1]
    gy_at = scal[0, 2]
    half = scal[0, 3]
    dev = scal[0, 4]
    gx_odd = gx_at % 2 == 1
    gy_odd = gy_at % 2 == 1

    for c in range(3):
        for x in range(SIDE):
            both = vel[c, 2 * x] + vel[c, 2 * x + 1]
            pool_s[c, x] = both
    rows = []
    for c in range(3):
        cols = []
        for x in range(SIDE):
            cols.append(pool_s[c, x, pl.ds(0, 8, stride=2), :] + pool_s[c, x, pl.ds(1, 8, stride=2), :])
        rows.append(jnp.concatenate(cols, axis=0))
    pooled = jnp.concatenate(rows, axis=0)
    zpool = jnp.where(iota((128, 1), 0) >> 1 == iota((1, 64), 1), 0.125, 0.0)
    filt = nn(pooled, zpool, HIGH).astype(BF16)
    tgt_rows = tgt[...].reshape(64, 64)
    zsel = jnp.concatenate([filt[0:64], filt[64:128], filt[128:192], tgt_rows], axis=1)
    spread = onehot(iota((ROWS, 1), 0) >> 3 == iota((1, 64), 1))
    by_block = nn(spread, zsel)
    mine = (iota((1, 256), 1) & 63) >> 3 == iota((ROWS, 1), 0) & 7
    by_block = jnp.where(mine, by_block, 0.0).astype(BF16)
    lane_in = iota((1, 256), 1)
    lane_off = lax.div(lane_in, 24)
    lane_cz = lane_in - lane_off * 24
    src = iota((256, 1), 0)
    pick = onehot(jnp.where(lane_in < 216, lane_cz, -1) == (src >> 6) * 8 + (src & 7))
    cells = nn(by_block, pick)
    pick_t = onehot(jnp.where(src >= 192, src & 7, -1) == iota((1, SIDE), 1))
    target = nn(by_block, pick_t)

    fp_s[...] = jnp.zeros(fp_s.shape, F32)
    fp_s[1:9, 1:9] = cells.reshape(SIDE, SIDE, BLK, 256)
    group = lax.div(iota((1, 1, 1, 256), 3), 24)
    for x in range(SIDE):
        acc = jnp.zeros((1, SIDE, BLK, 256), F32)
        for k in range(9):
            part = fp_s[x + k // 3 : x + k // 3 + 1, k % 3 : k % 3 + SIDE]
            acc = jnp.where(group == k, part, acc)
        i1_s[x * SLAB : (x + 1) * SLAB, :] = acc.reshape(SLAB, 256).astype(BF16)

    j_at = iota((81, 1), 0)
    j_off, j_dz, j_c = lax.div(j_at, 9), lax.rem(lax.div(j_at, 3), 3) - 1, lax.rem(j_at, 3)
    lane_key = jnp.where(lane_in < 216, lane_off * 4 + (lane_cz >> 3), -1)
    same = lane_key == j_off * 4 + j_c
    delta = jnp.where(same, (lane_in & 7) - j_dz, -9)
    w1v = w1[...]
    t1 = jnp.concatenate([nn(w1v, onehot(delta == z)).astype(BF16) for z in range(SIDE)], axis=0)
    pre_s[...] = nt(i1_s[...], t1)

    src = iota((320, 1), 0) - 64
    dst = iota((1, 512), 1)
    wanted = ((dst >> 7) - 2 + ((dst & 127) >> 6)) * 64 + (dst & 63)
    chooser = onehot(jnp.where((src >= 0) & (src < 192), src - 64, -999) == wanted)
    zero_tile = jnp.zeros((64, 128), BF16)
    for k in range(9):
        base = (192 * k) // 128 * 128
        off = 192 * k - base
        width = min(256, 1728 - base)
        tiles = nn(w2[:, base : base + width], chooser[64 - off : 64 - off + width]).astype(BF16)
        ks, js = k // 3, k % 3
        kb, jb = (8 - k) // 3, (8 - k) % 3
        for z in range(SIDE):
            for m in range(4):
                d = 2 * m - z
                tile = tiles[:, (d + 2) * 128 : (d + 3) * 128] if -2 <= d <= 1 else zero_tile
                tt_s[ks, z * 64 : (z + 1) * 64, js * 512 + m * 128 : js * 512 + (m + 1) * 128] = tile
                tb_s[kb, jb * 512 + z * 64 : jb * 512 + (z + 1) * 64, m * 128 : (m + 1) * 128] = tile

    def shifted_store(dst_ref, x, val):
        zero = jnp.zeros((1, BLK, WIDE), F32)
        lo, hi = (x + 1) * SLAB, (x + 2) * SLAB
        dst_ref[lo:hi, 0:512] = jnp.concatenate([zero, val[:-1]], axis=0).reshape(SLAB, WIDE).astype(BF16)
        dst_ref[lo:hi, 512:1024] = val.reshape(SLAB, WIDE).astype(BF16)
        dst_ref[lo:hi, 1024:1536] = jnp.concatenate([val[1:], zero], axis=0).reshape(SLAB, WIDE).astype(BF16)

    for ref in (a_s, d_s):
        ref[0:SLAB, :] = jnp.zeros((SLAB, 1536), BF16)
        ref[9 * SLAB :, :] = jnp.zeros((SLAB, 1536), BF16)

    for x in range(SIDE):
        pre = pre_s[x * SLAB : (x + 1) * SLAB, :]
        sig = jax.nn.sigmoid(pre)
        slope1_s[x * SLAB : (x + 1) * SLAB, :] = sig * (1.0 + pre * (1.0 - sig))
        shifted_store(a_s, x, (pre * sig).reshape(SIDE, BLK, WIDE))

    acc = nt(a_s[0:ROWS, :], tt_s[0])
    acc = acc + nt(a_s[SLAB : SLAB + ROWS, :], tt_s[1])
    pre_s[...] = acc + nt(a_s[2 * SLAB : 2 * SLAB + ROWS, :], tt_s[2])
    for x in range(SIDE):
        pre = pre_s[x * SLAB : (x + 1) * SLAB, :]
        sig = jax.nn.sigmoid(pre)
        slope2_s[x * SLAB : (x + 1) * SLAB, :] = sig * (1.0 + pre * (1.0 - sig))
        ah_s[x * SLAB : (x + 1) * SLAB, :] = (pre * sig).astype(BF16)

    tile8 = onehot(iota((64, 1), 0) == iota((1, WIDE), 1) & 63)
    w3_wide = nn(w3[...], tile8)
    diag = iota((1, WIDE), 1) >> 6 == iota((SIDE, 1), 0)
    last = jnp.where(diag, w3_wide, 0.0).astype(BF16)
    logits = nt(ah_s[...], last)
    eddy = 0.5 * (jnp.maximum(logits, 0.0) + jnp.log1p(jnp.exp(-jnp.abs(logits))))
    error = eddy - target
    losses = jnp.sum(jnp.sum((error * error).reshape(64, BLK, SIDE), axis=0), axis=1, keepdims=True) / CELLS
    d_logit = (error * jax.nn.sigmoid(logits) / (trainers.astype(F32) * CELLS)).astype(BF16)

    zrep = onehot(iota((SIDE, 1), 0) == (iota((1, 128), 1) & 15) >> 1, F32)
    fine = nn(eddy, zrep, HIGH)
    fine = jnp.where(iota((1, 128), 1) >> 4 == iota((ROWS, 1), 0) & 7, fine, 0.0)
    fine = jnp.sum(fine.reshape(64, BLK, 128), axis=1)
    eddy_out[...] = fine

    for c in range(3):
        for i in range(2):
            lo, hi = vel[c, i], vel[c, 14 + i]
            at = (c * 2 + i) * 16
            hx_a[at : at + 16, :] = jnp.where(gx_odd, lo, hi)
            hx_b[at : at + 16, :] = jnp.where(gx_odd, hi, lo)
    hx_a[96:104, :] = jnp.where(gx_odd, fine[0:8], fine[56:64])
    hx_b[96:104, :] = jnp.where(gx_odd, fine[56:64], fine[0:8])
    core = send.at[480:584]
    for c in range(3):
        for i in range(2):
            lo = jnp.concatenate([vel[c, x, i : i + 1, :] for x in range(16)], axis=0)
            hi = jnp.concatenate([vel[c, x, 14 + i : 15 + i, :] for x in range(16)], axis=0)
            at = (c * 2 + i) * 16
            core[at : at + 16, :] = jnp.where(gy_odd, lo, hi)
            hy_b[at : at + 16, :] = jnp.where(gy_odd, hi, lo)
    lo = eddy_out[pl.ds(0, 8, stride=8), :]
    hi = eddy_out[pl.ds(7, 8, stride=8), :]
    core[96:104, :] = jnp.where(gy_odd, lo, hi)
    hy_b[96:104, :] = jnp.where(gy_odd, hi, lo)
    vt = jnp.transpose(vel[...].reshape(768, 128))
    et = jnp.transpose(jnp.concatenate([fine, jnp.zeros((64, 128), F32)], axis=0))
    hz[...] = jnp.zeros(hz.shape, F32)
    for t in range(6):
        hz[t * 8 : t * 8 + 2, :] = vt[0:2, t * 128 : (t + 1) * 128]
        hz[t * 8 + 2 : t * 8 + 4, :] = vt[126:128, t * 128 : (t + 1) * 128]
    hz[48:49, :] = et[0:1]
    hz[49:50, :] = et[127:128]
    second = half == 1
    halo1[...] = jnp.where(second, hx_a[...], hy_b[...])
    halo2[...] = jnp.where(second, hy_b[...], hz[...])
    halo3[...] = jnp.where(second, hx_b[...], hx_a[...])
    halo4[...] = jnp.where(second, hz[...], hx_b[...])

    code = own[...] * BLK + blk[...]
    listed = code.shape[1]
    wanted = gx_at * BLK + iota((BLK, listed), 0)
    count = jnp.sum(jnp.where(code == wanted, 1.0, 0.0), axis=1, keepdims=True)
    count_rows = jnp.broadcast_to(count.reshape(1, BLK, 1), (64, BLK, 1)).reshape(ROWS, 1)

    big_s[:, 0:512] = nn(d_logit, last)
    for x in range(SIDE):
        d_hid = big_s[x * SLAB : (x + 1) * SLAB, 0:512] * slope2_s[x * SLAB : (x + 1) * SLAB, :]
        d_hid = d_hid.astype(BF16).astype(F32).reshape(SIDE, BLK, WIDE)
        shifted_store(d_s, x, d_hid)
        dw_s[x * SLAB : (x + 1) * SLAB, :] = (d_hid * count[None]).reshape(SLAB, WIDE)
    dwt = jnp.transpose(dw_s[...]).astype(BF16)

    gh_s[...] = jnp.zeros(gh_s.shape, F32)
    low_half = iota((64, 128), 1) < 64
    for k in range(9):
        dx, j = k // 3, k % 3
        big_s[:, 0:512] = nn(dwt, a_s[dx * SLAB : dx * SLAB + ROWS, j * 512 : (j + 1) * 512])
        sums = []
        for m in (-1, 0, 1, 2):
            tot = None
            for p in range(4):
                z = 2 * p + m
                if 0 <= z < SIDE:
                    part = big_s[z * 64 : (z + 1) * 64, p * 128 : (p + 1) * 128]
                    tot = part if tot is None else tot + part
            sums.append(tot)
        for dz in (-1, 0, 1):
            low, high = sums[1 - dz], sums[2 - dz]
            at = (k * 3 + dz + 1) * 64
            tile, odd = at // 128 * 128, at % 128 != 0
            if odd:
                val = high + pltpu.roll(low, 64, 1)
                gh_s[:, tile : tile + 128] += jnp.where(low_half, 0.0, val)
            else:
                val = low + pltpu.roll(high, 64, 1)
                gh_s[:, tile : tile + 128] += jnp.where(low_half, val, 0.0)

    acc = nn(d_s[0:ROWS, :], tb_s[0])
    acc = acc + nn(d_s[SLAB : SLAB + ROWS, :], tb_s[1])
    acc = acc + nn(d_s[2 * SLAB : 2 * SLAB + ROWS, :], tb_s[2])
    d_first = (acc * slope1_s[...]).astype(BF16).astype(F32)
    dw_s[...] = (d_first.reshape(64, BLK, WIDE) * count[None]).reshape(ROWS, WIDE)
    d1t = jnp.transpose(dw_s[...])
    d1_hi = d1t.astype(BF16)
    d1_lo = (d1t - d1_hi.astype(F32)).astype(BF16)
    i1 = i1_s[...]
    g1 = nn(d1_hi, i1) + nn(d1_lo, i1)
    z_in = iota((1, 256), 1) & 7
    parts = []
    for dz in (-1, 0, 1):
        tot = jnp.zeros((64, 256), F32)
        for z in range(SIDE):
            if 0 <= z + dz < SIDE:
                tot = tot + jnp.where(z_in == z + dz, g1[z * 64 : (z + 1) * 64], 0.0)
        parts.append(tot)
    r_at = iota((768, 1), 0)
    c_at = iota((1, 128), 1)
    r_lane = r_at & 255
    r_off = lax.div(r_lane, 24)
    r_col = (r_off * 3 + (r_at >> 8)) * 3 + ((r_lane - r_off * 24) >> 3)
    fold = onehot(jnp.where(r_lane < 216, r_col, -1) == c_at, F32)
    g_first = nn(jnp.concatenate(parts, axis=1), fold, HIGH)

    dlw = d_logit.astype(F32) * count_rows
    dl_hi = dlw.astype(BF16)
    dl_lo = (dlw - dl_hi.astype(F32)).astype(BF16)
    ah = ah_s[...]
    gl = tn(dl_hi, ah) + tn(dl_lo, ah)
    gl = jnp.where(diag, gl, 0.0)
    fold_o = onehot(iota((1, WIDE), 1) & 63 == iota((64, 1), 0), F32)
    g_last = jnp.sum(nt(fold_o, gl, HIGH), axis=1, keepdims=True)

    lane8 = iota((BLK, 128), 1)
    loss_row = jnp.where(lane8 - (LOSS_COL + BLK * (dev // 64)) == iota((BLK, 128), 0), losses, 0.0)
    loss_row = jnp.sum(loss_row, axis=0, keepdims=True)
    lane = iota((64, 128), 1)
    extra = jnp.where(lane == LAST_COL, g_last, g_first)
    extra = extra + jnp.where(iota((64, 128), 0) == dev % 64, loss_row, 0.0)

    for t in range(PAY // 128):
        if t == 0:
            top, bottom = extra[0:32], extra[32:64]
        else:
            top, bottom = (gh_s[r : r + 32, (t - 1) * 128 : t * 128] for r in (0, 32))
        keep[t * 32 : (t + 1) * 32, :] = jnp.where(second, bottom, top)
        send[t * 32 : (t + 1) * 32, :] = jnp.where(second, top, bottom)


def vmem_spec():
    return pl.BlockSpec(memory_space=pltpu.VMEM)


def run_net(scal, velocity, target, w1, w2, w3, own, blk):
    f = lambda *s: jax.ShapeDtypeStruct(s, F32)
    return pl.pallas_call(
        net_kernel,
        out_shape=(f(480, 128), f(584, 128), f(64, 128)) + (f(104, 128),) * 4,
        in_specs=[pl.BlockSpec(memory_space=pltpu.SMEM)] + [vmem_spec()] * 7,
        out_specs=tuple(vmem_spec() for _ in range(7)),
        scratch_shapes=[
            pltpu.VMEM((104, 128), F32),
            pltpu.VMEM((104, 128), F32),
            pltpu.VMEM((104, 128), F32),
            pltpu.VMEM((104, 128), F32),
            pltpu.VMEM((3, SIDE, 16, 128), F32),
            pltpu.VMEM((10, 10, BLK, 256), F32),
            pltpu.VMEM((ROWS, 256), BF16),
            pltpu.VMEM((ROWS + 2 * SLAB, 1536), BF16),
            pltpu.VMEM((ROWS + 2 * SLAB, 1536), BF16),
            pltpu.VMEM((3, 512, 1536), BF16),
            pltpu.VMEM((3, 1536, 512), BF16),
            pltpu.VMEM((ROWS, WIDE), F32),
            pltpu.VMEM((ROWS, WIDE), F32),
            pltpu.VMEM((ROWS, WIDE), BF16),
            pltpu.VMEM((ROWS, WIDE), F32),
            pltpu.VMEM((ROWS, WIDE), F32),
            pltpu.VMEM((ROWS, WIDE), F32),
            pltpu.VMEM((64, PAY - 128), F32),
        ],
        compiler_params=pltpu.CompilerParams(vmem_limit_bytes=56 * 1024 * 1024),
        name="net",
    )(scal, velocity, target, w1, w2, w3, own, blk)


def flow_kernel(
    scal, vel, eddy, got0, got1, got2, got3, got4, out, rx_a, rx_b, ry_a, ry_b, rz, vx_s, vy_s, visc_s, ez_s
):
    gx_odd = scal[0, 1] % 2 == 1
    gy_odd = scal[0, 2] % 2 == 1
    second = scal[0, 3] == 1
    ry_a[...] = got0[...]
    ry_b[...] = jnp.where(second, got2[...], got1[...])
    rx_a[...] = jnp.where(second, got1[...], got3[...])
    rx_b[...] = jnp.where(second, got3[...], got4[...])
    rz[...] = jnp.where(second, got4[...], got2[...])
    lane = iota((1, 128), 1)

    def sides(odd, a, b, at, rows):
        one, two = a[at : at + rows, :], b[at : at + rows, :]
        return jnp.where(odd, one, two), jnp.where(odd, two, one)

    for c in range(3):
        for x in range(16):
            vy_s[(c * 16 + x) * 32 + 8 : (c * 16 + x) * 32 + 24, :] = vel[c, x]
        for i in range(2):
            below, above = sides(gy_odd, ry_a, ry_b, (c * 2 + i) * 16, 16)
            vy_s[pl.ds(c * 512 + 6 + i, 16, stride=32), :] = below
            vy_s[pl.ds(c * 512 + 24 + i, 16, stride=32), :] = above
            below, above = sides(gx_odd, rx_a, rx_b, (c * 2 + i) * 16, 16)
            vx_s[c, i] = below
            vx_s[c, 2 + i] = above

    zcols = jnp.concatenate([jnp.transpose(rz[t * 8 : t * 8 + 8, :]) for t in range(7)], axis=0)
    coarse = eddy[...]
    e_first, e_last = zcols[768:832, 0:1], zcols[768:832, 1:2]
    ahead = jnp.where(lane == 127, e_first, pltpu.roll(coarse, 127, 1))
    behind = jnp.where(lane == 0, e_last, pltpu.roll(coarse, 1, 1))
    below_x, above_x = sides(gx_odd, rx_a, rx_b, 96, 8)
    below_y, above_y = sides(gy_odd, ry_a, ry_b, 96, 8)

    def put(dst, plane, val):
        dst[pl.ds(plane * 32 + 8, 8, stride=2), :] = val
        dst[pl.ds(plane * 32 + 9, 8, stride=2), :] = val

    put(visc_s, 0, base_visc + below_x)
    put(visc_s, 17, base_visc + above_x)
    for x in range(8):
        for r in range(2):
            plane = 2 * x + 1 + r
            put(visc_s, plane, base_visc + coarse[x * 8 : x * 8 + 8])
            visc_s[plane * 32 + 7 : plane * 32 + 8, :] = base_visc + below_y[x : x + 1]
            visc_s[plane * 32 + 24 : plane * 32 + 25, :] = base_visc + above_y[x : x + 1]
        put(ez_s, 2 * x, base_visc + ahead[x * 8 : x * 8 + 8])
        put(ez_s, 2 * x + 1, base_visc + behind[x * 8 : x * 8 + 8])

    def plane_of(c, x):
        if x < 0:
            return vx_s[c, x + 2]
        if x > 15:
            return vx_s[c, x - 14]
        return vel[c, x]

    for x in range(16):
        vat = (x + 1) * 32
        visc = visc_s[vat + 8 : vat + 24, :]
        faces = (
            (visc_s[vat + 40 : vat + 56, :], visc_s[vat - 24 : vat - 8, :]),
            (visc_s[vat + 9 : vat + 25, :], visc_s[vat + 7 : vat + 23, :]),
            (
                ez_s[(x // 2 * 2) * 32 + 8 : (x // 2 * 2) * 32 + 24, :],
                ez_s[(x // 2 * 2 + 1) * 32 + 8 : (x // 2 * 2 + 1) * 32 + 24, :],
            ),
        )
        faces = [(0.5 * (visc + a), 0.5 * (visc + b)) for a, b in faces]
        wind = [vel[a, x] for a in range(3)]
        for c in range(3):
            u = vel[c, x]
            at = (c * 16 + x) * 32
            zat = (c * 16 + x) * 16
            zc = zcols[zat : zat + 16]
            p1 = jnp.where(lane == 127, zc[:, 0:1], pltpu.roll(u, 127, 1))
            p2 = jnp.where(lane == 127, zc[:, 1:2], jnp.where(lane == 126, zc[:, 0:1], pltpu.roll(u, 126, 1)))
            m1 = jnp.where(lane == 0, zc[:, 3:4], pltpu.roll(u, 1, 1))
            m2 = jnp.where(lane == 0, zc[:, 2:3], jnp.where(lane == 1, zc[:, 3:4], pltpu.roll(u, 2, 1)))
            near = (
                (plane_of(c, x + 1), plane_of(c, x - 1), plane_of(c, x + 2), plane_of(c, x - 2)),
                (
                    vy_s[at + 9 : at + 25, :], vy_s[at + 7 : at + 23, :],
                    vy_s[at + 10 : at + 26, :], vy_s[at + 6 : at + 22, :],
                ),
                (p1, m1, p2, m2),
            )
            advect = None
            diffuse = None
            for a in range(3):
                q1, b1, q2, b2 = near[a]
                slope = (8.0 * (q1 - b1) - (q2 - b2)) * (1.0 / 12.0)
                term = wind[a] * slope
                advect = term if advect is None else advect + term
                flux = faces[a][0] * (q1 - u) - faces[a][1] * (u - b1)
                diffuse = flux if diffuse is None else diffuse + flux
            out[c, x] = u + time_step * (diffuse - advect)


def run_flow(scal, velocity, eddy, *got):
    return pl.pallas_call(
        flow_kernel,
        out_shape=jax.ShapeDtypeStruct(velocity.shape, F32),
        in_specs=[pl.BlockSpec(memory_space=pltpu.SMEM)] + [vmem_spec()] * 7,
        out_specs=vmem_spec(),
        scratch_shapes=[
            pltpu.VMEM((104, 128), F32),
            pltpu.VMEM((104, 128), F32),
            pltpu.VMEM((104, 128), F32),
            pltpu.VMEM((104, 128), F32),
            pltpu.VMEM((104, 128), F32),
            pltpu.VMEM((3, 4, 16, 128), F32),
            pltpu.VMEM((3 * 16 * 32, 128), F32),
            pltpu.VMEM((18 * 32, 128), F32),
            pltpu.VMEM((16 * 32, 128), F32),
        ],
        compiler_params=pltpu.CompilerParams(vmem_limit_bytes=32 * 1024 * 1024),
        name="flow",
    )(scal, velocity, eddy, *got)


def finish_kernel(scal, own, blk, mine, other, loss_out, first_out, hidden_out, last_out, ext_s):
    second = scal[0, 3] == 1
    for t in range(PAY // 128):
        one, two = mine[t * 32 : (t + 1) * 32, :], other[t * 32 : (t + 1) * 32, :]
        top, bottom = jnp.where(second, two, one), jnp.where(second, one, two)
        if t == 0:
            ext_s[0:32, :] = top
            ext_s[32:64, :] = bottom
        else:
            at = (t - 1) * 128
            width = min(128, 27 * CH - at)
            hidden_out[0:32, at : at + width] = top[:, :width]
            hidden_out[32:64, at : at + width] = bottom[:, :width]
    extra = ext_s[...]
    first_out[...] = extra[:, 0:81]
    turned = jnp.transpose(jnp.concatenate([extra, jnp.zeros((64, 128), F32)], axis=0))
    last_out[...] = turned[LAST_COL : LAST_COL + 1, 0:64]
    slots = loss_out.shape[1]
    lane = iota((1, 128), 1)
    slot_lane = iota((1, slots), 1)
    picked = jnp.zeros((1, slots), F32)
    for s in range(slots):
        at = scal[0, 1] * slots + s
        dev = own[0, at] * scal[0, 5] + scal[0, 6]
        row = ext_s[pl.ds(dev % 64, 1), :]
        col = LOSS_COL + BLK * (dev // 64) + blk[0, at]
        value = jnp.sum(jnp.where(lane == col, row, 0.0), axis=1, keepdims=True)
        picked = jnp.where(slot_lane == s, value, picked)
    loss_out[...] = picked


def run_finish(scal, own, blk, mine, other, slots):
    smem = pl.BlockSpec(memory_space=pltpu.SMEM)
    f = lambda *s: jax.ShapeDtypeStruct(s, F32)
    return pl.pallas_call(
        finish_kernel,
        out_shape=(f(1, slots), f(64, 81), f(64, 27 * CH), f(1, 64)),
        in_specs=[smem] * 3 + [vmem_spec()] * 2,
        out_specs=tuple(vmem_spec() for _ in range(4)),
        scratch_shapes=[pltpu.VMEM((64, 128), F32)],
        compiler_params=pltpu.CompilerParams(vmem_limit_bytes=32 * 1024 * 1024),
        name="finish",
    )(scal, own, blk, mine, other)


def on_device(velocity, target_visc, w_first, w_hidden, w_last, sample_owner, sample_block):
    n_x, n_y, n_z = lax.axis_size("gx"), lax.axis_size("gy"), lax.axis_size("role")
    trainers = n_x * n_y * n_z
    at_x, at_y, at_z = lax.axis_index("gx"), lax.axis_index("gy"), lax.axis_index("role")
    group = at_y * n_z + at_z
    half = (at_y ^ (at_y >> 1)) & 1
    scal = jnp.stack(
        [jnp.int32(trainers), at_x, at_y, half, at_x * (n_y * n_z) + group, jnp.int32(n_y * n_z), group, jnp.int32(0)]
    ).astype(jnp.int32)[None]
    own = sample_owner.reshape(1, -1)
    blk = sample_block.reshape(1, -1)
    slots = own.shape[1] // n_x

    axes = ("gx", "gy", "role")

    def even_odd(i, count):
        return i ^ 1

    def odd_even(i, count):
        return (i - 1) % count if i % 2 == 0 else (i + 1) % count

    def partner(kind, i, j, r):
        if kind == "x":
            j = odd_even(j, n_y)
        elif kind == "y":
            r = r ^ 1
        elif kind == "z_a":
            i = even_odd(i, n_x)
        else:
            i = odd_even(i, n_x)
        return (i * n_y + j) * n_z + r

    def mixed(kinds):
        pairs = []
        for i in range(n_x):
            for j in range(n_y):
                for r in range(n_z):
                    pairs.append(((i * n_y + j) * n_z + r, partner(kinds[(j ^ (j >> 1)) & 1], i, j, r)))
        return pairs

    core_pairs = [(j, even_odd(j, n_y)) for j in range(n_y)]
    size = PAY // 4

    keep, send, eddy, *halos = run_net(
        scal, velocity, target_visc, w_first, w_hidden, w_last.reshape(1, CH), own, blk
    )
    got = lax.ppermute(send, "gy", core_pairs)
    total = keep + got[:size]
    rims = [got[size:]]
    orders = (("x", "y", "z_a", "z_b"), ("z_a", "x", "z_b", "y"))
    for s in range(4):
        kinds = (orders[0][s], orders[1][s])
        got = lax.ppermute(jnp.concatenate([total, halos[s]], axis=0), axes, mixed(kinds))
        part = got[:size]
        if n_x != 4 and "z_b" in kinds:
            part = jnp.where(half == kinds.index("z_b"), 0.0, part)
        total = total + part
        rims.append(got[size:])
    if n_x != 4:
        for bit in range(1, n_x.bit_length() - 1):
            total = total + lax.ppermute(total, "gx", [(i, i ^ (1 << bit)) for i in range(n_x)])
    other = lax.ppermute(total, "gy", core_pairs)

    u_next = run_flow(scal, velocity, eddy, *rims)
    losses, first, hidden, last = run_finish(scal, own, blk, total, other, slots)
    return (u_next, losses.reshape(1, 1, slots), first, hidden, last.reshape(CH))


def solution(mesh):
    return jax.shard_map(
        on_device,
        mesh=mesh,
        in_specs=(
            P(None, "gx", "gy", "role"),
            P("gx", "gy", "role"),
            P(),
            P(),
            P(),
            P("gy", "role", None, None),
            P("gy", "role", None, None),
        ),
        out_specs=(P(None, "gx", "gy", "role"), P("gy", "role", "gx"), P(), P(), P()),
        check_vma=False,
    )
```

```python
import jax
import jax.numpy as jnp
from jax import lax
from jax.experimental import pallas as pl
from jax.experimental.pallas import tpu as pltpu
from jax.sharding import PartitionSpec as P

F32 = jnp.float32
BF16 = jnp.bfloat16
HIGH = lax.Precision.HIGHEST

SIDE = 8
CELLS = SIDE**3
CH = 64
BLK = 8
ROWS = SIDE * SIDE * BLK
WIDE = SIDE * CH
SLAB = SIDE * BLK
PAY_ROWS = 15 * 64
PAY_PAD = 1024
LAST_COL = 81
LOSS_COL = 82

base_visc = 0.02
time_step = 0.2


def iota(shape, dim):
    return lax.broadcasted_iota(jnp.int32, shape, dim)


def onehot(cond, dtype=BF16):
    return jnp.where(cond, 1.0, 0.0).astype(dtype)


def nt(a, b, precision=None):
    return lax.dot_general(a, b, (((1,), (1,)), ((), ())), preferred_element_type=F32, precision=precision)


def tn(a, b, precision=None):
    return lax.dot_general(a, b, (((0,), (0,)), ((), ())), preferred_element_type=F32, precision=precision)


def nn(a, b, precision=None):
    return lax.dot_general(a, b, (((1,), (0,)), ((), ())), preferred_element_type=F32, precision=precision)


def net_kernel(
    scal, vel, tgt, w1, w2, w3, own, blk,
    pay, eddy_out, hx_a, hx_b, hy_a, hy_b, hz,
    pool_s, fp_s, i1_s, a_s, d_s, tt_s, tb_s, pre_s, slope1_s, ah_s, slope2_s, dw_s, big_s, gh_s,
):
    trainers = scal[0, 0]
    gx_at = scal[0, 1]
    gy_at = scal[0, 2]
    half = scal[0, 3]
    dev = scal[0, 4]
    gx_odd = gx_at % 2 == 1
    gy_odd = gy_at % 2 == 1

    for c in range(3):
        for x in range(SIDE):
            both = vel[c, 2 * x] + vel[c, 2 * x + 1]
            pool_s[c, x] = both
    rows = []
    for c in range(3):
        cols = []
        for x in range(SIDE):
            cols.append(pool_s[c, x, pl.ds(0, 8, stride=2), :] + pool_s[c, x, pl.ds(1, 8, stride=2), :])
        rows.append(jnp.concatenate(cols, axis=0))
    pooled = jnp.concatenate(rows, axis=0)
    zpool = jnp.where(iota((128, 1), 0) >> 1 == iota((1, 64), 1), 0.125, 0.0)
    filt = nn(pooled, zpool, HIGH).astype(BF16)
    tgt_rows = tgt[...].reshape(64, 64)
    zsel = jnp.concatenate([filt[0:64], filt[64:128], filt[128:192], tgt_rows], axis=1)
    spread = onehot(iota((ROWS, 1), 0) >> 3 == iota((1, 64), 1))
    by_block = nn(spread, zsel)
    mine = (iota((1, 256), 1) & 63) >> 3 == iota((ROWS, 1), 0) & 7
    by_block = jnp.where(mine, by_block, 0.0).astype(BF16)
    lane_in = iota((1, 256), 1)
    lane_off = lax.div(lane_in, 24)
    lane_cz = lane_in - lane_off * 24
    src = iota((256, 1), 0)
    pick = onehot(jnp.where(lane_in < 216, lane_cz, -1) == (src >> 6) * 8 + (src & 7))
    cells = nn(by_block, pick)
    pick_t = onehot(jnp.where(src >= 192, src & 7, -1) == iota((1, SIDE), 1))
    target = nn(by_block, pick_t)

    fp_s[...] = jnp.zeros(fp_s.shape, F32)
    fp_s[1:9, 1:9] = cells.reshape(SIDE, SIDE, BLK, 256)
    group = lax.div(iota((1, 1, 1, 256), 3), 24)
    for x in range(SIDE):
        acc = jnp.zeros((1, SIDE, BLK, 256), F32)
        for k in range(9):
            part = fp_s[x + k // 3 : x + k // 3 + 1, k % 3 : k % 3 + SIDE]
            acc = jnp.where(group == k, part, acc)
        i1_s[x * SLAB : (x + 1) * SLAB, :] = acc.reshape(SLAB, 256).astype(BF16)

    j_at = iota((81, 1), 0)
    j_off, j_dz, j_c = lax.div(j_at, 9), lax.rem(lax.div(j_at, 3), 3) - 1, lax.rem(j_at, 3)
    lane_key = jnp.where(lane_in < 216, lane_off * 4 + (lane_cz >> 3), -1)
    same = lane_key == j_off * 4 + j_c
    delta = jnp.where(same, (lane_in & 7) - j_dz, -9)
    w1v = w1[...]
    t1 = jnp.concatenate([nn(w1v, onehot(delta == z)).astype(BF16) for z in range(SIDE)], axis=0)
    pre_s[...] = nt(i1_s[...], t1)

    src = iota((320, 1), 0) - 64
    dst = iota((1, 512), 1)
    wanted = ((dst >> 7) - 2 + ((dst & 127) >> 6)) * 64 + (dst & 63)
    chooser = onehot(jnp.where((src >= 0) & (src < 192), src - 64, -999) == wanted)
    zero_tile = jnp.zeros((64, 128), BF16)
    for k in range(9):
        base = (192 * k) // 128 * 128
        off = 192 * k - base
        width = min(256, 1728 - base)
        tiles = nn(w2[:, base : base + width], chooser[64 - off : 64 - off + width]).astype(BF16)
        ks, js = k // 3, k % 3
        kb, jb = (8 - k) // 3, (8 - k) % 3
        for z in range(SIDE):
            for m in range(4):
                d = 2 * m - z
                tile = tiles[:, (d + 2) * 128 : (d + 3) * 128] if -2 <= d <= 1 else zero_tile
                tt_s[ks, z * 64 : (z + 1) * 64, js * 512 + m * 128 : js * 512 + (m + 1) * 128] = tile
                tb_s[kb, jb * 512 + z * 64 : jb * 512 + (z + 1) * 64, m * 128 : (m + 1) * 128] = tile

    def shifted_store(dst_ref, x, val):
        zero = jnp.zeros((1, BLK, WIDE), F32)
        lo, hi = (x + 1) * SLAB, (x + 2) * SLAB
        dst_ref[lo:hi, 0:512] = jnp.concatenate([zero, val[:-1]], axis=0).reshape(SLAB, WIDE).astype(BF16)
        dst_ref[lo:hi, 512:1024] = val.reshape(SLAB, WIDE).astype(BF16)
        dst_ref[lo:hi, 1024:1536] = jnp.concatenate([val[1:], zero], axis=0).reshape(SLAB, WIDE).astype(BF16)

    for ref in (a_s, d_s):
        ref[0:SLAB, :] = jnp.zeros((SLAB, 1536), BF16)
        ref[9 * SLAB :, :] = jnp.zeros((SLAB, 1536), BF16)

    for x in range(SIDE):
        pre = pre_s[x * SLAB : (x + 1) * SLAB, :]
        sig = jax.nn.sigmoid(pre)
        slope1_s[x * SLAB : (x + 1) * SLAB, :] = sig * (1.0 + pre * (1.0 - sig))
        shifted_store(a_s, x, (pre * sig).reshape(SIDE, BLK, WIDE))

    acc = nt(a_s[0:ROWS, :], tt_s[0])
    acc = acc + nt(a_s[SLAB : SLAB + ROWS, :], tt_s[1])
    pre_s[...] = acc + nt(a_s[2 * SLAB : 2 * SLAB + ROWS, :], tt_s[2])
    for x in range(SIDE):
        pre = pre_s[x * SLAB : (x + 1) * SLAB, :]
        sig = jax.nn.sigmoid(pre)
        slope2_s[x * SLAB : (x + 1) * SLAB, :] = sig * (1.0 + pre * (1.0 - sig))
        ah_s[x * SLAB : (x + 1) * SLAB, :] = (pre * sig).astype(BF16)

    tile8 = onehot(iota((64, 1), 0) == iota((1, WIDE), 1) & 63)
    w3_wide = nn(w3[...], tile8)
    diag = iota((1, WIDE), 1) >> 6 == iota((SIDE, 1), 0)
    last = jnp.where(diag, w3_wide, 0.0).astype(BF16)
    logits = nt(ah_s[...], last)
    eddy = 0.5 * (jnp.maximum(logits, 0.0) + jnp.log1p(jnp.exp(-jnp.abs(logits))))
    error = eddy - target
    losses = jnp.sum(jnp.sum((error * error).reshape(64, BLK, SIDE), axis=0), axis=1, keepdims=True) / CELLS
    d_logit = (error * jax.nn.sigmoid(logits) / (trainers.astype(F32) * CELLS)).astype(BF16)

    zrep = onehot(iota((SIDE, 1), 0) == (iota((1, 128), 1) & 15) >> 1, F32)
    fine = nn(eddy, zrep, HIGH)
    fine = jnp.where(iota((1, 128), 1) >> 4 == iota((ROWS, 1), 0) & 7, fine, 0.0)
    fine = jnp.sum(fine.reshape(64, BLK, 128), axis=1)
    eddy_out[...] = fine

    for c in range(3):
        for i in range(2):
            lo, hi = vel[c, i], vel[c, 14 + i]
            at = (c * 2 + i) * 16
            hx_a[at : at + 16, :] = jnp.where(gx_odd, lo, hi)
            hx_b[at : at + 16, :] = jnp.where(gx_odd, hi, lo)
    hx_a[96:104, :] = jnp.where(gx_odd, fine[0:8], fine[56:64])
    hx_b[96:104, :] = jnp.where(gx_odd, fine[56:64], fine[0:8])
    for c in range(3):
        for i in range(2):
            lo = jnp.concatenate([vel[c, x, i : i + 1, :] for x in range(16)], axis=0)
            hi = jnp.concatenate([vel[c, x, 14 + i : 15 + i, :] for x in range(16)], axis=0)
            at = (c * 2 + i) * 16
            hy_a[at : at + 16, :] = jnp.where(gy_odd, lo, hi)
            hy_b[at : at + 16, :] = jnp.where(gy_odd, hi, lo)
    lo = eddy_out[pl.ds(0, 8, stride=8), :]
    hi = eddy_out[pl.ds(7, 8, stride=8), :]
    hy_a[96:104, :] = jnp.where(gy_odd, lo, hi)
    hy_b[96:104, :] = jnp.where(gy_odd, hi, lo)
    vt = jnp.transpose(vel[...].reshape(768, 128))
    et = jnp.transpose(jnp.concatenate([fine, jnp.zeros((64, 128), F32)], axis=0))
    hz[...] = jnp.zeros(hz.shape, F32)
    for t in range(6):
        hz[t * 8 : t * 8 + 2, :] = vt[0:2, t * 128 : (t + 1) * 128]
        hz[t * 8 + 2 : t * 8 + 4, :] = vt[126:128, t * 128 : (t + 1) * 128]
    hz[48:49, :] = et[0:1]
    hz[49:50, :] = et[127:128]

    code = own[...] * BLK + blk[...]
    listed = code.shape[1]
    wanted = gx_at * BLK + iota((BLK, listed), 0)
    count = jnp.sum(jnp.where(code == wanted, 1.0, 0.0), axis=1, keepdims=True)
    count_rows = jnp.broadcast_to(count.reshape(1, BLK, 1), (64, BLK, 1)).reshape(ROWS, 1)

    big_s[:, 0:512] = nn(d_logit, last)
    for x in range(SIDE):
        d_hid = big_s[x * SLAB : (x + 1) * SLAB, 0:512] * slope2_s[x * SLAB : (x + 1) * SLAB, :]
        d_hid = d_hid.astype(BF16).astype(F32).reshape(SIDE, BLK, WIDE)
        shifted_store(d_s, x, d_hid)
        dw_s[x * SLAB : (x + 1) * SLAB, :] = (d_hid * count[None]).reshape(SLAB, WIDE)
    dwt = jnp.transpose(dw_s[...]).astype(BF16)

    gh_s[...] = jnp.zeros(gh_s.shape, F32)
    low_half = iota((64, 128), 1) < 64
    for k in range(9):
        dx, j = k // 3, k % 3
        big_s[:, 0:512] = nn(dwt, a_s[dx * SLAB : dx * SLAB + ROWS, j * 512 : (j + 1) * 512])
        sums = []
        for m in (-1, 0, 1, 2):
            tot = None
            for p in range(4):
                z = 2 * p + m
                if 0 <= z < SIDE:
                    part = big_s[z * 64 : (z + 1) * 64, p * 128 : (p + 1) * 128]
                    tot = part if tot is None else tot + part
            sums.append(tot)
        for dz in (-1, 0, 1):
            low, high = sums[1 - dz], sums[2 - dz]
            at = (k * 3 + dz + 1) * 64
            tile, odd = at // 128 * 128, at % 128 != 0
            if odd:
                val = high + pltpu.roll(low, 64, 1)
                gh_s[:, tile : tile + 128] += jnp.where(low_half, 0.0, val)
            else:
                val = low + pltpu.roll(high, 64, 1)
                gh_s[:, tile : tile + 128] += jnp.where(low_half, val, 0.0)

    acc = nn(d_s[0:ROWS, :], tb_s[0])
    acc = acc + nn(d_s[SLAB : SLAB + ROWS, :], tb_s[1])
    acc = acc + nn(d_s[2 * SLAB : 2 * SLAB + ROWS, :], tb_s[2])
    d_first = (acc * slope1_s[...]).astype(BF16).astype(F32)
    dw_s[...] = (d_first.reshape(64, BLK, WIDE) * count[None]).reshape(ROWS, WIDE)
    d1t = jnp.transpose(dw_s[...])
    d1_hi = d1t.astype(BF16)
    d1_lo = (d1t - d1_hi.astype(F32)).astype(BF16)
    i1 = i1_s[...]
    g1 = nn(d1_hi, i1) + nn(d1_lo, i1)
    z_in = iota((1, 256), 1) & 7
    parts = []
    for dz in (-1, 0, 1):
        tot = jnp.zeros((64, 256), F32)
        for z in range(SIDE):
            if 0 <= z + dz < SIDE:
                tot = tot + jnp.where(z_in == z + dz, g1[z * 64 : (z + 1) * 64], 0.0)
        parts.append(tot)
    r_at = iota((768, 1), 0)
    c_at = iota((1, 128), 1)
    r_lane = r_at & 255
    r_off = lax.div(r_lane, 24)
    r_col = (r_off * 3 + (r_at >> 8)) * 3 + ((r_lane - r_off * 24) >> 3)
    fold = onehot(jnp.where(r_lane < 216, r_col, -1) == c_at, F32)
    g_first = nn(jnp.concatenate(parts, axis=1), fold, HIGH)

    dlw = d_logit.astype(F32) * count_rows
    dl_hi = dlw.astype(BF16)
    dl_lo = (dlw - dl_hi.astype(F32)).astype(BF16)
    ah = ah_s[...]
    gl = tn(dl_hi, ah) + tn(dl_lo, ah)
    gl = jnp.where(diag, gl, 0.0)
    fold_o = onehot(iota((1, WIDE), 1) & 63 == iota((64, 1), 0), F32)
    g_last = jnp.sum(nt(fold_o, gl, HIGH), axis=1, keepdims=True)

    lane8 = iota((BLK, 128), 1)
    loss_row = jnp.where(lane8 - (LOSS_COL + BLK * (dev // 64)) == iota((BLK, 128), 0), losses, 0.0)
    loss_row = jnp.sum(loss_row, axis=0, keepdims=True)
    lane = iota((64, 128), 1)
    extra = jnp.where(lane == LAST_COL, g_last, g_first)
    extra = extra + jnp.where(iota((64, 128), 0) == dev % 64, loss_row, 0.0)

    pay[0:64, :] = extra
    for t in range(14):
        pay[(t + 1) * 64 : (t + 2) * 64, :] = gh_s[:, t * 128 : (t + 1) * 128]
    pay[PAY_ROWS:, :] = jnp.zeros((PAY_PAD - PAY_ROWS, 128), F32)


def vmem_spec():
    return pl.BlockSpec(memory_space=pltpu.VMEM)


def run_net(scal, velocity, target, w1, w2, w3, own, blk):
    f = lambda *s: jax.ShapeDtypeStruct(s, F32)
    return pl.pallas_call(
        net_kernel,
        out_shape=(f(PAY_PAD, 128), f(64, 128)) + (f(104, 128),) * 5,
        in_specs=[pl.BlockSpec(memory_space=pltpu.SMEM)] + [vmem_spec()] * 7,
        out_specs=tuple(vmem_spec() for _ in range(7)),
        scratch_shapes=[
            pltpu.VMEM((3, SIDE, 16, 128), F32),
            pltpu.VMEM((10, 10, BLK, 256), F32),
            pltpu.VMEM((ROWS, 256), BF16),
            pltpu.VMEM((ROWS + 2 * SLAB, 1536), BF16),
            pltpu.VMEM((ROWS + 2 * SLAB, 1536), BF16),
            pltpu.VMEM((3, 512, 1536), BF16),
            pltpu.VMEM((3, 1536, 512), BF16),
            pltpu.VMEM((ROWS, WIDE), F32),
            pltpu.VMEM((ROWS, WIDE), F32),
            pltpu.VMEM((ROWS, WIDE), BF16),
            pltpu.VMEM((ROWS, WIDE), F32),
            pltpu.VMEM((ROWS, WIDE), F32),
            pltpu.VMEM((ROWS, WIDE), F32),
            pltpu.VMEM((64, 14 * 128), F32),
        ],
        compiler_params=pltpu.CompilerParams(vmem_limit_bytes=56 * 1024 * 1024),
        name="net",
    )(scal, velocity, target, w1, w2, w3, own, blk)


def flow_kernel(
    scal, vel, eddy, rx_a, rx_b, ry_a, ry_b, rz, out, vx_s, vy_s, visc_s, ez_s
):
    gx_odd = scal[0, 1] % 2 == 1
    gy_odd = scal[0, 2] % 2 == 1
    lane = iota((1, 128), 1)

    def sides(odd, a, b, at, rows):
        one, two = a[at : at + rows, :], b[at : at + rows, :]
        return jnp.where(odd, one, two), jnp.where(odd, two, one)

    for c in range(3):
        for x in range(16):
            vy_s[(c * 16 + x) * 32 + 8 : (c * 16 + x) * 32 + 24, :] = vel[c, x]
        for i in range(2):
            below, above = sides(gy_odd, ry_a, ry_b, (c * 2 + i) * 16, 16)
            vy_s[pl.ds(c * 512 + 6 + i, 16, stride=32), :] = below
            vy_s[pl.ds(c * 512 + 24 + i, 16, stride=32), :] = above
            below, above = sides(gx_odd, rx_a, rx_b, (c * 2 + i) * 16, 16)
            vx_s[c, i] = below
            vx_s[c, 2 + i] = above

    zcols = jnp.concatenate([jnp.transpose(rz[t * 8 : t * 8 + 8, :]) for t in range(7)], axis=0)
    coarse = eddy[...]
    e_first, e_last = zcols[768:832, 0:1], zcols[768:832, 1:2]
    ahead = jnp.where(lane == 127, e_first, pltpu.roll(coarse, 127, 1))
    behind = jnp.where(lane == 0, e_last, pltpu.roll(coarse, 1, 1))
    below_x, above_x = sides(gx_odd, rx_a, rx_b, 96, 8)
    below_y, above_y = sides(gy_odd, ry_a, ry_b, 96, 8)

    def put(dst, plane, val):
        dst[pl.ds(plane * 32 + 8, 8, stride=2), :] = val
        dst[pl.ds(plane * 32 + 9, 8, stride=2), :] = val

    put(visc_s, 0, base_visc + below_x)
    put(visc_s, 17, base_visc + above_x)
    for x in range(8):
        for r in range(2):
            plane = 2 * x + 1 + r
            put(visc_s, plane, base_visc + coarse[x * 8 : x * 8 + 8])
            visc_s[plane * 32 + 7 : plane * 32 + 8, :] = base_visc + below_y[x : x + 1]
            visc_s[plane * 32 + 24 : plane * 32 + 25, :] = base_visc + above_y[x : x + 1]
        put(ez_s, 2 * x, base_visc + ahead[x * 8 : x * 8 + 8])
        put(ez_s, 2 * x + 1, base_visc + behind[x * 8 : x * 8 + 8])

    def plane_of(c, x):
        if x < 0:
            return vx_s[c, x + 2]
        if x > 15:
            return vx_s[c, x - 14]
        return vel[c, x]

    for x in range(16):
        vat = (x + 1) * 32
        visc = visc_s[vat + 8 : vat + 24, :]
        faces = (
            (visc_s[vat + 40 : vat + 56, :], visc_s[vat - 24 : vat - 8, :]),
            (visc_s[vat + 9 : vat + 25, :], visc_s[vat + 7 : vat + 23, :]),
            (
                ez_s[(x // 2 * 2) * 32 + 8 : (x // 2 * 2) * 32 + 24, :],
                ez_s[(x // 2 * 2 + 1) * 32 + 8 : (x // 2 * 2 + 1) * 32 + 24, :],
            ),
        )
        faces = [(0.5 * (visc + a), 0.5 * (visc + b)) for a, b in faces]
        wind = [vel[a, x] for a in range(3)]
        for c in range(3):
            u = vel[c, x]
            at = (c * 16 + x) * 32
            zat = (c * 16 + x) * 16
            zc = zcols[zat : zat + 16]
            p1 = jnp.where(lane == 127, zc[:, 0:1], pltpu.roll(u, 127, 1))
            p2 = jnp.where(lane == 127, zc[:, 1:2], jnp.where(lane == 126, zc[:, 0:1], pltpu.roll(u, 126, 1)))
            m1 = jnp.where(lane == 0, zc[:, 3:4], pltpu.roll(u, 1, 1))
            m2 = jnp.where(lane == 0, zc[:, 2:3], jnp.where(lane == 1, zc[:, 3:4], pltpu.roll(u, 2, 1)))
            near = (
                (plane_of(c, x + 1), plane_of(c, x - 1), plane_of(c, x + 2), plane_of(c, x - 2)),
                (
                    vy_s[at + 9 : at + 25, :], vy_s[at + 7 : at + 23, :],
                    vy_s[at + 10 : at + 26, :], vy_s[at + 6 : at + 22, :],
                ),
                (p1, m1, p2, m2),
            )
            advect = None
            diffuse = None
            for a in range(3):
                q1, b1, q2, b2 = near[a]
                slope = (8.0 * (q1 - b1) - (q2 - b2)) * (1.0 / 12.0)
                term = wind[a] * slope
                advect = term if advect is None else advect + term
                flux = faces[a][0] * (q1 - u) - faces[a][1] * (u - b1)
                diffuse = flux if diffuse is None else diffuse + flux
            out[c, x] = u + time_step * (diffuse - advect)


def run_flow(scal, velocity, eddy, *got):
    return pl.pallas_call(
        flow_kernel,
        out_shape=jax.ShapeDtypeStruct(velocity.shape, F32),
        in_specs=[pl.BlockSpec(memory_space=pltpu.SMEM)] + [vmem_spec()] * 7,
        out_specs=vmem_spec(),
        scratch_shapes=[
            pltpu.VMEM((3, 4, 16, 128), F32),
            pltpu.VMEM((3 * 16 * 32, 128), F32),
            pltpu.VMEM((18 * 32, 128), F32),
            pltpu.VMEM((16 * 32, 128), F32),
        ],
        compiler_params=pltpu.CompilerParams(vmem_limit_bytes=32 * 1024 * 1024),
        name="flow",
    )(scal, velocity, eddy, *got)


def finish_kernel(scal, own, blk, total, loss_out, first_out, hidden_out, last_out, ext_s):
    ext_s[...] = total[0:64, :]
    for t in range(14):
        width = min(128, 27 * CH - t * 128)
        hidden_out[:, t * 128 : t * 128 + width] = total[(t + 1) * 64 : (t + 2) * 64, :width]
    extra = ext_s[...]
    first_out[...] = extra[:, 0:81]
    turned = jnp.transpose(jnp.concatenate([extra, jnp.zeros((64, 128), F32)], axis=0))
    last_out[...] = turned[LAST_COL : LAST_COL + 1, 0:64]
    slots = loss_out.shape[1]
    lane = iota((1, 128), 1)
    slot_lane = iota((1, slots), 1)
    picked = jnp.zeros((1, slots), F32)
    for s in range(slots):
        at = scal[0, 1] * slots + s
        dev = own[0, at] * scal[0, 5] + scal[0, 6]
        row = ext_s[pl.ds(dev % 64, 1), :]
        col = LOSS_COL + BLK * (dev // 64) + blk[0, at]
        value = jnp.sum(jnp.where(lane == col, row, 0.0), axis=1, keepdims=True)
        picked = jnp.where(slot_lane == s, value, picked)
    loss_out[...] = picked


def run_finish(scal, own, blk, total, slots):
    smem = pl.BlockSpec(memory_space=pltpu.SMEM)
    f = lambda *s: jax.ShapeDtypeStruct(s, F32)
    return pl.pallas_call(
        finish_kernel,
        out_shape=(f(1, slots), f(64, 81), f(64, 27 * CH), f(1, 64)),
        in_specs=[smem] * 3 + [vmem_spec()],
        out_specs=tuple(vmem_spec() for _ in range(4)),
        scratch_shapes=[pltpu.VMEM((64, 128), F32)],
        compiler_params=pltpu.CompilerParams(vmem_limit_bytes=32 * 1024 * 1024),
        name="finish",
    )(scal, own, blk, total)


def on_device(velocity, target_visc, w_first, w_hidden, w_last, sample_owner, sample_block):
    n_x, n_y, n_z = lax.axis_size("gx"), lax.axis_size("gy"), lax.axis_size("role")
    trainers = n_x * n_y * n_z
    at_x, at_y, at_z = lax.axis_index("gx"), lax.axis_index("gy"), lax.axis_index("role")
    group = at_y * n_z + at_z
    half = (at_y ^ (at_y >> 1)) & 1
    scal = jnp.stack(
        [jnp.int32(trainers), at_x, at_y, half, at_x * (n_y * n_z) + group, jnp.int32(n_y * n_z), group, jnp.int32(0)]
    ).astype(jnp.int32)[None]
    own = sample_owner.reshape(1, -1)
    blk = sample_block.reshape(1, -1)
    slots = own.shape[1] // n_x

    axes = ("gx", "gy", "role")

    def even_odd(count):
        return [(i, i ^ 1) for i in range(count)]

    def odd_even(count):
        return [(i, (i - 1) % count if i % 2 == 0 else (i + 1) % count) for i in range(count)]

    pay, eddy, hx_a, hx_b, hy_a, hy_b, hz = run_net(
        scal, velocity, target_visc, w_first, w_hidden, w_last.reshape(1, CH), own, blk
    )
    rims = [
        lax.ppermute(hx_a, "gx", even_odd(n_x)),
        lax.ppermute(hx_b, "gx", odd_even(n_x)),
        lax.ppermute(hy_a, "gy", even_odd(n_y)),
        lax.ppermute(hy_b, "gy", odd_even(n_y)),
        lax.ppermute(hz, "role", even_odd(n_z)),
    ]
    if trainers <= PAY_PAD // 8:
        parts = lax.all_to_all(pay.reshape(trainers, PAY_PAD // trainers, 128), axes, 0, 0)
        mine = jnp.sum(parts, axis=0)
        total = lax.all_to_all(jnp.broadcast_to(mine[None], parts.shape), axes, 0, 0).reshape(PAY_PAD, 128)
    else:
        total = lax.psum(pay, axes)

    u_next = run_flow(scal, velocity, eddy, *rims)
    losses, first, hidden, last = run_finish(scal, own, blk, total, slots)
    return (u_next, losses.reshape(1, 1, slots), first, hidden, last.reshape(CH))


def solution(mesh):
    return jax.shard_map(
        on_device,
        mesh=mesh,
        in_specs=(
            P(None, "gx", "gy", "role"),
            P("gx", "gy", "role"),
            P(),
            P(),
            P(),
            P("gy", "role", None, None),
            P("gy", "role", None, None),
        ),
        out_specs=(P(None, "gx", "gy", "role"), P("gy", "role", "gx"), P(), P(), P()),
        check_vma=False,
    )
```

```python
import jax
import jax.numpy as jnp
from jax import lax
from jax.experimental import pallas as pl
from jax.experimental.pallas import tpu as pltpu
from jax.sharding import PartitionSpec as P

F32 = jnp.float32
BF16 = jnp.bfloat16
HIGH = lax.Precision.HIGHEST

SIDE = 8
CELLS = SIDE**3
CH = 64
BLK = 8
ROWS = SIDE * SIDE * BLK
WIDE = SIDE * CH
SLAB = SIDE * BLK
TILES = 15
HALF = 512
LAST_COL = 81
LOSS_COL = 82

base_visc = 0.02
time_step = 0.2


def iota(shape, dim):
    return lax.broadcasted_iota(jnp.int32, shape, dim)


def onehot(cond, dtype=BF16):
    return jnp.where(cond, 1.0, 0.0).astype(dtype)


def nt(a, b, precision=None):
    return lax.dot_general(a, b, (((1,), (1,)), ((), ())), preferred_element_type=F32, precision=precision)


def tn(a, b, precision=None):
    return lax.dot_general(a, b, (((0,), (0,)), ((), ())), preferred_element_type=F32, precision=precision)


def nn(a, b, precision=None):
    return lax.dot_general(a, b, (((1,), (0,)), ((), ())), preferred_element_type=F32, precision=precision)


def net_kernel(
    scal, vel, tgt, w1, w2, w3, own, blk,
    keep, send, eddy_out, hx_a, hx_b, hy_a, hy_b, hz,
    pool_s, fp_s, i1_s, a_s, d_s, tt_s, tb_s, pre_s, slope1_s, ah_s, slope2_s, dw_s, big_s, gh_s,
):
    trainers = scal[0, 0]
    gx_at = scal[0, 1]
    gy_at = scal[0, 2]
    half = scal[0, 3]
    dev = scal[0, 4]
    gx_odd = gx_at % 2 == 1
    gy_odd = gy_at % 2 == 1

    for c in range(3):
        for x in range(SIDE):
            both = vel[c, 2 * x] + vel[c, 2 * x + 1]
            pool_s[c, x] = both
    rows = []
    for c in range(3):
        cols = []
        for x in range(SIDE):
            cols.append(pool_s[c, x, pl.ds(0, 8, stride=2), :] + pool_s[c, x, pl.ds(1, 8, stride=2), :])
        rows.append(jnp.concatenate(cols, axis=0))
    pooled = jnp.concatenate(rows, axis=0)
    zpool = jnp.where(iota((128, 1), 0) >> 1 == iota((1, 64), 1), 0.125, 0.0)
    filt = nn(pooled, zpool, HIGH).astype(BF16)
    tgt_rows = tgt[...].reshape(64, 64)
    zsel = jnp.concatenate([filt[0:64], filt[64:128], filt[128:192], tgt_rows], axis=1)
    spread = onehot(iota((ROWS, 1), 0) >> 3 == iota((1, 64), 1))
    by_block = nn(spread, zsel)
    mine = (iota((1, 256), 1) & 63) >> 3 == iota((ROWS, 1), 0) & 7
    by_block = jnp.where(mine, by_block, 0.0).astype(BF16)
    lane_in = iota((1, 256), 1)
    lane_off = lax.div(lane_in, 24)
    lane_cz = lane_in - lane_off * 24
    src = iota((256, 1), 0)
    pick = onehot(jnp.where(lane_in < 216, lane_cz, -1) == (src >> 6) * 8 + (src & 7))
    cells = nn(by_block, pick)
    pick_t = onehot(jnp.where(src >= 192, src & 7, -1) == iota((1, SIDE), 1))
    target = nn(by_block, pick_t)

    fp_s[...] = jnp.zeros(fp_s.shape, F32)
    fp_s[1:9, 1:9] = cells.reshape(SIDE, SIDE, BLK, 256)
    group = lax.div(iota((1, 1, 1, 256), 3), 24)
    for x in range(SIDE):
        acc = jnp.zeros((1, SIDE, BLK, 256), F32)
        for k in range(9):
            part = fp_s[x + k // 3 : x + k // 3 + 1, k % 3 : k % 3 + SIDE]
            acc = jnp.where(group == k, part, acc)
        i1_s[x * SLAB : (x + 1) * SLAB, :] = acc.reshape(SLAB, 256).astype(BF16)

    j_at = iota((81, 1), 0)
    j_off, j_dz, j_c = lax.div(j_at, 9), lax.rem(lax.div(j_at, 3), 3) - 1, lax.rem(j_at, 3)
    lane_key = jnp.where(lane_in < 216, lane_off * 4 + (lane_cz >> 3), -1)
    same = lane_key == j_off * 4 + j_c
    delta = jnp.where(same, (lane_in & 7) - j_dz, -9)
    w1v = w1[...]
    t1 = jnp.concatenate([nn(w1v, onehot(delta == z)).astype(BF16) for z in range(SIDE)], axis=0)
    pre_s[...] = nt(i1_s[...], t1)

    src = iota((320, 1), 0) - 64
    dst = iota((1, 512), 1)
    wanted = ((dst >> 7) - 2 + ((dst & 127) >> 6)) * 64 + (dst & 63)
    chooser = onehot(jnp.where((src >= 0) & (src < 192), src - 64, -999) == wanted)
    zero_tile = jnp.zeros((64, 128), BF16)
    for k in range(9):
        base = (192 * k) // 128 * 128
        off = 192 * k - base
        width = min(256, 1728 - base)
        tiles = nn(w2[:, base : base + width], chooser[64 - off : 64 - off + width]).astype(BF16)
        ks, js = k // 3, k % 3
        kb, jb = (8 - k) // 3, (8 - k) % 3
        for z in range(SIDE):
            for m in range(4):
                d = 2 * m - z
                tile = tiles[:, (d + 2) * 128 : (d + 3) * 128] if -2 <= d <= 1 else zero_tile
                tt_s[ks, z * 64 : (z + 1) * 64, js * 512 + m * 128 : js * 512 + (m + 1) * 128] = tile
                tb_s[kb, jb * 512 + z * 64 : jb * 512 + (z + 1) * 64, m * 128 : (m + 1) * 128] = tile

    def shifted_store(dst_ref, x, val):
        zero = jnp.zeros((1, BLK, WIDE), F32)
        lo, hi = (x + 1) * SLAB, (x + 2) * SLAB
        dst_ref[lo:hi, 0:512] = jnp.concatenate([zero, val[:-1]], axis=0).reshape(SLAB, WIDE).astype(BF16)
        dst_ref[lo:hi, 512:1024] = val.reshape(SLAB, WIDE).astype(BF16)
        dst_ref[lo:hi, 1024:1536] = jnp.concatenate([val[1:], zero], axis=0).reshape(SLAB, WIDE).astype(BF16)

    for ref in (a_s, d_s):
        ref[0:SLAB, :] = jnp.zeros((SLAB, 1536), BF16)
        ref[9 * SLAB :, :] = jnp.zeros((SLAB, 1536), BF16)

    for x in range(SIDE):
        pre = pre_s[x * SLAB : (x + 1) * SLAB, :]
        sig = jax.nn.sigmoid(pre)
        slope1_s[x * SLAB : (x + 1) * SLAB, :] = sig * (1.0 + pre * (1.0 - sig))
        shifted_store(a_s, x, (pre * sig).reshape(SIDE, BLK, WIDE))

    acc = nt(a_s[0:ROWS, :], tt_s[0])
    acc = acc + nt(a_s[SLAB : SLAB + ROWS, :], tt_s[1])
    pre_s[...] = acc + nt(a_s[2 * SLAB : 2 * SLAB + ROWS, :], tt_s[2])
    for x in range(SIDE):
        pre = pre_s[x * SLAB : (x + 1) * SLAB, :]
        sig = jax.nn.sigmoid(pre)
        slope2_s[x * SLAB : (x + 1) * SLAB, :] = sig * (1.0 + pre * (1.0 - sig))
        ah_s[x * SLAB : (x + 1) * SLAB, :] = (pre * sig).astype(BF16)

    tile8 = onehot(iota((64, 1), 0) == iota((1, WIDE), 1) & 63)
    w3_wide = nn(w3[...], tile8)
    diag = iota((1, WIDE), 1) >> 6 == iota((SIDE, 1), 0)
    last = jnp.where(diag, w3_wide, 0.0).astype(BF16)
    logits = nt(ah_s[...], last)
    eddy = 0.5 * (jnp.maximum(logits, 0.0) + jnp.log1p(jnp.exp(-jnp.abs(logits))))
    error = eddy - target
    losses = jnp.sum(jnp.sum((error * error).reshape(64, BLK, SIDE), axis=0), axis=1, keepdims=True) / CELLS
    d_logit = (error * jax.nn.sigmoid(logits) / (trainers.astype(F32) * CELLS)).astype(BF16)

    zrep = onehot(iota((SIDE, 1), 0) == (iota((1, 128), 1) & 15) >> 1, F32)
    fine = nn(eddy, zrep, HIGH)
    fine = jnp.where(iota((1, 128), 1) >> 4 == iota((ROWS, 1), 0) & 7, fine, 0.0)
    fine = jnp.sum(fine.reshape(64, BLK, 128), axis=1)
    eddy_out[...] = fine

    for c in range(3):
        for i in range(2):
            lo, hi = vel[c, i], vel[c, 14 + i]
            at = (c * 2 + i) * 16
            hx_a[at : at + 16, :] = jnp.where(gx_odd, lo, hi)
            hx_b[at : at + 16, :] = jnp.where(gx_odd, hi, lo)
    hx_a[96:104, :] = jnp.where(gx_odd, fine[0:8], fine[56:64])
    hx_b[96:104, :] = jnp.where(gx_odd, fine[56:64], fine[0:8])
    for c in range(3):
        for i in range(2):
            lo = jnp.concatenate([vel[c, x, i : i + 1, :] for x in range(16)], axis=0)
            hi = jnp.concatenate([vel[c, x, 14 + i : 15 + i, :] for x in range(16)], axis=0)
            at = (c * 2 + i) * 16
            hy_a[at : at + 16, :] = jnp.where(gy_odd, lo, hi)
            hy_b[at : at + 16, :] = jnp.where(gy_odd, hi, lo)
    lo = eddy_out[pl.ds(0, 8, stride=8), :]
    hi = eddy_out[pl.ds(7, 8, stride=8), :]
    hy_a[96:104, :] = jnp.where(gy_odd, lo, hi)
    hy_b[96:104, :] = jnp.where(gy_odd, hi, lo)
    vt = jnp.transpose(vel[...].reshape(768, 128))
    et = jnp.transpose(jnp.concatenate([fine, jnp.zeros((64, 128), F32)], axis=0))
    hz[...] = jnp.zeros(hz.shape, F32)
    for t in range(6):
        hz[t * 8 : t * 8 + 2, :] = vt[0:2, t * 128 : (t + 1) * 128]
        hz[t * 8 + 2 : t * 8 + 4, :] = vt[126:128, t * 128 : (t + 1) * 128]
    hz[48:49, :] = et[0:1]
    hz[49:50, :] = et[127:128]

    code = own[...] * BLK + blk[...]
    listed = code.shape[1]
    wanted = gx_at * BLK + iota((BLK, listed), 0)
    count = jnp.sum(jnp.where(code == wanted, 1.0, 0.0), axis=1, keepdims=True)
    count_rows = jnp.broadcast_to(count.reshape(1, BLK, 1), (64, BLK, 1)).reshape(ROWS, 1)

    big_s[:, 0:512] = nn(d_logit, last)
    for x in range(SIDE):
        d_hid = big_s[x * SLAB : (x + 1) * SLAB, 0:512] * slope2_s[x * SLAB : (x + 1) * SLAB, :]
        d_hid = d_hid.astype(BF16).astype(F32).reshape(SIDE, BLK, WIDE)
        shifted_store(d_s, x, d_hid)
        dw_s[x * SLAB : (x + 1) * SLAB, :] = (d_hid * count[None]).reshape(SLAB, WIDE)
    dwt = jnp.transpose(dw_s[...]).astype(BF16)

    gh_s[...] = jnp.zeros(gh_s.shape, F32)
    low_half = iota((64, 128), 1) < 64
    for k in range(9):
        dx, j = k // 3, k % 3
        big_s[:, 0:512] = nn(dwt, a_s[dx * SLAB : dx * SLAB + ROWS, j * 512 : (j + 1) * 512])
        sums = []
        for m in (-1, 0, 1, 2):
            tot = None
            for p in range(4):
                z = 2 * p + m
                if 0 <= z < SIDE:
                    part = big_s[z * 64 : (z + 1) * 64, p * 128 : (p + 1) * 128]
                    tot = part if tot is None else tot + part
            sums.append(tot)
        for dz in (-1, 0, 1):
            low, high = sums[1 - dz], sums[2 - dz]
            at = (k * 3 + dz + 1) * 64
            tile, odd = at // 128 * 128, at % 128 != 0
            if odd:
                val = high + pltpu.roll(low, 64, 1)
                gh_s[:, tile : tile + 128] += jnp.where(low_half, 0.0, val)
            else:
                val = low + pltpu.roll(high, 64, 1)
                gh_s[:, tile : tile + 128] += jnp.where(low_half, val, 0.0)

    acc = nn(d_s[0:ROWS, :], tb_s[0])
    acc = acc + nn(d_s[SLAB : SLAB + ROWS, :], tb_s[1])
    acc = acc + nn(d_s[2 * SLAB : 2 * SLAB + ROWS, :], tb_s[2])
    d_first = (acc * slope1_s[...]).astype(BF16).astype(F32)
    dw_s[...] = (d_first.reshape(64, BLK, WIDE) * count[None]).reshape(ROWS, WIDE)
    d1t = jnp.transpose(dw_s[...])
    d1_hi = d1t.astype(BF16)
    d1_lo = (d1t - d1_hi.astype(F32)).astype(BF16)
    i1 = i1_s[...]
    g1 = nn(d1_hi, i1) + nn(d1_lo, i1)
    z_in = iota((1, 256), 1) & 7
    parts = []
    for dz in (-1, 0, 1):
        tot = jnp.zeros((64, 256), F32)
        for z in range(SIDE):
            if 0 <= z + dz < SIDE:
                tot = tot + jnp.where(z_in == z + dz, g1[z * 64 : (z + 1) * 64], 0.0)
        parts.append(tot)
    r_at = iota((768, 1), 0)
    c_at = iota((1, 128), 1)
    r_lane = r_at & 255
    r_off = lax.div(r_lane, 24)
    r_col = (r_off * 3 + (r_at >> 8)) * 3 + ((r_lane - r_off * 24) >> 3)
    fold = onehot(jnp.where(r_lane < 216, r_col, -1) == c_at, F32)
    g_first = nn(jnp.concatenate(parts, axis=1), fold, HIGH)

    dlw = d_logit.astype(F32) * count_rows
    dl_hi = dlw.astype(BF16)
    dl_lo = (dlw - dl_hi.astype(F32)).astype(BF16)
    ah = ah_s[...]
    gl = tn(dl_hi, ah) + tn(dl_lo, ah)
    gl = jnp.where(diag, gl, 0.0)
    fold_o = onehot(iota((1, WIDE), 1) & 63 == iota((64, 1), 0), F32)
    g_last = jnp.sum(nt(fold_o, gl, HIGH), axis=1, keepdims=True)

    lane8 = iota((BLK, 128), 1)
    loss_row = jnp.where(lane8 - (LOSS_COL + BLK * (dev // 64)) == iota((BLK, 128), 0), losses, 0.0)
    loss_row = jnp.sum(loss_row, axis=0, keepdims=True)
    lane = iota((64, 128), 1)
    extra = jnp.where(lane == LAST_COL, g_last, g_first)
    extra = extra + jnp.where(iota((64, 128), 0) == dev % 64, loss_row, 0.0)

    second = half == 1
    for t in range(TILES):
        if t == 0:
            top, bottom = extra[0:32], extra[32:64]
        else:
            top, bottom = (gh_s[r : r + 32, (t - 1) * 128 : t * 128] for r in (0, 32))
        keep[t * 32 : (t + 1) * 32, :] = jnp.where(second, bottom, top)
        send[t * 32 : (t + 1) * 32, :] = jnp.where(second, top, bottom)
    for ref in (keep, send):
        ref[TILES * 32 :, :] = jnp.zeros((HALF - TILES * 32, 128), F32)


def vmem_spec():
    return pl.BlockSpec(memory_space=pltpu.VMEM)


def run_net(scal, velocity, target, w1, w2, w3, own, blk):
    f = lambda *s: jax.ShapeDtypeStruct(s, F32)
    return pl.pallas_call(
        net_kernel,
        out_shape=(f(HALF, 128), f(HALF, 128), f(64, 128)) + (f(104, 128),) * 5,
        in_specs=[pl.BlockSpec(memory_space=pltpu.SMEM)] + [vmem_spec()] * 7,
        out_specs=tuple(vmem_spec() for _ in range(8)),
        scratch_shapes=[
            pltpu.VMEM((3, SIDE, 16, 128), F32),
            pltpu.VMEM((10, 10, BLK, 256), F32),
            pltpu.VMEM((ROWS, 256), BF16),
            pltpu.VMEM((ROWS + 2 * SLAB, 1536), BF16),
            pltpu.VMEM((ROWS + 2 * SLAB, 1536), BF16),
            pltpu.VMEM((3, 512, 1536), BF16),
            pltpu.VMEM((3, 1536, 512), BF16),
            pltpu.VMEM((ROWS, WIDE), F32),
            pltpu.VMEM((ROWS, WIDE), F32),
            pltpu.VMEM((ROWS, WIDE), BF16),
            pltpu.VMEM((ROWS, WIDE), F32),
            pltpu.VMEM((ROWS, WIDE), F32),
            pltpu.VMEM((ROWS, WIDE), F32),
            pltpu.VMEM((64, 14 * 128), F32),
        ],
        compiler_params=pltpu.CompilerParams(vmem_limit_bytes=56 * 1024 * 1024),
        name="net",
    )(scal, velocity, target, w1, w2, w3, own, blk)


def flow_kernel(
    scal, vel, eddy, rx_a, rx_b, ry_a, ry_b, rz, out, vx_s, vy_s, visc_s, ez_s
):
    gx_odd = scal[0, 1] % 2 == 1
    gy_odd = scal[0, 2] % 2 == 1
    lane = iota((1, 128), 1)

    def sides(odd, a, b, at, rows):
        one, two = a[at : at + rows, :], b[at : at + rows, :]
        return jnp.where(odd, one, two), jnp.where(odd, two, one)

    for c in range(3):
        for x in range(16):
            vy_s[(c * 16 + x) * 32 + 8 : (c * 16 + x) * 32 + 24, :] = vel[c, x]
        for i in range(2):
            below, above = sides(gy_odd, ry_a, ry_b, (c * 2 + i) * 16, 16)
            vy_s[pl.ds(c * 512 + 6 + i, 16, stride=32), :] = below
            vy_s[pl.ds(c * 512 + 24 + i, 16, stride=32), :] = above
            below, above = sides(gx_odd, rx_a, rx_b, (c * 2 + i) * 16, 16)
            vx_s[c, i] = below
            vx_s[c, 2 + i] = above

    zcols = jnp.concatenate([jnp.transpose(rz[t * 8 : t * 8 + 8, :]) for t in range(7)], axis=0)
    coarse = eddy[...]
    e_first, e_last = zcols[768:832, 0:1], zcols[768:832, 1:2]
    ahead = jnp.where(lane == 127, e_first, pltpu.roll(coarse, 127, 1))
    behind = jnp.where(lane == 0, e_last, pltpu.roll(coarse, 1, 1))
    below_x, above_x = sides(gx_odd, rx_a, rx_b, 96, 8)
    below_y, above_y = sides(gy_odd, ry_a, ry_b, 96, 8)

    def put(dst, plane, val):
        dst[pl.ds(plane * 32 + 8, 8, stride=2), :] = val
        dst[pl.ds(plane * 32 + 9, 8, stride=2), :] = val

    put(visc_s, 0, base_visc + below_x)
    put(visc_s, 17, base_visc + above_x)
    for x in range(8):
        for r in range(2):
            plane = 2 * x + 1 + r
            put(visc_s, plane, base_visc + coarse[x * 8 : x * 8 + 8])
            visc_s[plane * 32 + 7 : plane * 32 + 8, :] = base_visc + below_y[x : x + 1]
            visc_s[plane * 32 + 24 : plane * 32 + 25, :] = base_visc + above_y[x : x + 1]
        put(ez_s, 2 * x, base_visc + ahead[x * 8 : x * 8 + 8])
        put(ez_s, 2 * x + 1, base_visc + behind[x * 8 : x * 8 + 8])

    def plane_of(c, x):
        if x < 0:
            return vx_s[c, x + 2]
        if x > 15:
            return vx_s[c, x - 14]
        return vel[c, x]

    for x in range(16):
        vat = (x + 1) * 32
        visc = visc_s[vat + 8 : vat + 24, :]
        faces = (
            (visc_s[vat + 40 : vat + 56, :], visc_s[vat - 24 : vat - 8, :]),
            (visc_s[vat + 9 : vat + 25, :], visc_s[vat + 7 : vat + 23, :]),
            (
                ez_s[(x // 2 * 2) * 32 + 8 : (x // 2 * 2) * 32 + 24, :],
                ez_s[(x // 2 * 2 + 1) * 32 + 8 : (x // 2 * 2 + 1) * 32 + 24, :],
            ),
        )
        faces = [(0.5 * (visc + a), 0.5 * (visc + b)) for a, b in faces]
        wind = [vel[a, x] for a in range(3)]
        for c in range(3):
            u = vel[c, x]
            at = (c * 16 + x) * 32
            zat = (c * 16 + x) * 16
            zc = zcols[zat : zat + 16]
            p1 = jnp.where(lane == 127, zc[:, 0:1], pltpu.roll(u, 127, 1))
            p2 = jnp.where(lane == 127, zc[:, 1:2], jnp.where(lane == 126, zc[:, 0:1], pltpu.roll(u, 126, 1)))
            m1 = jnp.where(lane == 0, zc[:, 3:4], pltpu.roll(u, 1, 1))
            m2 = jnp.where(lane == 0, zc[:, 2:3], jnp.where(lane == 1, zc[:, 3:4], pltpu.roll(u, 2, 1)))
            near = (
                (plane_of(c, x + 1), plane_of(c, x - 1), plane_of(c, x + 2), plane_of(c, x - 2)),
                (
                    vy_s[at + 9 : at + 25, :], vy_s[at + 7 : at + 23, :],
                    vy_s[at + 10 : at + 26, :], vy_s[at + 6 : at + 22, :],
                ),
                (p1, m1, p2, m2),
            )
            advect = None
            diffuse = None
            for a in range(3):
                q1, b1, q2, b2 = near[a]
                slope = (8.0 * (q1 - b1) - (q2 - b2)) * (1.0 / 12.0)
                term = wind[a] * slope
                advect = term if advect is None else advect + term
                flux = faces[a][0] * (q1 - u) - faces[a][1] * (u - b1)
                diffuse = flux if diffuse is None else diffuse + flux
            out[c, x] = u + time_step * (diffuse - advect)


def run_flow(scal, velocity, eddy, *got):
    return pl.pallas_call(
        flow_kernel,
        out_shape=jax.ShapeDtypeStruct(velocity.shape, F32),
        in_specs=[pl.BlockSpec(memory_space=pltpu.SMEM)] + [vmem_spec()] * 7,
        out_specs=vmem_spec(),
        scratch_shapes=[
            pltpu.VMEM((3, 4, 16, 128), F32),
            pltpu.VMEM((3 * 16 * 32, 128), F32),
            pltpu.VMEM((18 * 32, 128), F32),
            pltpu.VMEM((16 * 32, 128), F32),
        ],
        compiler_params=pltpu.CompilerParams(vmem_limit_bytes=32 * 1024 * 1024),
        name="flow",
    )(scal, velocity, eddy, *got)


def finish_kernel(scal, own, blk, mine, other, loss_out, first_out, hidden_out, last_out, ext_s):
    second = scal[0, 3] == 1
    for t in range(TILES):
        one, two = mine[t * 32 : (t + 1) * 32, :], other[t * 32 : (t + 1) * 32, :]
        top, bottom = jnp.where(second, two, one), jnp.where(second, one, two)
        if t == 0:
            ext_s[0:32, :] = top
            ext_s[32:64, :] = bottom
        else:
            at = (t - 1) * 128
            width = min(128, 27 * CH - at)
            hidden_out[0:32, at : at + width] = top[:, :width]
            hidden_out[32:64, at : at + width] = bottom[:, :width]
    extra = ext_s[...]
    first_out[...] = extra[:, 0:81]
    turned = jnp.transpose(jnp.concatenate([extra, jnp.zeros((64, 128), F32)], axis=0))
    last_out[...] = turned[LAST_COL : LAST_COL + 1, 0:64]
    slots = loss_out.shape[1]
    lane = iota((1, 128), 1)
    slot_lane = iota((1, slots), 1)
    picked = jnp.zeros((1, slots), F32)
    for s in range(slots):
        at = scal[0, 1] * slots + s
        dev = own[0, at] * scal[0, 5] + scal[0, 6]
        row = ext_s[pl.ds(dev % 64, 1), :]
        col = LOSS_COL + BLK * (dev // 64) + blk[0, at]
        value = jnp.sum(jnp.where(lane == col, row, 0.0), axis=1, keepdims=True)
        picked = jnp.where(slot_lane == s, value, picked)
    loss_out[...] = picked


def run_finish(scal, own, blk, mine, other, slots):
    smem = pl.BlockSpec(memory_space=pltpu.SMEM)
    f = lambda *s: jax.ShapeDtypeStruct(s, F32)
    return pl.pallas_call(
        finish_kernel,
        out_shape=(f(1, slots), f(64, 81), f(64, 27 * CH), f(1, 64)),
        in_specs=[smem] * 3 + [vmem_spec()] * 2,
        out_specs=tuple(vmem_spec() for _ in range(4)),
        scratch_shapes=[pltpu.VMEM((64, 128), F32)],
        compiler_params=pltpu.CompilerParams(vmem_limit_bytes=32 * 1024 * 1024),
        name="finish",
    )(scal, own, blk, mine, other)


def on_device(velocity, target_visc, w_first, w_hidden, w_last, sample_owner, sample_block):
    n_x, n_y, n_z = lax.axis_size("gx"), lax.axis_size("gy"), lax.axis_size("role")
    trainers = n_x * n_y * n_z
    at_x, at_y, at_z = lax.axis_index("gx"), lax.axis_index("gy"), lax.axis_index("role")
    group = at_y * n_z + at_z
    half = at_y & 1
    scal = jnp.stack(
        [jnp.int32(trainers), at_x, at_y, half, at_x * (n_y * n_z) + group, jnp.int32(n_y * n_z), group, jnp.int32(0)]
    ).astype(jnp.int32)[None]
    own = sample_owner.reshape(1, -1)
    blk = sample_block.reshape(1, -1)
    slots = own.shape[1] // n_x

    axes = ("gx", "gy", "role")

    def even_odd(count):
        return [(i, i ^ 1) for i in range(count)]

    def odd_even(count):
        return [(i, (i - 1) % count if i % 2 == 0 else (i + 1) % count) for i in range(count)]

    keep, send, eddy, hx_a, hx_b, hy_a, hy_b, hz = run_net(
        scal, velocity, target_visc, w_first, w_hidden, w_last.reshape(1, CH), own, blk
    )
    rims = [
        lax.ppermute(hx_a, "gx", even_odd(n_x)),
        lax.ppermute(hx_b, "gx", odd_even(n_x)),
        lax.ppermute(hy_a, "gy", even_odd(n_y)),
        lax.ppermute(hy_b, "gy", odd_even(n_y)),
        lax.ppermute(hz, "role", even_odd(n_z)),
    ]
    total = keep + lax.ppermute(send, "gy", even_odd(n_y))
    peers = trainers // 2
    if peers == 16:
        groups = [
            [(i * n_y + j) * n_z + r for i in range(n_x) for j in range(p, n_y, 2) for r in range(n_z)] for p in range(2)
        ]
        parts = lax.all_to_all(total.reshape(peers, HALF // peers, 128), axes, 0, 0, axis_index_groups=groups)
        mine = jnp.broadcast_to(jnp.sum(parts, axis=0)[None], parts.shape)
        total = lax.all_to_all(mine, axes, 0, 0, axis_index_groups=groups).reshape(HALF, 128)
    else:
        total = total + lax.ppermute(total, "gy", [(j, (j + 2) % n_y) for j in range(n_y)])
        total = lax.psum(total, ("gx", "role"))
    other = lax.ppermute(total, "gy", even_odd(n_y))

    u_next = run_flow(scal, velocity, eddy, *rims)
    losses, first, hidden, last = run_finish(scal, own, blk, total, other, slots)
    return (u_next, losses.reshape(1, 1, slots), first, hidden, last.reshape(CH))


def solution(mesh):
    return jax.shard_map(
        on_device,
        mesh=mesh,
        in_specs=(
            P(None, "gx", "gy", "role"),
            P("gx", "gy", "role"),
            P(),
            P(),
            P(),
            P("gy", "role", None, None),
            P("gy", "role", None, None),
        ),
        out_specs=(P(None, "gx", "gy", "role"), P("gy", "role", "gx"), P(), P(), P()),
        check_vma=False,
    )
```

```python
import jax
import jax.numpy as jnp
from jax import lax
from jax.experimental import pallas as pl
from jax.experimental.pallas import tpu as pltpu
from jax.sharding import PartitionSpec as P

F32 = jnp.float32
BF16 = jnp.bfloat16
HIGH = lax.Precision.HIGHEST

SIDE = 8
CELLS = SIDE**3
CH = 64
BLK = 8
ROWS = SIDE * SIDE * BLK
WIDE = SIDE * CH
SLAB = SIDE * BLK
PAY = 1920
LAST_COL = 81
LOSS_COL = 82

base_visc = 0.02
time_step = 0.2


def iota(shape, dim):
    return lax.broadcasted_iota(jnp.int32, shape, dim)


def onehot(cond, dtype=BF16):
    return jnp.where(cond, 1.0, 0.0).astype(dtype)


def nt(a, b, precision=None):
    return lax.dot_general(a, b, (((1,), (1,)), ((), ())), preferred_element_type=F32, precision=precision)


def tn(a, b, precision=None):
    return lax.dot_general(a, b, (((0,), (0,)), ((), ())), preferred_element_type=F32, precision=precision)


def nn(a, b, precision=None):
    return lax.dot_general(a, b, (((1,), (0,)), ((), ())), preferred_element_type=F32, precision=precision)


def core_half(at):
    return (at ^ (at >> 1)) & 1


def net_kernel(
    vel, tgt, w1, w2, w3, own, blk,
    keep, send, eddy_out, halo1, halo2, halo3, halo4,
    hx_a, hx_b, hy_b, hz, pool_s, fp_s, i1_s, a_s, d_s, tt_s, tb_s, pre_s, slope1_s, ah_s, slope2_s, dw_s, big_s, gh_s,
):
    gx_at, gy_at = lax.axis_index("gx"), lax.axis_index("gy")
    half = core_half(gy_at)
    dev = (gx_at * lax.axis_size("gy") + gy_at) * lax.axis_size("role") + lax.axis_index("role")
    trainers = lax.axis_size("gx") * lax.axis_size("gy") * lax.axis_size("role")
    gx_odd, gy_odd = gx_at & 1 == 1, gy_at & 1 == 1

    for c in range(3):
        for x in range(SIDE):
            both = vel[c, 2 * x] + vel[c, 2 * x + 1]
            pool_s[c, x] = both
    rows = []
    for c in range(3):
        cols = []
        for x in range(SIDE):
            cols.append(pool_s[c, x, pl.ds(0, 8, stride=2), :] + pool_s[c, x, pl.ds(1, 8, stride=2), :])
        rows.append(jnp.concatenate(cols, axis=0))
    pooled = jnp.concatenate(rows, axis=0)
    zpool = jnp.where(iota((128, 1), 0) >> 1 == iota((1, 64), 1), 0.125, 0.0)
    filt = nn(pooled, zpool, HIGH).astype(BF16)
    tgt_rows = tgt[...].reshape(64, 64)
    zsel = jnp.concatenate([filt[0:64], filt[64:128], filt[128:192], tgt_rows], axis=1)
    spread = onehot(iota((ROWS, 1), 0) >> 3 == iota((1, 64), 1))
    by_block = nn(spread, zsel)
    mine = (iota((1, 256), 1) & 63) >> 3 == iota((ROWS, 1), 0) & 7
    by_block = jnp.where(mine, by_block, 0.0).astype(BF16)
    lane_in = iota((1, 256), 1)
    lane_off = lax.div(lane_in, 24)
    lane_cz = lane_in - lane_off * 24
    src = iota((256, 1), 0)
    pick = onehot(jnp.where(lane_in < 216, lane_cz, -1) == (src >> 6) * 8 + (src & 7))
    cells = nn(by_block, pick)
    pick_t = onehot(jnp.where(src >= 192, src & 7, -1) == iota((1, SIDE), 1))
    target = nn(by_block, pick_t)

    fp_s[...] = jnp.zeros(fp_s.shape, F32)
    fp_s[1:9, 1:9] = cells.reshape(SIDE, SIDE, BLK, 256)
    group = lax.div(iota((1, 1, 1, 256), 3), 24)
    for x in range(SIDE):
        acc = jnp.zeros((1, SIDE, BLK, 256), F32)
        for k in range(9):
            part = fp_s[x + k // 3 : x + k // 3 + 1, k % 3 : k % 3 + SIDE]
            acc = jnp.where(group == k, part, acc)
        i1_s[x * SLAB : (x + 1) * SLAB, :] = acc.reshape(SLAB, 256).astype(BF16)

    j_at = iota((81, 1), 0)
    j_off, j_dz, j_c = lax.div(j_at, 9), lax.rem(lax.div(j_at, 3), 3) - 1, lax.rem(j_at, 3)
    lane_key = jnp.where(lane_in < 216, lane_off * 4 + (lane_cz >> 3), -1)
    same = lane_key == j_off * 4 + j_c
    delta = jnp.where(same, (lane_in & 7) - j_dz, -9)
    w1v = w1[...]
    t1 = jnp.concatenate([nn(w1v, onehot(delta == z)).astype(BF16) for z in range(SIDE)], axis=0)
    pre_s[...] = nt(i1_s[...], t1)

    src = iota((320, 1), 0) - 64
    dst = iota((1, 512), 1)
    wanted = ((dst >> 7) - 2 + ((dst & 127) >> 6)) * 64 + (dst & 63)
    chooser = onehot(jnp.where((src >= 0) & (src < 192), src - 64, -999) == wanted)
    zero_tile = jnp.zeros((64, 128), BF16)
    for k in range(9):
        base = (192 * k) // 128 * 128
        off = 192 * k - base
        width = min(256, 1728 - base)
        tiles = nn(w2[:, base : base + width], chooser[64 - off : 64 - off + width]).astype(BF16)
        ks, js = k // 3, k % 3
        kb, jb = (8 - k) // 3, (8 - k) % 3
        for z in range(SIDE):
            for m in range(4):
                d = 2 * m - z
                tile = tiles[:, (d + 2) * 128 : (d + 3) * 128] if -2 <= d <= 1 else zero_tile
                tt_s[ks, z * 64 : (z + 1) * 64, js * 512 + m * 128 : js * 512 + (m + 1) * 128] = tile
                tb_s[kb, jb * 512 + z * 64 : jb * 512 + (z + 1) * 64, m * 128 : (m + 1) * 128] = tile

    def shifted_store(dst_ref, x, val):
        zero = jnp.zeros((1, BLK, WIDE), F32)
        lo, hi = (x + 1) * SLAB, (x + 2) * SLAB
        dst_ref[lo:hi, 0:512] = jnp.concatenate([zero, val[:-1]], axis=0).reshape(SLAB, WIDE).astype(BF16)
        dst_ref[lo:hi, 512:1024] = val.reshape(SLAB, WIDE).astype(BF16)
        dst_ref[lo:hi, 1024:1536] = jnp.concatenate([val[1:], zero], axis=0).reshape(SLAB, WIDE).astype(BF16)

    for ref in (a_s, d_s):
        ref[0:SLAB, :] = jnp.zeros((SLAB, 1536), BF16)
        ref[9 * SLAB :, :] = jnp.zeros((SLAB, 1536), BF16)

    for x in range(SIDE):
        pre = pre_s[x * SLAB : (x + 1) * SLAB, :]
        sig = jax.nn.sigmoid(pre)
        slope1_s[x * SLAB : (x + 1) * SLAB, :] = sig * (1.0 + pre * (1.0 - sig))
        shifted_store(a_s, x, (pre * sig).reshape(SIDE, BLK, WIDE))

    acc = nt(a_s[0:ROWS, :], tt_s[0])
    acc = acc + nt(a_s[SLAB : SLAB + ROWS, :], tt_s[1])
    pre_s[...] = acc + nt(a_s[2 * SLAB : 2 * SLAB + ROWS, :], tt_s[2])
    for x in range(SIDE):
        pre = pre_s[x * SLAB : (x + 1) * SLAB, :]
        sig = jax.nn.sigmoid(pre)
        slope2_s[x * SLAB : (x + 1) * SLAB, :] = sig * (1.0 + pre * (1.0 - sig))
        ah_s[x * SLAB : (x + 1) * SLAB, :] = (pre * sig).astype(BF16)

    tile8 = onehot(iota((64, 1), 0) == iota((1, WIDE), 1) & 63)
    w3_wide = nn(w3[...], tile8)
    diag = iota((1, WIDE), 1) >> 6 == iota((SIDE, 1), 0)
    last = jnp.where(diag, w3_wide, 0.0).astype(BF16)
    logits = nt(ah_s[...], last)
    eddy = 0.5 * (jnp.maximum(logits, 0.0) + jnp.log1p(jnp.exp(-jnp.abs(logits))))
    error = eddy - target
    losses = jnp.sum(jnp.sum((error * error).reshape(64, BLK, SIDE), axis=0), axis=1, keepdims=True) / CELLS
    d_logit = (error * jax.nn.sigmoid(logits) / (trainers * CELLS)).astype(BF16)

    zrep = onehot(iota((SIDE, 1), 0) == (iota((1, 128), 1) & 15) >> 1, F32)
    fine = nn(eddy, zrep, HIGH)
    fine = jnp.where(iota((1, 128), 1) >> 4 == iota((ROWS, 1), 0) & 7, fine, 0.0)
    fine = jnp.sum(fine.reshape(64, BLK, 128), axis=1)
    eddy_out[...] = fine

    for c in range(3):
        for i in range(2):
            lo, hi = vel[c, i], vel[c, 14 + i]
            at = (c * 2 + i) * 16
            hx_a[at : at + 16, :] = jnp.where(gx_odd, lo, hi)
            hx_b[at : at + 16, :] = jnp.where(gx_odd, hi, lo)
    hx_a[96:104, :] = jnp.where(gx_odd, fine[0:8], fine[56:64])
    hx_b[96:104, :] = jnp.where(gx_odd, fine[56:64], fine[0:8])
    core = send.at[480:584]
    for c in range(3):
        for i in range(2):
            lo = jnp.concatenate([vel[c, x, i : i + 1, :] for x in range(16)], axis=0)
            hi = jnp.concatenate([vel[c, x, 14 + i : 15 + i, :] for x in range(16)], axis=0)
            at = (c * 2 + i) * 16
            core[at : at + 16, :] = jnp.where(gy_odd, lo, hi)
            hy_b[at : at + 16, :] = jnp.where(gy_odd, hi, lo)
    lo = eddy_out[pl.ds(0, 8, stride=8), :]
    hi = eddy_out[pl.ds(7, 8, stride=8), :]
    core[96:104, :] = jnp.where(gy_odd, lo, hi)
    hy_b[96:104, :] = jnp.where(gy_odd, hi, lo)
    vt = jnp.transpose(vel[...].reshape(768, 128))
    et = jnp.transpose(jnp.concatenate([fine, jnp.zeros((64, 128), F32)], axis=0))
    hz[...] = jnp.zeros(hz.shape, F32)
    for t in range(6):
        hz[t * 8 : t * 8 + 2, :] = vt[0:2, t * 128 : (t + 1) * 128]
        hz[t * 8 + 2 : t * 8 + 4, :] = vt[126:128, t * 128 : (t + 1) * 128]
    hz[48:49, :] = et[0:1]
    hz[49:50, :] = et[127:128]
    second = half == 1
    halo1[...] = jnp.where(second, hx_a[...], hy_b[...])
    halo2[...] = jnp.where(second, hy_b[...], hz[...])
    halo3[...] = jnp.where(second, hx_b[...], hx_a[...])
    halo4[...] = jnp.where(second, hz[...], hx_b[...])

    code = own[...] * BLK + blk[...]
    listed = code.shape[1]
    wanted = gx_at * BLK + iota((BLK, listed), 0)
    count = jnp.sum(jnp.where(code == wanted, 1.0, 0.0), axis=1, keepdims=True)
    count_rows = jnp.broadcast_to(count.reshape(1, BLK, 1), (64, BLK, 1)).reshape(ROWS, 1)

    big_s[:, 0:512] = nn(d_logit, last)
    for x in range(SIDE):
        d_hid = big_s[x * SLAB : (x + 1) * SLAB, 0:512] * slope2_s[x * SLAB : (x + 1) * SLAB, :]
        d_hid = d_hid.astype(BF16).astype(F32).reshape(SIDE, BLK, WIDE)
        shifted_store(d_s, x, d_hid)
        dw_s[x * SLAB : (x + 1) * SLAB, :] = (d_hid * count[None]).reshape(SLAB, WIDE)
    dwt = jnp.transpose(dw_s[...]).astype(BF16)

    gh_s[...] = jnp.zeros(gh_s.shape, F32)
    low_half = iota((64, 128), 1) < 64
    for k in range(9):
        dx, j = k // 3, k % 3
        for q in range(2):
            zs = slice(q * 192, q * 192 + 320)
            cols = slice(j * 512 + q * 256, j * 512 + (q + 1) * 256)
            big_s[zs, q * 256 : (q + 1) * 256] = nn(dwt[zs], a_s[dx * SLAB : dx * SLAB + ROWS, cols])
        sums = []
        for m in (-1, 0, 1, 2):
            tot = None
            for p in range(4):
                z = 2 * p + m
                if 0 <= z < SIDE:
                    part = big_s[z * 64 : (z + 1) * 64, p * 128 : (p + 1) * 128]
                    tot = part if tot is None else tot + part
            sums.append(tot)
        for dz in (-1, 0, 1):
            low, high = sums[1 - dz], sums[2 - dz]
            at = (k * 3 + dz + 1) * 64
            tile, odd = at // 128 * 128, at % 128 != 0
            if odd:
                val = high + pltpu.roll(low, 64, 1)
                gh_s[:, tile : tile + 128] += jnp.where(low_half, 0.0, val)
            else:
                val = low + pltpu.roll(high, 64, 1)
                gh_s[:, tile : tile + 128] += jnp.where(low_half, val, 0.0)

    acc = nn(d_s[0:ROWS, :], tb_s[0])
    acc = acc + nn(d_s[SLAB : SLAB + ROWS, :], tb_s[1])
    acc = acc + nn(d_s[2 * SLAB : 2 * SLAB + ROWS, :], tb_s[2])
    d_first = (acc * slope1_s[...]).astype(BF16).astype(F32)
    dw_s[...] = (d_first.reshape(64, BLK, WIDE) * count[None]).reshape(ROWS, WIDE)
    d1t = jnp.transpose(dw_s[...])
    d1_hi = d1t.astype(BF16)
    d1_lo = (d1t - d1_hi.astype(F32)).astype(BF16)
    i1 = i1_s[...]
    g1 = nn(d1_hi, i1) + nn(d1_lo, i1)
    z_in = iota((1, 256), 1) & 7
    parts = []
    for dz in (-1, 0, 1):
        tot = jnp.zeros((64, 256), F32)
        for z in range(SIDE):
            if 0 <= z + dz < SIDE:
                tot = tot + jnp.where(z_in == z + dz, g1[z * 64 : (z + 1) * 64], 0.0)
        parts.append(tot)
    r_at = iota((768, 1), 0)
    c_at = iota((1, 128), 1)
    r_lane = r_at & 255
    r_off = lax.div(r_lane, 24)
    r_col = (r_off * 3 + (r_at >> 8)) * 3 + ((r_lane - r_off * 24) >> 3)
    fold = onehot(jnp.where(r_lane < 216, r_col, -1) == c_at, F32)
    g_first = nn(jnp.concatenate(parts, axis=1), fold, HIGH)

    dlw = d_logit.astype(F32) * count_rows
    dl_hi = dlw.astype(BF16)
    dl_lo = (dlw - dl_hi.astype(F32)).astype(BF16)
    ah = ah_s[...]
    gl = tn(dl_hi, ah) + tn(dl_lo, ah)
    gl = jnp.where(diag, gl, 0.0)
    fold_o = onehot(iota((1, WIDE), 1) & 63 == iota((64, 1), 0), F32)
    g_last = jnp.sum(nt(fold_o, gl, HIGH), axis=1, keepdims=True)

    lane8 = iota((BLK, 128), 1)
    loss_row = jnp.where(lane8 - (LOSS_COL + BLK * (dev >> 6)) == iota((BLK, 128), 0), losses, 0.0)
    loss_row = jnp.sum(loss_row, axis=0, keepdims=True)
    lane = iota((64, 128), 1)
    extra = jnp.where(lane == LAST_COL, g_last, g_first)
    extra = extra + jnp.where(iota((64, 128), 0) == dev & 63, loss_row, 0.0)

    for t in range(PAY // 128):
        if t == 0:
            top, bottom = extra[0:32], extra[32:64]
        else:
            top, bottom = (gh_s[r : r + 32, (t - 1) * 128 : t * 128] for r in (0, 32))
        keep[t * 32 : (t + 1) * 32, :] = jnp.where(second, bottom, top)
        send[t * 32 : (t + 1) * 32, :] = jnp.where(second, top, bottom)


def vmem_spec():
    return pl.BlockSpec(memory_space=pltpu.VMEM)


def run_net(velocity, target, w1, w2, w3, own, blk):
    f = lambda *s: jax.ShapeDtypeStruct(s, F32)
    return pl.pallas_call(
        net_kernel,
        out_shape=(f(480, 128), f(584, 128), f(64, 128)) + (f(104, 128),) * 4,
        in_specs=[vmem_spec()] * 7,
        out_specs=tuple(vmem_spec() for _ in range(7)),
        scratch_shapes=[
            pltpu.VMEM((104, 128), F32),
            pltpu.VMEM((104, 128), F32),
            pltpu.VMEM((104, 128), F32),
            pltpu.VMEM((104, 128), F32),
            pltpu.VMEM((3, SIDE, 16, 128), F32),
            pltpu.VMEM((10, 10, BLK, 256), F32),
            pltpu.VMEM((ROWS, 256), BF16),
            pltpu.VMEM((ROWS + 2 * SLAB, 1536), BF16),
            pltpu.VMEM((ROWS + 2 * SLAB, 1536), BF16),
            pltpu.VMEM((3, 512, 1536), BF16),
            pltpu.VMEM((3, 1536, 512), BF16),
            pltpu.VMEM((ROWS, WIDE), F32),
            pltpu.VMEM((ROWS, WIDE), F32),
            pltpu.VMEM((ROWS, WIDE), BF16),
            pltpu.VMEM((ROWS, WIDE), F32),
            pltpu.VMEM((ROWS, WIDE), F32),
            pltpu.VMEM((ROWS, WIDE), F32),
            pltpu.VMEM((64, PAY - 128), F32),
        ],
        compiler_params=pltpu.CompilerParams(vmem_limit_bytes=56 * 1024 * 1024),
        name="net",
    )(velocity, target, w1, w2, w3, own, blk)


def flow_kernel(
    vel, eddy, got0, got1, got2, got3, got4, out, rx_a, rx_b, ry_a, ry_b, rz, vx_s, vy_s, visc_s, ez_s
):
    gx_at, gy_at = lax.axis_index("gx"), lax.axis_index("gy")
    gx_odd, gy_odd = gx_at & 1 == 1, gy_at & 1 == 1
    second = core_half(gy_at) == 1
    ry_a[...] = got0[...]
    ry_b[...] = jnp.where(second, got2[...], got1[...])
    rx_a[...] = jnp.where(second, got1[...], got3[...])
    rx_b[...] = jnp.where(second, got3[...], got4[...])
    rz[...] = jnp.where(second, got4[...], got2[...])
    lane = iota((1, 128), 1)

    def sides(odd, a, b, at, rows):
        one, two = a[at : at + rows, :], b[at : at + rows, :]
        return jnp.where(odd, one, two), jnp.where(odd, two, one)

    for c in range(3):
        for x in range(16):
            vy_s[(c * 16 + x) * 32 + 8 : (c * 16 + x) * 32 + 24, :] = vel[c, x]
        for i in range(2):
            below, above = sides(gy_odd, ry_a, ry_b, (c * 2 + i) * 16, 16)
            vy_s[pl.ds(c * 512 + 6 + i, 16, stride=32), :] = below
            vy_s[pl.ds(c * 512 + 24 + i, 16, stride=32), :] = above
            below, above = sides(gx_odd, rx_a, rx_b, (c * 2 + i) * 16, 16)
            vx_s[c, i] = below
            vx_s[c, 2 + i] = above

    zcols = jnp.concatenate([jnp.transpose(rz[t * 8 : t * 8 + 8, :]) for t in range(7)], axis=0)
    coarse = eddy[...]
    e_first, e_last = zcols[768:832, 0:1], zcols[768:832, 1:2]
    ahead = jnp.where(lane == 127, e_first, pltpu.roll(coarse, 127, 1))
    behind = jnp.where(lane == 0, e_last, pltpu.roll(coarse, 1, 1))
    below_x, above_x = sides(gx_odd, rx_a, rx_b, 96, 8)
    below_y, above_y = sides(gy_odd, ry_a, ry_b, 96, 8)

    def put(dst, plane, val):
        dst[pl.ds(plane * 32 + 8, 8, stride=2), :] = val
        dst[pl.ds(plane * 32 + 9, 8, stride=2), :] = val

    put(visc_s, 0, base_visc + below_x)
    put(visc_s, 17, base_visc + above_x)
    for x in range(8):
        for r in range(2):
            plane = 2 * x + 1 + r
            put(visc_s, plane, base_visc + coarse[x * 8 : x * 8 + 8])
            visc_s[plane * 32 + 7 : plane * 32 + 8, :] = base_visc + below_y[x : x + 1]
            visc_s[plane * 32 + 24 : plane * 32 + 25, :] = base_visc + above_y[x : x + 1]
        put(ez_s, 2 * x, base_visc + ahead[x * 8 : x * 8 + 8])
        put(ez_s, 2 * x + 1, base_visc + behind[x * 8 : x * 8 + 8])

    def plane_of(c, x):
        if x < 0:
            return vx_s[c, x + 2]
        if x > 15:
            return vx_s[c, x - 14]
        return vel[c, x]

    for x in range(16):
        vat = (x + 1) * 32
        visc = visc_s[vat + 8 : vat + 24, :]
        faces = (
            (visc_s[vat + 40 : vat + 56, :], visc_s[vat - 24 : vat - 8, :]),
            (visc_s[vat + 9 : vat + 25, :], visc_s[vat + 7 : vat + 23, :]),
            (
                ez_s[(x // 2 * 2) * 32 + 8 : (x // 2 * 2) * 32 + 24, :],
                ez_s[(x // 2 * 2 + 1) * 32 + 8 : (x // 2 * 2 + 1) * 32 + 24, :],
            ),
        )
        faces = [(0.5 * (visc + a), 0.5 * (visc + b)) for a, b in faces]
        wind = [vel[a, x] for a in range(3)]
        for c in range(3):
            u = vel[c, x]
            at = (c * 16 + x) * 32
            zat = (c * 16 + x) * 16
            zc = zcols[zat : zat + 16]
            p1 = jnp.where(lane == 127, zc[:, 0:1], pltpu.roll(u, 127, 1))
            p2 = jnp.where(lane == 127, zc[:, 1:2], jnp.where(lane == 126, zc[:, 0:1], pltpu.roll(u, 126, 1)))
            m1 = jnp.where(lane == 0, zc[:, 3:4], pltpu.roll(u, 1, 1))
            m2 = jnp.where(lane == 0, zc[:, 2:3], jnp.where(lane == 1, zc[:, 3:4], pltpu.roll(u, 2, 1)))
            near = (
                (plane_of(c, x + 1), plane_of(c, x - 1), plane_of(c, x + 2), plane_of(c, x - 2)),
                (
                    vy_s[at + 9 : at + 25, :], vy_s[at + 7 : at + 23, :],
                    vy_s[at + 10 : at + 26, :], vy_s[at + 6 : at + 22, :],
                ),
                (p1, m1, p2, m2),
            )
            advect = None
            diffuse = None
            for a in range(3):
                q1, b1, q2, b2 = near[a]
                slope = (8.0 * (q1 - b1) - (q2 - b2)) * (1.0 / 12.0)
                term = wind[a] * slope
                advect = term if advect is None else advect + term
                flux = faces[a][0] * (q1 - u) - faces[a][1] * (u - b1)
                diffuse = flux if diffuse is None else diffuse + flux
            out[c, x] = u + time_step * (diffuse - advect)


def run_flow(velocity, eddy, *got):
    return pl.pallas_call(
        flow_kernel,
        out_shape=jax.ShapeDtypeStruct(velocity.shape, F32),
        in_specs=[vmem_spec()] * 7,
        out_specs=vmem_spec(),
        scratch_shapes=[
            pltpu.VMEM((104, 128), F32),
            pltpu.VMEM((104, 128), F32),
            pltpu.VMEM((104, 128), F32),
            pltpu.VMEM((104, 128), F32),
            pltpu.VMEM((104, 128), F32),
            pltpu.VMEM((3, 4, 16, 128), F32),
            pltpu.VMEM((3 * 16 * 32, 128), F32),
            pltpu.VMEM((18 * 32, 128), F32),
            pltpu.VMEM((16 * 32, 128), F32),
        ],
        compiler_params=pltpu.CompilerParams(vmem_limit_bytes=32 * 1024 * 1024),
        name="flow",
    )(velocity, eddy, *got)


def finish_kernel(own, blk, mine, other, loss_out, first_out, hidden_out, last_out, ext_s):
    gx_at, gy_at = lax.axis_index("gx"), lax.axis_index("gy")
    n_z = lax.axis_size("role")
    in_group = gy_at * n_z + lax.axis_index("role")
    second = core_half(gy_at) == 1
    for t in range(PAY // 128):
        one, two = mine[t * 32 : (t + 1) * 32, :], other[t * 32 : (t + 1) * 32, :]
        top, bottom = jnp.where(second, two, one), jnp.where(second, one, two)
        if t == 0:
            ext_s[0:32, :] = top
            ext_s[32:64, :] = bottom
        else:
            at = (t - 1) * 128
            width = min(128, 27 * CH - at)
            hidden_out[0:32, at : at + width] = top[:, :width]
            hidden_out[32:64, at : at + width] = bottom[:, :width]
    extra = ext_s[...]
    first_out[...] = extra[:, 0:81]
    turned = jnp.transpose(jnp.concatenate([extra, jnp.zeros((64, 128), F32)], axis=0))
    last_out[...] = turned[LAST_COL : LAST_COL + 1, 0:64]
    slots = loss_out.shape[1]
    lane = iota((1, 128), 1)
    slot_lane = iota((1, slots), 1)
    picked = jnp.zeros((1, slots), F32)
    for s in range(slots):
        at = gx_at * slots + s
        dev = own[0, at] * (lax.axis_size("gy") * n_z) + in_group
        row = ext_s[pl.ds(dev & 63, 1), :]
        col = LOSS_COL + BLK * (dev >> 6) + blk[0, at]
        value = jnp.sum(jnp.where(lane == col, row, 0.0), axis=1, keepdims=True)
        picked = jnp.where(slot_lane == s, value, picked)
    loss_out[...] = picked


def run_finish(own, blk, mine, other, slots):
    smem = pl.BlockSpec(memory_space=pltpu.SMEM)
    f = lambda *s: jax.ShapeDtypeStruct(s, F32)
    return pl.pallas_call(
        finish_kernel,
        out_shape=(f(1, slots), f(64, 81), f(64, 27 * CH), f(1, 64)),
        in_specs=[smem] * 2 + [vmem_spec()] * 2,
        out_specs=tuple(vmem_spec() for _ in range(4)),
        scratch_shapes=[pltpu.VMEM((64, 128), F32)],
        compiler_params=pltpu.CompilerParams(vmem_limit_bytes=32 * 1024 * 1024),
        name="finish",
    )(own, blk, mine, other)


def on_device(velocity, target_visc, w_first, w_hidden, w_last, sample_owner, sample_block):
    n_x, n_y, n_z = lax.axis_size("gx"), lax.axis_size("gy"), lax.axis_size("role")
    trainers = n_x * n_y * n_z
    own = sample_owner.reshape(1, -1)
    blk = sample_block.reshape(1, -1)
    slots = own.shape[1] // n_x

    axes = ("gx", "gy", "role")

    def even_odd(i, count):
        return i ^ 1

    def odd_even(i, count):
        return (i - 1) % count if i % 2 == 0 else (i + 1) % count

    def partner(kind, i, j, r):
        if kind == "x":
            j = odd_even(j, n_y)
        elif kind == "y":
            r = r ^ 1
        elif kind == "z_a":
            i = even_odd(i, n_x)
        else:
            i = odd_even(i, n_x)
        return (i * n_y + j) * n_z + r

    def mixed(kinds):
        pairs = []
        for i in range(n_x):
            for j in range(n_y):
                for r in range(n_z):
                    pairs.append(((i * n_y + j) * n_z + r, partner(kinds[(j ^ (j >> 1)) & 1], i, j, r)))
        return pairs

    core_pairs = [(j, even_odd(j, n_y)) for j in range(n_y)]
    size = PAY // 4

    keep, send, eddy, *halos = run_net(
        velocity, target_visc, w_first, w_hidden, w_last.reshape(1, CH), own, blk
    )
    half = core_half(lax.axis_index("gy"))
    got = lax.ppermute(send, "gy", core_pairs)
    total = keep + got[:size]
    rims = [got[size:]]
    orders = (("x", "y", "z_a", "z_b"), ("z_a", "x", "z_b", "y"))
    far = None
    for s in range(4):
        kinds = (orders[0][s], orders[1][s])
        if s == 1:
            far = lax.ppermute(halos[3], axes, mixed((orders[0][3], orders[1][3])))
        if s < 3:
            got = lax.ppermute(jnp.concatenate([total, halos[s]], axis=0), axes, mixed(kinds))
            rims.append(got[size:])
        else:
            got = lax.ppermute(total, axes, mixed(kinds))
        part = got[:size]
        if n_x != 4 and "z_b" in kinds:
            part = jnp.where(half == kinds.index("z_b"), 0.0, part)
        total = total + part
        if s == 1:
            total, far = lax.optimization_barrier((total, far))
        if s == 2:
            u_next = run_flow(velocity, eddy, *rims, far)
    total, u_next = lax.optimization_barrier((total, u_next))
    if n_x != 4:
        for bit in range(1, n_x.bit_length() - 1):
            total = total + lax.ppermute(total, "gx", [(i, i ^ (1 << bit)) for i in range(n_x)])
    other = lax.ppermute(total, "gy", core_pairs)

    losses, first, hidden, last = run_finish(own, blk, total, other, slots)
    return (u_next, losses.reshape(1, 1, slots), first, hidden, last.reshape(CH))


def solution(mesh):
    return jax.shard_map(
        on_device,
        mesh=mesh,
        in_specs=(
            P(None, "gx", "gy", "role"),
            P("gx", "gy", "role"),
            P(),
            P(),
            P(),
            P("gy", "role", None, None),
            P("gy", "role", None, None),
        ),
        out_specs=(P(None, "gx", "gy", "role"), P("gy", "role", "gx"), P(), P(), P()),
        check_vma=False,
    )
```

```python
import jax
import jax.numpy as jnp
from jax import lax
from jax.experimental import pallas as pl
from jax.experimental.pallas import tpu as pltpu
from jax.sharding import PartitionSpec as P

F32 = jnp.float32
BF16 = jnp.bfloat16
HIGH = lax.Precision.HIGHEST

SIDE = 8
CELLS = SIDE**3
CH = 64
BLK = 8
ROWS = SIDE * SIDE * BLK
WIDE = SIDE * CH
SLAB = SIDE * BLK
TILES = 15
PAY = TILES * 128
LAST_COL = 81
LOSS_COL = 82

EDDY_SCALE = 2.0**-9
F16 = jnp.float16

base_visc = 0.02
time_step = 0.2


def iota(shape, dim):
    return lax.broadcasted_iota(jnp.int32, shape, dim)


def onehot(cond, dtype=BF16):
    return jnp.where(cond, 1.0, 0.0).astype(dtype)


def nt(a, b, precision=None):
    return lax.dot_general(a, b, (((1,), (1,)), ((), ())), preferred_element_type=F32, precision=precision)


def tn(a, b, precision=None):
    return lax.dot_general(a, b, (((0,), (0,)), ((), ())), preferred_element_type=F32, precision=precision)


def nn(a, b, precision=None):
    return lax.dot_general(a, b, (((1,), (0,)), ((), ())), preferred_element_type=F32, precision=precision)


def core_half(at):
    return (at ^ (at >> 1)) & 1


def net_kernel(
    vel, tgt, w1, w2, w3, own, blk,
    keep, send, eddy_out, halo1, halo2, halo3, halo4,
    hx_a, hx_b, hy_b, hz, pool_s, fp_s, i1_s, a_s, d_s, tt_s, tb_s, pre_s, slope1_s, ah_s, slope2_s, dw_s, big_s, gh_s,
):
    gx_at, gy_at = lax.axis_index("gx"), lax.axis_index("gy")
    half = core_half(gy_at)
    dev = (gx_at * lax.axis_size("gy") + gy_at) * lax.axis_size("role") + lax.axis_index("role")
    trainers = lax.axis_size("gx") * lax.axis_size("gy") * lax.axis_size("role")
    gx_odd, gy_odd = gx_at & 1 == 1, gy_at & 1 == 1

    for c in range(3):
        for x in range(SIDE):
            both = vel[c, 2 * x] + vel[c, 2 * x + 1]
            pool_s[c, x] = both
    rows = []
    for c in range(3):
        cols = []
        for x in range(SIDE):
            cols.append(pool_s[c, x, pl.ds(0, 8, stride=2), :] + pool_s[c, x, pl.ds(1, 8, stride=2), :])
        rows.append(jnp.concatenate(cols, axis=0))
    pooled = jnp.concatenate(rows, axis=0)
    zpool = jnp.where(iota((128, 1), 0) >> 1 == iota((1, 64), 1), 0.125, 0.0)
    filt = nn(pooled, zpool, HIGH).astype(BF16)
    tgt_rows = tgt[...].reshape(64, 64)
    zsel = jnp.concatenate([filt[0:64], filt[64:128], filt[128:192], tgt_rows], axis=1)
    spread = onehot(iota((ROWS, 1), 0) >> 3 == iota((1, 64), 1))
    by_block = nn(spread, zsel)
    mine = (iota((1, 256), 1) & 63) >> 3 == iota((ROWS, 1), 0) & 7
    by_block = jnp.where(mine, by_block, 0.0).astype(BF16)
    lane_in = iota((1, 256), 1)
    lane_off = lax.div(lane_in, 24)
    lane_cz = lane_in - lane_off * 24
    src = iota((256, 1), 0)
    pick = onehot(jnp.where(lane_in < 216, lane_cz, -1) == (src >> 6) * 8 + (src & 7))
    cells = nn(by_block, pick)
    pick_t = onehot(jnp.where(src >= 192, src & 7, -1) == iota((1, SIDE), 1))
    target = nn(by_block, pick_t)

    fp_s[...] = jnp.zeros(fp_s.shape, F32)
    fp_s[1:9, 1:9] = cells.reshape(SIDE, SIDE, BLK, 256)
    group = lax.div(iota((1, 1, 1, 256), 3), 24)
    for x in range(SIDE):
        acc = jnp.zeros((1, SIDE, BLK, 256), F32)
        for k in range(9):
            part = fp_s[x + k // 3 : x + k // 3 + 1, k % 3 : k % 3 + SIDE]
            acc = jnp.where(group == k, part, acc)
        i1_s[x * SLAB : (x + 1) * SLAB, :] = acc.reshape(SLAB, 256).astype(BF16)

    j_at = iota((81, 1), 0)
    j_off, j_dz, j_c = lax.div(j_at, 9), lax.rem(lax.div(j_at, 3), 3) - 1, lax.rem(j_at, 3)
    lane_key = jnp.where(lane_in < 216, lane_off * 4 + (lane_cz >> 3), -1)
    same = lane_key == j_off * 4 + j_c
    delta = jnp.where(same, (lane_in & 7) - j_dz, -9)
    w1v = w1[...]
    t1 = jnp.concatenate([nn(w1v, onehot(delta == z)).astype(BF16) for z in range(SIDE)], axis=0)
    pre_s[...] = nt(i1_s[...], t1)

    src = iota((320, 1), 0) - 64
    dst = iota((1, 512), 1)
    wanted = ((dst >> 7) - 2 + ((dst & 127) >> 6)) * 64 + (dst & 63)
    chooser = onehot(jnp.where((src >= 0) & (src < 192), src - 64, -999) == wanted)
    zero_tile = jnp.zeros((64, 128), BF16)
    for k in range(9):
        base = (192 * k) // 128 * 128
        off = 192 * k - base
        width = min(256, 1728 - base)
        tiles = nn(w2[:, base : base + width], chooser[64 - off : 64 - off + width]).astype(BF16)
        ks, js = k // 3, k % 3
        kb, jb = (8 - k) // 3, (8 - k) % 3
        for z in range(SIDE):
            for m in range(4):
                d = 2 * m - z
                tile = tiles[:, (d + 2) * 128 : (d + 3) * 128] if -2 <= d <= 1 else zero_tile
                tt_s[ks, z * 64 : (z + 1) * 64, js * 512 + m * 128 : js * 512 + (m + 1) * 128] = tile
                tb_s[kb, jb * 512 + z * 64 : jb * 512 + (z + 1) * 64, m * 128 : (m + 1) * 128] = tile

    def shifted_store(dst_ref, x, val):
        zero = jnp.zeros((1, BLK, WIDE), F32)
        lo, hi = (x + 1) * SLAB, (x + 2) * SLAB
        dst_ref[lo:hi, 0:512] = jnp.concatenate([zero, val[:-1]], axis=0).reshape(SLAB, WIDE).astype(BF16)
        dst_ref[lo:hi, 512:1024] = val.reshape(SLAB, WIDE).astype(BF16)
        dst_ref[lo:hi, 1024:1536] = jnp.concatenate([val[1:], zero], axis=0).reshape(SLAB, WIDE).astype(BF16)

    for ref in (a_s, d_s):
        ref[0:SLAB, :] = jnp.zeros((SLAB, 1536), BF16)
        ref[9 * SLAB :, :] = jnp.zeros((SLAB, 1536), BF16)

    for x in range(SIDE):
        pre = pre_s[x * SLAB : (x + 1) * SLAB, :]
        sig = jax.nn.sigmoid(pre)
        slope1_s[x * SLAB : (x + 1) * SLAB, :] = sig * (1.0 + pre * (1.0 - sig))
        shifted_store(a_s, x, (pre * sig).reshape(SIDE, BLK, WIDE))

    acc = nt(a_s[0:ROWS, :], tt_s[0])
    acc = acc + nt(a_s[SLAB : SLAB + ROWS, :], tt_s[1])
    pre_s[...] = acc + nt(a_s[2 * SLAB : 2 * SLAB + ROWS, :], tt_s[2])
    for x in range(SIDE):
        pre = pre_s[x * SLAB : (x + 1) * SLAB, :]
        sig = jax.nn.sigmoid(pre)
        slope2_s[x * SLAB : (x + 1) * SLAB, :] = sig * (1.0 + pre * (1.0 - sig))
        ah_s[x * SLAB : (x + 1) * SLAB, :] = (pre * sig).astype(BF16)

    tile8 = onehot(iota((64, 1), 0) == iota((1, WIDE), 1) & 63)
    w3_wide = nn(w3[...], tile8)
    diag = iota((1, WIDE), 1) >> 6 == iota((SIDE, 1), 0)
    last = jnp.where(diag, w3_wide, 0.0).astype(BF16)
    logits = nt(ah_s[...], last)
    eddy = 0.5 * (jnp.maximum(logits, 0.0) + jnp.log1p(jnp.exp(-jnp.abs(logits))))
    error = eddy - target
    losses = jnp.sum(jnp.sum((error * error).reshape(64, BLK, SIDE), axis=0), axis=1, keepdims=True) / CELLS
    d_logit = (error * jax.nn.sigmoid(logits) / (trainers * CELLS)).astype(BF16)

    zrep = onehot(iota((SIDE, 1), 0) == (iota((1, 128), 1) & 15) >> 1, F32)
    fine = nn(eddy, zrep, HIGH)
    fine = jnp.where(iota((1, 128), 1) >> 4 == iota((ROWS, 1), 0) & 7, fine, 0.0)
    fine = jnp.sum(fine.reshape(64, BLK, 128), axis=1)
    eddy_out[...] = fine

    for c in range(3):
        for i in range(2):
            lo, hi = vel[c, i], vel[c, 14 + i]
            at = (c * 2 + i) * 16
            hx_a[at : at + 16, :] = jnp.where(gx_odd, lo, hi)
            hx_b[at : at + 16, :] = jnp.where(gx_odd, hi, lo)
    small = fine * EDDY_SCALE
    hx_a[96:104, :] = jnp.where(gx_odd, small[0:8], small[56:64])
    hx_b[96:104, :] = jnp.where(gx_odd, small[56:64], small[0:8])
    core = send.at[480:584]
    for c in range(3):
        for i in range(2):
            lo = jnp.concatenate([vel[c, x, i : i + 1, :] for x in range(16)], axis=0)
            hi = jnp.concatenate([vel[c, x, 14 + i : 15 + i, :] for x in range(16)], axis=0)
            at = (c * 2 + i) * 16
            core[at : at + 16, :] = jnp.where(gy_odd, lo, hi)
            hy_b[at : at + 16, :] = jnp.where(gy_odd, hi, lo)
    lo = eddy_out[pl.ds(0, 8, stride=8), :] * EDDY_SCALE
    hi = eddy_out[pl.ds(7, 8, stride=8), :] * EDDY_SCALE
    core[96:104, :] = jnp.where(gy_odd, lo, hi)
    hy_b[96:104, :] = jnp.where(gy_odd, hi, lo)
    vt = jnp.transpose(vel[...].reshape(768, 128))
    et = jnp.transpose(jnp.concatenate([small, jnp.zeros((64, 128), F32)], axis=0))
    hz[...] = jnp.zeros(hz.shape, F32)
    for t in range(6):
        hz[t * 8 : t * 8 + 2, :] = vt[0:2, t * 128 : (t + 1) * 128]
        hz[t * 8 + 2 : t * 8 + 4, :] = vt[126:128, t * 128 : (t + 1) * 128]
    hz[48:49, :] = et[0:1]
    hz[49:50, :] = et[127:128]
    second = half == 1
    halo1[...] = jnp.where(second, hx_a[...], hy_b[...])
    halo2[...] = jnp.where(second, hy_b[...], hz[...])
    halo3[...] = jnp.where(second, hx_b[...], hx_a[...])
    halo4[...] = jnp.where(second, hz[...], hx_b[...])

    code = own[...] * BLK + blk[...]
    listed = code.shape[1]
    wanted = gx_at * BLK + iota((BLK, listed), 0)
    count = jnp.sum(jnp.where(code == wanted, 1.0, 0.0), axis=1, keepdims=True)
    count_rows = jnp.broadcast_to(count.reshape(1, BLK, 1), (64, BLK, 1)).reshape(ROWS, 1)

    big_s[:, 0:512] = nn(d_logit, last)
    for x in range(SIDE):
        d_hid = big_s[x * SLAB : (x + 1) * SLAB, 0:512] * slope2_s[x * SLAB : (x + 1) * SLAB, :]
        d_hid = d_hid.astype(BF16).astype(F32).reshape(SIDE, BLK, WIDE)
        shifted_store(d_s, x, d_hid)
        dw_s[x * SLAB : (x + 1) * SLAB, :] = (d_hid * count[None]).reshape(SLAB, WIDE)
    dwt = jnp.transpose(dw_s[...]).astype(BF16)

    gh_s[...] = jnp.zeros(gh_s.shape, F32)
    low_half = iota((64, 128), 1) < 64
    for k in range(9):
        dx, j = k // 3, k % 3
        for q in range(2):
            zs = slice(q * 192, q * 192 + 320)
            cols = slice(j * 512 + q * 256, j * 512 + (q + 1) * 256)
            big_s[zs, q * 256 : (q + 1) * 256] = nn(dwt[zs], a_s[dx * SLAB : dx * SLAB + ROWS, cols])
        sums = []
        for m in (-1, 0, 1, 2):
            tot = None
            for p in range(4):
                z = 2 * p + m
                if 0 <= z < SIDE:
                    part = big_s[z * 64 : (z + 1) * 64, p * 128 : (p + 1) * 128]
                    tot = part if tot is None else tot + part
            sums.append(tot)
        for dz in (-1, 0, 1):
            low, high = sums[1 - dz], sums[2 - dz]
            at = (k * 3 + dz + 1) * 64
            tile, odd = at // 128 * 128, at % 128 != 0
            if odd:
                val = high + pltpu.roll(low, 64, 1)
                gh_s[:, tile : tile + 128] += jnp.where(low_half, 0.0, val)
            else:
                val = low + pltpu.roll(high, 64, 1)
                gh_s[:, tile : tile + 128] += jnp.where(low_half, val, 0.0)

    acc = nn(d_s[0:ROWS, :], tb_s[0])
    acc = acc + nn(d_s[SLAB : SLAB + ROWS, :], tb_s[1])
    acc = acc + nn(d_s[2 * SLAB : 2 * SLAB + ROWS, :], tb_s[2])
    d_first = (acc * slope1_s[...]).astype(BF16).astype(F32)
    dw_s[...] = (d_first.reshape(64, BLK, WIDE) * count[None]).reshape(ROWS, WIDE)
    d1t = jnp.transpose(dw_s[...])
    d1_hi = d1t.astype(BF16)
    d1_lo = (d1t - d1_hi.astype(F32)).astype(BF16)
    i1 = i1_s[...]
    g1 = nn(d1_hi, i1) + nn(d1_lo, i1)
    z_in = iota((1, 256), 1) & 7
    parts = []
    for dz in (-1, 0, 1):
        tot = jnp.zeros((64, 256), F32)
        for z in range(SIDE):
            if 0 <= z + dz < SIDE:
                tot = tot + jnp.where(z_in == z + dz, g1[z * 64 : (z + 1) * 64], 0.0)
        parts.append(tot)
    r_at = iota((768, 1), 0)
    c_at = iota((1, 128), 1)
    r_lane = r_at & 255
    r_off = lax.div(r_lane, 24)
    r_col = (r_off * 3 + (r_at >> 8)) * 3 + ((r_lane - r_off * 24) >> 3)
    fold = onehot(jnp.where(r_lane < 216, r_col, -1) == c_at, F32)
    g_first = nn(jnp.concatenate(parts, axis=1), fold, HIGH)

    dlw = d_logit.astype(F32) * count_rows
    dl_hi = dlw.astype(BF16)
    dl_lo = (dlw - dl_hi.astype(F32)).astype(BF16)
    ah = ah_s[...]
    gl = tn(dl_hi, ah) + tn(dl_lo, ah)
    gl = jnp.where(diag, gl, 0.0)
    fold_o = onehot(iota((1, WIDE), 1) & 63 == iota((64, 1), 0), F32)
    g_last = jnp.sum(nt(fold_o, gl, HIGH), axis=1, keepdims=True)

    lane8 = iota((BLK, 128), 1)
    loss_row = jnp.where(lane8 - (LOSS_COL + BLK * (dev >> 6)) == iota((BLK, 128), 0), losses, 0.0)
    loss_row = jnp.sum(loss_row, axis=0, keepdims=True)
    lane = iota((64, 128), 1)
    extra = jnp.where(lane == LAST_COL, g_last, g_first)
    extra = extra + jnp.where(iota((64, 128), 0) == dev & 63, loss_row, 0.0)

    for t in range(PAY // 128):
        if t == 0:
            top, bottom = extra[0:32], extra[32:64]
        else:
            top, bottom = (gh_s[r : r + 32, (t - 1) * 128 : t * 128] for r in (0, 32))
        keep[t * 32 : (t + 1) * 32, :] = jnp.where(second, bottom, top)
        send[t * 32 : (t + 1) * 32, :] = jnp.where(second, top, bottom)


def vmem_spec():
    return pl.BlockSpec(memory_space=pltpu.VMEM)


def run_net(velocity, target, w1, w2, w3, own, blk):
    f = lambda *s: pltpu.VMEM(s, F32)
    return pl.pallas_call(
        net_kernel,
        out_shape=(f(480, 128), f(584, 128), f(64, 128)) + (f(104, 128),) * 4,
        in_specs=[vmem_spec()] * 7,
        out_specs=tuple(vmem_spec() for _ in range(7)),
        scratch_shapes=[
            pltpu.VMEM((104, 128), F32),
            pltpu.VMEM((104, 128), F32),
            pltpu.VMEM((104, 128), F32),
            pltpu.VMEM((104, 128), F32),
            pltpu.VMEM((3, SIDE, 16, 128), F32),
            pltpu.VMEM((10, 10, BLK, 256), F32),
            pltpu.VMEM((ROWS, 256), BF16),
            pltpu.VMEM((ROWS + 2 * SLAB, 1536), BF16),
            pltpu.VMEM((ROWS + 2 * SLAB, 1536), BF16),
            pltpu.VMEM((3, 512, 1536), BF16),
            pltpu.VMEM((3, 1536, 512), BF16),
            pltpu.VMEM((ROWS, WIDE), F32),
            pltpu.VMEM((ROWS, WIDE), F32),
            pltpu.VMEM((ROWS, WIDE), BF16),
            pltpu.VMEM((ROWS, WIDE), F32),
            pltpu.VMEM((ROWS, WIDE), F32),
            pltpu.VMEM((ROWS, WIDE), F32),
            pltpu.VMEM((64, PAY - 128), F32),
        ],
        compiler_params=pltpu.CompilerParams(vmem_limit_bytes=56 * 1024 * 1024),
        name="net",
    )(velocity, target, w1, w2, w3, own, blk)


def flow_kernel(
    vel, eddy, got0, got1, got2, got3, got4, out, rx_a, rx_b, ry_a, ry_b, rz, vx_s, vy_s, visc_s, ez_s
):
    gx_at, gy_at = lax.axis_index("gx"), lax.axis_index("gy")
    gx_odd, gy_odd = gx_at & 1 == 1, gy_at & 1 == 1
    second = core_half(gy_at) == 1
    ry_a[...] = got0[...]
    ry_b[...] = jnp.where(second, got2[...], got1[...])
    rx_a[...] = jnp.where(second, got1[...], got3[...])
    rx_b[...] = jnp.where(second, got3[...], got4[...])
    rz[...] = jnp.where(second, got4[...], got2[...])
    lane = iota((1, 128), 1)

    def sides(odd, a, b, at, rows):
        one, two = a[at : at + rows, :], b[at : at + rows, :]
        return jnp.where(odd, one, two), jnp.where(odd, two, one)

    for c in range(3):
        for x in range(16):
            vy_s[(c * 16 + x) * 32 + 8 : (c * 16 + x) * 32 + 24, :] = vel[c, x]
        for i in range(2):
            below, above = sides(gy_odd, ry_a, ry_b, (c * 2 + i) * 16, 16)
            vy_s[pl.ds(c * 512 + 6 + i, 16, stride=32), :] = below
            vy_s[pl.ds(c * 512 + 24 + i, 16, stride=32), :] = above
            below, above = sides(gx_odd, rx_a, rx_b, (c * 2 + i) * 16, 16)
            vx_s[c, i] = below
            vx_s[c, 2 + i] = above

    zcols = jnp.concatenate([jnp.transpose(rz[t * 8 : t * 8 + 8, :]) for t in range(7)], axis=0)
    coarse = eddy[...]
    e_first, e_last = zcols[768:832, 0:1] / EDDY_SCALE, zcols[768:832, 1:2] / EDDY_SCALE
    ahead = jnp.where(lane == 127, e_first, pltpu.roll(coarse, 127, 1))
    behind = jnp.where(lane == 0, e_last, pltpu.roll(coarse, 1, 1))
    below_x, above_x = (v / EDDY_SCALE for v in sides(gx_odd, rx_a, rx_b, 96, 8))
    below_y, above_y = (v / EDDY_SCALE for v in sides(gy_odd, ry_a, ry_b, 96, 8))

    def put(dst, plane, val):
        dst[pl.ds(plane * 32 + 8, 8, stride=2), :] = val
        dst[pl.ds(plane * 32 + 9, 8, stride=2), :] = val

    put(visc_s, 0, base_visc + below_x)
    put(visc_s, 17, base_visc + above_x)
    for x in range(8):
        for r in range(2):
            plane = 2 * x + 1 + r
            put(visc_s, plane, base_visc + coarse[x * 8 : x * 8 + 8])
            visc_s[plane * 32 + 7 : plane * 32 + 8, :] = base_visc + below_y[x : x + 1]
            visc_s[plane * 32 + 24 : plane * 32 + 25, :] = base_visc + above_y[x : x + 1]
        put(ez_s, 2 * x, base_visc + ahead[x * 8 : x * 8 + 8])
        put(ez_s, 2 * x + 1, base_visc + behind[x * 8 : x * 8 + 8])

    def plane_of(c, x):
        if x < 0:
            return vx_s[c, x + 2]
        if x > 15:
            return vx_s[c, x - 14]
        return vel[c, x]

    for x in range(16):
        vat = (x + 1) * 32
        visc = visc_s[vat + 8 : vat + 24, :]
        faces = (
            (visc_s[vat + 40 : vat + 56, :], visc_s[vat - 24 : vat - 8, :]),
            (visc_s[vat + 9 : vat + 25, :], visc_s[vat + 7 : vat + 23, :]),
            (
                ez_s[(x // 2 * 2) * 32 + 8 : (x // 2 * 2) * 32 + 24, :],
                ez_s[(x // 2 * 2 + 1) * 32 + 8 : (x // 2 * 2 + 1) * 32 + 24, :],
            ),
        )
        faces = [(0.5 * (visc + a), 0.5 * (visc + b)) for a, b in faces]
        wind = [vel[a, x] for a in range(3)]
        for c in range(3):
            u = vel[c, x]
            at = (c * 16 + x) * 32
            zat = (c * 16 + x) * 16
            zc = zcols[zat : zat + 16]
            p1 = jnp.where(lane == 127, zc[:, 0:1], pltpu.roll(u, 127, 1))
            p2 = jnp.where(lane == 127, zc[:, 1:2], jnp.where(lane == 126, zc[:, 0:1], pltpu.roll(u, 126, 1)))
            m1 = jnp.where(lane == 0, zc[:, 3:4], pltpu.roll(u, 1, 1))
            m2 = jnp.where(lane == 0, zc[:, 2:3], jnp.where(lane == 1, zc[:, 3:4], pltpu.roll(u, 2, 1)))
            near = (
                (plane_of(c, x + 1), plane_of(c, x - 1), plane_of(c, x + 2), plane_of(c, x - 2)),
                (
                    vy_s[at + 9 : at + 25, :], vy_s[at + 7 : at + 23, :],
                    vy_s[at + 10 : at + 26, :], vy_s[at + 6 : at + 22, :],
                ),
                (p1, m1, p2, m2),
            )
            advect = None
            diffuse = None
            for a in range(3):
                q1, b1, q2, b2 = near[a]
                slope = (8.0 * (q1 - b1) - (q2 - b2)) * (1.0 / 12.0)
                term = wind[a] * slope
                advect = term if advect is None else advect + term
                flux = faces[a][0] * (q1 - u) - faces[a][1] * (u - b1)
                diffuse = flux if diffuse is None else diffuse + flux
            out[c, x] = u + time_step * (diffuse - advect)


def run_flow(velocity, eddy, *got):
    return pl.pallas_call(
        flow_kernel,
        out_shape=jax.ShapeDtypeStruct(velocity.shape, F32),
        in_specs=[vmem_spec()] * 7,
        out_specs=vmem_spec(),
        scratch_shapes=[
            pltpu.VMEM((104, 128), F32),
            pltpu.VMEM((104, 128), F32),
            pltpu.VMEM((104, 128), F32),
            pltpu.VMEM((104, 128), F32),
            pltpu.VMEM((104, 128), F32),
            pltpu.VMEM((3, 4, 16, 128), F32),
            pltpu.VMEM((3 * 16 * 32, 128), F32),
            pltpu.VMEM((18 * 32, 128), F32),
            pltpu.VMEM((16 * 32, 128), F32),
        ],
        compiler_params=pltpu.CompilerParams(vmem_limit_bytes=32 * 1024 * 1024),
        name="flow",
    )(velocity, eddy, *got)


def finish_kernel(own, blk, mine, other, loss_out, first_out, hidden_out, last_out, ext_s):
    gx_at, gy_at = lax.axis_index("gx"), lax.axis_index("gy")
    n_z = lax.axis_size("role")
    in_group = gy_at * n_z + lax.axis_index("role")
    second = core_half(gy_at) == 1
    for t in range(PAY // 128):
        one, two = mine[t * 32 : (t + 1) * 32, :], other[t * 32 : (t + 1) * 32, :]
        top, bottom = jnp.where(second, two, one), jnp.where(second, one, two)
        if t == 0:
            ext_s[0:32, :] = top
            ext_s[32:64, :] = bottom
        else:
            at = (t - 1) * 128
            width = min(128, 27 * CH - at)
            hidden_out[0:32, at : at + width] = top[:, :width]
            hidden_out[32:64, at : at + width] = bottom[:, :width]
    extra = ext_s[...]
    first_out[...] = extra[:, 0:81]
    turned = jnp.transpose(jnp.concatenate([extra, jnp.zeros((64, 128), F32)], axis=0))
    last_out[...] = turned[LAST_COL : LAST_COL + 1, 0:64]
    slots = loss_out.shape[1]
    lane = iota((1, 128), 1)
    slot_lane = iota((1, slots), 1)
    picked = jnp.zeros((1, slots), F32)
    for s in range(slots):
        at = gx_at * slots + s
        dev = own[0, at] * (lax.axis_size("gy") * n_z) + in_group
        row = ext_s[pl.ds(dev & 63, 1), :]
        col = LOSS_COL + BLK * (dev >> 6) + blk[0, at]
        value = jnp.sum(jnp.where(lane == col, row, 0.0), axis=1, keepdims=True)
        picked = jnp.where(slot_lane == s, value, picked)
    loss_out[...] = picked


def run_finish(own, blk, mine, other, slots):
    smem = pl.BlockSpec(memory_space=pltpu.SMEM)
    f = lambda *s: jax.ShapeDtypeStruct(s, F32)
    return pl.pallas_call(
        finish_kernel,
        out_shape=(f(1, slots), f(64, 81), f(64, 27 * CH), f(1, 64)),
        in_specs=[smem] * 2 + [vmem_spec()] * 2,
        out_specs=tuple(vmem_spec() for _ in range(4)),
        scratch_shapes=[pltpu.VMEM((64, 128), F32)],
        compiler_params=pltpu.CompilerParams(vmem_limit_bytes=32 * 1024 * 1024),
        name="finish",
    )(own, blk, mine, other)


def on_device(velocity, target_visc, w_first, w_hidden, w_last, sample_owner, sample_block):
    n_x, n_y, n_z = lax.axis_size("gx"), lax.axis_size("gy"), lax.axis_size("role")
    trainers = n_x * n_y * n_z
    own = sample_owner.reshape(1, -1)
    blk = sample_block.reshape(1, -1)
    slots = own.shape[1] // n_x

    axes = ("gx", "gy", "role")

    def even_odd(i, count):
        return i ^ 1

    def odd_even(i, count):
        return (i - 1) % count if i % 2 == 0 else (i + 1) % count

    def partner(kind, i, j, r):
        if kind == "x":
            j = odd_even(j, n_y)
        elif kind == "y":
            r = r ^ 1
        elif kind == "z_a":
            i = even_odd(i, n_x)
        else:
            i = odd_even(i, n_x)
        return (i * n_y + j) * n_z + r

    def mixed(kinds):
        pairs = []
        for i in range(n_x):
            for j in range(n_y):
                for r in range(n_z):
                    pairs.append(((i * n_y + j) * n_z + r, partner(kinds[(j ^ (j >> 1)) & 1], i, j, r)))
        return pairs

    core_pairs = [(j, even_odd(j, n_y)) for j in range(n_y)]
    size = TILES * 32

    keep, send, eddy, *halos = run_net(
        velocity, target_visc, w_first, w_hidden, w_last.reshape(1, CH), own, blk
    )
    half = core_half(lax.axis_index("gy"))
    got = lax.ppermute(send, "gy", core_pairs)
    total = keep + got[:size]
    rims = [got[size:]]
    halos = [h.astype(F16) for h in halos]

    def widen(values, exps):
        wide = values.astype(F32).reshape(TILES, 32, 128) * jnp.exp2(exps)[:, None, :]
        return wide.reshape(size, 128)

    top = jnp.max(jnp.abs(total.reshape(TILES, 32, 128)), axis=1)
    exps = jnp.clip(jnp.ceil(jnp.log2(jnp.maximum(top, 1e-30))) - 13.0, -110.0, 110.0)
    orders = (("x", "y", "z_a", "z_b"), ("z_a", "x", "z_b", "y"))
    far = None
    for s in range(4):
        kinds = (orders[0][s], orders[1][s])
        if s == 1:
            far = lax.ppermute(halos[3], axes, mixed((orders[0][3], orders[1][3])))
        scaled = total.reshape(TILES, 32, 128) * jnp.exp2(-exps)[:, None, :]
        pieces = [scaled.reshape(size, 128).astype(F16), jnp.pad(exps, ((0, 1), (0, 0))).astype(F16)]
        message = jnp.concatenate(pieces + [halos[s]] if s < 3 else pieces, axis=0)
        message = lax.optimization_barrier(message)
        got = lax.ppermute(message, axes, mixed(kinds))
        their_exps = got[size : size + TILES].astype(F32)
        mine, theirs = widen(message[:size], exps), widen(got[:size], their_exps)
        if n_x != 4 and "z_b" in kinds:
            theirs = jnp.where(half == kinds.index("z_b"), 0.0, theirs)
        total = mine + theirs
        exps = jnp.maximum(exps, their_exps) + 1.0
        if s < 3:
            rims.append(got[size + 16 :].astype(F32))
        if s == 1:
            total, far = lax.optimization_barrier((total, far))
        if s == 2:
            u_next = run_flow(velocity, eddy, *rims, far.astype(F32))
    total, u_next = lax.optimization_barrier((total, u_next))
    if n_x != 4:
        for bit in range(1, n_x.bit_length() - 1):
            total = total + lax.ppermute(total, "gx", [(i, i ^ (1 << bit)) for i in range(n_x)])
    other = lax.ppermute(total, "gy", core_pairs)

    losses, first, hidden, last = run_finish(own, blk, total, other, slots)
    return (u_next, losses.reshape(1, 1, slots), first, hidden, last.reshape(CH))


def solution(mesh):
    return jax.shard_map(
        on_device,
        mesh=mesh,
        in_specs=(
            P(None, "gx", "gy", "role"),
            P("gx", "gy", "role"),
            P(),
            P(),
            P(),
            P("gy", "role", None, None),
            P("gy", "role", None, None),
        ),
        out_specs=(P(None, "gx", "gy", "role"), P("gy", "role", "gx"), P(), P(), P()),
        check_vma=False,
    )
```

```python
import jax
import jax.numpy as jnp
from jax import lax
from jax.experimental import pallas as pl
from jax.experimental.pallas import tpu as pltpu
from jax.sharding import PartitionSpec as P

F32 = jnp.float32
BF16 = jnp.bfloat16
HIGH = lax.Precision.HIGHEST

SIDE = 8
CELLS = SIDE**3
CH = 64
BLK = 8
ROWS = SIDE * SIDE * BLK
WIDE = SIDE * CH
SLAB = SIDE * BLK
TILES = 15
PAY = TILES * 128
LAST_COL = 81
LOSS_COL = 82

EDDY_SCALE = 2.0**-9
F16 = jnp.float16

base_visc = 0.02
time_step = 0.2


def iota(shape, dim):
    return lax.broadcasted_iota(jnp.int32, shape, dim)


def onehot(cond, dtype=BF16):
    return jnp.where(cond, 1.0, 0.0).astype(dtype)


def sigmoid(v):
    return 0.5 + 0.5 * jnp.tanh(0.5 * v)


def nt(a, b, precision=None):
    return lax.dot_general(a, b, (((1,), (1,)), ((), ())), preferred_element_type=F32, precision=precision)


def tn(a, b, precision=None):
    return lax.dot_general(a, b, (((0,), (0,)), ((), ())), preferred_element_type=F32, precision=precision)


def nn(a, b, precision=None):
    return lax.dot_general(a, b, (((1,), (0,)), ((), ())), preferred_element_type=F32, precision=precision)


def core_half(at):
    return (at ^ (at >> 1)) & 1


def net_kernel(
    vel, tgt, w1, w2, w3, own, blk,
    keep, send, eddy_out, halo1, halo2, halo3, halo4,
    hx_a, hx_b, hy_b, hz, pool_s, fp_s, i1_s, a_s, d_s, tt_s, tb_s, pre_s, slope1_s, ah_s, slope2_s, dw_s, big_s, gh_s, w2_s,
):
    gx_at, gy_at = lax.axis_index("gx"), lax.axis_index("gy")
    half = core_half(gy_at)
    dev = (gx_at * lax.axis_size("gy") + gy_at) * lax.axis_size("role") + lax.axis_index("role")
    trainers = lax.axis_size("gx") * lax.axis_size("gy") * lax.axis_size("role")
    gx_odd, gy_odd = gx_at & 1 == 1, gy_at & 1 == 1

    for c in range(3):
        for x in range(SIDE):
            both = vel[c, 2 * x] + vel[c, 2 * x + 1]
            pool_s[c, x] = both
    rows = []
    for c in range(3):
        cols = []
        for x in range(SIDE):
            cols.append(pool_s[c, x, pl.ds(0, 8, stride=2), :] + pool_s[c, x, pl.ds(1, 8, stride=2), :])
        rows.append(jnp.concatenate(cols, axis=0))
    pooled = jnp.concatenate(rows, axis=0)
    zpool = jnp.where(iota((128, 1), 0) >> 1 == iota((1, 64), 1), 0.125, 0.0)
    filt = nn(pooled, zpool, HIGH).astype(BF16)
    tgt_rows = tgt[...].reshape(64, 64)
    zsel = jnp.concatenate([filt[0:64], filt[64:128], filt[128:192], tgt_rows], axis=1)
    spread = onehot(iota((ROWS, 1), 0) >> 3 == iota((1, 64), 1))
    by_block = nn(spread, zsel)
    mine = (iota((1, 256), 1) & 63) >> 3 == iota((ROWS, 1), 0) & 7
    by_block = jnp.where(mine, by_block, 0.0).astype(BF16)
    lane_in = iota((1, 256), 1)
    lane_off = lax.div(lane_in, 24)
    lane_cz = lane_in - lane_off * 24
    src = iota((256, 1), 0)
    pick = onehot(jnp.where(lane_in < 216, lane_cz, -1) == (src >> 6) * 8 + (src & 7))
    cells = nn(by_block, pick)
    pick_t = onehot(jnp.where(src >= 192, src & 7, -1) == iota((1, SIDE), 1))
    target = nn(by_block, pick_t)

    fp_s[...] = jnp.zeros(fp_s.shape, F32)
    fp_s[1:9, 1:9] = cells.reshape(SIDE, SIDE, BLK, 256)
    group = lax.div(iota((1, 1, 1, 256), 3), 24)
    for x in range(SIDE):
        acc = jnp.zeros((1, SIDE, BLK, 256), F32)
        for k in range(9):
            part = fp_s[x + k // 3 : x + k // 3 + 1, k % 3 : k % 3 + SIDE]
            acc = jnp.where(group == k, part, acc)
        i1_s[x * SLAB : (x + 1) * SLAB, :] = acc.reshape(SLAB, 256).astype(BF16)

    j_at = iota((81, 1), 0)
    j_off, j_dz, j_c = lax.div(j_at, 9), lax.rem(lax.div(j_at, 3), 3) - 1, lax.rem(j_at, 3)
    lane_key = jnp.where(lane_in < 216, lane_off * 4 + (lane_cz >> 3), -1)
    same = lane_key == j_off * 4 + j_c
    delta = jnp.where(same, (lane_in & 7) - j_dz, -9)
    w1v = w1[...]
    t1 = jnp.concatenate([nn(w1v, onehot(delta == z)).astype(BF16) for z in range(SIDE)], axis=0)
    pre_s[...] = nt(i1_s[...], t1)

    src = iota((320, 1), 0) - 64
    dst = iota((1, 512), 1)
    wanted = ((dst >> 7) - 2 + ((dst & 127) >> 6)) * 64 + (dst & 63)
    chooser = onehot(jnp.where((src >= 0) & (src < 192), src - 64, -999) == wanted)
    zero_tile = jnp.zeros((64, 128), BF16)
    left = iota((64, 128), 1) < 64
    w2_s[:, 1664:1792] = jnp.zeros((64, 128), F32)
    w2_s[:, 0:1728] = w2[...].astype(F32)
    w2t = jnp.concatenate(
        [
            jnp.transpose(jnp.concatenate([w2_s[:, t * 128 : (t + 1) * 128]] * 2, axis=0))
            for t in range(14)
        ],
        axis=0,
    )
    for k in range(9):
        base = (192 * k) // 128 * 128
        off = 192 * k - base
        width = min(256, 1728 - base)
        tiles = nn(w2[:, base : base + width], chooser[64 - off : 64 - off + width]).astype(BF16)
        kb = 8 - k
        turned = {dz: w2t[(3 * k + dz + 1) * 64 : (3 * k + dz + 2) * 64] for dz in (-1, 0, 1)}
        turned[-2] = turned[2] = jnp.zeros((64, 128), F32)
        forward = {d: jnp.where(left, turned[d], turned[d - 1]).astype(BF16) for d in (-1, 0, 1, 2)}
        for q in range(2):
            for w in range(6):
                z = 2 * q + w
                for h in range(2):
                    m = 2 * q + h
                    at, cols = k * 384 + w * 64, slice(h * 128, (h + 1) * 128)
                    tt_s[q, at : at + 64, cols] = forward.get(z - 2 * m, zero_tile)
                    d = 2 * m - z
                    tile = tiles[:, (d + 2) * 128 : (d + 3) * 128] if -2 <= d <= 1 else zero_tile
                    at = kb * 384 + w * 64
                    tb_s[q, at : at + 64, cols] = tile

    def windows(ref, q):
        return jnp.concatenate(
            [
                ref[dx * SLAB : dx * SLAB + ROWS, j * 512 + q * 128 : j * 512 + q * 128 + 384]
                for dx in range(3)
                for j in range(3)
            ],
            axis=1,
        )

    def shifted_store(dst_ref, x, val):
        zero = jnp.zeros((1, BLK, WIDE), F32)
        lo, hi = (x + 1) * SLAB, (x + 2) * SLAB
        dst_ref[lo:hi, 0:512] = jnp.concatenate([zero, val[:-1]], axis=0).reshape(SLAB, WIDE).astype(BF16)
        dst_ref[lo:hi, 512:1024] = val.reshape(SLAB, WIDE).astype(BF16)
        dst_ref[lo:hi, 1024:1536] = jnp.concatenate([val[1:], zero], axis=0).reshape(SLAB, WIDE).astype(BF16)

    for ref in (a_s, d_s):
        ref[0:SLAB, :] = jnp.zeros((SLAB, 1536), BF16)
        ref[9 * SLAB :, :] = jnp.zeros((SLAB, 1536), BF16)

    for x in range(SIDE):
        pre = pre_s[x * SLAB : (x + 1) * SLAB, :]
        sig = sigmoid(pre)
        slope1_s[x * SLAB : (x + 1) * SLAB, :] = sig * (1.0 + pre * (1.0 - sig))
        shifted_store(a_s, x, (pre * sig).reshape(SIDE, BLK, WIDE))

    for q in range(2):
        pre_s[:, q * 256 : (q + 1) * 256] = nn(windows(a_s, q), tt_s[q])
    for x in range(SIDE):
        pre = pre_s[x * SLAB : (x + 1) * SLAB, :]
        sig = sigmoid(pre)
        slope2_s[x * SLAB : (x + 1) * SLAB, :] = sig * (1.0 + pre * (1.0 - sig))
        ah_s[x * SLAB : (x + 1) * SLAB, :] = (pre * sig).astype(BF16)

    tile8 = onehot(iota((64, 1), 0) == iota((1, WIDE), 1) & 63)
    w3_wide = nn(w3[...], tile8)
    diag = iota((1, WIDE), 1) >> 6 == iota((SIDE, 1), 0)
    last = jnp.where(diag, w3_wide, 0.0).astype(BF16)
    logits = nt(ah_s[...], last)
    eddy = 0.5 * (jnp.maximum(logits, 0.0) + jnp.log1p(jnp.exp(-jnp.abs(logits))))
    error = eddy - target
    losses = jnp.sum(jnp.sum((error * error).reshape(64, BLK, SIDE), axis=0), axis=1, keepdims=True) / CELLS
    d_logit = (error * sigmoid(logits) / (trainers * CELLS)).astype(BF16)

    zrep = onehot(iota((SIDE, 1), 0) == (iota((1, 128), 1) & 15) >> 1, F32)
    fine = nn(eddy, zrep, HIGH)
    fine = jnp.where(iota((1, 128), 1) >> 4 == iota((ROWS, 1), 0) & 7, fine, 0.0)
    fine = jnp.sum(fine.reshape(64, BLK, 128), axis=1)
    eddy_out[...] = fine

    for c in range(3):
        for i in range(2):
            lo, hi = vel[c, i], vel[c, 14 + i]
            at = (c * 2 + i) * 16
            hx_a[at : at + 16, :] = jnp.where(gx_odd, lo, hi)
            hx_b[at : at + 16, :] = jnp.where(gx_odd, hi, lo)
    small = fine * EDDY_SCALE
    hx_a[96:104, :] = jnp.where(gx_odd, small[0:8], small[56:64])
    hx_b[96:104, :] = jnp.where(gx_odd, small[56:64], small[0:8])
    core = send.at[480:584]
    for c in range(3):
        for i in range(2):
            lo = jnp.concatenate([vel[c, x, i : i + 1, :] for x in range(16)], axis=0)
            hi = jnp.concatenate([vel[c, x, 14 + i : 15 + i, :] for x in range(16)], axis=0)
            at = (c * 2 + i) * 16
            core[at : at + 16, :] = jnp.where(gy_odd, lo, hi)
            hy_b[at : at + 16, :] = jnp.where(gy_odd, hi, lo)
    lo = eddy_out[pl.ds(0, 8, stride=8), :] * EDDY_SCALE
    hi = eddy_out[pl.ds(7, 8, stride=8), :] * EDDY_SCALE
    core[96:104, :] = jnp.where(gy_odd, lo, hi)
    hy_b[96:104, :] = jnp.where(gy_odd, hi, lo)
    vt = jnp.transpose(vel[...].reshape(768, 128))
    et = jnp.transpose(jnp.concatenate([small, jnp.zeros((64, 128), F32)], axis=0))
    hz[...] = jnp.zeros(hz.shape, F32)
    for t in range(6):
        hz[t * 8 : t * 8 + 2, :] = vt[0:2, t * 128 : (t + 1) * 128]
        hz[t * 8 + 2 : t * 8 + 4, :] = vt[126:128, t * 128 : (t + 1) * 128]
    hz[48:49, :] = et[0:1]
    hz[49:50, :] = et[127:128]
    second = half == 1
    halo1[...] = jnp.where(second, hx_a[...], hy_b[...])
    halo2[...] = jnp.where(second, hy_b[...], hz[...])
    halo3[...] = jnp.where(second, hx_b[...], hx_a[...])
    halo4[...] = jnp.where(second, hz[...], hx_b[...])

    code = own[...] * BLK + blk[...]
    listed = code.shape[1]
    wanted = gx_at * BLK + iota((BLK, listed), 0)
    count = jnp.sum(jnp.where(code == wanted, 1.0, 0.0), axis=1, keepdims=True)
    count_rows = jnp.broadcast_to(count.reshape(1, BLK, 1), (64, BLK, 1)).reshape(ROWS, 1)

    big_s[:, 0:512] = nn(d_logit, last)
    for x in range(SIDE):
        d_hid = big_s[x * SLAB : (x + 1) * SLAB, 0:512] * slope2_s[x * SLAB : (x + 1) * SLAB, :]
        d_hid = d_hid.astype(BF16).astype(F32).reshape(SIDE, BLK, WIDE)
        shifted_store(d_s, x, d_hid)
        dw_s[x * SLAB : (x + 1) * SLAB, :] = (d_hid * count[None]).reshape(SLAB, WIDE).astype(BF16)
    dwt = jnp.transpose(dw_s[...])

    gh_s[...] = jnp.zeros(gh_s.shape, F32)
    low_half = iota((64, 128), 1) < 64
    for k in range(9):
        dx, j = k // 3, k % 3
        for q in range(2):
            zs = slice(q * 192, q * 192 + 320)
            cols = slice(j * 512 + q * 256, j * 512 + (q + 1) * 256)
            big_s[zs, q * 256 : (q + 1) * 256] = nn(dwt[zs], a_s[dx * SLAB : dx * SLAB + ROWS, cols])
        sums = []
        for m in (-1, 0, 1, 2):
            tot = None
            for p in range(4):
                z = 2 * p + m
                if 0 <= z < SIDE:
                    part = big_s[z * 64 : (z + 1) * 64, p * 128 : (p + 1) * 128]
                    tot = part if tot is None else tot + part
            sums.append(tot)
        for dz in (-1, 0, 1):
            low, high = sums[1 - dz], sums[2 - dz]
            at = (k * 3 + dz + 1) * 64
            tile, odd = at // 128 * 128, at % 128 != 0
            if odd:
                val = high + pltpu.roll(low, 64, 1)
                gh_s[:, tile : tile + 128] += jnp.where(low_half, 0.0, val)
            else:
                val = low + pltpu.roll(high, 64, 1)
                gh_s[:, tile : tile + 128] += jnp.where(low_half, val, 0.0)

    for q in range(2):
        pre_s[:, q * 256 : (q + 1) * 256] = nn(windows(d_s, q), tb_s[q])
    for x in range(SIDE):
        rows = slice(x * SLAB, (x + 1) * SLAB)
        d_first = (pre_s[rows, :] * slope1_s[rows, :]).astype(BF16).astype(F32)
        dw_s[rows, :] = (d_first.reshape(SIDE, BLK, WIDE) * count[None]).reshape(SLAB, WIDE).astype(BF16)
    g1 = nn(jnp.transpose(dw_s[...]), i1_s[...])
    z_in = iota((1, 256), 1) & 7
    parts = []
    for dz in (-1, 0, 1):
        tot = jnp.zeros((64, 256), F32)
        for z in range(SIDE):
            if 0 <= z + dz < SIDE:
                tot = tot + jnp.where(z_in == z + dz, g1[z * 64 : (z + 1) * 64], 0.0)
        parts.append(tot)
    r_at = iota((768, 1), 0)
    c_at = iota((1, 128), 1)
    r_lane = r_at & 255
    r_off = lax.div(r_lane, 24)
    r_col = (r_off * 3 + (r_at >> 8)) * 3 + ((r_lane - r_off * 24) >> 3)
    fold = onehot(jnp.where(r_lane < 216, r_col, -1) == c_at, F32)
    g_first = nn(jnp.concatenate(parts, axis=1), fold, HIGH)

    dlw = d_logit.astype(F32) * count_rows
    dl_hi = dlw.astype(BF16)
    dl_lo = (dlw - dl_hi.astype(F32)).astype(BF16)
    ah = ah_s[...]
    gl = tn(dl_hi, ah) + tn(dl_lo, ah)
    gl = jnp.where(diag, gl, 0.0)
    fold_o = onehot(iota((1, WIDE), 1) & 63 == iota((64, 1), 0), F32)
    g_last = jnp.sum(nt(fold_o, gl, HIGH), axis=1, keepdims=True)

    lane8 = iota((BLK, 128), 1)
    loss_row = jnp.where(lane8 - (LOSS_COL + BLK * (dev >> 6)) == iota((BLK, 128), 0), losses, 0.0)
    loss_row = jnp.sum(loss_row, axis=0, keepdims=True)
    lane = iota((64, 128), 1)
    extra = jnp.where(lane == LAST_COL, g_last, g_first)
    extra = extra + jnp.where(iota((64, 128), 0) == dev & 63, loss_row, 0.0)

    for t in range(PAY // 128):
        if t == 0:
            top, bottom = extra[0:32], extra[32:64]
        else:
            top, bottom = (gh_s[r : r + 32, (t - 1) * 128 : t * 128] for r in (0, 32))
        keep[t * 32 : (t + 1) * 32, :] = jnp.where(second, bottom, top)
        send[t * 32 : (t + 1) * 32, :] = jnp.where(second, top, bottom)


def vmem_spec():
    return pl.BlockSpec(memory_space=pltpu.VMEM)


def run_net(velocity, target, w1, w2, w3, own, blk):
    f = lambda *s: pltpu.VMEM(s, F32)
    return pl.pallas_call(
        net_kernel,
        out_shape=(f(480, 128), f(584, 128), f(64, 128)) + (f(104, 128),) * 4,
        in_specs=[vmem_spec()] * 7,
        out_specs=tuple(vmem_spec() for _ in range(7)),
        scratch_shapes=[
            pltpu.VMEM((104, 128), F32),
            pltpu.VMEM((104, 128), F32),
            pltpu.VMEM((104, 128), F32),
            pltpu.VMEM((104, 128), F32),
            pltpu.VMEM((3, SIDE, 16, 128), F32),
            pltpu.VMEM((10, 10, BLK, 256), F32),
            pltpu.VMEM((ROWS, 256), BF16),
            pltpu.VMEM((ROWS + 2 * SLAB, 1536), BF16),
            pltpu.VMEM((ROWS + 2 * SLAB, 1536), BF16),
            pltpu.VMEM((2, 3456, 256), BF16),
            pltpu.VMEM((2, 3456, 256), BF16),
            pltpu.VMEM((ROWS, WIDE), F32),
            pltpu.VMEM((ROWS, WIDE), F32),
            pltpu.VMEM((ROWS, WIDE), BF16),
            pltpu.VMEM((ROWS, WIDE), F32),
            pltpu.VMEM((ROWS, WIDE), BF16),
            pltpu.VMEM((ROWS, WIDE), F32),
            pltpu.VMEM((64, PAY - 128), F32),
            pltpu.VMEM((64, 1792), F32),
        ],
        compiler_params=pltpu.CompilerParams(vmem_limit_bytes=56 * 1024 * 1024),
        name="net",
    )(velocity, target, w1, w2, w3, own, blk)


def flow_kernel(
    vel, eddy, got0, got1, got2, got3, got4, out, rx_a, rx_b, ry_a, ry_b, rz, vx_s, vy_s, visc_s, ez_s
):
    gx_at, gy_at = lax.axis_index("gx"), lax.axis_index("gy")
    gx_odd, gy_odd = gx_at & 1 == 1, gy_at & 1 == 1
    second = core_half(gy_at) == 1
    ry_a[...] = got0[...]
    ry_b[...] = jnp.where(second, got2[...], got1[...])
    rx_a[...] = jnp.where(second, got1[...], got3[...])
    rx_b[...] = jnp.where(second, got3[...], got4[...])
    rz[...] = jnp.where(second, got4[...], got2[...])
    lane = iota((1, 128), 1)

    def sides(odd, a, b, at, rows):
        one, two = a[at : at + rows, :], b[at : at + rows, :]
        return jnp.where(odd, one, two), jnp.where(odd, two, one)

    for c in range(3):
        for x in range(16):
            vy_s[(c * 16 + x) * 32 + 8 : (c * 16 + x) * 32 + 24, :] = vel[c, x]
        for i in range(2):
            below, above = sides(gy_odd, ry_a, ry_b, (c * 2 + i) * 16, 16)
            vy_s[pl.ds(c * 512 + 6 + i, 16, stride=32), :] = below
            vy_s[pl.ds(c * 512 + 24 + i, 16, stride=32), :] = above
            below, above = sides(gx_odd, rx_a, rx_b, (c * 2 + i) * 16, 16)
            vx_s[c, i] = below
            vx_s[c, 2 + i] = above

    zcols = jnp.concatenate([jnp.transpose(rz[t * 8 : t * 8 + 8, :]) for t in range(7)], axis=0)
    coarse = eddy[...]
    e_first, e_last = zcols[768:832, 0:1] / EDDY_SCALE, zcols[768:832, 1:2] / EDDY_SCALE
    ahead = jnp.where(lane == 127, e_first, pltpu.roll(coarse, 127, 1))
    behind = jnp.where(lane == 0, e_last, pltpu.roll(coarse, 1, 1))
    below_x, above_x = (v / EDDY_SCALE for v in sides(gx_odd, rx_a, rx_b, 96, 8))
    below_y, above_y = (v / EDDY_SCALE for v in sides(gy_odd, ry_a, ry_b, 96, 8))

    def put(dst, plane, val):
        dst[pl.ds(plane * 32 + 8, 8, stride=2), :] = val
        dst[pl.ds(plane * 32 + 9, 8, stride=2), :] = val

    put(visc_s, 0, base_visc + below_x)
    put(visc_s, 17, base_visc + above_x)
    for x in range(8):
        for r in range(2):
            plane = 2 * x + 1 + r
            put(visc_s, plane, base_visc + coarse[x * 8 : x * 8 + 8])
            visc_s[plane * 32 + 7 : plane * 32 + 8, :] = base_visc + below_y[x : x + 1]
            visc_s[plane * 32 + 24 : plane * 32 + 25, :] = base_visc + above_y[x : x + 1]
        put(ez_s, 2 * x, base_visc + ahead[x * 8 : x * 8 + 8])
        put(ez_s, 2 * x + 1, base_visc + behind[x * 8 : x * 8 + 8])

    def plane_of(c, x):
        if x < 0:
            return vx_s[c, x + 2]
        if x > 15:
            return vx_s[c, x - 14]
        return vel[c, x]

    for x in range(16):
        vat = (x + 1) * 32
        visc = visc_s[vat + 8 : vat + 24, :]
        faces = (
            (visc_s[vat + 40 : vat + 56, :], visc_s[vat - 24 : vat - 8, :]),
            (visc_s[vat + 9 : vat + 25, :], visc_s[vat + 7 : vat + 23, :]),
            (
                ez_s[(x // 2 * 2) * 32 + 8 : (x // 2 * 2) * 32 + 24, :],
                ez_s[(x // 2 * 2 + 1) * 32 + 8 : (x // 2 * 2 + 1) * 32 + 24, :],
            ),
        )
        faces = [(0.5 * (visc + a), 0.5 * (visc + b)) for a, b in faces]
        wind = [vel[a, x] for a in range(3)]
        for c in range(3):
            u = vel[c, x]
            at = (c * 16 + x) * 32
            zat = (c * 16 + x) * 16
            zc = zcols[zat : zat + 16]
            p1 = jnp.where(lane == 127, zc[:, 0:1], pltpu.roll(u, 127, 1))
            p2 = jnp.where(lane == 127, zc[:, 1:2], jnp.where(lane == 126, zc[:, 0:1], pltpu.roll(u, 126, 1)))
            m1 = jnp.where(lane == 0, zc[:, 3:4], pltpu.roll(u, 1, 1))
            m2 = jnp.where(lane == 0, zc[:, 2:3], jnp.where(lane == 1, zc[:, 3:4], pltpu.roll(u, 2, 1)))
            near = (
                (plane_of(c, x + 1), plane_of(c, x - 1), plane_of(c, x + 2), plane_of(c, x - 2)),
                (
                    vy_s[at + 9 : at + 25, :], vy_s[at + 7 : at + 23, :],
                    vy_s[at + 10 : at + 26, :], vy_s[at + 6 : at + 22, :],
                ),
                (p1, m1, p2, m2),
            )
            advect = None
            diffuse = None
            for a in range(3):
                q1, b1, q2, b2 = near[a]
                slope = (8.0 * (q1 - b1) - (q2 - b2)) * (1.0 / 12.0)
                term = wind[a] * slope
                advect = term if advect is None else advect + term
                flux = faces[a][0] * (q1 - u) - faces[a][1] * (u - b1)
                diffuse = flux if diffuse is None else diffuse + flux
            out[c, x] = u + time_step * (diffuse - advect)


def run_flow(velocity, eddy, *got):
    return pl.pallas_call(
        flow_kernel,
        out_shape=jax.ShapeDtypeStruct(velocity.shape, F32),
        in_specs=[vmem_spec()] * 7,
        out_specs=vmem_spec(),
        scratch_shapes=[
            pltpu.VMEM((104, 128), F32),
            pltpu.VMEM((104, 128), F32),
            pltpu.VMEM((104, 128), F32),
            pltpu.VMEM((104, 128), F32),
            pltpu.VMEM((104, 128), F32),
            pltpu.VMEM((3, 4, 16, 128), F32),
            pltpu.VMEM((3 * 16 * 32, 128), F32),
            pltpu.VMEM((18 * 32, 128), F32),
            pltpu.VMEM((16 * 32, 128), F32),
        ],
        compiler_params=pltpu.CompilerParams(vmem_limit_bytes=32 * 1024 * 1024),
        name="flow",
    )(velocity, eddy, *got)


def finish_kernel(own, blk, mine, other, loss_out, first_out, hidden_out, last_out, ext_s):
    gx_at, gy_at = lax.axis_index("gx"), lax.axis_index("gy")
    n_z = lax.axis_size("role")
    in_group = gy_at * n_z + lax.axis_index("role")
    second = core_half(gy_at) == 1
    for t in range(PAY // 128):
        one, two = mine[t * 32 : (t + 1) * 32, :], other[t * 32 : (t + 1) * 32, :]
        top, bottom = jnp.where(second, two, one), jnp.where(second, one, two)
        if t == 0:
            ext_s[0:32, :] = top
            ext_s[32:64, :] = bottom
        else:
            at = (t - 1) * 128
            width = min(128, 27 * CH - at)
            hidden_out[0:32, at : at + width] = top[:, :width]
            hidden_out[32:64, at : at + width] = bottom[:, :width]
    extra = ext_s[...]
    first_out[...] = extra[:, 0:81]
    turned = jnp.transpose(jnp.concatenate([extra, jnp.zeros((64, 128), F32)], axis=0))
    last_out[...] = turned[LAST_COL : LAST_COL + 1, 0:64]
    slots = loss_out.shape[1]
    lane = iota((1, 128), 1)
    slot_lane = iota((1, slots), 1)
    picked = jnp.zeros((1, slots), F32)
    for s in range(slots):
        at = gx_at * slots + s
        dev = own[0, at] * (lax.axis_size("gy") * n_z) + in_group
        row = ext_s[pl.ds(dev & 63, 1), :]
        col = LOSS_COL + BLK * (dev >> 6) + blk[0, at]
        value = jnp.sum(jnp.where(lane == col, row, 0.0), axis=1, keepdims=True)
        picked = jnp.where(slot_lane == s, value, picked)
    loss_out[...] = picked


def run_finish(own, blk, mine, other, slots):
    smem = pl.BlockSpec(memory_space=pltpu.SMEM)
    f = lambda *s: jax.ShapeDtypeStruct(s, F32)
    return pl.pallas_call(
        finish_kernel,
        out_shape=(f(1, slots), f(64, 81), f(64, 27 * CH), f(1, 64)),
        in_specs=[smem] * 2 + [vmem_spec()] * 2,
        out_specs=tuple(vmem_spec() for _ in range(4)),
        scratch_shapes=[pltpu.VMEM((64, 128), F32)],
        compiler_params=pltpu.CompilerParams(vmem_limit_bytes=32 * 1024 * 1024),
        name="finish",
    )(own, blk, mine, other)


def on_device(velocity, target_visc, w_first, w_hidden, w_last, sample_owner, sample_block):
    n_x, n_y, n_z = lax.axis_size("gx"), lax.axis_size("gy"), lax.axis_size("role")
    trainers = n_x * n_y * n_z
    own = sample_owner.reshape(1, -1)
    blk = sample_block.reshape(1, -1)
    slots = own.shape[1] // n_x

    axes = ("gx", "gy", "role")

    def even_odd(i, count):
        return i ^ 1

    def odd_even(i, count):
        return (i - 1) % count if i % 2 == 0 else (i + 1) % count

    def partner(kind, i, j, r):
        if kind == "x":
            j = odd_even(j, n_y)
        elif kind == "y":
            r = r ^ 1
        elif kind == "z_a":
            i = even_odd(i, n_x)
        else:
            i = odd_even(i, n_x)
        return (i * n_y + j) * n_z + r

    def mixed(kinds):
        pairs = []
        for i in range(n_x):
            for j in range(n_y):
                for r in range(n_z):
                    pairs.append(((i * n_y + j) * n_z + r, partner(kinds[(j ^ (j >> 1)) & 1], i, j, r)))
        return pairs

    core_pairs = [(j, even_odd(j, n_y)) for j in range(n_y)]
    size = TILES * 32

    keep, send, eddy, *halos = run_net(
        velocity, target_visc, w_first, w_hidden, w_last.reshape(1, CH), own, blk
    )
    half = core_half(lax.axis_index("gy"))
    got = lax.ppermute(send, "gy", core_pairs)
    total = keep + got[:size]
    rims = [got[size:]]
    halos = [h.astype(F16) for h in halos]

    def widen(values, exps):
        wide = values.astype(F32).reshape(TILES, 32, 128) * jnp.exp2(exps)[:, None, :]
        return wide.reshape(size, 128)

    top = jnp.max(jnp.abs(total.reshape(TILES, 32, 128)), axis=1)
    exps = jnp.clip(jnp.ceil(jnp.log2(jnp.maximum(top, 1e-30))) - 13.0, -110.0, 110.0)
    orders = (("x", "y", "z_a", "z_b"), ("z_a", "x", "z_b", "y"))
    far = None
    for s in range(4):
        kinds = (orders[0][s], orders[1][s])
        if s == 1:
            far = lax.ppermute(halos[3], axes, mixed((orders[0][3], orders[1][3])))
        scaled = total.reshape(TILES, 32, 128) * jnp.exp2(-exps)[:, None, :]
        pieces = [scaled.reshape(size, 128).astype(F16), jnp.pad(exps, ((0, 1), (0, 0))).astype(F16)]
        message = jnp.concatenate(pieces + [halos[s]] if s < 3 else pieces, axis=0)
        message = lax.optimization_barrier(message)
        got = lax.ppermute(message, axes, mixed(kinds))
        their_exps = got[size : size + TILES].astype(F32)
        mine, theirs = widen(message[:size], exps), widen(got[:size], their_exps)
        if n_x != 4 and "z_b" in kinds:
            theirs = jnp.where(half == kinds.index("z_b"), 0.0, theirs)
        total = mine + theirs
        exps = jnp.maximum(exps, their_exps) + 1.0
        if s < 3:
            rims.append(got[size + 16 :].astype(F32))
        if s == 1:
            total, far = lax.optimization_barrier((total, far))
        if s == 2:
            u_next = run_flow(velocity, eddy, *rims, far.astype(F32))
    total, u_next = lax.optimization_barrier((total, u_next))
    if n_x != 4:
        for bit in range(1, n_x.bit_length() - 1):
            total = total + lax.ppermute(total, "gx", [(i, i ^ (1 << bit)) for i in range(n_x)])
    other = lax.ppermute(total, "gy", core_pairs)

    losses, first, hidden, last = run_finish(own, blk, total, other, slots)
    return (u_next, losses.reshape(1, 1, slots), first, hidden, last.reshape(CH))


def solution(mesh):
    return jax.shard_map(
        on_device,
        mesh=mesh,
        in_specs=(
            P(None, "gx", "gy", "role"),
            P("gx", "gy", "role"),
            P(),
            P(),
            P(),
            P("gy", "role", None, None),
            P("gy", "role", None, None),
        ),
        out_specs=(P(None, "gx", "gy", "role"), P("gy", "role", "gx"), P(), P(), P()),
        check_vma=False,
    )
```

```python
import jax
import jax.numpy as jnp
from jax import lax
from jax.experimental import pallas as pl
from jax.experimental.pallas import tpu as pltpu
from jax.sharding import PartitionSpec as P

F32 = jnp.float32
BF16 = jnp.bfloat16
HIGH = lax.Precision.HIGHEST

SIDE = 8
CELLS = SIDE**3
CH = 64
BLK = 8
ROWS = SIDE * SIDE * BLK
WIDE = SIDE * CH
SLAB = SIDE * BLK
TILES = 15
PAY = TILES * 128
LAST_COL = 81
LOSS_COL = 82

EDDY_SCALE = 2.0**-9
F16 = jnp.float16

base_visc = 0.02
time_step = 0.2


def iota(shape, dim):
    return lax.broadcasted_iota(jnp.int32, shape, dim)


def onehot(cond, dtype=BF16):
    return jnp.where(cond, 1.0, 0.0).astype(dtype)


def sigmoid(v):
    return 0.5 + 0.5 * jnp.tanh(0.5 * v)


def nt(a, b, precision=None):
    return lax.dot_general(a, b, (((1,), (1,)), ((), ())), preferred_element_type=F32, precision=precision)


def tn(a, b, precision=None):
    return lax.dot_general(a, b, (((0,), (0,)), ((), ())), preferred_element_type=F32, precision=precision)


def nn(a, b, precision=None):
    return lax.dot_general(a, b, (((1,), (0,)), ((), ())), preferred_element_type=F32, precision=precision)


def core_half(at):
    return (at ^ (at >> 1)) & 1


def net_kernel(
    vel, tgt, w1, w2, w3, own, blk,
    keep, send, eddy_out, halo1, halo2, hz, hx_b,
    hx_a, hy_b, pool_s, fp_s, i1_s, a_s, d_s, tt_s, tb_s, pre_s, slope1_s, ah_s, slope2_s, dw_s, big_s, gh_s, w2_s,
):
    gx_at, gy_at = lax.axis_index("gx"), lax.axis_index("gy")
    half = core_half(gy_at)
    dev = (gx_at * lax.axis_size("gy") + gy_at) * lax.axis_size("role") + lax.axis_index("role")
    trainers = lax.axis_size("gx") * lax.axis_size("gy") * lax.axis_size("role")
    gx_odd, gy_odd = gx_at & 1 == 1, gy_at & 1 == 1

    src = iota((320, 1), 0) - 64
    dst = iota((1, 512), 1)
    wanted = ((dst >> 7) - 2 + ((dst & 127) >> 6)) * 64 + (dst & 63)
    chooser = onehot(jnp.where((src >= 0) & (src < 192), src - 64, -999) == wanted)
    zero_tile = jnp.zeros((64, 128), BF16)
    left = iota((64, 128), 1) < 64
    w2_s[:, 1664:1792] = jnp.zeros((64, 128), F32)
    w2_s[:, 0:1728] = w2[...].astype(F32)
    w2t = jnp.concatenate(
        [
            jnp.transpose(jnp.concatenate([w2_s[:, t * 128 : (t + 1) * 128]] * 2, axis=0))
            for t in range(14)
        ],
        axis=0,
    )
    def build(k):
        base = (192 * k) // 128 * 128
        off = 192 * k - base
        width = min(256, 1728 - base)
        tiles = nn(w2[:, base : base + width], chooser[64 - off : 64 - off + width]).astype(BF16)
        kb = 8 - k
        turned = {dz: w2t[(3 * k + dz + 1) * 64 : (3 * k + dz + 2) * 64] for dz in (-1, 0, 1)}
        turned[-2] = turned[2] = jnp.zeros((64, 128), F32)
        forward = {d: jnp.where(left, turned[d], turned[d - 1]).astype(BF16) for d in (-1, 0, 1, 2)}
        for q in range(2):
            for w in range(6):
                z = 2 * q + w
                for h in range(2):
                    m = 2 * q + h
                    at, cols = k * 384 + w * 64, slice(h * 128, (h + 1) * 128)
                    tt_s[q, at : at + 64, cols] = forward.get(z - 2 * m, zero_tile)
                    d = 2 * m - z
                    tile = tiles[:, (d + 2) * 128 : (d + 3) * 128] if -2 <= d <= 1 else zero_tile
                    at = kb * 384 + w * 64
                    tb_s[q, at : at + 64, cols] = tile

    for c in range(3):
        for x in range(SIDE):
            both = vel[c, 2 * x] + vel[c, 2 * x + 1]
            pool_s[c, x] = both
    rows = []
    for c in range(3):
        cols = []
        for x in range(SIDE):
            cols.append(pool_s[c, x, pl.ds(0, 8, stride=2), :] + pool_s[c, x, pl.ds(1, 8, stride=2), :])
        rows.append(jnp.concatenate(cols, axis=0))
    pooled = jnp.concatenate(rows, axis=0)
    zpool = jnp.where(iota((128, 1), 0) >> 1 == iota((1, 64), 1), 0.125, 0.0)
    filt = nn(pooled, zpool, HIGH).astype(BF16)
    build(0)
    build(1)
    tgt_rows = tgt[...].reshape(64, 64)
    zsel = jnp.concatenate([filt[0:64], filt[64:128], filt[128:192], tgt_rows], axis=1)
    spread = onehot(iota((ROWS, 1), 0) >> 3 == iota((1, 64), 1))
    by_block = nn(spread, zsel)
    build(2)
    build(3)
    mine = (iota((1, 256), 1) & 63) >> 3 == iota((ROWS, 1), 0) & 7
    by_block = jnp.where(mine, by_block, 0.0).astype(BF16)
    lane_in = iota((1, 256), 1)
    lane_off = lax.div(lane_in, 24)
    lane_cz = lane_in - lane_off * 24
    src = iota((256, 1), 0)
    pick = onehot(jnp.where(lane_in < 216, lane_cz, -1) == (src >> 6) * 8 + (src & 7))
    cells = nn(by_block, pick)
    build(4)
    build(5)
    pick_t = onehot(jnp.where(src >= 192, src & 7, -1) == iota((1, SIDE), 1))
    target = nn(by_block, pick_t)

    build(6)
    fp_s[...] = jnp.zeros(fp_s.shape, F32)
    fp_s[1:9, 1:9] = cells.reshape(SIDE, SIDE, BLK, 256)
    group = lax.div(iota((1, 1, 1, 256), 3), 24)
    for x in range(SIDE):
        acc = jnp.zeros((1, SIDE, BLK, 256), F32)
        for k in range(9):
            part = fp_s[x + k // 3 : x + k // 3 + 1, k % 3 : k % 3 + SIDE]
            acc = jnp.where(group == k, part, acc)
        i1_s[x * SLAB : (x + 1) * SLAB, :] = acc.reshape(SLAB, 256).astype(BF16)

    j_at = iota((81, 1), 0)
    j_off, j_dz, j_c = lax.div(j_at, 9), lax.rem(lax.div(j_at, 3), 3) - 1, lax.rem(j_at, 3)
    lane_key = jnp.where(lane_in < 216, lane_off * 4 + (lane_cz >> 3), -1)
    same = lane_key == j_off * 4 + j_c
    delta = jnp.where(same, (lane_in & 7) - j_dz, -9)
    w1v = w1[...]
    t1 = jnp.concatenate([nn(w1v, onehot(delta == z)).astype(BF16) for z in range(SIDE)], axis=0)
    build(7)
    pre_s[...] = nt(i1_s[...], t1)
    build(8)

    def windows(ref, q):
        return jnp.concatenate(
            [
                ref[dx * SLAB : dx * SLAB + ROWS, j * 512 + q * 128 : j * 512 + q * 128 + 384]
                for dx in range(3)
                for j in range(3)
            ],
            axis=1,
        )

    def shifted_store(dst_ref, x, val):
        zero = jnp.zeros((1, BLK, WIDE), F32)
        lo, hi = (x + 1) * SLAB, (x + 2) * SLAB
        dst_ref[lo:hi, 0:512] = jnp.concatenate([zero, val[:-1]], axis=0).reshape(SLAB, WIDE).astype(BF16)
        dst_ref[lo:hi, 512:1024] = val.reshape(SLAB, WIDE).astype(BF16)
        dst_ref[lo:hi, 1024:1536] = jnp.concatenate([val[1:], zero], axis=0).reshape(SLAB, WIDE).astype(BF16)

    for ref in (a_s, d_s):
        ref[0:SLAB, :] = jnp.zeros((SLAB, 1536), BF16)
        ref[9 * SLAB :, :] = jnp.zeros((SLAB, 1536), BF16)

    for x in range(SIDE):
        pre = pre_s[x * SLAB : (x + 1) * SLAB, :]
        sig = sigmoid(pre)
        slope1_s[x * SLAB : (x + 1) * SLAB, :] = sig * (1.0 + pre * (1.0 - sig))
        shifted_store(a_s, x, (pre * sig).reshape(SIDE, BLK, WIDE))

    for q in range(2):
        pre_s[:, q * 256 : (q + 1) * 256] = nn(windows(a_s, q), tt_s[q])
    for x in range(SIDE):
        pre = pre_s[x * SLAB : (x + 1) * SLAB, :]
        sig = sigmoid(pre)
        slope2_s[x * SLAB : (x + 1) * SLAB, :] = sig * (1.0 + pre * (1.0 - sig))
        ah_s[x * SLAB : (x + 1) * SLAB, :] = (pre * sig).astype(BF16)

    tile8 = onehot(iota((64, 1), 0) == iota((1, WIDE), 1) & 63)
    w3_wide = nn(w3[...], tile8)
    diag = iota((1, WIDE), 1) >> 6 == iota((SIDE, 1), 0)
    last = jnp.where(diag, w3_wide, 0.0).astype(BF16)
    logits = nt(ah_s[...], last)
    eddy = 0.5 * (jnp.maximum(logits, 0.0) + jnp.log1p(jnp.exp(-jnp.abs(logits))))
    error = eddy - target
    losses = jnp.sum(jnp.sum((error * error).reshape(64, BLK, SIDE), axis=0), axis=1, keepdims=True) / CELLS
    d_logit = (error * sigmoid(logits) / (trainers * CELLS)).astype(BF16)

    zrep = onehot(iota((SIDE, 1), 0) == (iota((1, 128), 1) & 15) >> 1, F32)
    fine = nn(eddy, zrep, HIGH)
    fine = jnp.where(iota((1, 128), 1) >> 4 == iota((ROWS, 1), 0) & 7, fine, 0.0)
    fine = jnp.sum(fine.reshape(64, BLK, 128), axis=1)
    eddy_out[...] = fine

    for c in range(3):
        for i in range(2):
            lo, hi = vel[c, i], vel[c, 14 + i]
            at = (c * 2 + i) * 16
            hx_a[at : at + 16, :] = jnp.where(gx_odd, lo, hi)
            hx_b[at : at + 16, :] = jnp.where(gx_odd, hi, lo)
    small = fine * EDDY_SCALE
    hx_a[96:104, :] = jnp.where(gx_odd, small[0:8], small[56:64])
    hx_b[96:104, :] = jnp.where(gx_odd, small[56:64], small[0:8])
    core = send.at[480:584]
    for c in range(3):
        for i in range(2):
            lo = jnp.concatenate([vel[c, x, i : i + 1, :] for x in range(16)], axis=0)
            hi = jnp.concatenate([vel[c, x, 14 + i : 15 + i, :] for x in range(16)], axis=0)
            at = (c * 2 + i) * 16
            core[at : at + 16, :] = jnp.where(gy_odd, lo, hi)
            hy_b[at : at + 16, :] = jnp.where(gy_odd, hi, lo)
    lo = eddy_out[pl.ds(0, 8, stride=8), :] * EDDY_SCALE
    hi = eddy_out[pl.ds(7, 8, stride=8), :] * EDDY_SCALE
    core[96:104, :] = jnp.where(gy_odd, lo, hi)
    hy_b[96:104, :] = jnp.where(gy_odd, hi, lo)
    vt = jnp.transpose(vel[...].reshape(768, 128))
    et = jnp.transpose(jnp.concatenate([small, jnp.zeros((64, 128), F32)], axis=0))
    hz[...] = jnp.zeros(hz.shape, F32)
    for t in range(6):
        hz[t * 8 : t * 8 + 2, :] = vt[0:2, t * 128 : (t + 1) * 128]
        hz[t * 8 + 2 : t * 8 + 4, :] = vt[126:128, t * 128 : (t + 1) * 128]
    hz[48:49, :] = et[0:1]
    hz[49:50, :] = et[127:128]
    second = half == 1
    halo1[...] = jnp.where(second, hx_a[...], hy_b[...])
    halo2[...] = jnp.where(second, hy_b[...], hx_a[...])

    code = own[...] * BLK + blk[...]
    listed = code.shape[1]
    wanted = gx_at * BLK + iota((BLK, listed), 0)
    count = jnp.sum(jnp.where(code == wanted, 1.0, 0.0), axis=1, keepdims=True)
    count_rows = jnp.broadcast_to(count.reshape(1, BLK, 1), (64, BLK, 1)).reshape(ROWS, 1)

    big_s[:, 0:512] = nn(d_logit, last)
    for x in range(SIDE):
        d_hid = big_s[x * SLAB : (x + 1) * SLAB, 0:512] * slope2_s[x * SLAB : (x + 1) * SLAB, :]
        d_hid = d_hid.astype(BF16).astype(F32).reshape(SIDE, BLK, WIDE)
        shifted_store(d_s, x, d_hid)
        dw_s[x * SLAB : (x + 1) * SLAB, :] = (d_hid * count[None]).reshape(SLAB, WIDE).astype(BF16)
    dwt = jnp.transpose(dw_s[...])

    held = None
    low_half = iota((64, 128), 1) < 64
    for k in range(9):
        dx, j = k // 3, k % 3
        for q in range(2):
            zs = slice(q * 192, q * 192 + 320)
            cols = slice(j * 512 + q * 256, j * 512 + (q + 1) * 256)
            big_s[zs, q * 256 : (q + 1) * 256] = nn(dwt[zs], a_s[dx * SLAB : dx * SLAB + ROWS, cols])
        sums = []
        for m in (-1, 0, 1, 2):
            tot = None
            for p in range(4):
                z = 2 * p + m
                if 0 <= z < SIDE:
                    part = big_s[z * 64 : (z + 1) * 64, p * 128 : (p + 1) * 128]
                    tot = part if tot is None else tot + part
            sums.append(tot)
        for dz in (-1, 0, 1):
            low, high = sums[1 - dz], sums[2 - dz]
            at = (k * 3 + dz + 1) * 64
            if at % 128:
                gh_s[:, at - 64 : at + 64] = jnp.where(low_half, held, high + pltpu.roll(low, 64, 1))
            else:
                held = low + pltpu.roll(high, 64, 1)
    gh_s[:, 1664:1792] = jnp.where(low_half, held, 0.0)

    for q in range(2):
        pre_s[:, q * 256 : (q + 1) * 256] = nn(windows(d_s, q), tb_s[q])
    for x in range(SIDE):
        rows = slice(x * SLAB, (x + 1) * SLAB)
        d_first = (pre_s[rows, :] * slope1_s[rows, :]).astype(BF16).astype(F32)
        dw_s[rows, :] = (d_first.reshape(SIDE, BLK, WIDE) * count[None]).reshape(SLAB, WIDE).astype(BF16)
    g1 = nn(jnp.transpose(dw_s[...]), i1_s[...])
    z_in = iota((1, 256), 1) & 7
    parts = []
    for dz in (-1, 0, 1):
        tot = jnp.zeros((64, 256), F32)
        for z in range(SIDE):
            if 0 <= z + dz < SIDE:
                tot = tot + jnp.where(z_in == z + dz, g1[z * 64 : (z + 1) * 64], 0.0)
        parts.append(tot)
    r_at = iota((768, 1), 0)
    c_at = iota((1, 128), 1)
    r_lane = r_at & 255
    r_off = lax.div(r_lane, 24)
    r_col = (r_off * 3 + (r_at >> 8)) * 3 + ((r_lane - r_off * 24) >> 3)
    fold = onehot(jnp.where(r_lane < 216, r_col, -1) == c_at, F32)
    g_first = nn(jnp.concatenate(parts, axis=1), fold, HIGH)

    dlw = d_logit.astype(F32) * count_rows
    dl_hi = dlw.astype(BF16)
    dl_lo = (dlw - dl_hi.astype(F32)).astype(BF16)
    ah = ah_s[...]
    gl = tn(dl_hi, ah) + tn(dl_lo, ah)
    gl = jnp.where(diag, gl, 0.0)
    fold_o = onehot(iota((1, WIDE), 1) & 63 == iota((64, 1), 0), F32)
    g_last = jnp.sum(nt(fold_o, gl, HIGH), axis=1, keepdims=True)

    lane8 = iota((BLK, 128), 1)
    loss_row = jnp.where(lane8 - (LOSS_COL + BLK * (dev >> 6)) == iota((BLK, 128), 0), losses, 0.0)
    loss_row = jnp.sum(loss_row, axis=0, keepdims=True)
    lane = iota((64, 128), 1)
    extra = jnp.where(lane == LAST_COL, g_last, g_first)
    extra = extra + jnp.where(iota((64, 128), 0) == dev & 63, loss_row, 0.0)

    for t in range(PAY // 128):
        if t == 0:
            top, bottom = extra[0:32], extra[32:64]
        else:
            top, bottom = (gh_s[r : r + 32, (t - 1) * 128 : t * 128] for r in (0, 32))
        keep[t * 32 : (t + 1) * 32, :] = jnp.where(second, bottom, top)
        send[t * 32 : (t + 1) * 32, :] = jnp.where(second, top, bottom)


def vmem_spec():
    return pl.BlockSpec(memory_space=pltpu.VMEM)


def run_net(velocity, target, w1, w2, w3, own, blk):
    f = lambda *s: pltpu.VMEM(s, F32)
    return pl.pallas_call(
        net_kernel,
        out_shape=(f(480, 128), f(584, 128), f(64, 128)) + (f(104, 128),) * 4,
        in_specs=[vmem_spec()] * 7,
        out_specs=tuple(vmem_spec() for _ in range(7)),
        scratch_shapes=[
            pltpu.VMEM((104, 128), F32),
            pltpu.VMEM((104, 128), F32),
            pltpu.VMEM((3, SIDE, 16, 128), F32),
            pltpu.VMEM((10, 10, BLK, 256), F32),
            pltpu.VMEM((ROWS, 256), BF16),
            pltpu.VMEM((ROWS + 2 * SLAB, 1536), BF16),
            pltpu.VMEM((ROWS + 2 * SLAB, 1536), BF16),
            pltpu.VMEM((2, 3456, 256), BF16),
            pltpu.VMEM((2, 3456, 256), BF16),
            pltpu.VMEM((ROWS, WIDE), F32),
            pltpu.VMEM((ROWS, WIDE), F32),
            pltpu.VMEM((ROWS, WIDE), BF16),
            pltpu.VMEM((ROWS, WIDE), F32),
            pltpu.VMEM((ROWS, WIDE), BF16),
            pltpu.VMEM((ROWS, WIDE), F32),
            pltpu.VMEM((64, PAY - 128), F32),
            pltpu.VMEM((64, 1792), F32),
        ],
        compiler_params=pltpu.CompilerParams(vmem_limit_bytes=56 * 1024 * 1024),
        name="net",
    )(velocity, target, w1, w2, w3, own, blk)


def flow_kernel(
    vel, eddy, ry_a, got1, got2, got3, rx_b, far, out, rx_a, ry_b, rz, vx_s, vy_s, visc_s, ez_s
):
    gx_at, gy_at = lax.axis_index("gx"), lax.axis_index("gy")
    gx_odd, gy_odd = gx_at & 1 == 1, gy_at & 1 == 1
    second = core_half(gy_at) == 1
    ry_b[...] = jnp.where(second, got2[...], got1[...])
    rx_a[...] = jnp.where(second, got1[...], got2[...])
    rz[...] = jnp.where(second, far[...], got3[...])
    lane = iota((1, 128), 1)

    def sides(odd, a, b, at, rows):
        one, two = a[at : at + rows, :], b[at : at + rows, :]
        return jnp.where(odd, one, two), jnp.where(odd, two, one)

    for c in range(3):
        for x in range(16):
            vy_s[(c * 16 + x) * 32 + 8 : (c * 16 + x) * 32 + 24, :] = vel[c, x]
        for i in range(2):
            below, above = sides(gy_odd, ry_a, ry_b, (c * 2 + i) * 16, 16)
            vy_s[pl.ds(c * 512 + 6 + i, 16, stride=32), :] = below
            vy_s[pl.ds(c * 512 + 24 + i, 16, stride=32), :] = above
            below, above = sides(gx_odd, rx_a, rx_b, (c * 2 + i) * 16, 16)
            vx_s[c, i] = below
            vx_s[c, 2 + i] = above

    zcols = jnp.concatenate([jnp.transpose(rz[t * 8 : t * 8 + 8, :]) for t in range(7)], axis=0)
    coarse = eddy[...]
    e_first, e_last = zcols[768:832, 0:1] / EDDY_SCALE, zcols[768:832, 1:2] / EDDY_SCALE
    ahead = jnp.where(lane == 127, e_first, pltpu.roll(coarse, 127, 1))
    behind = jnp.where(lane == 0, e_last, pltpu.roll(coarse, 1, 1))
    below_x, above_x = (v / EDDY_SCALE for v in sides(gx_odd, rx_a, rx_b, 96, 8))
    below_y, above_y = (v / EDDY_SCALE for v in sides(gy_odd, ry_a, ry_b, 96, 8))

    def put(dst, plane, val):
        dst[pl.ds(plane * 32 + 8, 8, stride=2), :] = val
        dst[pl.ds(plane * 32 + 9, 8, stride=2), :] = val

    put(visc_s, 0, base_visc + below_x)
    put(visc_s, 17, base_visc + above_x)
    for x in range(8):
        for r in range(2):
            plane = 2 * x + 1 + r
            put(visc_s, plane, base_visc + coarse[x * 8 : x * 8 + 8])
            visc_s[plane * 32 + 7 : plane * 32 + 8, :] = base_visc + below_y[x : x + 1]
            visc_s[plane * 32 + 24 : plane * 32 + 25, :] = base_visc + above_y[x : x + 1]
        put(ez_s, 2 * x, base_visc + ahead[x * 8 : x * 8 + 8])
        put(ez_s, 2 * x + 1, base_visc + behind[x * 8 : x * 8 + 8])

    def plane_of(c, x):
        if x < 0:
            return vx_s[c, x + 2]
        if x > 15:
            return vx_s[c, x - 14]
        return vel[c, x]

    for x in range(16):
        vat = (x + 1) * 32
        visc = visc_s[vat + 8 : vat + 24, :]
        faces = (
            (visc_s[vat + 40 : vat + 56, :], visc_s[vat - 24 : vat - 8, :]),
            (visc_s[vat + 9 : vat + 25, :], visc_s[vat + 7 : vat + 23, :]),
            (
                ez_s[(x // 2 * 2) * 32 + 8 : (x // 2 * 2) * 32 + 24, :],
                ez_s[(x // 2 * 2 + 1) * 32 + 8 : (x // 2 * 2 + 1) * 32 + 24, :],
            ),
        )
        faces = [(0.5 * (visc + a), 0.5 * (visc + b)) for a, b in faces]
        wind = [vel[a, x] for a in range(3)]
        for c in range(3):
            u = vel[c, x]
            at = (c * 16 + x) * 32
            zat = (c * 16 + x) * 16
            zc = zcols[zat : zat + 16]
            p1 = jnp.where(lane == 127, zc[:, 0:1], pltpu.roll(u, 127, 1))
            p2 = jnp.where(lane == 127, zc[:, 1:2], jnp.where(lane == 126, zc[:, 0:1], pltpu.roll(u, 126, 1)))
            m1 = jnp.where(lane == 0, zc[:, 3:4], pltpu.roll(u, 1, 1))
            m2 = jnp.where(lane == 0, zc[:, 2:3], jnp.where(lane == 1, zc[:, 3:4], pltpu.roll(u, 2, 1)))
            near = (
                (plane_of(c, x + 1), plane_of(c, x - 1), plane_of(c, x + 2), plane_of(c, x - 2)),
                (
                    vy_s[at + 9 : at + 25, :], vy_s[at + 7 : at + 23, :],
                    vy_s[at + 10 : at + 26, :], vy_s[at + 6 : at + 22, :],
                ),
                (p1, m1, p2, m2),
            )
            advect = None
            diffuse = None
            for a in range(3):
                q1, b1, q2, b2 = near[a]
                slope = (8.0 * (q1 - b1) - (q2 - b2)) * (1.0 / 12.0)
                term = wind[a] * slope
                advect = term if advect is None else advect + term
                flux = faces[a][0] * (q1 - u) - faces[a][1] * (u - b1)
                diffuse = flux if diffuse is None else diffuse + flux
            out[c, x] = u + time_step * (diffuse - advect)


def run_flow(velocity, eddy, *got):
    return pl.pallas_call(
        flow_kernel,
        out_shape=jax.ShapeDtypeStruct(velocity.shape, F32),
        in_specs=[vmem_spec()] * 8,
        out_specs=vmem_spec(),
        scratch_shapes=[
            pltpu.VMEM((104, 128), F32),
            pltpu.VMEM((104, 128), F32),
            pltpu.VMEM((104, 128), F32),
            pltpu.VMEM((3, 4, 16, 128), F32),
            pltpu.VMEM((3 * 16 * 32, 128), F32),
            pltpu.VMEM((18 * 32, 128), F32),
            pltpu.VMEM((16 * 32, 128), F32),
        ],
        compiler_params=pltpu.CompilerParams(vmem_limit_bytes=32 * 1024 * 1024),
        name="flow",
    )(velocity, eddy, *got)


def finish_kernel(own, blk, mine, other, loss_out, first_out, hidden_out, last_out, ext_s):
    gx_at, gy_at = lax.axis_index("gx"), lax.axis_index("gy")
    n_z = lax.axis_size("role")
    in_group = gy_at * n_z + lax.axis_index("role")
    second = core_half(gy_at) == 1
    for t in range(PAY // 128):
        one, two = mine[t * 32 : (t + 1) * 32, :], other[t * 32 : (t + 1) * 32, :]
        top, bottom = jnp.where(second, two, one), jnp.where(second, one, two)
        if t == 0:
            ext_s[0:32, :] = top
            ext_s[32:64, :] = bottom
        else:
            at = (t - 1) * 128
            width = min(128, 27 * CH - at)
            hidden_out[0:32, at : at + width] = top[:, :width]
            hidden_out[32:64, at : at + width] = bottom[:, :width]
    extra = ext_s[...]
    first_out[...] = extra[:, 0:81]
    turned = jnp.transpose(jnp.concatenate([extra, jnp.zeros((64, 128), F32)], axis=0))
    last_out[...] = turned[LAST_COL : LAST_COL + 1, 0:64]
    slots = loss_out.shape[1]
    lane = iota((1, 128), 1)
    slot_lane = iota((1, slots), 1)
    picked = jnp.zeros((1, slots), F32)
    for s in range(slots):
        at = gx_at * slots + s
        dev = own[0, at] * (lax.axis_size("gy") * n_z) + in_group
        row = ext_s[pl.ds(dev & 63, 1), :]
        col = LOSS_COL + BLK * (dev >> 6) + blk[0, at]
        value = jnp.sum(jnp.where(lane == col, row, 0.0), axis=1, keepdims=True)
        picked = jnp.where(slot_lane == s, value, picked)
    loss_out[...] = picked


def run_finish(own, blk, mine, other, slots):
    smem = pl.BlockSpec(memory_space=pltpu.SMEM)
    f = lambda *s: jax.ShapeDtypeStruct(s, F32)
    return pl.pallas_call(
        finish_kernel,
        out_shape=(f(1, slots), f(64, 81), f(64, 27 * CH), f(1, 64)),
        in_specs=[smem] * 2 + [vmem_spec()] * 2,
        out_specs=tuple(vmem_spec() for _ in range(4)),
        scratch_shapes=[pltpu.VMEM((64, 128), F32)],
        compiler_params=pltpu.CompilerParams(vmem_limit_bytes=32 * 1024 * 1024),
        name="finish",
    )(own, blk, mine, other)


def on_device(velocity, target_visc, w_first, w_hidden, w_last, sample_owner, sample_block):
    n_x, n_y, n_z = lax.axis_size("gx"), lax.axis_size("gy"), lax.axis_size("role")
    trainers = n_x * n_y * n_z
    own = sample_owner.reshape(1, -1)
    blk = sample_block.reshape(1, -1)
    slots = own.shape[1] // n_x

    axes = ("gx", "gy", "role")

    def even_odd(i, count):
        return i ^ 1

    def odd_even(i, count):
        return (i - 1) % count if i % 2 == 0 else (i + 1) % count

    def partner(kind, i, j, r):
        if kind == "x":
            j = odd_even(j, n_y)
        elif kind == "y":
            r = r ^ 1
        elif kind == "z_a":
            i = even_odd(i, n_x)
        elif kind == "z_b":
            i = odd_even(i, n_x)
        else:
            i = i ^ 2
        return (i * n_y + j) * n_z + r

    def mixed(kinds):
        pairs = []
        for i in range(n_x):
            for j in range(n_y):
                for r in range(n_z):
                    kind = kinds[core_half(j)]
                    if kind:
                        pairs.append(((i * n_y + j) * n_z + r, partner(kind, i, j, r)))
        return pairs

    core_pairs = [(j, even_odd(j, n_y)) for j in range(n_y)]
    size = TILES * 32

    keep, send, eddy, *halos = run_net(
        velocity, target_visc, w_first, w_hidden, w_last.reshape(1, CH), own, blk
    )
    got = lax.ppermute(send, "gy", core_pairs)
    total = keep + got[:size]
    rims = [got[size:]]
    halo1, halo2, halo_y, halo_b = (h.astype(F16) for h in halos)
    halos = [halo1, halo2, halo_y]

    def widen(values, exps):
        wide = values.astype(F32).reshape(TILES, 32, 128) * jnp.exp2(exps)[:, None, :]
        return wide.reshape(size, 128)

    top = jnp.max(jnp.abs(total.reshape(TILES, 32, 128)), axis=1)
    exps = jnp.clip(jnp.ceil(jnp.log2(jnp.maximum(top, 1e-30))) - 13.0, -110.0, 110.0)
    orders = (("x", "z_a", "y", "z_2"), ("z_a", "x", "z_2", "y"))
    for s in range(4):
        if s == 0:
            alone = lax.ppermute(halo_b, axes, mixed(("z_b", "z_b")))
        if s == 2:
            alone = lax.ppermute(halo_y, axes, mixed((None, "y")))
        scaled = total.reshape(TILES, 32, 128) * jnp.exp2(-exps)[:, None, :]
        pieces = [scaled.reshape(size, 128).astype(F16), jnp.pad(exps, ((0, 1), (0, 0))).astype(F16)]
        message = jnp.concatenate(pieces + [halos[s]] if s < 3 else pieces, axis=0)
        message = lax.optimization_barrier(message)
        got = lax.ppermute(message, axes, mixed((orders[0][s], orders[1][s])))
        their_exps = got[size : size + TILES].astype(F32)
        total = widen(message[:size], exps) + widen(got[:size], their_exps)
        exps = jnp.maximum(exps, their_exps) + 1.0
        if s < 3:
            rims.append(got[size + 16 :].astype(F32))
        if s == 0 or s == 2:
            total, alone = lax.optimization_barrier((total, alone))
        if s == 0:
            rim_b = alone.astype(F32)
        if s == 2:
            u_next = run_flow(velocity, eddy, *rims, rim_b, alone.astype(F32))
    total, u_next = lax.optimization_barrier((total, u_next))
    for bit in range(2, n_x.bit_length() - 1):
        total = total + lax.ppermute(total, "gx", [(i, i ^ (1 << bit)) for i in range(n_x)])
    other = lax.ppermute(total, "gy", core_pairs)

    losses, first, hidden, last = run_finish(own, blk, total, other, slots)
    return (u_next, losses.reshape(1, 1, slots), first, hidden, last.reshape(CH))


def solution(mesh):
    return jax.shard_map(
        on_device,
        mesh=mesh,
        in_specs=(
            P(None, "gx", "gy", "role"),
            P("gx", "gy", "role"),
            P(),
            P(),
            P(),
            P("gy", "role", None, None),
            P("gy", "role", None, None),
        ),
        out_specs=(P(None, "gx", "gy", "role"), P("gy", "role", "gx"), P(), P(), P()),
        check_vma=False,
    )
```

```python
import jax
import jax.numpy as jnp
from jax import lax
from jax.experimental import pallas as pl
from jax.experimental.pallas import tpu as pltpu
from jax.sharding import PartitionSpec as P

F32 = jnp.float32
BF16 = jnp.bfloat16
HIGH = lax.Precision.HIGHEST

SIDE = 8
CELLS = SIDE**3
CH = 64
BLK = 8
ROWS = SIDE * SIDE * BLK
WIDE = SIDE * CH
SLAB = SIDE * BLK
TILES = 15
PAY = TILES * 128
LAST_COL = 81
LOSS_COL = 82

EDDY_SCALE = 2.0**-9
F16 = jnp.float16

base_visc = 0.02
time_step = 0.2


def iota(shape, dim):
    return lax.broadcasted_iota(jnp.int32, shape, dim)


def onehot(cond, dtype=BF16):
    return jnp.where(cond, 1.0, 0.0).astype(dtype)


def sigmoid(v):
    return 0.5 + 0.5 * jnp.tanh(0.5 * v)


def nt(a, b, precision=None):
    return lax.dot_general(a, b, (((1,), (1,)), ((), ())), preferred_element_type=F32, precision=precision)


def tn(a, b, precision=None):
    return lax.dot_general(a, b, (((0,), (0,)), ((), ())), preferred_element_type=F32, precision=precision)


def nn(a, b, precision=None):
    return lax.dot_general(a, b, (((1,), (0,)), ((), ())), preferred_element_type=F32, precision=precision)


def core_half(at):
    return (at ^ (at >> 1)) & 1


def net_kernel(
    vel, tgt, w1, w2, w3, own, blk,
    keep, send, eddy_out, halo1, halo2, halo3, halo4,
    hx_a, hx_b, hy_b, hz, pool_s, fp_s, i1_s, a_s, d_s, tt_s, tb_s, pre_s, slope1_s, ah_s, slope2_s, dw_s, big_s, gh_s, w2_s,
):
    gx_at, gy_at = lax.axis_index("gx"), lax.axis_index("gy")
    half = core_half(gy_at)
    dev = (gx_at * lax.axis_size("gy") + gy_at) * lax.axis_size("role") + lax.axis_index("role")
    trainers = lax.axis_size("gx") * lax.axis_size("gy") * lax.axis_size("role")
    gx_odd, gy_odd = gx_at & 1 == 1, gy_at & 1 == 1

    for c in range(3):
        for x in range(SIDE):
            both = vel[c, 2 * x] + vel[c, 2 * x + 1]
            pool_s[c, x] = both
    rows = []
    for c in range(3):
        cols = []
        for x in range(SIDE):
            cols.append(pool_s[c, x, pl.ds(0, 8, stride=2), :] + pool_s[c, x, pl.ds(1, 8, stride=2), :])
        rows.append(jnp.concatenate(cols, axis=0))
    pooled = jnp.concatenate(rows, axis=0)
    zpool = jnp.where(iota((128, 1), 0) >> 1 == iota((1, 64), 1), 0.125, 0.0)
    filt = nn(pooled, zpool, HIGH).astype(BF16)
    tgt_rows = tgt[...].reshape(64, 64)
    zsel = jnp.concatenate([filt[0:64], filt[64:128], filt[128:192], tgt_rows], axis=1)
    spread = onehot(iota((ROWS, 1), 0) >> 3 == iota((1, 64), 1))
    by_block = nn(spread, zsel)
    mine = (iota((1, 256), 1) & 63) >> 3 == iota((ROWS, 1), 0) & 7
    by_block = jnp.where(mine, by_block, 0.0).astype(BF16)
    lane_in = iota((1, 256), 1)
    lane_off = lax.div(lane_in, 24)
    lane_cz = lane_in - lane_off * 24
    src = iota((256, 1), 0)
    pick = onehot(jnp.where(lane_in < 216, lane_cz, -1) == (src >> 6) * 8 + (src & 7))
    cells = nn(by_block, pick)
    pick_t = onehot(jnp.where(src >= 192, src & 7, -1) == iota((1, SIDE), 1))
    target = nn(by_block, pick_t)

    fp_s[...] = jnp.zeros(fp_s.shape, F32)
    fp_s[1:9, 1:9] = cells.reshape(SIDE, SIDE, BLK, 256)
    group = lax.div(iota((1, 1, 1, 256), 3), 24)
    for x in range(SIDE):
        acc = jnp.zeros((1, SIDE, BLK, 256), F32)
        for k in range(9):
            part = fp_s[x + k // 3 : x + k // 3 + 1, k % 3 : k % 3 + SIDE]
            acc = jnp.where(group == k, part, acc)
        i1_s[x * SLAB : (x + 1) * SLAB, :] = acc.reshape(SLAB, 256).astype(BF16)

    j_at = iota((81, 1), 0)
    j_off, j_dz, j_c = lax.div(j_at, 9), lax.rem(lax.div(j_at, 3), 3) - 1, lax.rem(j_at, 3)
    lane_key = jnp.where(lane_in < 216, lane_off * 4 + (lane_cz >> 3), -1)
    same = lane_key == j_off * 4 + j_c
    delta = jnp.where(same, (lane_in & 7) - j_dz, -9)
    w1v = w1[...]
    t1 = jnp.concatenate([nn(w1v, onehot(delta == z)).astype(BF16) for z in range(SIDE)], axis=0)
    pre_s[...] = nt(i1_s[...], t1)

    src = iota((320, 1), 0) - 64
    dst = iota((1, 512), 1)
    wanted = ((dst >> 7) - 2 + ((dst & 127) >> 6)) * 64 + (dst & 63)
    chooser = onehot(jnp.where((src >= 0) & (src < 192), src - 64, -999) == wanted)
    zero_tile = jnp.zeros((64, 128), BF16)
    left = iota((64, 128), 1) < 64
    w2_s[:, 1664:1792] = jnp.zeros((64, 128), F32)
    w2_s[:, 0:1728] = w2[...].astype(F32)
    w2t = jnp.concatenate(
        [
            jnp.transpose(jnp.concatenate([w2_s[:, t * 128 : (t + 1) * 128]] * 2, axis=0))
            for t in range(14)
        ],
        axis=0,
    )
    for k in range(9):
        base = (192 * k) // 128 * 128
        off = 192 * k - base
        width = min(256, 1728 - base)
        tiles = nn(w2[:, base : base + width], chooser[64 - off : 64 - off + width]).astype(BF16)
        kb = 8 - k
        turned = {dz: w2t[(3 * k + dz + 1) * 64 : (3 * k + dz + 2) * 64] for dz in (-1, 0, 1)}
        turned[-2] = turned[2] = jnp.zeros((64, 128), F32)
        forward = {d: jnp.where(left, turned[d], turned[d - 1]).astype(BF16) for d in (-1, 0, 1, 2)}
        for q in range(2):
            for w in range(6):
                z = 2 * q + w
                for h in range(2):
                    m = 2 * q + h
                    at, cols = k * 384 + w * 64, slice(h * 128, (h + 1) * 128)
                    tt_s[q, at : at + 64, cols] = forward.get(z - 2 * m, zero_tile)
                    d = 2 * m - z
                    tile = tiles[:, (d + 2) * 128 : (d + 3) * 128] if -2 <= d <= 1 else zero_tile
                    at = kb * 384 + w * 64
                    tb_s[q, at : at + 64, cols] = tile

    def windows(ref, q):
        return jnp.concatenate(
            [
                ref[dx * SLAB : dx * SLAB + ROWS, j * 512 + q * 128 : j * 512 + q * 128 + 384]
                for dx in range(3)
                for j in range(3)
            ],
            axis=1,
        )

    def shifted_store(dst_ref, x, val):
        zero = jnp.zeros((1, BLK, WIDE), F32)
        lo, hi = (x + 1) * SLAB, (x + 2) * SLAB
        dst_ref[lo:hi, 0:512] = jnp.concatenate([zero, val[:-1]], axis=0).reshape(SLAB, WIDE).astype(BF16)
        dst_ref[lo:hi, 512:1024] = val.reshape(SLAB, WIDE).astype(BF16)
        dst_ref[lo:hi, 1024:1536] = jnp.concatenate([val[1:], zero], axis=0).reshape(SLAB, WIDE).astype(BF16)

    for ref in (a_s, d_s):
        ref[0:SLAB, :] = jnp.zeros((SLAB, 1536), BF16)
        ref[9 * SLAB :, :] = jnp.zeros((SLAB, 1536), BF16)

    for x in range(SIDE):
        pre = pre_s[x * SLAB : (x + 1) * SLAB, :]
        sig = sigmoid(pre)
        slope1_s[x * SLAB : (x + 1) * SLAB, :] = sig * (1.0 + pre * (1.0 - sig))
        shifted_store(a_s, x, (pre * sig).reshape(SIDE, BLK, WIDE))

    for q in range(2):
        pre_s[:, q * 256 : (q + 1) * 256] = nn(windows(a_s, q), tt_s[q])
    for x in range(SIDE):
        pre = pre_s[x * SLAB : (x + 1) * SLAB, :]
        sig = sigmoid(pre)
        slope2_s[x * SLAB : (x + 1) * SLAB, :] = sig * (1.0 + pre * (1.0 - sig))
        ah_s[x * SLAB : (x + 1) * SLAB, :] = (pre * sig).astype(BF16)

    tile8 = onehot(iota((64, 1), 0) == iota((1, WIDE), 1) & 63)
    w3_wide = nn(w3[...], tile8)
    diag = iota((1, WIDE), 1) >> 6 == iota((SIDE, 1), 0)
    last = jnp.where(diag, w3_wide, 0.0).astype(BF16)
    logits = nt(ah_s[...], last)
    eddy = 0.5 * (jnp.maximum(logits, 0.0) + jnp.log1p(jnp.exp(-jnp.abs(logits))))
    error = eddy - target
    losses = jnp.sum(jnp.sum((error * error).reshape(64, BLK, SIDE), axis=0), axis=1, keepdims=True) / CELLS
    d_logit = (error * sigmoid(logits) / (trainers * CELLS)).astype(BF16)

    zrep = onehot(iota((SIDE, 1), 0) == (iota((1, 128), 1) & 15) >> 1, F32)
    fine = nn(eddy, zrep, HIGH)
    fine = jnp.where(iota((1, 128), 1) >> 4 == iota((ROWS, 1), 0) & 7, fine, 0.0)
    fine = jnp.sum(fine.reshape(64, BLK, 128), axis=1)
    eddy_out[...] = fine

    for c in range(3):
        for i in range(2):
            lo, hi = vel[c, i], vel[c, 14 + i]
            at = (c * 2 + i) * 16
            hx_a[at : at + 16, :] = jnp.where(gx_odd, lo, hi)
            hx_b[at : at + 16, :] = jnp.where(gx_odd, hi, lo)
    small = fine * EDDY_SCALE
    hx_a[96:104, :] = jnp.where(gx_odd, small[0:8], small[56:64])
    hx_b[96:104, :] = jnp.where(gx_odd, small[56:64], small[0:8])
    core = send.at[480:584]
    for c in range(3):
        for i in range(2):
            lo = jnp.concatenate([vel[c, x, i : i + 1, :] for x in range(16)], axis=0)
            hi = jnp.concatenate([vel[c, x, 14 + i : 15 + i, :] for x in range(16)], axis=0)
            at = (c * 2 + i) * 16
            core[at : at + 16, :] = jnp.where(gy_odd, lo, hi)
            hy_b[at : at + 16, :] = jnp.where(gy_odd, hi, lo)
    lo = eddy_out[pl.ds(0, 8, stride=8), :] * EDDY_SCALE
    hi = eddy_out[pl.ds(7, 8, stride=8), :] * EDDY_SCALE
    core[96:104, :] = jnp.where(gy_odd, lo, hi)
    hy_b[96:104, :] = jnp.where(gy_odd, hi, lo)
    vt = jnp.transpose(vel[...].reshape(768, 128))
    et = jnp.transpose(jnp.concatenate([small, jnp.zeros((64, 128), F32)], axis=0))
    hz[...] = jnp.zeros(hz.shape, F32)
    for t in range(6):
        hz[t * 8 : t * 8 + 2, :] = vt[0:2, t * 128 : (t + 1) * 128]
        hz[t * 8 + 2 : t * 8 + 4, :] = vt[126:128, t * 128 : (t + 1) * 128]
    hz[48:49, :] = et[0:1]
    hz[49:50, :] = et[127:128]
    second = half == 1
    halo1[...] = jnp.where(second, hx_a[...], hy_b[...])
    halo2[...] = jnp.where(second, hy_b[...], hz[...])
    halo3[...] = jnp.where(second, hx_b[...], hx_a[...])
    halo4[...] = jnp.where(second, hz[...], hx_b[...])

    code = own[...] * BLK + blk[...]
    listed = code.shape[1]
    wanted = gx_at * BLK + iota((BLK, listed), 0)
    count = jnp.sum(jnp.where(code == wanted, 1.0, 0.0), axis=1, keepdims=True)
    count_rows = jnp.broadcast_to(count.reshape(1, BLK, 1), (64, BLK, 1)).reshape(ROWS, 1)

    big_s[:, 0:512] = nn(d_logit, last)
    for x in range(SIDE):
        d_hid = big_s[x * SLAB : (x + 1) * SLAB, 0:512] * slope2_s[x * SLAB : (x + 1) * SLAB, :]
        d_hid = d_hid.astype(BF16).astype(F32).reshape(SIDE, BLK, WIDE)
        shifted_store(d_s, x, d_hid)
        dw_s[x * SLAB : (x + 1) * SLAB, :] = (d_hid * count[None]).reshape(SLAB, WIDE).astype(BF16)
    dwt = jnp.transpose(dw_s[...])

    sums = {}
    for p in range(4):
        first, last_z = max(2 * p - 1, 0), min(2 * p + 2, SIDE - 1)
        shifts = [
            a_s[dx * SLAB : dx * SLAB + ROWS, j * 512 + p * 128 : j * 512 + (p + 1) * 128]
            for dx in range(3)
            for j in range(3)
        ]
        found = nn(dwt[first * 64 : (last_z + 1) * 64], jnp.concatenate(shifts, axis=1))
        for z in range(first, last_z + 1):
            part = found[(z - first) * 64 : (z - first + 1) * 64]
            m = z - 2 * p
            sums[m] = part if m not in sums else sums[m] + part
    low_half = iota((64, 128), 1) < 64
    held = None
    for k in range(9):
        for dz in (-1, 0, 1):
            low, high = (sums[m][:, k * 128 : (k + 1) * 128] for m in (-dz, 1 - dz))
            at = (k * 3 + dz + 1) * 64
            if at % 128:
                gh_s[:, at - 64 : at + 64] = jnp.where(low_half, held, high + pltpu.roll(low, 64, 1))
            else:
                held = low + pltpu.roll(high, 64, 1)
    gh_s[:, 1664:1792] = jnp.where(low_half, held, 0.0)

    for q in range(2):
        pre_s[:, q * 256 : (q + 1) * 256] = nn(windows(d_s, q), tb_s[q])
    for x in range(SIDE):
        rows = slice(x * SLAB, (x + 1) * SLAB)
        d_first = (pre_s[rows, :] * slope1_s[rows, :]).astype(BF16).astype(F32)
        dw_s[rows, :] = (d_first.reshape(SIDE, BLK, WIDE) * count[None]).reshape(SLAB, WIDE).astype(BF16)
    g1 = nn(jnp.transpose(dw_s[...]), i1_s[...])
    z_in = iota((1, 256), 1) & 7
    parts = []
    for dz in (-1, 0, 1):
        tot = jnp.zeros((64, 256), F32)
        for z in range(SIDE):
            if 0 <= z + dz < SIDE:
                tot = tot + jnp.where(z_in == z + dz, g1[z * 64 : (z + 1) * 64], 0.0)
        parts.append(tot)
    r_at = iota((768, 1), 0)
    c_at = iota((1, 128), 1)
    r_lane = r_at & 255
    r_off = lax.div(r_lane, 24)
    r_col = (r_off * 3 + (r_at >> 8)) * 3 + ((r_lane - r_off * 24) >> 3)
    fold = onehot(jnp.where(r_lane < 216, r_col, -1) == c_at, F32)
    g_first = nn(jnp.concatenate(parts, axis=1), fold, HIGH)

    dlw = d_logit.astype(F32) * count_rows
    dl_hi = dlw.astype(BF16)
    dl_lo = (dlw - dl_hi.astype(F32)).astype(BF16)
    ah = ah_s[...]
    gl = tn(dl_hi, ah) + tn(dl_lo, ah)
    gl = jnp.where(diag, gl, 0.0)
    fold_o = onehot(iota((1, WIDE), 1) & 63 == iota((64, 1), 0), F32)
    g_last = jnp.sum(nt(fold_o, gl, HIGH), axis=1, keepdims=True)

    lane8 = iota((BLK, 128), 1)
    loss_row = jnp.where(lane8 - (LOSS_COL + BLK * (dev >> 6)) == iota((BLK, 128), 0), losses, 0.0)
    loss_row = jnp.sum(loss_row, axis=0, keepdims=True)
    lane = iota((64, 128), 1)
    extra = jnp.where(lane == LAST_COL, g_last, g_first)
    extra = extra + jnp.where(iota((64, 128), 0) == dev & 63, loss_row, 0.0)

    for t in range(PAY // 128):
        if t == 0:
            top, bottom = extra[0:32], extra[32:64]
        else:
            top, bottom = (gh_s[r : r + 32, (t - 1) * 128 : t * 128] for r in (0, 32))
        keep[t * 32 : (t + 1) * 32, :] = jnp.where(second, bottom, top)
        send[t * 32 : (t + 1) * 32, :] = jnp.where(second, top, bottom)


def vmem_spec():
    return pl.BlockSpec(memory_space=pltpu.VMEM)


def run_net(velocity, target, w1, w2, w3, own, blk):
    f = lambda *s: pltpu.VMEM(s, F32)
    return pl.pallas_call(
        net_kernel,
        out_shape=(f(480, 128), f(584, 128), f(64, 128)) + (f(104, 128),) * 4,
        in_specs=[vmem_spec()] * 7,
        out_specs=tuple(vmem_spec() for _ in range(7)),
        scratch_shapes=[
            pltpu.VMEM((104, 128), F32),
            pltpu.VMEM((104, 128), F32),
            pltpu.VMEM((104, 128), F32),
            pltpu.VMEM((104, 128), F32),
            pltpu.VMEM((3, SIDE, 16, 128), F32),
            pltpu.VMEM((10, 10, BLK, 256), F32),
            pltpu.VMEM((ROWS, 256), BF16),
            pltpu.VMEM((ROWS + 2 * SLAB, 1536), BF16),
            pltpu.VMEM((ROWS + 2 * SLAB, 1536), BF16),
            pltpu.VMEM((2, 3456, 256), BF16),
            pltpu.VMEM((2, 3456, 256), BF16),
            pltpu.VMEM((ROWS, WIDE), F32),
            pltpu.VMEM((ROWS, WIDE), F32),
            pltpu.VMEM((ROWS, WIDE), BF16),
            pltpu.VMEM((ROWS, WIDE), F32),
            pltpu.VMEM((ROWS, WIDE), BF16),
            pltpu.VMEM((ROWS, WIDE), F32),
            pltpu.VMEM((64, PAY - 128), F32),
            pltpu.VMEM((64, 1792), F32),
        ],
        compiler_params=pltpu.CompilerParams(vmem_limit_bytes=56 * 1024 * 1024),
        name="net",
    )(velocity, target, w1, w2, w3, own, blk)


def flow_kernel(
    vel, eddy, got0, got1, got2, got3, got4, out, rx_a, rx_b, ry_a, ry_b, rz, vx_s, vy_s, visc_s, ez_s
):
    gx_at, gy_at = lax.axis_index("gx"), lax.axis_index("gy")
    gx_odd, gy_odd = gx_at & 1 == 1, gy_at & 1 == 1
    second = core_half(gy_at) == 1
    ry_a[...] = got0[...]
    ry_b[...] = jnp.where(second, got2[...], got1[...])
    rx_a[...] = jnp.where(second, got1[...], got3[...])
    rx_b[...] = jnp.where(second, got3[...], got4[...])
    rz[...] = jnp.where(second, got4[...], got2[...])
    lane = iota((1, 128), 1)

    def sides(odd, a, b, at, rows):
        one, two = a[at : at + rows, :], b[at : at + rows, :]
        return jnp.where(odd, one, two), jnp.where(odd, two, one)

    for c in range(3):
        for x in range(16):
            vy_s[(c * 16 + x) * 32 + 8 : (c * 16 + x) * 32 + 24, :] = vel[c, x]
        for i in range(2):
            below, above = sides(gy_odd, ry_a, ry_b, (c * 2 + i) * 16, 16)
            vy_s[pl.ds(c * 512 + 6 + i, 16, stride=32), :] = below
            vy_s[pl.ds(c * 512 + 24 + i, 16, stride=32), :] = above
            below, above = sides(gx_odd, rx_a, rx_b, (c * 2 + i) * 16, 16)
            vx_s[c, i] = below
            vx_s[c, 2 + i] = above

    zcols = jnp.concatenate([jnp.transpose(rz[t * 8 : t * 8 + 8, :]) for t in range(7)], axis=0)
    coarse = eddy[...]
    e_first, e_last = zcols[768:832, 0:1] / EDDY_SCALE, zcols[768:832, 1:2] / EDDY_SCALE
    ahead = jnp.where(lane == 127, e_first, pltpu.roll(coarse, 127, 1))
    behind = jnp.where(lane == 0, e_last, pltpu.roll(coarse, 1, 1))
    below_x, above_x = (v / EDDY_SCALE for v in sides(gx_odd, rx_a, rx_b, 96, 8))
    below_y, above_y = (v / EDDY_SCALE for v in sides(gy_odd, ry_a, ry_b, 96, 8))

    def put(dst, plane, val):
        dst[pl.ds(plane * 32 + 8, 8, stride=2), :] = val
        dst[pl.ds(plane * 32 + 9, 8, stride=2), :] = val

    put(visc_s, 0, base_visc + below_x)
    put(visc_s, 17, base_visc + above_x)
    for x in range(8):
        for r in range(2):
            plane = 2 * x + 1 + r
            put(visc_s, plane, base_visc + coarse[x * 8 : x * 8 + 8])
            visc_s[plane * 32 + 7 : plane * 32 + 8, :] = base_visc + below_y[x : x + 1]
            visc_s[plane * 32 + 24 : plane * 32 + 25, :] = base_visc + above_y[x : x + 1]
        put(ez_s, 2 * x, base_visc + ahead[x * 8 : x * 8 + 8])
        put(ez_s, 2 * x + 1, base_visc + behind[x * 8 : x * 8 + 8])

    def plane_of(c, x):
        if x < 0:
            return vx_s[c, x + 2]
        if x > 15:
            return vx_s[c, x - 14]
        return vel[c, x]

    for x in range(16):
        vat = (x + 1) * 32
        visc = visc_s[vat + 8 : vat + 24, :]
        faces = (
            (visc_s[vat + 40 : vat + 56, :], visc_s[vat - 24 : vat - 8, :]),
            (visc_s[vat + 9 : vat + 25, :], visc_s[vat + 7 : vat + 23, :]),
            (
                ez_s[(x // 2 * 2) * 32 + 8 : (x // 2 * 2) * 32 + 24, :],
                ez_s[(x // 2 * 2 + 1) * 32 + 8 : (x // 2 * 2 + 1) * 32 + 24, :],
            ),
        )
        faces = [(0.5 * (visc + a), 0.5 * (visc + b)) for a, b in faces]
        wind = [vel[a, x] for a in range(3)]
        for c in range(3):
            u = vel[c, x]
            at = (c * 16 + x) * 32
            zat = (c * 16 + x) * 16
            zc = zcols[zat : zat + 16]
            p1 = jnp.where(lane == 127, zc[:, 0:1], pltpu.roll(u, 127, 1))
            p2 = jnp.where(lane == 127, zc[:, 1:2], jnp.where(lane == 126, zc[:, 0:1], pltpu.roll(u, 126, 1)))
            m1 = jnp.where(lane == 0, zc[:, 3:4], pltpu.roll(u, 1, 1))
            m2 = jnp.where(lane == 0, zc[:, 2:3], jnp.where(lane == 1, zc[:, 3:4], pltpu.roll(u, 2, 1)))
            near = (
                (plane_of(c, x + 1), plane_of(c, x - 1), plane_of(c, x + 2), plane_of(c, x - 2)),
                (
                    vy_s[at + 9 : at + 25, :], vy_s[at + 7 : at + 23, :],
                    vy_s[at + 10 : at + 26, :], vy_s[at + 6 : at + 22, :],
                ),
                (p1, m1, p2, m2),
            )
            advect = None
            diffuse = None
            for a in range(3):
                q1, b1, q2, b2 = near[a]
                slope = (8.0 * (q1 - b1) - (q2 - b2)) * (1.0 / 12.0)
                term = wind[a] * slope
                advect = term if advect is None else advect + term
                flux = faces[a][0] * (q1 - u) - faces[a][1] * (u - b1)
                diffuse = flux if diffuse is None else diffuse + flux
            out[c, x] = u + time_step * (diffuse - advect)


def run_flow(velocity, eddy, *got):
    return pl.pallas_call(
        flow_kernel,
        out_shape=jax.ShapeDtypeStruct(velocity.shape, F32),
        in_specs=[vmem_spec()] * 7,
        out_specs=vmem_spec(),
        scratch_shapes=[
            pltpu.VMEM((104, 128), F32),
            pltpu.VMEM((104, 128), F32),
            pltpu.VMEM((104, 128), F32),
            pltpu.VMEM((104, 128), F32),
            pltpu.VMEM((104, 128), F32),
            pltpu.VMEM((3, 4, 16, 128), F32),
            pltpu.VMEM((3 * 16 * 32, 128), F32),
            pltpu.VMEM((18 * 32, 128), F32),
            pltpu.VMEM((16 * 32, 128), F32),
        ],
        compiler_params=pltpu.CompilerParams(vmem_limit_bytes=32 * 1024 * 1024),
        name="flow",
    )(velocity, eddy, *got)


def finish_kernel(own, blk, mine, other, loss_out, first_out, hidden_out, last_out, ext_s):
    gx_at, gy_at = lax.axis_index("gx"), lax.axis_index("gy")
    n_z = lax.axis_size("role")
    in_group = gy_at * n_z + lax.axis_index("role")
    second = core_half(gy_at) == 1
    for t in range(PAY // 128):
        one, two = mine[t * 32 : (t + 1) * 32, :], other[t * 32 : (t + 1) * 32, :]
        top, bottom = jnp.where(second, two, one), jnp.where(second, one, two)
        if t == 0:
            ext_s[0:32, :] = top
            ext_s[32:64, :] = bottom
        else:
            at = (t - 1) * 128
            width = min(128, 27 * CH - at)
            hidden_out[0:32, at : at + width] = top[:, :width]
            hidden_out[32:64, at : at + width] = bottom[:, :width]
    extra = ext_s[...]
    first_out[...] = extra[:, 0:81]
    turned = jnp.transpose(jnp.concatenate([extra, jnp.zeros((64, 128), F32)], axis=0))
    last_out[...] = turned[LAST_COL : LAST_COL + 1, 0:64]
    slots = loss_out.shape[1]
    dev = own[...] * (lax.axis_size("gy") * n_z) + in_group
    listed = dev.shape[1]
    pick = onehot(iota((64, listed), 0) == dev & 63, F32)
    rows = nn(turned[:, 0:64], pick, HIGH)
    rows = jnp.where(iota((128, listed), 0) == LOSS_COL + BLK * (dev >> 6) + blk[...], rows, 0.0)
    found = jnp.sum(rows, axis=0, keepdims=True)
    picked = jnp.zeros((1, slots), F32)
    for g in range(listed // slots):
        picked = jnp.where(gx_at == g, found[:, g * slots : (g + 1) * slots], picked)
    loss_out[...] = picked


def run_finish(own, blk, mine, other, slots):
    f = lambda *s: jax.ShapeDtypeStruct(s, F32)
    return pl.pallas_call(
        finish_kernel,
        out_shape=(f(1, slots), f(64, 81), f(64, 27 * CH), f(1, 64)),
        in_specs=[vmem_spec()] * 4,
        out_specs=tuple(vmem_spec() for _ in range(4)),
        scratch_shapes=[pltpu.VMEM((64, 128), F32)],
        compiler_params=pltpu.CompilerParams(vmem_limit_bytes=32 * 1024 * 1024),
        name="finish",
    )(own, blk, mine, other)


def on_device(velocity, target_visc, w_first, w_hidden, w_last, sample_owner, sample_block):
    n_x, n_y, n_z = lax.axis_size("gx"), lax.axis_size("gy"), lax.axis_size("role")
    trainers = n_x * n_y * n_z
    own = sample_owner.reshape(1, -1)
    blk = sample_block.reshape(1, -1)
    slots = own.shape[1] // n_x

    axes = ("gx", "gy", "role")

    def even_odd(i, count):
        return i ^ 1

    def odd_even(i, count):
        return (i - 1) % count if i % 2 == 0 else (i + 1) % count

    def partner(kind, i, j, r):
        if kind == "x":
            j = odd_even(j, n_y)
        elif kind == "y":
            r = r ^ 1
        elif kind == "z_a":
            i = even_odd(i, n_x)
        else:
            i = odd_even(i, n_x)
        return (i * n_y + j) * n_z + r

    def mixed(kinds):
        pairs = []
        for i in range(n_x):
            for j in range(n_y):
                for r in range(n_z):
                    pairs.append(((i * n_y + j) * n_z + r, partner(kinds[(j ^ (j >> 1)) & 1], i, j, r)))
        return pairs

    core_pairs = [(j, even_odd(j, n_y)) for j in range(n_y)]
    size = TILES * 32

    keep, send, eddy, *halos = run_net(
        velocity, target_visc, w_first, w_hidden, w_last.reshape(1, CH), own, blk
    )
    half = core_half(lax.axis_index("gy"))
    got = lax.ppermute(send, "gy", core_pairs)
    total = keep + got[:size]
    rims = [got[size:]]
    halos = [h.astype(F16) for h in halos]

    def widen(values, exps):
        wide = values.astype(F32).reshape(TILES, 32, 128) * jnp.exp2(exps)[:, None, :]
        return wide.reshape(size, 128)

    top = jnp.max(jnp.abs(total.reshape(TILES, 32, 128)), axis=1)
    exps = jnp.clip(jnp.ceil(jnp.log2(jnp.maximum(top, 1e-30))) - 13.0, -110.0, 110.0)
    orders = (("x", "y", "z_a", "z_b"), ("z_a", "x", "z_b", "y"))
    for s in range(4):
        kinds = (orders[0][s], orders[1][s])
        scaled = total.reshape(TILES, 32, 128) * jnp.exp2(-exps)[:, None, :]
        pieces = [scaled.reshape(size, 128).astype(F16), jnp.pad(exps, ((0, 1), (0, 0))).astype(F16)]
        message = jnp.concatenate(pieces + [halos[s]] if s < 3 else pieces, axis=0)
        message = lax.optimization_barrier(message)
        if s == 2:
            lone = lax.optimization_barrier((rims[-1], halos[3]))[1]
        got = lax.ppermute(message, axes, mixed(kinds))
        if s == 2:
            far = lax.ppermute(lone, axes, mixed((orders[0][3], orders[1][3])))
        their_exps = got[size : size + TILES].astype(F32)
        mine, theirs = widen(message[:size], exps), widen(got[:size], their_exps)
        if n_x != 4 and "z_b" in kinds:
            theirs = jnp.where(half == kinds.index("z_b"), 0.0, theirs)
        total = mine + theirs
        exps = jnp.maximum(exps, their_exps) + 1.0
        if s < 3:
            rims.append(got[size + 16 :].astype(F32))
        if s == 2:
            total, far = lax.optimization_barrier((total, far))
            u_next = run_flow(velocity, eddy, *rims, far.astype(F32))
    total, u_next = lax.optimization_barrier((total, u_next))
    if n_x != 4:
        for bit in range(1, n_x.bit_length() - 1):
            total = total + lax.ppermute(total, "gx", [(i, i ^ (1 << bit)) for i in range(n_x)])
    other = lax.ppermute(total, "gy", core_pairs)

    losses, first, hidden, last = run_finish(own, blk, total, other, slots)
    return (u_next, losses.reshape(1, 1, slots), first, hidden, last.reshape(CH))


def solution(mesh):
    return jax.shard_map(
        on_device,
        mesh=mesh,
        in_specs=(
            P(None, "gx", "gy", "role"),
            P("gx", "gy", "role"),
            P(),
            P(),
            P(),
            P("gy", "role", None, None),
            P("gy", "role", None, None),
        ),
        out_specs=(P(None, "gx", "gy", "role"), P("gy", "role", "gx"), P(), P(), P()),
        check_vma=False,
    )
```

```python
import jax
import jax.numpy as jnp
from jax import lax
from jax.experimental import pallas as pl
from jax.experimental.pallas import tpu as pltpu
from jax.sharding import PartitionSpec as P

F32 = jnp.float32
BF16 = jnp.bfloat16
HIGH = lax.Precision.HIGHEST

SIDE = 8
CELLS = SIDE**3
CH = 64
BLK = 8
ROWS = SIDE * SIDE * BLK
WIDE = SIDE * CH
SLAB = SIDE * BLK
HIDDEN_TILES = 14
TILES = 16
LAST_COL = 81
LOSS_COL = 82

EDDY_SCALE = 2.0**-9
F16 = jnp.float16

base_visc = 0.02
time_step = 0.2


def iota(shape, dim):
    return lax.broadcasted_iota(jnp.int32, shape, dim)


def onehot(cond, dtype=BF16):
    return jnp.where(cond, 1.0, 0.0).astype(dtype)


def sigmoid(v):
    return 0.5 + 0.5 * jnp.tanh(0.5 * v)


def nt(a, b, precision=None):
    return lax.dot_general(a, b, (((1,), (1,)), ((), ())), preferred_element_type=F32, precision=precision)


def tn(a, b, precision=None):
    return lax.dot_general(a, b, (((0,), (0,)), ((), ())), preferred_element_type=F32, precision=precision)


def nn(a, b, precision=None):
    return lax.dot_general(a, b, (((1,), (0,)), ((), ())), preferred_element_type=F32, precision=precision)


def core_half(at):
    return (at ^ (at >> 1)) & 1


def place():
    gx_at, gy_at = lax.axis_index("gx"), lax.axis_index("gy")
    return gx_at, gy_at, core_half(gy_at) == 1


def times_sampled(own, blk, gx_at):
    code = own[...] * BLK + blk[...]
    wanted = gx_at * BLK + iota((BLK, code.shape[1]), 0)
    return jnp.sum(jnp.where(code == wanted, 1.0, 0.0), axis=1, keepdims=True)


def diagonal():
    return iota((1, WIDE), 1) >> 6 == iota((SIDE, 1), 0)


def windows(ref, q):
    return jnp.concatenate(
        [
            ref[dx * SLAB : dx * SLAB + ROWS, j * 512 + q * 128 : j * 512 + q * 128 + 384]
            for dx in range(3)
            for j in range(3)
        ],
        axis=1,
    )


def shifted_store(dst_ref, x, val):
    zero = jnp.zeros((1, BLK, WIDE), F32)
    lo, hi = (x + 1) * SLAB, (x + 2) * SLAB
    dst_ref[lo:hi, 0:512] = jnp.concatenate([zero, val[:-1]], axis=0).reshape(SLAB, WIDE).astype(BF16)
    dst_ref[lo:hi, 512:1024] = val.reshape(SLAB, WIDE).astype(BF16)
    dst_ref[lo:hi, 1024:1536] = jnp.concatenate([val[1:], zero], axis=0).reshape(SLAB, WIDE).astype(BF16)


def clear_ends(ref):
    ref[0:SLAB, :] = jnp.zeros((SLAB, 1536), BF16)
    ref[9 * SLAB :, :] = jnp.zeros((SLAB, 1536), BF16)


def forward_kernel(
    vel, tgt, w1, w2, w3, own, blk,
    keep, send, eddy_out, loss_out, dl_out, ah_s, slope1_s, i1_s, dh_s, tb_s,
    pool_s, fp_s, a_s, tt_s, pre_s, slope2_s, dw_s, big_s, gh_s, w2_s,
):
    gx_at, gy_at, second = place()
    trainers = lax.axis_size("gx") * lax.axis_size("gy") * lax.axis_size("role")

    for c in range(3):
        for x in range(SIDE):
            both = vel[c, 2 * x] + vel[c, 2 * x + 1]
            pool_s[c, x] = both
    rows = []
    for c in range(3):
        cols = []
        for x in range(SIDE):
            cols.append(pool_s[c, x, pl.ds(0, 8, stride=2), :] + pool_s[c, x, pl.ds(1, 8, stride=2), :])
        rows.append(jnp.concatenate(cols, axis=0))
    pooled = jnp.concatenate(rows, axis=0)
    zpool = jnp.where(iota((128, 1), 0) >> 1 == iota((1, 64), 1), 0.125, 0.0)
    filt = nn(pooled, zpool, HIGH).astype(BF16)
    tgt_rows = tgt[...].reshape(64, 64)
    zsel = jnp.concatenate([filt[0:64], filt[64:128], filt[128:192], tgt_rows], axis=1)
    spread = onehot(iota((ROWS, 1), 0) >> 3 == iota((1, 64), 1))
    by_block = nn(spread, zsel)
    mine = (iota((1, 256), 1) & 63) >> 3 == iota((ROWS, 1), 0) & 7
    by_block = jnp.where(mine, by_block, 0.0).astype(BF16)
    lane_in = iota((1, 256), 1)
    lane_off = lax.div(lane_in, 24)
    lane_cz = lane_in - lane_off * 24
    src = iota((256, 1), 0)
    pick = onehot(jnp.where(lane_in < 216, lane_cz, -1) == (src >> 6) * 8 + (src & 7))
    cells = nn(by_block, pick)
    pick_t = onehot(jnp.where(src >= 192, src & 7, -1) == iota((1, SIDE), 1))
    target = nn(by_block, pick_t)

    fp_s[...] = jnp.zeros(fp_s.shape, F32)
    fp_s[1:9, 1:9] = cells.reshape(SIDE, SIDE, BLK, 256)
    group = lax.div(iota((1, 1, 1, 256), 3), 24)
    for x in range(SIDE):
        acc = jnp.zeros((1, SIDE, BLK, 256), F32)
        for k in range(9):
            part = fp_s[x + k // 3 : x + k // 3 + 1, k % 3 : k % 3 + SIDE]
            acc = jnp.where(group == k, part, acc)
        i1_s[x * SLAB : (x + 1) * SLAB, :] = acc.reshape(SLAB, 256).astype(BF16)

    j_at = iota((81, 1), 0)
    j_off, j_dz, j_c = lax.div(j_at, 9), lax.rem(lax.div(j_at, 3), 3) - 1, lax.rem(j_at, 3)
    lane_key = jnp.where(lane_in < 216, lane_off * 4 + (lane_cz >> 3), -1)
    same = lane_key == j_off * 4 + j_c
    delta = jnp.where(same, (lane_in & 7) - j_dz, -9)
    w1v = w1[...]
    t1 = jnp.concatenate([nn(w1v, onehot(delta == z)).astype(BF16) for z in range(SIDE)], axis=0)
    pre_s[...] = nt(i1_s[...], t1)

    src = iota((320, 1), 0) - 64
    dst = iota((1, 512), 1)
    wanted = ((dst >> 7) - 2 + ((dst & 127) >> 6)) * 64 + (dst & 63)
    chooser = onehot(jnp.where((src >= 0) & (src < 192), src - 64, -999) == wanted)
    zero_tile = jnp.zeros((64, 128), BF16)
    left = iota((64, 128), 1) < 64
    w2_s[:, 1664:1792] = jnp.zeros((64, 128), F32)
    w2_s[:, 0:1728] = w2[...].astype(F32)
    w2t = jnp.concatenate(
        [
            jnp.transpose(jnp.concatenate([w2_s[:, t * 128 : (t + 1) * 128]] * 2, axis=0))
            for t in range(14)
        ],
        axis=0,
    )
    for k in range(9):
        base = (192 * k) // 128 * 128
        off = 192 * k - base
        width = min(256, 1728 - base)
        tiles = nn(w2[:, base : base + width], chooser[64 - off : 64 - off + width]).astype(BF16)
        kb = 8 - k
        turned = {dz: w2t[(3 * k + dz + 1) * 64 : (3 * k + dz + 2) * 64] for dz in (-1, 0, 1)}
        turned[-2] = turned[2] = jnp.zeros((64, 128), F32)
        forward = {d: jnp.where(left, turned[d], turned[d - 1]).astype(BF16) for d in (-1, 0, 1, 2)}
        for q in range(2):
            for w in range(6):
                z = 2 * q + w
                for h in range(2):
                    m = 2 * q + h
                    at, cols = k * 384 + w * 64, slice(h * 128, (h + 1) * 128)
                    tt_s[q, at : at + 64, cols] = forward.get(z - 2 * m, zero_tile)
                    d = 2 * m - z
                    tile = tiles[:, (d + 2) * 128 : (d + 3) * 128] if -2 <= d <= 1 else zero_tile
                    at = kb * 384 + w * 64
                    tb_s[q, at : at + 64, cols] = tile

    clear_ends(a_s)

    for x in range(SIDE):
        pre = pre_s[x * SLAB : (x + 1) * SLAB, :]
        sig = sigmoid(pre)
        slope1_s[x * SLAB : (x + 1) * SLAB, :] = sig * (1.0 + pre * (1.0 - sig))
        shifted_store(a_s, x, (pre * sig).reshape(SIDE, BLK, WIDE))

    for q in range(2):
        pre_s[:, q * 256 : (q + 1) * 256] = nn(windows(a_s, q), tt_s[q])
    for x in range(SIDE):
        pre = pre_s[x * SLAB : (x + 1) * SLAB, :]
        sig = sigmoid(pre)
        slope2_s[x * SLAB : (x + 1) * SLAB, :] = sig * (1.0 + pre * (1.0 - sig))
        ah_s[x * SLAB : (x + 1) * SLAB, :] = (pre * sig).astype(BF16)

    tile8 = onehot(iota((64, 1), 0) == iota((1, WIDE), 1) & 63)
    w3_wide = nn(w3[...], tile8)
    diag = diagonal()
    last = jnp.where(diag, w3_wide, 0.0).astype(BF16)
    logits = nt(ah_s[...], last)
    eddy = 0.5 * (jnp.maximum(logits, 0.0) + jnp.log1p(jnp.exp(-jnp.abs(logits))))
    error = eddy - target
    losses = jnp.sum(jnp.sum((error * error).reshape(64, BLK, SIDE), axis=0), axis=1, keepdims=True) / CELLS
    d_logit = (error * sigmoid(logits) / (trainers * CELLS)).astype(BF16)

    zrep = onehot(iota((SIDE, 1), 0) == (iota((1, 128), 1) & 15) >> 1, F32)
    fine = nn(eddy, zrep, HIGH)
    fine = jnp.where(iota((1, 128), 1) >> 4 == iota((ROWS, 1), 0) & 7, fine, 0.0)
    fine = jnp.sum(fine.reshape(64, BLK, 128), axis=1)
    eddy_out[...] = fine
    loss_out[...] = jnp.broadcast_to(losses, (BLK, 128))
    dl_out[...] = d_logit.astype(F32)

    count = times_sampled(own, blk, gx_at)
    big_s[:, 0:512] = nn(d_logit, last)
    for x in range(SIDE):
        d_hid = big_s[x * SLAB : (x + 1) * SLAB, 0:512] * slope2_s[x * SLAB : (x + 1) * SLAB, :]
        d_hid = d_hid.astype(BF16)
        dh_s[x * SLAB : (x + 1) * SLAB, :] = d_hid
        d_hid = d_hid.astype(F32).reshape(SIDE, BLK, WIDE)
        dw_s[x * SLAB : (x + 1) * SLAB, :] = (d_hid * count[None]).reshape(SLAB, WIDE).astype(BF16)
    dwt = jnp.transpose(dw_s[...])

    sums = {}
    for p in range(4):
        first, last_z = max(2 * p - 1, 0), min(2 * p + 2, SIDE - 1)
        shifts = [
            a_s[dx * SLAB : dx * SLAB + ROWS, j * 512 + p * 128 : j * 512 + (p + 1) * 128]
            for dx in range(3)
            for j in range(3)
        ]
        found = nn(dwt[first * 64 : (last_z + 1) * 64], jnp.concatenate(shifts, axis=1))
        for z in range(first, last_z + 1):
            part = found[(z - first) * 64 : (z - first + 1) * 64]
            m = z - 2 * p
            sums[m] = part if m not in sums else sums[m] + part
    low_half = iota((64, 128), 1) < 64
    held = None
    for k in range(9):
        for dz in (-1, 0, 1):
            low, high = (sums[m][:, k * 128 : (k + 1) * 128] for m in (-dz, 1 - dz))
            at = (k * 3 + dz + 1) * 64
            if at % 128:
                gh_s[:, at - 64 : at + 64] = jnp.where(low_half, held, high + pltpu.roll(low, 64, 1))
            else:
                held = low + pltpu.roll(high, 64, 1)
    gh_s[:, 1664:1792] = jnp.where(low_half, held, 0.0)

    for t in range(HIDDEN_TILES):
        top, bottom = (gh_s[r : r + 32, t * 128 : (t + 1) * 128] for r in (0, 32))
        keep[t * 32 : (t + 1) * 32, :] = jnp.where(second, bottom, top)
        send[t * 32 : (t + 1) * 32, :] = jnp.where(second, top, bottom)


def backward_kernel(
    vel, own, blk, eddy, losses, dl_in, ah_s, slope1_s, i1_s, dh_s, tb_s,
    extra_out, hy_a, halo1, halo2, halo3, halo4, hx_a, hx_b, hy_b, hz, d_s, pre_s, dw_s,
):
    gx_at, gy_at, second = place()
    gx_odd, gy_odd = gx_at & 1 == 1, gy_at & 1 == 1
    dev = (gx_at * lax.axis_size("gy") + gy_at) * lax.axis_size("role") + lax.axis_index("role")
    count = times_sampled(own, blk, gx_at)

    clear_ends(d_s)
    for x in range(SIDE):
        d_hid = dh_s[x * SLAB : (x + 1) * SLAB, :].astype(F32)
        shifted_store(d_s, x, d_hid.reshape(SIDE, BLK, WIDE))

    for c in range(3):
        for i in range(2):
            lo, hi = vel[c, i], vel[c, 14 + i]
            at = (c * 2 + i) * 16
            hx_a[at : at + 16, :] = jnp.where(gx_odd, lo, hi)
            hx_b[at : at + 16, :] = jnp.where(gx_odd, hi, lo)
    fine = eddy[...]
    small = fine * EDDY_SCALE
    hx_a[96:104, :] = jnp.where(gx_odd, small[0:8], small[56:64])
    hx_b[96:104, :] = jnp.where(gx_odd, small[56:64], small[0:8])
    for c in range(3):
        for i in range(2):
            lo = jnp.concatenate([vel[c, x, i : i + 1, :] for x in range(16)], axis=0)
            hi = jnp.concatenate([vel[c, x, 14 + i : 15 + i, :] for x in range(16)], axis=0)
            at = (c * 2 + i) * 16
            hy_a[at : at + 16, :] = jnp.where(gy_odd, lo, hi)
            hy_b[at : at + 16, :] = jnp.where(gy_odd, hi, lo)
    lo = eddy[pl.ds(0, 8, stride=8), :] * EDDY_SCALE
    hi = eddy[pl.ds(7, 8, stride=8), :] * EDDY_SCALE
    hy_a[96:104, :] = jnp.where(gy_odd, lo, hi)
    hy_b[96:104, :] = jnp.where(gy_odd, hi, lo)
    vt = jnp.transpose(vel[...].reshape(768, 128))
    et = jnp.transpose(jnp.concatenate([small, jnp.zeros((64, 128), F32)], axis=0))
    hz[...] = jnp.zeros(hz.shape, F32)
    for t in range(6):
        hz[t * 8 : t * 8 + 2, :] = vt[0:2, t * 128 : (t + 1) * 128]
        hz[t * 8 + 2 : t * 8 + 4, :] = vt[126:128, t * 128 : (t + 1) * 128]
    hz[48:49, :] = et[0:1]
    hz[49:50, :] = et[127:128]
    halo1[...] = jnp.where(second, hx_a[...], hy_b[...])
    halo2[...] = jnp.where(second, hy_b[...], hz[...])
    halo3[...] = jnp.where(second, hx_b[...], hx_a[...])
    halo4[...] = jnp.where(second, hz[...], hx_b[...])

    for q in range(2):
        pre_s[:, q * 256 : (q + 1) * 256] = nn(windows(d_s, q), tb_s[q])
    for x in range(SIDE):
        rows = slice(x * SLAB, (x + 1) * SLAB)
        d_first = (pre_s[rows, :] * slope1_s[rows, :]).astype(BF16).astype(F32)
        dw_s[rows, :] = (d_first.reshape(SIDE, BLK, WIDE) * count[None]).reshape(SLAB, WIDE).astype(BF16)
    g1 = nn(jnp.transpose(dw_s[...]), i1_s[...])
    z_in = iota((1, 256), 1) & 7
    parts = []
    for dz in (-1, 0, 1):
        tot = jnp.zeros((64, 256), F32)
        for z in range(SIDE):
            if 0 <= z + dz < SIDE:
                tot = tot + jnp.where(z_in == z + dz, g1[z * 64 : (z + 1) * 64], 0.0)
        parts.append(tot)
    r_at = iota((768, 1), 0)
    c_at = iota((1, 128), 1)
    r_lane = r_at & 255
    r_off = lax.div(r_lane, 24)
    r_col = (r_off * 3 + (r_at >> 8)) * 3 + ((r_lane - r_off * 24) >> 3)
    fold = onehot(jnp.where(r_lane < 216, r_col, -1) == c_at, F32)
    g_first = nn(jnp.concatenate(parts, axis=1), fold, HIGH)

    count_rows = jnp.broadcast_to(count.reshape(1, BLK, 1), (64, BLK, 1)).reshape(ROWS, 1)
    dlw = dl_in[...] * count_rows
    dl_hi = dlw.astype(BF16)
    dl_lo = (dlw - dl_hi.astype(F32)).astype(BF16)
    ah = ah_s[...]
    gl = tn(dl_hi, ah) + tn(dl_lo, ah)
    gl = jnp.where(diagonal(), gl, 0.0)
    fold_o = onehot(iota((1, WIDE), 1) & 63 == iota((64, 1), 0), F32)
    g_last = jnp.sum(nt(fold_o, gl, HIGH), axis=1, keepdims=True)

    lane8 = iota((BLK, 128), 1)
    loss_row = jnp.where(lane8 - (LOSS_COL + BLK * (dev >> 6)) == iota((BLK, 128), 0), losses[...], 0.0)
    loss_row = jnp.sum(loss_row, axis=0, keepdims=True)
    lane = iota((64, 128), 1)
    extra = jnp.where(lane == LAST_COL, g_last, g_first)
    extra = extra + jnp.where(iota((64, 128), 0) == dev & 63, loss_row, 0.0)

    extra_out[...] = extra


def vmem_spec():
    return pl.BlockSpec(memory_space=pltpu.VMEM)


def run_forward(velocity, target, w1, w2, w3, own, blk):
    half = pltpu.VMEM((HIDDEN_TILES * 32, 128), F32)
    return pl.pallas_call(
        forward_kernel,
        out_shape=(
            half,
            half,
            pltpu.VMEM((64, 128), F32),
            pltpu.VMEM((BLK, 128), F32),
            pltpu.VMEM((ROWS, SIDE), F32),
            pltpu.VMEM((ROWS, WIDE), BF16),
            pltpu.VMEM((ROWS, WIDE), F32),
            pltpu.VMEM((ROWS, 256), BF16),
            pltpu.VMEM((ROWS, WIDE), BF16),
            pltpu.VMEM((2, 3456, 256), BF16),
        ),
        in_specs=[vmem_spec()] * 7,
        out_specs=tuple(vmem_spec() for _ in range(10)),
        scratch_shapes=[
            pltpu.VMEM((3, SIDE, 16, 128), F32),
            pltpu.VMEM((10, 10, BLK, 256), F32),
            pltpu.VMEM((ROWS + 2 * SLAB, 1536), BF16),
            pltpu.VMEM((2, 3456, 256), BF16),
            pltpu.VMEM((ROWS, WIDE), F32),
            pltpu.VMEM((ROWS, WIDE), F32),
            pltpu.VMEM((ROWS, WIDE), BF16),
            pltpu.VMEM((ROWS, WIDE), F32),
            pltpu.VMEM((64, HIDDEN_TILES * 128), F32),
            pltpu.VMEM((64, 1792), F32),
        ],
        compiler_params=pltpu.CompilerParams(vmem_limit_bytes=40 * 1024 * 1024),
        name="forward",
    )(velocity, target, w1, w2, w3, own, blk)


def run_backward(velocity, own, blk, *kept):
    face = pltpu.VMEM((104, 128), F32)
    return pl.pallas_call(
        backward_kernel,
        out_shape=(pltpu.VMEM((64, 128), F32),) + (face,) * 5,
        in_specs=[vmem_spec()] * 11,
        out_specs=tuple(vmem_spec() for _ in range(6)),
        scratch_shapes=[face] * 4
        + [
            pltpu.VMEM((ROWS + 2 * SLAB, 1536), BF16),
            pltpu.VMEM((ROWS, WIDE), F32),
            pltpu.VMEM((ROWS, WIDE), BF16),
        ],
        compiler_params=pltpu.CompilerParams(vmem_limit_bytes=40 * 1024 * 1024),
        name="backward",
    )(velocity, own, blk, *kept)


def flow_kernel(
    vel, eddy, got0, got1, got2, got3, got4, out, rx_a, rx_b, ry_a, ry_b, rz, vx_s, vy_s, visc_s, ez_s
):
    gx_at, gy_at = lax.axis_index("gx"), lax.axis_index("gy")
    gx_odd, gy_odd = gx_at & 1 == 1, gy_at & 1 == 1
    second = core_half(gy_at) == 1
    ry_a[...] = got0[...]
    ry_b[...] = jnp.where(second, got2[...], got1[...])
    rx_a[...] = jnp.where(second, got1[...], got3[...])
    rx_b[...] = jnp.where(second, got3[...], got4[...])
    rz[...] = jnp.where(second, got4[...], got2[...])
    lane = iota((1, 128), 1)

    def sides(odd, a, b, at, rows):
        one, two = a[at : at + rows, :], b[at : at + rows, :]
        return jnp.where(odd, one, two), jnp.where(odd, two, one)

    for c in range(3):
        for x in range(16):
            vy_s[(c * 16 + x) * 32 + 8 : (c * 16 + x) * 32 + 24, :] = vel[c, x]
        for i in range(2):
            below, above = sides(gy_odd, ry_a, ry_b, (c * 2 + i) * 16, 16)
            vy_s[pl.ds(c * 512 + 6 + i, 16, stride=32), :] = below
            vy_s[pl.ds(c * 512 + 24 + i, 16, stride=32), :] = above
            below, above = sides(gx_odd, rx_a, rx_b, (c * 2 + i) * 16, 16)
            vx_s[c, i] = below
            vx_s[c, 2 + i] = above

    zcols = jnp.concatenate([jnp.transpose(rz[t * 8 : t * 8 + 8, :]) for t in range(7)], axis=0)
    coarse = eddy[...]
    e_first, e_last = zcols[768:832, 0:1] / EDDY_SCALE, zcols[768:832, 1:2] / EDDY_SCALE
    ahead = jnp.where(lane == 127, e_first, pltpu.roll(coarse, 127, 1))
    behind = jnp.where(lane == 0, e_last, pltpu.roll(coarse, 1, 1))
    below_x, above_x = (v / EDDY_SCALE for v in sides(gx_odd, rx_a, rx_b, 96, 8))
    below_y, above_y = (v / EDDY_SCALE for v in sides(gy_odd, ry_a, ry_b, 96, 8))

    def put(dst, plane, val):
        dst[pl.ds(plane * 32 + 8, 8, stride=2), :] = val
        dst[pl.ds(plane * 32 + 9, 8, stride=2), :] = val

    put(visc_s, 0, base_visc + below_x)
    put(visc_s, 17, base_visc + above_x)
    for x in range(8):
        for r in range(2):
            plane = 2 * x + 1 + r
            put(visc_s, plane, base_visc + coarse[x * 8 : x * 8 + 8])
            visc_s[plane * 32 + 7 : plane * 32 + 8, :] = base_visc + below_y[x : x + 1]
            visc_s[plane * 32 + 24 : plane * 32 + 25, :] = base_visc + above_y[x : x + 1]
        put(ez_s, 2 * x, base_visc + ahead[x * 8 : x * 8 + 8])
        put(ez_s, 2 * x + 1, base_visc + behind[x * 8 : x * 8 + 8])

    def plane_of(c, x):
        if x < 0:
            return vx_s[c, x + 2]
        if x > 15:
            return vx_s[c, x - 14]
        return vel[c, x]

    for x in range(16):
        vat = (x + 1) * 32
        visc = visc_s[vat + 8 : vat + 24, :]
        faces = (
            (visc_s[vat + 40 : vat + 56, :], visc_s[vat - 24 : vat - 8, :]),
            (visc_s[vat + 9 : vat + 25, :], visc_s[vat + 7 : vat + 23, :]),
            (
                ez_s[(x // 2 * 2) * 32 + 8 : (x // 2 * 2) * 32 + 24, :],
                ez_s[(x // 2 * 2 + 1) * 32 + 8 : (x // 2 * 2 + 1) * 32 + 24, :],
            ),
        )
        faces = [(0.5 * (visc + a), 0.5 * (visc + b)) for a, b in faces]
        wind = [vel[a, x] for a in range(3)]
        for c in range(3):
            u = vel[c, x]
            at = (c * 16 + x) * 32
            zat = (c * 16 + x) * 16
            zc = zcols[zat : zat + 16]
            p1 = jnp.where(lane == 127, zc[:, 0:1], pltpu.roll(u, 127, 1))
            p2 = jnp.where(lane == 127, zc[:, 1:2], jnp.where(lane == 126, zc[:, 0:1], pltpu.roll(u, 126, 1)))
            m1 = jnp.where(lane == 0, zc[:, 3:4], pltpu.roll(u, 1, 1))
            m2 = jnp.where(lane == 0, zc[:, 2:3], jnp.where(lane == 1, zc[:, 3:4], pltpu.roll(u, 2, 1)))
            near = (
                (plane_of(c, x + 1), plane_of(c, x - 1), plane_of(c, x + 2), plane_of(c, x - 2)),
                (
                    vy_s[at + 9 : at + 25, :], vy_s[at + 7 : at + 23, :],
                    vy_s[at + 10 : at + 26, :], vy_s[at + 6 : at + 22, :],
                ),
                (p1, m1, p2, m2),
            )
            advect = None
            diffuse = None
            for a in range(3):
                q1, b1, q2, b2 = near[a]
                slope = (8.0 * (q1 - b1) - (q2 - b2)) * (1.0 / 12.0)
                term = wind[a] * slope
                advect = term if advect is None else advect + term
                flux = faces[a][0] * (q1 - u) - faces[a][1] * (u - b1)
                diffuse = flux if diffuse is None else diffuse + flux
            out[c, x] = u + time_step * (diffuse - advect)


def run_flow(velocity, eddy, *got):
    return pl.pallas_call(
        flow_kernel,
        out_shape=jax.ShapeDtypeStruct(velocity.shape, F32),
        in_specs=[vmem_spec()] * 7,
        out_specs=vmem_spec(),
        scratch_shapes=[
            pltpu.VMEM((104, 128), F32),
            pltpu.VMEM((104, 128), F32),
            pltpu.VMEM((104, 128), F32),
            pltpu.VMEM((104, 128), F32),
            pltpu.VMEM((104, 128), F32),
            pltpu.VMEM((3, 4, 16, 128), F32),
            pltpu.VMEM((3 * 16 * 32, 128), F32),
            pltpu.VMEM((18 * 32, 128), F32),
            pltpu.VMEM((16 * 32, 128), F32),
        ],
        compiler_params=pltpu.CompilerParams(vmem_limit_bytes=32 * 1024 * 1024),
        name="flow",
    )(velocity, eddy, *got)


def finish_kernel(own, blk, mine, other, loss_out, first_out, hidden_out, last_out):
    gx_at, gy_at = lax.axis_index("gx"), lax.axis_index("gy")
    n_z = lax.axis_size("role")
    in_group = gy_at * n_z + lax.axis_index("role")
    second = core_half(gy_at) == 1
    for t in range(HIDDEN_TILES):
        one, two = mine[t * 32 : (t + 1) * 32, :], other[t * 32 : (t + 1) * 32, :]
        top, bottom = jnp.where(second, two, one), jnp.where(second, one, two)
        width = min(128, 27 * CH - t * 128)
        hidden_out[0:32, t * 128 : t * 128 + width] = top[:, :width]
        hidden_out[32:64, t * 128 : t * 128 + width] = bottom[:, :width]
    extra = mine[HIDDEN_TILES * 32 :, :] + other[HIDDEN_TILES * 32 :, :]
    first_out[...] = extra[:, 0:81]
    turned = jnp.transpose(jnp.concatenate([extra, jnp.zeros((64, 128), F32)], axis=0))
    last_out[...] = turned[LAST_COL : LAST_COL + 1, 0:64]
    slots = loss_out.shape[1]
    dev = own[...] * (lax.axis_size("gy") * n_z) + in_group
    listed = dev.shape[1]
    pick = onehot(iota((64, listed), 0) == dev & 63, F32)
    rows = nn(turned[:, 0:64], pick, HIGH)
    rows = jnp.where(iota((128, listed), 0) == LOSS_COL + BLK * (dev >> 6) + blk[...], rows, 0.0)
    found = jnp.sum(rows, axis=0, keepdims=True)
    picked = jnp.zeros((1, slots), F32)
    for g in range(listed // slots):
        picked = jnp.where(gx_at == g, found[:, g * slots : (g + 1) * slots], picked)
    loss_out[...] = picked


def run_finish(own, blk, mine, other, slots):
    f = lambda *s: jax.ShapeDtypeStruct(s, F32)
    return pl.pallas_call(
        finish_kernel,
        out_shape=(f(1, slots), f(64, 81), f(64, 27 * CH), f(1, 64)),
        in_specs=[vmem_spec()] * 4,
        out_specs=tuple(vmem_spec() for _ in range(4)),
        compiler_params=pltpu.CompilerParams(vmem_limit_bytes=32 * 1024 * 1024),
        name="finish",
    )(own, blk, mine, other)


def on_device(velocity, target_visc, w_first, w_hidden, w_last, sample_owner, sample_block):
    n_x, n_y, n_z = lax.axis_size("gx"), lax.axis_size("gy"), lax.axis_size("role")
    trainers = n_x * n_y * n_z
    own = sample_owner.reshape(1, -1)
    blk = sample_block.reshape(1, -1)
    slots = own.shape[1] // n_x

    axes = ("gx", "gy", "role")

    def even_odd(i, count):
        return i ^ 1

    def odd_even(i, count):
        return (i - 1) % count if i % 2 == 0 else (i + 1) % count

    def partner(kind, i, j, r):
        if kind == "x":
            j = odd_even(j, n_y)
        elif kind == "y":
            r = r ^ 1
        elif kind == "z_a":
            i = even_odd(i, n_x)
        else:
            i = odd_even(i, n_x)
        return (i * n_y + j) * n_z + r

    def mixed(kinds):
        pairs = []
        for i in range(n_x):
            for j in range(n_y):
                for r in range(n_z):
                    pairs.append(((i * n_y + j) * n_z + r, partner(kinds[(j ^ (j >> 1)) & 1], i, j, r)))
        return pairs

    core_pairs = [(j, even_odd(j, n_y)) for j in range(n_y)]
    size = TILES * 32

    keep, send, eddy, *kept = run_forward(
        velocity, target_visc, w_first, w_hidden, w_last.reshape(1, CH), own, blk
    )
    half = core_half(lax.axis_index("gy"))
    got = lax.ppermute(send, "gy", core_pairs)
    extra, near, *halos = run_backward(velocity, own, blk, eddy, *kept)
    total = jnp.concatenate([keep + got, extra], axis=0)
    rims = [lax.ppermute(near, "gy", core_pairs)]
    halos = [h.astype(F16) for h in halos]

    def widen(values, exps):
        wide = values.astype(F32).reshape(TILES, 32, 128) * jnp.exp2(exps)[:, None, :]
        return wide.reshape(size, 128)

    top = jnp.max(jnp.abs(total.reshape(TILES, 32, 128)), axis=1)
    exps = jnp.clip(jnp.ceil(jnp.log2(jnp.maximum(top, 1e-30))) - 13.0, -110.0, 110.0)
    orders = (("x", "y", "z_a", "z_b"), ("z_a", "x", "z_b", "y"))
    for s in range(4):
        kinds = (orders[0][s], orders[1][s])
        scaled = total.reshape(TILES, 32, 128) * jnp.exp2(-exps)[:, None, :]
        pieces = [scaled.reshape(size, 128).astype(F16), exps.astype(F16)]
        message = jnp.concatenate(pieces + [halos[s]] if s < 3 else pieces, axis=0)
        message = lax.optimization_barrier(message)
        if s == 1:
            lone = lax.optimization_barrier((rims[-1], halos[3]))[1]
        got = lax.ppermute(message, axes, mixed(kinds))
        if s == 1:
            far = lax.ppermute(lone, axes, mixed((orders[0][3], orders[1][3])))
        their_exps = got[size : size + TILES].astype(F32)
        mine, theirs = widen(message[:size], exps), widen(got[:size], their_exps)
        if n_x != 4 and "z_b" in kinds:
            theirs = jnp.where(half == kinds.index("z_b"), 0.0, theirs)
        total = mine + theirs
        exps = jnp.maximum(exps, their_exps) + 1.0
        if s < 3:
            rims.append(got[size + 16 :].astype(F32))
        if s == 1:
            total, far = lax.optimization_barrier((total, far))
        if s == 2:
            u_next = run_flow(velocity, eddy, *rims, far.astype(F32))
    total, u_next = lax.optimization_barrier((total, u_next))
    if n_x != 4:
        for bit in range(1, n_x.bit_length() - 1):
            total = total + lax.ppermute(total, "gx", [(i, i ^ (1 << bit)) for i in range(n_x)])
    other = lax.ppermute(total, "gy", core_pairs)

    losses, first, hidden, last = run_finish(own, blk, total, other, slots)
    return (u_next, losses.reshape(1, 1, slots), first, hidden, last.reshape(CH))


def solution(mesh):
    return jax.shard_map(
        on_device,
        mesh=mesh,
        in_specs=(
            P(None, "gx", "gy", "role"),
            P("gx", "gy", "role"),
            P(),
            P(),
            P(),
            P("gy", "role", None, None),
            P("gy", "role", None, None),
        ),
        out_specs=(P(None, "gx", "gy", "role"), P("gy", "role", "gx"), P(), P(), P()),
        check_vma=False,
    )
```

```python
import jax
import jax.numpy as jnp
from jax import lax
from jax.experimental import pallas as pl
from jax.experimental.pallas import tpu as pltpu
from jax.sharding import PartitionSpec as P

F32 = jnp.float32
BF16 = jnp.bfloat16
HIGH = lax.Precision.HIGHEST

SIDE = 8
CELLS = SIDE**3
CH = 64
BLK = 8
ROWS = SIDE * SIDE * BLK
WIDE = SIDE * CH
SLAB = SIDE * BLK
HIDDEN_TILES = 14
TILES = 16
LAST_COL = 81
LOSS_COL = 82

EDDY_SCALE = 2.0**-9
F16 = jnp.float16

base_visc = 0.02
time_step = 0.2


def iota(shape, dim):
    return lax.broadcasted_iota(jnp.int32, shape, dim)


def onehot(cond, dtype=BF16):
    return jnp.where(cond, 1.0, 0.0).astype(dtype)


def sigmoid(v):
    return 0.5 + 0.5 * jnp.tanh(0.5 * v)


def nt(a, b, precision=None):
    return lax.dot_general(a, b, (((1,), (1,)), ((), ())), preferred_element_type=F32, precision=precision)


def tn(a, b, precision=None):
    return lax.dot_general(a, b, (((0,), (0,)), ((), ())), preferred_element_type=F32, precision=precision)


def nn(a, b, precision=None):
    return lax.dot_general(a, b, (((1,), (0,)), ((), ())), preferred_element_type=F32, precision=precision)


def core_half(at):
    return (at ^ (at >> 1)) & 1


def place():
    gx_at, gy_at = lax.axis_index("gx"), lax.axis_index("gy")
    return gx_at, gy_at, core_half(gy_at) == 1


def times_sampled(own, blk, gx_at):
    code = own[...] * BLK + blk[...]
    wanted = gx_at * BLK + iota((BLK, code.shape[1]), 0)
    return jnp.sum(jnp.where(code == wanted, 1.0, 0.0), axis=1, keepdims=True)


def diagonal():
    return iota((1, WIDE), 1) >> 6 == iota((SIDE, 1), 0)


def windows(ref, q):
    return jnp.concatenate(
        [
            ref[dx * SLAB : dx * SLAB + ROWS, j * 512 + q * 128 : j * 512 + q * 128 + 384]
            for dx in range(3)
            for j in range(3)
        ],
        axis=1,
    )


def shifted_store(dst_ref, x, val):
    zero = jnp.zeros((1, BLK, WIDE), F32)
    lo, hi = (x + 1) * SLAB, (x + 2) * SLAB
    dst_ref[lo:hi, 0:512] = jnp.concatenate([zero, val[:-1]], axis=0).reshape(SLAB, WIDE).astype(BF16)
    dst_ref[lo:hi, 512:1024] = val.reshape(SLAB, WIDE).astype(BF16)
    dst_ref[lo:hi, 1024:1536] = jnp.concatenate([val[1:], zero], axis=0).reshape(SLAB, WIDE).astype(BF16)


def clear_ends(ref):
    ref[0:SLAB, :] = jnp.zeros((SLAB, 1536), BF16)
    ref[9 * SLAB :, :] = jnp.zeros((SLAB, 1536), BF16)


def forward_kernel(
    vel_in, tgt_in, w1_in, w2_in, w3_in, own_in, blk_in,
    keep, send, eddy_out, loss_out, dl_out, ah_s, slope1_s, i1_s, dh_s, tb_s, vel, own, blk,
    pool_s, fp_s, a_s, tt_s, pre_s, slope2_s, dw_s, big_s, gh_s, w2_s,
    tgt, w1, w2, w3, sems,
):
    pairs = ((w2_in, w2), (vel_in, vel), (tgt_in, tgt), (w1_in, w1), (w3_in, w3), (own_in, own), (blk_in, blk))
    copies = [pltpu.make_async_copy(src, dst, sems.at[n]) for n, (src, dst) in enumerate(pairs)]
    for copy in copies:
        copy.start()
    copies[0].wait()

    gx_at, gy_at, second = place()
    trainers = lax.axis_size("gx") * lax.axis_size("gy") * lax.axis_size("role")

    src = iota((320, 1), 0) - 64
    dst = iota((1, 512), 1)
    wanted = ((dst >> 7) - 2 + ((dst & 127) >> 6)) * 64 + (dst & 63)
    chooser = onehot(jnp.where((src >= 0) & (src < 192), src - 64, -999) == wanted)
    zero_tile = jnp.zeros((64, 128), BF16)
    left = iota((64, 128), 1) < 64
    w2_s[:, 1664:1792] = jnp.zeros((64, 128), F32)
    w2_s[:, 0:1728] = w2[...].astype(F32)
    w2t = jnp.concatenate(
        [
            jnp.transpose(jnp.concatenate([w2_s[:, t * 128 : (t + 1) * 128]] * 2, axis=0))
            for t in range(14)
        ],
        axis=0,
    )
    for k in range(9):
        base = (192 * k) // 128 * 128
        off = 192 * k - base
        width = min(256, 1728 - base)
        tiles = nn(w2[:, base : base + width], chooser[64 - off : 64 - off + width]).astype(BF16)
        kb = 8 - k
        turned = {dz: w2t[(3 * k + dz + 1) * 64 : (3 * k + dz + 2) * 64] for dz in (-1, 0, 1)}
        turned[-2] = turned[2] = jnp.zeros((64, 128), F32)
        forward = {d: jnp.where(left, turned[d], turned[d - 1]).astype(BF16) for d in (-1, 0, 1, 2)}
        for q in range(2):
            for w in range(6):
                z = 2 * q + w
                for h in range(2):
                    m = 2 * q + h
                    at, cols = k * 384 + w * 64, slice(h * 128, (h + 1) * 128)
                    tt_s[q, at : at + 64, cols] = forward.get(z - 2 * m, zero_tile)
                    d = 2 * m - z
                    tile = tiles[:, (d + 2) * 128 : (d + 3) * 128] if -2 <= d <= 1 else zero_tile
                    at = kb * 384 + w * 64
                    tb_s[q, at : at + 64, cols] = tile

    for copy in copies[1:]:
        copy.wait()

    for c in range(3):
        for x in range(SIDE):
            both = vel[c, 2 * x] + vel[c, 2 * x + 1]
            pool_s[c, x] = both
    rows = []
    for c in range(3):
        cols = []
        for x in range(SIDE):
            cols.append(pool_s[c, x, pl.ds(0, 8, stride=2), :] + pool_s[c, x, pl.ds(1, 8, stride=2), :])
        rows.append(jnp.concatenate(cols, axis=0))
    pooled = jnp.concatenate(rows, axis=0)
    zpool = jnp.where(iota((128, 1), 0) >> 1 == iota((1, 64), 1), 0.125, 0.0)
    filt = nn(pooled, zpool, HIGH).astype(BF16)
    tgt_rows = tgt[...].reshape(64, 64)
    zsel = jnp.concatenate([filt[0:64], filt[64:128], filt[128:192], tgt_rows], axis=1)
    spread = onehot(iota((ROWS, 1), 0) >> 3 == iota((1, 64), 1))
    by_block = nn(spread, zsel)
    mine = (iota((1, 256), 1) & 63) >> 3 == iota((ROWS, 1), 0) & 7
    by_block = jnp.where(mine, by_block, 0.0).astype(BF16)
    lane_in = iota((1, 256), 1)
    lane_off = lax.div(lane_in, 24)
    lane_cz = lane_in - lane_off * 24
    src = iota((256, 1), 0)
    pick = onehot(jnp.where(lane_in < 216, lane_cz, -1) == (src >> 6) * 8 + (src & 7))
    cells = nn(by_block, pick)
    pick_t = onehot(jnp.where(src >= 192, src & 7, -1) == iota((1, SIDE), 1))
    target = nn(by_block, pick_t)

    fp_s[...] = jnp.zeros(fp_s.shape, F32)
    fp_s[1:9, 1:9] = cells.reshape(SIDE, SIDE, BLK, 256)
    group = lax.div(iota((1, 1, 1, 256), 3), 24)
    for x in range(SIDE):
        acc = jnp.zeros((1, SIDE, BLK, 256), F32)
        for k in range(9):
            part = fp_s[x + k // 3 : x + k // 3 + 1, k % 3 : k % 3 + SIDE]
            acc = jnp.where(group == k, part, acc)
        i1_s[x * SLAB : (x + 1) * SLAB, :] = acc.reshape(SLAB, 256).astype(BF16)

    j_at = iota((81, 1), 0)
    j_off, j_dz, j_c = lax.div(j_at, 9), lax.rem(lax.div(j_at, 3), 3) - 1, lax.rem(j_at, 3)
    lane_key = jnp.where(lane_in < 216, lane_off * 4 + (lane_cz >> 3), -1)
    same = lane_key == j_off * 4 + j_c
    delta = jnp.where(same, (lane_in & 7) - j_dz, -9)
    w1v = w1[...]
    t1 = jnp.concatenate([nn(w1v, onehot(delta == z)).astype(BF16) for z in range(SIDE)], axis=0)
    pre_s[...] = nt(i1_s[...], t1)

    clear_ends(a_s)

    for x in range(SIDE):
        pre = pre_s[x * SLAB : (x + 1) * SLAB, :]
        sig = sigmoid(pre)
        slope1_s[x * SLAB : (x + 1) * SLAB, :] = sig * (1.0 + pre * (1.0 - sig))
        shifted_store(a_s, x, (pre * sig).reshape(SIDE, BLK, WIDE))

    for q in range(2):
        pre_s[:, q * 256 : (q + 1) * 256] = nn(windows(a_s, q), tt_s[q])
    for x in range(SIDE):
        pre = pre_s[x * SLAB : (x + 1) * SLAB, :]
        sig = sigmoid(pre)
        slope2_s[x * SLAB : (x + 1) * SLAB, :] = sig * (1.0 + pre * (1.0 - sig))
        ah_s[x * SLAB : (x + 1) * SLAB, :] = (pre * sig).astype(BF16)

    tile8 = onehot(iota((64, 1), 0) == iota((1, WIDE), 1) & 63)
    w3_wide = nn(w3[...], tile8)
    diag = diagonal()
    last = jnp.where(diag, w3_wide, 0.0).astype(BF16)
    logits = nt(ah_s[...], last)
    eddy = 0.5 * (jnp.maximum(logits, 0.0) + jnp.log1p(jnp.exp(-jnp.abs(logits))))
    error = eddy - target
    losses = jnp.sum(jnp.sum((error * error).reshape(64, BLK, SIDE), axis=0), axis=1, keepdims=True) / CELLS
    d_logit = (error * sigmoid(logits) / (trainers * CELLS)).astype(BF16)

    zrep = onehot(iota((SIDE, 1), 0) == (iota((1, 128), 1) & 15) >> 1, F32)
    fine = nn(eddy, zrep, HIGH)
    fine = jnp.where(iota((1, 128), 1) >> 4 == iota((ROWS, 1), 0) & 7, fine, 0.0)
    fine = jnp.sum(fine.reshape(64, BLK, 128), axis=1)
    eddy_out[...] = fine
    loss_out[...] = jnp.broadcast_to(losses, (BLK, 128))
    dl_out[...] = d_logit.astype(F32)

    count = times_sampled(own, blk, gx_at)
    big_s[:, 0:512] = nn(d_logit, last)
    for x in range(SIDE):
        d_hid = big_s[x * SLAB : (x + 1) * SLAB, 0:512] * slope2_s[x * SLAB : (x + 1) * SLAB, :]
        d_hid = d_hid.astype(BF16)
        dh_s[x * SLAB : (x + 1) * SLAB, :] = d_hid
        d_hid = d_hid.astype(F32).reshape(SIDE, BLK, WIDE)
        dw_s[x * SLAB : (x + 1) * SLAB, :] = (d_hid * count[None]).reshape(SLAB, WIDE).astype(BF16)
    dwt = jnp.transpose(dw_s[...])

    sums = {}
    for p in range(4):
        first, last_z = max(2 * p - 1, 0), min(2 * p + 2, SIDE - 1)
        shifts = [
            a_s[dx * SLAB : dx * SLAB + ROWS, j * 512 + p * 128 : j * 512 + (p + 1) * 128]
            for dx in range(3)
            for j in range(3)
        ]
        found = nn(dwt[first * 64 : (last_z + 1) * 64], jnp.concatenate(shifts, axis=1))
        for z in range(first, last_z + 1):
            part = found[(z - first) * 64 : (z - first + 1) * 64]
            m = z - 2 * p
            sums[m] = part if m not in sums else sums[m] + part
    low_half = iota((64, 128), 1) < 64
    held = None
    for k in range(9):
        for dz in (-1, 0, 1):
            low, high = (sums[m][:, k * 128 : (k + 1) * 128] for m in (-dz, 1 - dz))
            at = (k * 3 + dz + 1) * 64
            if at % 128:
                gh_s[:, at - 64 : at + 64] = jnp.where(low_half, held, high + pltpu.roll(low, 64, 1))
            else:
                held = low + pltpu.roll(high, 64, 1)
    gh_s[:, 1664:1792] = jnp.where(low_half, held, 0.0)

    for t in range(HIDDEN_TILES):
        top, bottom = (gh_s[r : r + 32, t * 128 : (t + 1) * 128] for r in (0, 32))
        keep[t * 32 : (t + 1) * 32, :] = jnp.where(second, bottom, top)
        send[t * 32 : (t + 1) * 32, :] = jnp.where(second, top, bottom)


def backward_kernel(
    vel, own, blk, eddy, losses, dl_in, ah_s, slope1_s, i1_s, dh_s, tb_s,
    extra_out, hy_a, halo1, halo2, halo3, halo4, hx_a, hx_b, hy_b, hz, d_s, pre_s, dw_s,
):
    gx_at, gy_at, second = place()
    gx_odd, gy_odd = gx_at & 1 == 1, gy_at & 1 == 1
    dev = (gx_at * lax.axis_size("gy") + gy_at) * lax.axis_size("role") + lax.axis_index("role")
    count = times_sampled(own, blk, gx_at)

    clear_ends(d_s)
    for x in range(SIDE):
        d_hid = dh_s[x * SLAB : (x + 1) * SLAB, :].astype(F32)
        shifted_store(d_s, x, d_hid.reshape(SIDE, BLK, WIDE))

    for c in range(3):
        for i in range(2):
            lo, hi = vel[c, i], vel[c, 14 + i]
            at = (c * 2 + i) * 16
            hx_a[at : at + 16, :] = jnp.where(gx_odd, lo, hi)
            hx_b[at : at + 16, :] = jnp.where(gx_odd, hi, lo)
    fine = eddy[...]
    small = fine * EDDY_SCALE
    hx_a[96:104, :] = jnp.where(gx_odd, small[0:8], small[56:64])
    hx_b[96:104, :] = jnp.where(gx_odd, small[56:64], small[0:8])
    for c in range(3):
        for i in range(2):
            lo = jnp.concatenate([vel[c, x, i : i + 1, :] for x in range(16)], axis=0)
            hi = jnp.concatenate([vel[c, x, 14 + i : 15 + i, :] for x in range(16)], axis=0)
            at = (c * 2 + i) * 16
            hy_a[at : at + 16, :] = jnp.where(gy_odd, lo, hi)
            hy_b[at : at + 16, :] = jnp.where(gy_odd, hi, lo)
    lo = eddy[pl.ds(0, 8, stride=8), :] * EDDY_SCALE
    hi = eddy[pl.ds(7, 8, stride=8), :] * EDDY_SCALE
    hy_a[96:104, :] = jnp.where(gy_odd, lo, hi)
    hy_b[96:104, :] = jnp.where(gy_odd, hi, lo)
    vt = jnp.transpose(vel[...].reshape(768, 128))
    et = jnp.transpose(jnp.concatenate([small, jnp.zeros((64, 128), F32)], axis=0))
    hz[...] = jnp.zeros(hz.shape, F32)
    for t in range(6):
        hz[t * 8 : t * 8 + 2, :] = vt[0:2, t * 128 : (t + 1) * 128]
        hz[t * 8 + 2 : t * 8 + 4, :] = vt[126:128, t * 128 : (t + 1) * 128]
    hz[48:49, :] = et[0:1]
    hz[49:50, :] = et[127:128]
    halo1[...] = jnp.where(second, hx_a[...], hy_b[...])
    halo2[...] = jnp.where(second, hy_b[...], hx_a[...])
    halo3[...] = jnp.where(second, hx_b[...], hz[...])
    halo4[...] = jnp.where(second, hz[...], hx_b[...])

    for q in range(2):
        pre_s[:, q * 256 : (q + 1) * 256] = nn(windows(d_s, q), tb_s[q])
    for x in range(SIDE):
        rows = slice(x * SLAB, (x + 1) * SLAB)
        d_first = (pre_s[rows, :] * slope1_s[rows, :]).astype(BF16).astype(F32)
        dw_s[rows, :] = (d_first.reshape(SIDE, BLK, WIDE) * count[None]).reshape(SLAB, WIDE).astype(BF16)
    g1 = nn(jnp.transpose(dw_s[...]), i1_s[...])
    z_in = iota((1, 256), 1) & 7
    parts = []
    for dz in (-1, 0, 1):
        tot = jnp.zeros((64, 256), F32)
        for z in range(SIDE):
            if 0 <= z + dz < SIDE:
                tot = tot + jnp.where(z_in == z + dz, g1[z * 64 : (z + 1) * 64], 0.0)
        parts.append(tot)
    r_at = iota((768, 1), 0)
    c_at = iota((1, 128), 1)
    r_lane = r_at & 255
    r_off = lax.div(r_lane, 24)
    r_col = (r_off * 3 + (r_at >> 8)) * 3 + ((r_lane - r_off * 24) >> 3)
    fold = onehot(jnp.where(r_lane < 216, r_col, -1) == c_at, F32)
    g_first = nn(jnp.concatenate(parts, axis=1), fold, HIGH)

    count_rows = jnp.broadcast_to(count.reshape(1, BLK, 1), (64, BLK, 1)).reshape(ROWS, 1)
    dlw = dl_in[...] * count_rows
    dl_hi = dlw.astype(BF16)
    dl_lo = (dlw - dl_hi.astype(F32)).astype(BF16)
    ah = ah_s[...]
    gl = tn(dl_hi, ah) + tn(dl_lo, ah)
    gl = jnp.where(diagonal(), gl, 0.0)
    fold_o = onehot(iota((1, WIDE), 1) & 63 == iota((64, 1), 0), F32)
    g_last = jnp.sum(nt(fold_o, gl, HIGH), axis=1, keepdims=True)

    lane8 = iota((BLK, 128), 1)
    loss_row = jnp.where(lane8 - (LOSS_COL + BLK * (dev >> 6)) == iota((BLK, 128), 0), losses[...], 0.0)
    loss_row = jnp.sum(loss_row, axis=0, keepdims=True)
    lane = iota((64, 128), 1)
    extra = jnp.where(lane == LAST_COL, g_last, g_first)
    extra = extra + jnp.where(iota((64, 128), 0) == dev & 63, loss_row, 0.0)

    extra_out[...] = extra


def vmem_spec():
    return pl.BlockSpec(memory_space=pltpu.VMEM)


def run_forward(*given):
    velocity, target, w1, w2, w3, own, blk = (pltpu.with_memory_space_constraint(a, pltpu.HBM) for a in given)
    half = pltpu.VMEM((HIDDEN_TILES * 32, 128), F32)
    return pl.pallas_call(
        forward_kernel,
        out_shape=(
            half,
            half,
            pltpu.VMEM((64, 128), F32),
            pltpu.VMEM((BLK, 128), F32),
            pltpu.VMEM((ROWS, SIDE), F32),
            pltpu.VMEM((ROWS, WIDE), BF16),
            pltpu.VMEM((ROWS, WIDE), F32),
            pltpu.VMEM((ROWS, 256), BF16),
            pltpu.VMEM((ROWS, WIDE), BF16),
            pltpu.VMEM((2, 3456, 256), BF16),
        )
        + tuple(pltpu.VMEM(a.shape, a.dtype) for a in (velocity, own, blk)),
        in_specs=[pl.BlockSpec(memory_space=pltpu.HBM)] * 7,
        out_specs=tuple(vmem_spec() for _ in range(13)),
        scratch_shapes=[
            pltpu.VMEM((3, SIDE, 16, 128), F32),
            pltpu.VMEM((10, 10, BLK, 256), F32),
            pltpu.VMEM((ROWS + 2 * SLAB, 1536), BF16),
            pltpu.VMEM((2, 3456, 256), BF16),
            pltpu.VMEM((ROWS, WIDE), F32),
            pltpu.VMEM((ROWS, WIDE), F32),
            pltpu.VMEM((ROWS, WIDE), BF16),
            pltpu.VMEM((ROWS, WIDE), F32),
            pltpu.VMEM((64, HIDDEN_TILES * 128), F32),
            pltpu.VMEM((64, 1792), F32),
        ]
        + [pltpu.VMEM(a.shape, a.dtype) for a in (target, w1, w2, w3)]
        + [pltpu.SemaphoreType.DMA((7,))],
        compiler_params=pltpu.CompilerParams(vmem_limit_bytes=40 * 1024 * 1024),
        name="forward",
    )(velocity, target, w1, w2, w3, own, blk)


def run_backward(velocity, own, blk, *kept):
    face = pltpu.VMEM((104, 128), F32)
    return pl.pallas_call(
        backward_kernel,
        out_shape=(pltpu.VMEM((64, 128), F32),) + (face,) * 5,
        in_specs=[vmem_spec()] * 11,
        out_specs=tuple(vmem_spec() for _ in range(6)),
        scratch_shapes=[face] * 4
        + [
            pltpu.VMEM((ROWS + 2 * SLAB, 1536), BF16),
            pltpu.VMEM((ROWS, WIDE), F32),
            pltpu.VMEM((ROWS, WIDE), BF16),
        ],
        compiler_params=pltpu.CompilerParams(vmem_limit_bytes=40 * 1024 * 1024),
        name="backward",
    )(velocity, own, blk, *kept)


def flow_kernel(
    vel, eddy, got0, got1, got2, got3, got4, out, rx_a, rx_b, ry_a, ry_b, rz, vx_s, vy_s, visc_s, ez_s
):
    gx_at, gy_at = lax.axis_index("gx"), lax.axis_index("gy")
    gx_odd, gy_odd = gx_at & 1 == 1, gy_at & 1 == 1
    second = core_half(gy_at) == 1
    ry_a[...] = got0[...]
    ry_b[...] = jnp.where(second, got2[...], got1[...])
    rx_a[...] = jnp.where(second, got1[...], got2[...])
    rx_b[...] = jnp.where(second, got3[...], got4[...])
    rz[...] = jnp.where(second, got4[...], got3[...])
    lane = iota((1, 128), 1)

    def sides(odd, a, b, at, rows):
        one, two = a[at : at + rows, :], b[at : at + rows, :]
        return jnp.where(odd, one, two), jnp.where(odd, two, one)

    for c in range(3):
        for x in range(16):
            vy_s[(c * 16 + x) * 32 + 8 : (c * 16 + x) * 32 + 24, :] = vel[c, x]
        for i in range(2):
            below, above = sides(gy_odd, ry_a, ry_b, (c * 2 + i) * 16, 16)
            vy_s[pl.ds(c * 512 + 6 + i, 16, stride=32), :] = below
            vy_s[pl.ds(c * 512 + 24 + i, 16, stride=32), :] = above
            below, above = sides(gx_odd, rx_a, rx_b, (c * 2 + i) * 16, 16)
            vx_s[c, i] = below
            vx_s[c, 2 + i] = above

    zcols = jnp.concatenate([jnp.transpose(rz[t * 8 : t * 8 + 8, :]) for t in range(7)], axis=0)
    coarse = eddy[...]
    e_first, e_last = zcols[768:832, 0:1] / EDDY_SCALE, zcols[768:832, 1:2] / EDDY_SCALE
    ahead = jnp.where(lane == 127, e_first, pltpu.roll(coarse, 127, 1))
    behind = jnp.where(lane == 0, e_last, pltpu.roll(coarse, 1, 1))
    below_x, above_x = (v / EDDY_SCALE for v in sides(gx_odd, rx_a, rx_b, 96, 8))
    below_y, above_y = (v / EDDY_SCALE for v in sides(gy_odd, ry_a, ry_b, 96, 8))

    def put(dst, plane, val):
        dst[pl.ds(plane * 32 + 8, 8, stride=2), :] = val
        dst[pl.ds(plane * 32 + 9, 8, stride=2), :] = val

    put(visc_s, 0, base_visc + below_x)
    put(visc_s, 17, base_visc + above_x)
    for x in range(8):
        for r in range(2):
            plane = 2 * x + 1 + r
            put(visc_s, plane, base_visc + coarse[x * 8 : x * 8 + 8])
            visc_s[plane * 32 + 7 : plane * 32 + 8, :] = base_visc + below_y[x : x + 1]
            visc_s[plane * 32 + 24 : plane * 32 + 25, :] = base_visc + above_y[x : x + 1]
        put(ez_s, 2 * x, base_visc + ahead[x * 8 : x * 8 + 8])
        put(ez_s, 2 * x + 1, base_visc + behind[x * 8 : x * 8 + 8])

    def plane_of(c, x):
        if x < 0:
            return vx_s[c, x + 2]
        if x > 15:
            return vx_s[c, x - 14]
        return vel[c, x]

    for x in range(16):
        vat = (x + 1) * 32
        visc = visc_s[vat + 8 : vat + 24, :]
        faces = (
            (visc_s[vat + 40 : vat + 56, :], visc_s[vat - 24 : vat - 8, :]),
            (visc_s[vat + 9 : vat + 25, :], visc_s[vat + 7 : vat + 23, :]),
            (
                ez_s[(x // 2 * 2) * 32 + 8 : (x // 2 * 2) * 32 + 24, :],
                ez_s[(x // 2 * 2 + 1) * 32 + 8 : (x // 2 * 2 + 1) * 32 + 24, :],
            ),
        )
        faces = [(0.5 * (visc + a), 0.5 * (visc + b)) for a, b in faces]
        wind = [vel[a, x] for a in range(3)]
        for c in range(3):
            u = vel[c, x]
            at = (c * 16 + x) * 32
            zat = (c * 16 + x) * 16
            zc = zcols[zat : zat + 16]
            p1 = jnp.where(lane == 127, zc[:, 0:1], pltpu.roll(u, 127, 1))
            p2 = jnp.where(lane == 127, zc[:, 1:2], jnp.where(lane == 126, zc[:, 0:1], pltpu.roll(u, 126, 1)))
            m1 = jnp.where(lane == 0, zc[:, 3:4], pltpu.roll(u, 1, 1))
            m2 = jnp.where(lane == 0, zc[:, 2:3], jnp.where(lane == 1, zc[:, 3:4], pltpu.roll(u, 2, 1)))
            near = (
                (plane_of(c, x + 1), plane_of(c, x - 1), plane_of(c, x + 2), plane_of(c, x - 2)),
                (
                    vy_s[at + 9 : at + 25, :], vy_s[at + 7 : at + 23, :],
                    vy_s[at + 10 : at + 26, :], vy_s[at + 6 : at + 22, :],
                ),
                (p1, m1, p2, m2),
            )
            advect = None
            diffuse = None
            for a in range(3):
                q1, b1, q2, b2 = near[a]
                slope = (8.0 * (q1 - b1) - (q2 - b2)) * (1.0 / 12.0)
                term = wind[a] * slope
                advect = term if advect is None else advect + term
                flux = faces[a][0] * (q1 - u) - faces[a][1] * (u - b1)
                diffuse = flux if diffuse is None else diffuse + flux
            out[c, x] = u + time_step * (diffuse - advect)


def run_flow(velocity, eddy, *got):
    return pl.pallas_call(
        flow_kernel,
        out_shape=jax.ShapeDtypeStruct(velocity.shape, F32),
        in_specs=[vmem_spec()] * 7,
        out_specs=vmem_spec(),
        scratch_shapes=[
            pltpu.VMEM((104, 128), F32),
            pltpu.VMEM((104, 128), F32),
            pltpu.VMEM((104, 128), F32),
            pltpu.VMEM((104, 128), F32),
            pltpu.VMEM((104, 128), F32),
            pltpu.VMEM((3, 4, 16, 128), F32),
            pltpu.VMEM((3 * 16 * 32, 128), F32),
            pltpu.VMEM((18 * 32, 128), F32),
            pltpu.VMEM((16 * 32, 128), F32),
        ],
        compiler_params=pltpu.CompilerParams(vmem_limit_bytes=32 * 1024 * 1024),
        name="flow",
    )(velocity, eddy, *got)


def finish_kernel(own, blk, mine, other, loss_out, first_out, hidden_out, last_out):
    gx_at, gy_at = lax.axis_index("gx"), lax.axis_index("gy")
    n_z = lax.axis_size("role")
    in_group = gy_at * n_z + lax.axis_index("role")
    second = core_half(gy_at) == 1
    for t in range(HIDDEN_TILES):
        one, two = mine[t * 32 : (t + 1) * 32, :], other[t * 32 : (t + 1) * 32, :]
        top, bottom = jnp.where(second, two, one), jnp.where(second, one, two)
        width = min(128, 27 * CH - t * 128)
        hidden_out[0:32, t * 128 : t * 128 + width] = top[:, :width]
        hidden_out[32:64, t * 128 : t * 128 + width] = bottom[:, :width]
    extra = mine[HIDDEN_TILES * 32 :, :] + other[HIDDEN_TILES * 32 :, :]
    first_out[...] = extra[:, 0:81]
    turned = jnp.transpose(jnp.concatenate([extra, jnp.zeros((64, 128), F32)], axis=0))
    last_out[...] = turned[LAST_COL : LAST_COL + 1, 0:64]
    slots = loss_out.shape[1]
    dev = own[...] * (lax.axis_size("gy") * n_z) + in_group
    listed = dev.shape[1]
    pick = onehot(iota((64, listed), 0) == dev & 63, F32)
    rows = nn(turned[:, 0:64], pick, HIGH)
    rows = jnp.where(iota((128, listed), 0) == LOSS_COL + BLK * (dev >> 6) + blk[...], rows, 0.0)
    found = jnp.sum(rows, axis=0, keepdims=True)
    picked = jnp.zeros((1, slots), F32)
    for g in range(listed // slots):
        picked = jnp.where(gx_at == g, found[:, g * slots : (g + 1) * slots], picked)
    loss_out[...] = picked


def run_finish(own, blk, mine, other, slots):
    f = lambda *s: jax.ShapeDtypeStruct(s, F32)
    return pl.pallas_call(
        finish_kernel,
        out_shape=(f(1, slots), f(64, 81), f(64, 27 * CH), f(1, 64)),
        in_specs=[vmem_spec()] * 4,
        out_specs=tuple(vmem_spec() for _ in range(4)),
        compiler_params=pltpu.CompilerParams(vmem_limit_bytes=32 * 1024 * 1024),
        name="finish",
    )(own, blk, mine, other)


def on_device(velocity, target_visc, w_first, w_hidden, w_last, sample_owner, sample_block):
    n_x, n_y, n_z = lax.axis_size("gx"), lax.axis_size("gy"), lax.axis_size("role")
    trainers = n_x * n_y * n_z
    own = sample_owner.reshape(1, -1)
    blk = sample_block.reshape(1, -1)
    slots = own.shape[1] // n_x

    axes = ("gx", "gy", "role")

    def even_odd(i, count):
        return i ^ 1

    def odd_even(i, count):
        return (i - 1) % count if i % 2 == 0 else (i + 1) % count

    def partner(kind, i, j, r):
        if kind == "x":
            j = odd_even(j, n_y)
        elif kind == "y":
            r = r ^ 1
        elif kind == "z_a":
            i = even_odd(i, n_x)
        else:
            i = odd_even(i, n_x)
        return (i * n_y + j) * n_z + r

    def mixed(kinds):
        pairs = []
        for i in range(n_x):
            for j in range(n_y):
                for r in range(n_z):
                    pairs.append(((i * n_y + j) * n_z + r, partner(kinds[(j ^ (j >> 1)) & 1], i, j, r)))
        return pairs

    core_pairs = [(j, even_odd(j, n_y)) for j in range(n_y)]
    size = TILES * 32

    keep, send, eddy, *kept, velocity, own, blk = run_forward(
        velocity, target_visc, w_first, w_hidden, w_last.reshape(1, CH), own, blk
    )
    half = core_half(lax.axis_index("gy"))
    got = lax.ppermute(send, "gy", core_pairs)
    extra, near, *halos = run_backward(velocity, own, blk, eddy, *kept)
    total = jnp.concatenate([keep + got, extra], axis=0)
    rims = [lax.ppermute(near, "gy", core_pairs)]
    halos = [h.astype(F16) for h in halos]

    def widen(values, exps):
        wide = values.astype(F32).reshape(TILES, 32, 128) * jnp.exp2(exps)[:, None, :]
        return wide.reshape(size, 128)

    top = jnp.max(jnp.abs(total.reshape(TILES, 32, 128)), axis=1)
    exps = jnp.clip(jnp.ceil(jnp.log2(jnp.maximum(top, 1e-30))) - 13.0, -110.0, 110.0)
    orders = (("x", "z_a", "y", "z_b"), ("z_a", "x", "z_b", "y"))
    for s in range(4):
        kinds = (orders[0][s], orders[1][s])
        scaled = total.reshape(TILES, 32, 128) * jnp.exp2(-exps)[:, None, :]
        pieces = [scaled.reshape(size, 128).astype(F16), exps.astype(F16)]
        message = jnp.concatenate(pieces + [halos[s]] if s < 3 else pieces, axis=0)
        message = lax.optimization_barrier(message)
        got = lax.ppermute(message, axes, mixed(kinds))
        if s == 1:
            far = lax.ppermute(halos[3], axes, mixed((orders[0][3], orders[1][3])))
        their_exps = got[size : size + TILES].astype(F32)
        mine, theirs = widen(message[:size], exps), widen(got[:size], their_exps)
        if n_x != 4 and "z_b" in kinds:
            theirs = jnp.where(half == kinds.index("z_b"), 0.0, theirs)
        total = mine + theirs
        exps = jnp.maximum(exps, their_exps) + 1.0
        if s < 3:
            rims.append(got[size + 16 :].astype(F32))
        if s == 1:
            total, far = lax.optimization_barrier((total, far))
        if s == 2:
            u_next = run_flow(velocity, eddy, *rims, far.astype(F32))
    total, u_next = lax.optimization_barrier((total, u_next))
    if n_x != 4:
        for bit in range(1, n_x.bit_length() - 1):
            total = total + lax.ppermute(total, "gx", [(i, i ^ (1 << bit)) for i in range(n_x)])
    other = lax.ppermute(total, "gy", core_pairs)

    losses, first, hidden, last = run_finish(own, blk, total, other, slots)
    return (u_next, losses.reshape(1, 1, slots), first, hidden, last.reshape(CH))


def solution(mesh):
    return jax.shard_map(
        on_device,
        mesh=mesh,
        in_specs=(
            P(None, "gx", "gy", "role"),
            P("gx", "gy", "role"),
            P(),
            P(),
            P(),
            P("gy", "role", None, None),
            P("gy", "role", None, None),
        ),
        out_specs=(P(None, "gx", "gy", "role"), P("gy", "role", "gx"), P(), P(), P()),
        check_vma=False,
    )
```

```python
import jax
import jax.numpy as jnp
from jax import lax
from jax.experimental import pallas as pl
from jax.experimental.pallas import tpu as pltpu
from jax.sharding import PartitionSpec as P

F32 = jnp.float32
BF16 = jnp.bfloat16
HIGH = lax.Precision.HIGHEST

SIDE = 8
CELLS = SIDE**3
CH = 64
BLK = 8
ROWS = SIDE * SIDE * BLK
WIDE = SIDE * CH
SLAB = SIDE * BLK
HIDDEN_TILES = 14
TILES = 16
LAST_COL = 81
LOSS_COL = 82

EDDY_SCALE = 2.0**-9
F16 = jnp.float16

base_visc = 0.02
time_step = 0.2


def iota(shape, dim):
    return lax.broadcasted_iota(jnp.int32, shape, dim)


def onehot(cond, dtype=BF16):
    return jnp.where(cond, 1.0, 0.0).astype(dtype)


def sigmoid(v):
    return 0.5 + 0.5 * jnp.tanh(0.5 * v)


def nt(a, b, precision=None):
    return lax.dot_general(a, b, (((1,), (1,)), ((), ())), preferred_element_type=F32, precision=precision)


def tn(a, b, precision=None):
    return lax.dot_general(a, b, (((0,), (0,)), ((), ())), preferred_element_type=F32, precision=precision)


def nn(a, b, precision=None):
    return lax.dot_general(a, b, (((1,), (0,)), ((), ())), preferred_element_type=F32, precision=precision)


def core_half(at):
    return (at ^ (at >> 1)) & 1


def place():
    gx_at, gy_at = lax.axis_index("gx"), lax.axis_index("gy")
    return gx_at, gy_at, core_half(gy_at) == 1


def times_sampled(own, blk, gx_at):
    code = own[...] * BLK + blk[...]
    wanted = gx_at * BLK + iota((BLK, code.shape[1]), 0)
    return jnp.sum(jnp.where(code == wanted, 1.0, 0.0), axis=1, keepdims=True)


def tile_places():
    return [(q, w, h, 2 * q + w, 2 * q + h) for q in range(2) for w in range(6) for h in range(2)]


def exact(a, selector):
    high = a.astype(BF16)
    rest = a - high.astype(F32)
    mid = rest.astype(BF16)
    low = (rest - mid.astype(F32)).astype(BF16)
    return nn(high, selector) + (nn(mid, selector) + nn(low, selector))


def y_face(dst, vel, eddy, high):
    for c in range(3):
        for i in range(2):
            lo = jnp.concatenate([vel[c, x, i : i + 1, :] for x in range(16)], axis=0)
            hi = jnp.concatenate([vel[c, x, 14 + i : 15 + i, :] for x in range(16)], axis=0)
            dst[(c * 2 + i) * 16 : (c * 2 + i + 1) * 16, :] = jnp.where(high, hi, lo)
    dst[96:104, :] = jnp.where(high, eddy[pl.ds(7, 8, stride=8), :], eddy[pl.ds(0, 8, stride=8), :]) * EDDY_SCALE


def diagonal():
    return iota((1, WIDE), 1) >> 6 == iota((SIDE, 1), 0)


def windows(ref, q):
    return jnp.concatenate(
        [
            ref[dx * SLAB : dx * SLAB + ROWS, j * 512 + q * 128 : j * 512 + q * 128 + 384]
            for dx in range(3)
            for j in range(3)
        ],
        axis=1,
    )


def shifted_store(dst_ref, x, val):
    zero = jnp.zeros((1, BLK, WIDE), F32)
    lo, hi = (x + 1) * SLAB, (x + 2) * SLAB
    dst_ref[lo:hi, 0:512] = jnp.concatenate([zero, val[:-1]], axis=0).reshape(SLAB, WIDE).astype(BF16)
    dst_ref[lo:hi, 512:1024] = val.reshape(SLAB, WIDE).astype(BF16)
    dst_ref[lo:hi, 1024:1536] = jnp.concatenate([val[1:], zero], axis=0).reshape(SLAB, WIDE).astype(BF16)


def clear_ends(ref):
    ref[0:SLAB, :] = jnp.zeros((SLAB, 1536), BF16)
    ref[9 * SLAB :, :] = jnp.zeros((SLAB, 1536), BF16)


def forward_kernel(
    vel_in, tgt_in, w1_in, w2_in, w3_in, own_in, blk_in,
    keep, send, eddy_out, loss_out, dl_out, ah_s, slope1_s, i1_s, dh_s, tb_s, vel, own, blk,
    pool_s, fp_s, a_s, tt_s, pre_s, slope2_s, dw_s, big_s, gh_s, w2_s,
    tgt, w1, w2, w3, sems,
):
    pairs = ((w2_in, w2), (vel_in, vel), (tgt_in, tgt), (w1_in, w1), (w3_in, w3), (own_in, own), (blk_in, blk))
    copies = [pltpu.make_async_copy(src, dst, sems.at[n]) for n, (src, dst) in enumerate(pairs)]
    for copy in copies:
        copy.start()
    gx_at, gy_at, second = place()
    trainers = lax.axis_size("gx") * lax.axis_size("gy") * lax.axis_size("role")

    fp_s[...] = jnp.zeros(fp_s.shape, F32)
    clear_ends(a_s)
    w2_s[:, 1664:1792] = jnp.zeros((64, 128), F32)
    zero_tile = jnp.zeros((64, 128), BF16)
    for q, w, h, z, m in tile_places():
        for k in range(9):
            at, cols = k * 384 + w * 64, slice(h * 128, (h + 1) * 128)
            if not -1 <= z - 2 * m <= 2:
                tt_s[q, at : at + 64, cols] = zero_tile
                tb_s[q, at : at + 64, cols] = zero_tile
    for copy in copies:
        copy.wait()

    for c in range(3):
        for x in range(SIDE):
            both = vel[c, 2 * x] + vel[c, 2 * x + 1]
            pool_s[c, x] = both
    rows = []
    for c in range(3):
        cols = []
        for x in range(SIDE):
            cols.append(pool_s[c, x, pl.ds(0, 8, stride=2), :] + pool_s[c, x, pl.ds(1, 8, stride=2), :])
        rows.append(jnp.concatenate(cols, axis=0))
    pooled = jnp.concatenate(rows, axis=0)
    zpool = jnp.where(iota((128, 1), 0) >> 1 == iota((1, 64), 1), 0.125, 0.0).astype(BF16)
    filt = exact(pooled, zpool).astype(BF16)
    tgt_rows = tgt[...].reshape(64, 64)
    zsel = jnp.concatenate([filt[0:64], filt[64:128], filt[128:192], tgt_rows], axis=1)
    spread = onehot(iota((ROWS, 1), 0) >> 3 == iota((1, 64), 1))
    by_block = nn(spread, zsel)
    mine = (iota((1, 256), 1) & 63) >> 3 == iota((ROWS, 1), 0) & 7
    by_block = jnp.where(mine, by_block, 0.0).astype(BF16)
    lane_in = iota((1, 256), 1)
    lane_off = lax.div(lane_in, 24)
    lane_cz = lane_in - lane_off * 24
    src = iota((256, 1), 0)
    pick = onehot(jnp.where(lane_in < 216, lane_cz, -1) == (src >> 6) * 8 + (src & 7))
    cells = nn(by_block, pick)
    pick_t = onehot(jnp.where(src >= 192, src & 7, -1) == iota((1, SIDE), 1))
    target = nn(by_block, pick_t)

    fp_s[1:9, 1:9] = cells.reshape(SIDE, SIDE, BLK, 256)
    group = lax.div(iota((1, 1, 1, 256), 3), 24)
    for x in range(SIDE):
        acc = jnp.zeros((1, SIDE, BLK, 256), F32)
        for k in range(9):
            part = fp_s[x + k // 3 : x + k // 3 + 1, k % 3 : k % 3 + SIDE]
            acc = jnp.where(group == k, part, acc)
        i1_s[x * SLAB : (x + 1) * SLAB, :] = acc.reshape(SLAB, 256).astype(BF16)

    j_at = iota((81, 1), 0)
    j_off, j_dz, j_c = lax.div(j_at, 9), lax.rem(lax.div(j_at, 3), 3) - 1, lax.rem(j_at, 3)
    lane_key = jnp.where(lane_in < 216, lane_off * 4 + (lane_cz >> 3), -1)
    same = lane_key == j_off * 4 + j_c
    delta = jnp.where(same, (lane_in & 7) - j_dz, -9)
    w1v = w1[...]
    t1 = jnp.concatenate([nn(w1v, onehot(delta == z)).astype(BF16) for z in range(SIDE)], axis=0)
    pre_s[...] = nt(i1_s[...], t1)

    src = iota((320, 1), 0) - 64
    dst = iota((1, 512), 1)
    wanted = ((dst >> 7) - 2 + ((dst & 127) >> 6)) * 64 + (dst & 63)
    chooser = onehot(jnp.where((src >= 0) & (src < 192), src - 64, -999) == wanted)
    left = iota((64, 128), 1) < 64
    w2_s[:, 0:1728] = w2[...].astype(F32)
    w2t = jnp.concatenate(
        [
            jnp.transpose(jnp.concatenate([w2_s[:, t * 128 : (t + 1) * 128]] * 2, axis=0))
            for t in range(14)
        ],
        axis=0,
    )
    for k in range(9):
        base = (192 * k) // 128 * 128
        off = 192 * k - base
        width = min(256, 1728 - base)
        tiles = nn(w2[:, base : base + width], chooser[64 - off : 64 - off + width]).astype(BF16)
        kb = 8 - k
        turned = {dz: w2t[(3 * k + dz + 1) * 64 : (3 * k + dz + 2) * 64] for dz in (-1, 0, 1)}
        turned[-2] = turned[2] = jnp.zeros((64, 128), F32)
        forward = {d: jnp.where(left, turned[d], turned[d - 1]).astype(BF16) for d in (-1, 0, 1, 2)}
        for q, w, h, z, m in tile_places():
            at, cols = k * 384 + w * 64, slice(h * 128, (h + 1) * 128)
            if z - 2 * m in forward:
                tt_s[q, at : at + 64, cols] = forward[z - 2 * m]
            d = 2 * m - z
            at = kb * 384 + w * 64
            if -2 <= d <= 1:
                tb_s[q, at : at + 64, cols] = tiles[:, (d + 2) * 128 : (d + 3) * 128]

    for x in range(SIDE):
        pre = pre_s[x * SLAB : (x + 1) * SLAB, :]
        sig = sigmoid(pre)
        slope1_s[x * SLAB : (x + 1) * SLAB, :] = sig * (1.0 + pre * (1.0 - sig))
        shifted_store(a_s, x, (pre * sig).reshape(SIDE, BLK, WIDE))

    for q in range(2):
        pre_s[:, q * 256 : (q + 1) * 256] = nn(windows(a_s, q), tt_s[q])
    for x in range(SIDE):
        pre = pre_s[x * SLAB : (x + 1) * SLAB, :]
        sig = sigmoid(pre)
        slope2_s[x * SLAB : (x + 1) * SLAB, :] = sig * (1.0 + pre * (1.0 - sig))
        ah_s[x * SLAB : (x + 1) * SLAB, :] = (pre * sig).astype(BF16)

    tile8 = onehot(iota((64, 1), 0) == iota((1, WIDE), 1) & 63)
    w3_wide = nn(w3[...], tile8)
    diag = diagonal()
    last = jnp.where(diag, w3_wide, 0.0).astype(BF16)
    logits = nt(ah_s[...], last)
    eddy = 0.5 * (jnp.maximum(logits, 0.0) + jnp.log1p(jnp.exp(-jnp.abs(logits))))
    error = eddy - target
    losses = jnp.sum(jnp.sum((error * error).reshape(64, BLK, SIDE), axis=0), axis=1, keepdims=True) / CELLS
    d_logit = (error * sigmoid(logits) / (trainers * CELLS)).astype(BF16)

    zrep = onehot(iota((SIDE, 1), 0) == (iota((1, 128), 1) & 15) >> 1)
    fine = exact(eddy, zrep)
    fine = jnp.where(iota((1, 128), 1) >> 4 == iota((ROWS, 1), 0) & 7, fine, 0.0)
    fine = jnp.sum(fine.reshape(64, BLK, 128), axis=1)
    eddy_out[...] = fine
    y_face(send.at[HIDDEN_TILES * 32 : HIDDEN_TILES * 32 + 104], vel, eddy_out, gy_at & 1 == 0)
    loss_out[...] = jnp.broadcast_to(losses, (BLK, 128))
    dl_out[...] = d_logit.astype(F32)

    count = times_sampled(own, blk, gx_at)
    big_s[:, 0:512] = nn(d_logit, last)
    for x in range(SIDE):
        d_hid = big_s[x * SLAB : (x + 1) * SLAB, 0:512] * slope2_s[x * SLAB : (x + 1) * SLAB, :]
        d_hid = d_hid.astype(BF16)
        dh_s[x * SLAB : (x + 1) * SLAB, :] = d_hid
        d_hid = d_hid.astype(F32).reshape(SIDE, BLK, WIDE)
        dw_s[x * SLAB : (x + 1) * SLAB, :] = (d_hid * count[None]).reshape(SLAB, WIDE).astype(BF16)
    dwt = jnp.transpose(dw_s[...])

    sums = {}
    for p in range(4):
        first, last_z = max(2 * p - 1, 0), min(2 * p + 2, SIDE - 1)
        shifts = [
            a_s[dx * SLAB : dx * SLAB + ROWS, j * 512 + p * 128 : j * 512 + (p + 1) * 128]
            for dx in range(3)
            for j in range(3)
        ]
        found = nn(dwt[first * 64 : (last_z + 1) * 64], jnp.concatenate(shifts, axis=1))
        for z in range(first, last_z + 1):
            part = found[(z - first) * 64 : (z - first + 1) * 64]
            m = z - 2 * p
            sums[m] = part if m not in sums else sums[m] + part
    low_half = iota((64, 128), 1) < 64
    held = None
    for k in range(9):
        for dz in (-1, 0, 1):
            low, high = (sums[m][:, k * 128 : (k + 1) * 128] for m in (-dz, 1 - dz))
            at = (k * 3 + dz + 1) * 64
            if at % 128:
                gh_s[:, at - 64 : at + 64] = jnp.where(low_half, held, high + pltpu.roll(low, 64, 1))
            else:
                held = low + pltpu.roll(high, 64, 1)
    gh_s[:, 1664:1792] = jnp.where(low_half, held, 0.0)

    for t in range(HIDDEN_TILES):
        top, bottom = (gh_s[r : r + 32, t * 128 : (t + 1) * 128] for r in (0, 32))
        keep[t * 32 : (t + 1) * 32, :] = jnp.where(second, bottom, top)
        send[t * 32 : (t + 1) * 32, :] = jnp.where(second, top, bottom)


def backward_kernel(
    vel, own, blk, eddy, losses, dl_in, ah_s, slope1_s, i1_s, dh_s, tb_s,
    extra_out, halo1, halo2, halo3, halo4, hx_a, hx_b, hy_b, hz, d_s, pre_s, dw_s,
):
    gx_at, gy_at, second = place()
    gx_odd, gy_odd = gx_at & 1 == 1, gy_at & 1 == 1
    dev = (gx_at * lax.axis_size("gy") + gy_at) * lax.axis_size("role") + lax.axis_index("role")
    count = times_sampled(own, blk, gx_at)

    clear_ends(d_s)
    for x in range(SIDE):
        d_hid = dh_s[x * SLAB : (x + 1) * SLAB, :].astype(F32)
        shifted_store(d_s, x, d_hid.reshape(SIDE, BLK, WIDE))

    for c in range(3):
        for i in range(2):
            lo, hi = vel[c, i], vel[c, 14 + i]
            at = (c * 2 + i) * 16
            hx_a[at : at + 16, :] = jnp.where(gx_odd, lo, hi)
            hx_b[at : at + 16, :] = jnp.where(gx_odd, hi, lo)
    fine = eddy[...]
    small = fine * EDDY_SCALE
    hx_a[96:104, :] = jnp.where(gx_odd, small[0:8], small[56:64])
    hx_b[96:104, :] = jnp.where(gx_odd, small[56:64], small[0:8])
    y_face(hy_b, vel, eddy, gy_odd)
    vt = jnp.transpose(vel[...].reshape(768, 128))
    et = jnp.transpose(jnp.concatenate([small, jnp.zeros((64, 128), F32)], axis=0))
    hz[...] = jnp.zeros(hz.shape, F32)
    for t in range(6):
        hz[t * 8 : t * 8 + 2, :] = vt[0:2, t * 128 : (t + 1) * 128]
        hz[t * 8 + 2 : t * 8 + 4, :] = vt[126:128, t * 128 : (t + 1) * 128]
    hz[48:49, :] = et[0:1]
    hz[49:50, :] = et[127:128]
    halo1[...] = jnp.where(second, hx_a[...], hy_b[...])
    halo2[...] = jnp.where(second, hy_b[...], hx_a[...])
    halo3[...] = jnp.where(second, hx_b[...], hz[...])
    halo4[...] = jnp.where(second, hz[...], hx_b[...])

    for q in range(2):
        pre_s[:, q * 256 : (q + 1) * 256] = nn(windows(d_s, q), tb_s[q])
    for x in range(SIDE):
        rows = slice(x * SLAB, (x + 1) * SLAB)
        d_first = (pre_s[rows, :] * slope1_s[rows, :]).astype(BF16).astype(F32)
        dw_s[rows, :] = (d_first.reshape(SIDE, BLK, WIDE) * count[None]).reshape(SLAB, WIDE).astype(BF16)
    g1 = nn(jnp.transpose(dw_s[...]), i1_s[...])
    z_in = iota((1, 256), 1) & 7
    parts = []
    for dz in (-1, 0, 1):
        tot = jnp.zeros((64, 256), F32)
        for z in range(SIDE):
            if 0 <= z + dz < SIDE:
                tot = tot + jnp.where(z_in == z + dz, g1[z * 64 : (z + 1) * 64], 0.0)
        parts.append(tot)
    r_at = iota((768, 1), 0)
    c_at = iota((1, 128), 1)
    r_lane = r_at & 255
    r_off = lax.div(r_lane, 24)
    r_col = (r_off * 3 + (r_at >> 8)) * 3 + ((r_lane - r_off * 24) >> 3)
    fold = onehot(jnp.where(r_lane < 216, r_col, -1) == c_at)
    g_first = exact(jnp.concatenate(parts, axis=1), fold)

    count_rows = jnp.broadcast_to(count.reshape(1, BLK, 1), (64, BLK, 1)).reshape(ROWS, 1)
    dlw = dl_in[...] * count_rows
    dl_hi = dlw.astype(BF16)
    dl_lo = (dlw - dl_hi.astype(F32)).astype(BF16)
    ah = ah_s[...]
    gl = tn(dl_hi, ah) + tn(dl_lo, ah)
    gl = jnp.where(diagonal(), gl, 0.0)
    fold_o = onehot(iota((1, WIDE), 1) & 63 == iota((64, 1), 0), F32)
    g_last = jnp.sum(nt(fold_o, gl, HIGH), axis=1, keepdims=True)

    lane8 = iota((BLK, 128), 1)
    loss_row = jnp.where(lane8 - (LOSS_COL + BLK * (dev >> 6)) == iota((BLK, 128), 0), losses[...], 0.0)
    loss_row = jnp.sum(loss_row, axis=0, keepdims=True)
    lane = iota((64, 128), 1)
    extra = jnp.where(lane == LAST_COL, g_last, g_first)
    extra = extra + jnp.where(iota((64, 128), 0) == dev & 63, loss_row, 0.0)

    extra_out[...] = extra


def vmem_spec():
    return pl.BlockSpec(memory_space=pltpu.VMEM)


def run_forward(*given):
    velocity, target, w1, w2, w3, own, blk = (pltpu.with_memory_space_constraint(a, pltpu.HBM) for a in given)
    half = pltpu.VMEM((HIDDEN_TILES * 32, 128), F32)
    return pl.pallas_call(
        forward_kernel,
        out_shape=(
            half,
            pltpu.VMEM((HIDDEN_TILES * 32 + 104, 128), F32),
            pltpu.VMEM((64, 128), F32),
            pltpu.VMEM((BLK, 128), F32),
            pltpu.VMEM((ROWS, SIDE), F32),
            pltpu.VMEM((ROWS, WIDE), BF16),
            pltpu.VMEM((ROWS, WIDE), F32),
            pltpu.VMEM((ROWS, 256), BF16),
            pltpu.VMEM((ROWS, WIDE), BF16),
            pltpu.VMEM((2, 3456, 256), BF16),
        )
        + tuple(pltpu.VMEM(a.shape, a.dtype) for a in (velocity, own, blk)),
        in_specs=[pl.BlockSpec(memory_space=pltpu.HBM)] * 7,
        out_specs=tuple(vmem_spec() for _ in range(13)),
        scratch_shapes=[
            pltpu.VMEM((3, SIDE, 16, 128), F32),
            pltpu.VMEM((10, 10, BLK, 256), F32),
            pltpu.VMEM((ROWS + 2 * SLAB, 1536), BF16),
            pltpu.VMEM((2, 3456, 256), BF16),
            pltpu.VMEM((ROWS, WIDE), F32),
            pltpu.VMEM((ROWS, WIDE), F32),
            pltpu.VMEM((ROWS, WIDE), BF16),
            pltpu.VMEM((ROWS, WIDE), F32),
            pltpu.VMEM((64, HIDDEN_TILES * 128), F32),
            pltpu.VMEM((64, 1792), F32),
        ]
        + [pltpu.VMEM(a.shape, a.dtype) for a in (target, w1, w2, w3)]
        + [pltpu.SemaphoreType.DMA((7,))],
        compiler_params=pltpu.CompilerParams(vmem_limit_bytes=40 * 1024 * 1024),
        name="forward",
    )(velocity, target, w1, w2, w3, own, blk)


def run_backward(velocity, own, blk, *kept):
    face = pltpu.VMEM((104, 128), F32)
    return pl.pallas_call(
        backward_kernel,
        out_shape=(pltpu.VMEM((64, 128), F32),) + (face,) * 4,
        in_specs=[vmem_spec()] * 11,
        out_specs=tuple(vmem_spec() for _ in range(5)),
        scratch_shapes=[face] * 4
        + [
            pltpu.VMEM((ROWS + 2 * SLAB, 1536), BF16),
            pltpu.VMEM((ROWS, WIDE), F32),
            pltpu.VMEM((ROWS, WIDE), BF16),
        ],
        compiler_params=pltpu.CompilerParams(vmem_limit_bytes=40 * 1024 * 1024),
        name="backward",
    )(velocity, own, blk, *kept)


def flow_kernel(
    vel, eddy, got0, got1, got2, got3, got4, out, rx_a, rx_b, ry_a, ry_b, rz, vx_s, vy_s, visc_s, ez_s
):
    gx_at, gy_at = lax.axis_index("gx"), lax.axis_index("gy")
    gx_odd, gy_odd = gx_at & 1 == 1, gy_at & 1 == 1
    second = core_half(gy_at) == 1
    ry_a[...] = got0[...]
    ry_b[...] = jnp.where(second, got2[...], got1[...])
    rx_a[...] = jnp.where(second, got1[...], got2[...])
    rx_b[...] = jnp.where(second, got3[...], got4[...])
    rz[...] = jnp.where(second, got4[...], got3[...])
    lane = iota((1, 128), 1)

    def sides(odd, a, b, at, rows):
        one, two = a[at : at + rows, :], b[at : at + rows, :]
        return jnp.where(odd, one, two), jnp.where(odd, two, one)

    for c in range(3):
        for x in range(16):
            vy_s[(c * 16 + x) * 32 + 8 : (c * 16 + x) * 32 + 24, :] = vel[c, x]
        for i in range(2):
            below, above = sides(gy_odd, ry_a, ry_b, (c * 2 + i) * 16, 16)
            vy_s[pl.ds(c * 512 + 6 + i, 16, stride=32), :] = below
            vy_s[pl.ds(c * 512 + 24 + i, 16, stride=32), :] = above
            below, above = sides(gx_odd, rx_a, rx_b, (c * 2 + i) * 16, 16)
            vx_s[c, i] = below
            vx_s[c, 2 + i] = above

    zcols = jnp.concatenate([jnp.transpose(rz[t * 8 : t * 8 + 8, :]) for t in range(7)], axis=0)
    coarse = eddy[...]
    e_first, e_last = zcols[768:832, 0:1] / EDDY_SCALE, zcols[768:832, 1:2] / EDDY_SCALE
    ahead = jnp.where(lane == 127, e_first, pltpu.roll(coarse, 127, 1))
    behind = jnp.where(lane == 0, e_last, pltpu.roll(coarse, 1, 1))
    below_x, above_x = (v / EDDY_SCALE for v in sides(gx_odd, rx_a, rx_b, 96, 8))
    below_y, above_y = (v / EDDY_SCALE for v in sides(gy_odd, ry_a, ry_b, 96, 8))

    def put(dst, plane, val):
        dst[pl.ds(plane * 32 + 8, 8, stride=2), :] = val
        dst[pl.ds(plane * 32 + 9, 8, stride=2), :] = val

    put(visc_s, 0, base_visc + below_x)
    put(visc_s, 17, base_visc + above_x)
    for x in range(8):
        for r in range(2):
            plane = 2 * x + 1 + r
            put(visc_s, plane, base_visc + coarse[x * 8 : x * 8 + 8])
            visc_s[plane * 32 + 7 : plane * 32 + 8, :] = base_visc + below_y[x : x + 1]
            visc_s[plane * 32 + 24 : plane * 32 + 25, :] = base_visc + above_y[x : x + 1]
        put(ez_s, 2 * x, base_visc + ahead[x * 8 : x * 8 + 8])
        put(ez_s, 2 * x + 1, base_visc + behind[x * 8 : x * 8 + 8])

    def plane_of(c, x):
        if x < 0:
            return vx_s[c, x + 2]
        if x > 15:
            return vx_s[c, x - 14]
        return vel[c, x]

    for x in range(16):
        vat = (x + 1) * 32
        visc = visc_s[vat + 8 : vat + 24, :]
        faces = (
            (visc_s[vat + 40 : vat + 56, :], visc_s[vat - 24 : vat - 8, :]),
            (visc_s[vat + 9 : vat + 25, :], visc_s[vat + 7 : vat + 23, :]),
            (
                ez_s[(x // 2 * 2) * 32 + 8 : (x // 2 * 2) * 32 + 24, :],
                ez_s[(x // 2 * 2 + 1) * 32 + 8 : (x // 2 * 2 + 1) * 32 + 24, :],
            ),
        )
        faces = [(0.5 * (visc + a), 0.5 * (visc + b)) for a, b in faces]
        wind = [vel[a, x] for a in range(3)]
        for c in range(3):
            u = vel[c, x]
            at = (c * 16 + x) * 32
            zat = (c * 16 + x) * 16
            zc = zcols[zat : zat + 16]
            p1 = jnp.where(lane == 127, zc[:, 0:1], pltpu.roll(u, 127, 1))
            p2 = jnp.where(lane == 127, zc[:, 1:2], jnp.where(lane == 126, zc[:, 0:1], pltpu.roll(u, 126, 1)))
            m1 = jnp.where(lane == 0, zc[:, 3:4], pltpu.roll(u, 1, 1))
            m2 = jnp.where(lane == 0, zc[:, 2:3], jnp.where(lane == 1, zc[:, 3:4], pltpu.roll(u, 2, 1)))
            near = (
                (plane_of(c, x + 1), plane_of(c, x - 1), plane_of(c, x + 2), plane_of(c, x - 2)),
                (
                    vy_s[at + 9 : at + 25, :], vy_s[at + 7 : at + 23, :],
                    vy_s[at + 10 : at + 26, :], vy_s[at + 6 : at + 22, :],
                ),
                (p1, m1, p2, m2),
            )
            advect = None
            diffuse = None
            for a in range(3):
                q1, b1, q2, b2 = near[a]
                slope = (8.0 * (q1 - b1) - (q2 - b2)) * (1.0 / 12.0)
                term = wind[a] * slope
                advect = term if advect is None else advect + term
                flux = faces[a][0] * (q1 - u) - faces[a][1] * (u - b1)
                diffuse = flux if diffuse is None else diffuse + flux
            out[c, x] = u + time_step * (diffuse - advect)


def run_flow(velocity, eddy, *got):
    return pl.pallas_call(
        flow_kernel,
        out_shape=jax.ShapeDtypeStruct(velocity.shape, F32),
        in_specs=[vmem_spec()] * 7,
        out_specs=vmem_spec(),
        scratch_shapes=[
            pltpu.VMEM((104, 128), F32),
            pltpu.VMEM((104, 128), F32),
            pltpu.VMEM((104, 128), F32),
            pltpu.VMEM((104, 128), F32),
            pltpu.VMEM((104, 128), F32),
            pltpu.VMEM((3, 4, 16, 128), F32),
            pltpu.VMEM((3 * 16 * 32, 128), F32),
            pltpu.VMEM((18 * 32, 128), F32),
            pltpu.VMEM((16 * 32, 128), F32),
        ],
        compiler_params=pltpu.CompilerParams(vmem_limit_bytes=32 * 1024 * 1024),
        name="flow",
    )(velocity, eddy, *got)


def finish_kernel(own, blk, mine, other, loss_out, first_out, hidden_out, last_out):
    gx_at, gy_at = lax.axis_index("gx"), lax.axis_index("gy")
    n_z = lax.axis_size("role")
    in_group = gy_at * n_z + lax.axis_index("role")
    second = core_half(gy_at) == 1
    for t in range(HIDDEN_TILES):
        one, two = mine[t * 32 : (t + 1) * 32, :], other[t * 32 : (t + 1) * 32, :]
        top, bottom = jnp.where(second, two, one), jnp.where(second, one, two)
        width = min(128, 27 * CH - t * 128)
        hidden_out[0:32, t * 128 : t * 128 + width] = top[:, :width]
        hidden_out[32:64, t * 128 : t * 128 + width] = bottom[:, :width]
    extra = mine[HIDDEN_TILES * 32 :, :] + other[HIDDEN_TILES * 32 :, :]
    first_out[...] = extra[:, 0:81]
    turned = jnp.transpose(jnp.concatenate([extra, jnp.zeros((64, 128), F32)], axis=0))
    last_out[...] = turned[LAST_COL : LAST_COL + 1, 0:64]
    slots = loss_out.shape[1]
    dev = own[...] * (lax.axis_size("gy") * n_z) + in_group
    listed = dev.shape[1]
    pick = onehot(iota((64, listed), 0) == dev & 63, F32)
    rows = nn(turned[:, 0:64], pick, HIGH)
    rows = jnp.where(iota((128, listed), 0) == LOSS_COL + BLK * (dev >> 6) + blk[...], rows, 0.0)
    found = jnp.sum(rows, axis=0, keepdims=True)
    picked = jnp.zeros((1, slots), F32)
    for g in range(listed // slots):
        picked = jnp.where(gx_at == g, found[:, g * slots : (g + 1) * slots], picked)
    loss_out[...] = picked


def run_finish(own, blk, mine, other, slots):
    f = lambda *s: jax.ShapeDtypeStruct(s, F32)
    return pl.pallas_call(
        finish_kernel,
        out_shape=(f(1, slots), f(64, 81), f(64, 27 * CH), f(1, 64)),
        in_specs=[vmem_spec()] * 4,
        out_specs=tuple(vmem_spec() for _ in range(4)),
        compiler_params=pltpu.CompilerParams(vmem_limit_bytes=32 * 1024 * 1024),
        name="finish",
    )(own, blk, mine, other)


def on_device(velocity, target_visc, w_first, w_hidden, w_last, sample_owner, sample_block):
    n_x, n_y, n_z = lax.axis_size("gx"), lax.axis_size("gy"), lax.axis_size("role")
    trainers = n_x * n_y * n_z
    own = sample_owner.reshape(1, -1)
    blk = sample_block.reshape(1, -1)
    slots = own.shape[1] // n_x

    axes = ("gx", "gy", "role")

    def even_odd(i, count):
        return i ^ 1

    def odd_even(i, count):
        return (i - 1) % count if i % 2 == 0 else (i + 1) % count

    def partner(kind, i, j, r):
        if kind == "x":
            j = odd_even(j, n_y)
        elif kind == "y":
            r = r ^ 1
        elif kind == "z_a":
            i = even_odd(i, n_x)
        else:
            i = odd_even(i, n_x)
        return (i * n_y + j) * n_z + r

    def mixed(kinds):
        pairs = []
        for i in range(n_x):
            for j in range(n_y):
                for r in range(n_z):
                    pairs.append(((i * n_y + j) * n_z + r, partner(kinds[(j ^ (j >> 1)) & 1], i, j, r)))
        return pairs

    core_pairs = [(j, even_odd(j, n_y)) for j in range(n_y)]
    size = TILES * 32

    keep, send, eddy, *kept, velocity, own, blk = run_forward(
        velocity, target_visc, w_first, w_hidden, w_last.reshape(1, CH), own, blk
    )
    half = core_half(lax.axis_index("gy"))
    got = lax.ppermute(send, "gy", core_pairs)
    extra, *halos = run_backward(velocity, own, blk, eddy, *kept)
    total = jnp.concatenate([keep + got[: HIDDEN_TILES * 32], extra], axis=0)
    rims = [got[HIDDEN_TILES * 32 :]]
    halos = [h.astype(F16) for h in halos]

    def widen(values, exps):
        wide = values.astype(F32).reshape(TILES, 32, 128) * jnp.exp2(exps)[:, None, :]
        return wide.reshape(size, 128)

    top = jnp.max(jnp.abs(total.reshape(TILES, 32, 128)), axis=1)
    exps = jnp.clip(jnp.ceil(jnp.log2(jnp.maximum(top, 1e-30))) - 13.0, -110.0, 110.0)
    orders = (("x", "z_a", "y", "z_b"), ("z_a", "x", "z_b", "y"))
    for s in range(4):
        kinds = (orders[0][s], orders[1][s])
        scaled = total.reshape(TILES, 32, 128) * jnp.exp2(-exps)[:, None, :]
        pieces = [scaled.reshape(size, 128).astype(F16), exps.astype(F16)]
        message = jnp.concatenate(pieces + [halos[s]] if s < 3 else pieces, axis=0)
        message = lax.optimization_barrier(message)
        got = lax.ppermute(message, axes, mixed(kinds))
        if s == 1:
            far = lax.ppermute(halos[3], axes, mixed((orders[0][3], orders[1][3])))
        their_exps = got[size : size + TILES].astype(F32)
        mine, theirs = widen(message[:size], exps), widen(got[:size], their_exps)
        if n_x != 4 and "z_b" in kinds:
            theirs = jnp.where(half == kinds.index("z_b"), 0.0, theirs)
        total = mine + theirs
        exps = jnp.maximum(exps, their_exps) + 1.0
        if s < 3:
            rims.append(got[size + 16 :].astype(F32))
        if s == 1:
            total, far = lax.optimization_barrier((total, far))
        if s == 2:
            u_next = run_flow(velocity, eddy, *rims, far.astype(F32))
    total, u_next = lax.optimization_barrier((total, u_next))
    if n_x != 4:
        for bit in range(1, n_x.bit_length() - 1):
            total = total + lax.ppermute(total, "gx", [(i, i ^ (1 << bit)) for i in range(n_x)])
    other = lax.ppermute(total, "gy", core_pairs)

    losses, first, hidden, last = run_finish(own, blk, total, other, slots)
    return (u_next, losses.reshape(1, 1, slots), first, hidden, last.reshape(CH))


def solution(mesh):
    return jax.shard_map(
        on_device,
        mesh=mesh,
        in_specs=(
            P(None, "gx", "gy", "role"),
            P("gx", "gy", "role"),
            P(),
            P(),
            P(),
            P("gy", "role", None, None),
            P("gy", "role", None, None),
        ),
        out_specs=(P(None, "gx", "gy", "role"), P("gy", "role", "gx"), P(), P(), P()),
        check_vma=False,
    )
```

```python
import jax
import jax.numpy as jnp
from jax import lax
from jax.experimental import pallas as pl
from jax.experimental.pallas import tpu as pltpu
from jax.sharding import PartitionSpec as P

F32 = jnp.float32
BF16 = jnp.bfloat16
HIGH = lax.Precision.HIGHEST

SIDE = 8
CELLS = SIDE**3
CH = 64
BLK = 8
ROWS = SIDE * SIDE * BLK
WIDE = SIDE * CH
SLAB = SIDE * BLK
HIDDEN_TILES = 14
TILES = 16
LAST_COL = 81
LOSS_COL = 82

EDDY_SCALE = 2.0**-9
F16 = jnp.float16

base_visc = 0.02
time_step = 0.2


def iota(shape, dim):
    return lax.broadcasted_iota(jnp.int32, shape, dim)


def onehot(cond, dtype=BF16):
    return jnp.where(cond, 1.0, 0.0).astype(dtype)


def sigmoid(v):
    return 0.5 + 0.5 * jnp.tanh(0.5 * v)


def nt(a, b, precision=None):
    return lax.dot_general(a, b, (((1,), (1,)), ((), ())), preferred_element_type=F32, precision=precision)


def tn(a, b, precision=None):
    return lax.dot_general(a, b, (((0,), (0,)), ((), ())), preferred_element_type=F32, precision=precision)


def nn(a, b, precision=None):
    return lax.dot_general(a, b, (((1,), (0,)), ((), ())), preferred_element_type=F32, precision=precision)


def core_half(at):
    return (at ^ (at >> 1)) & 1


def place():
    gx_at, gy_at = lax.axis_index("gx"), lax.axis_index("gy")
    return gx_at, gy_at, core_half(gy_at) == 1


def times_sampled(own, blk, gx_at):
    code = own[...] * BLK + blk[...]
    wanted = gx_at * BLK + iota((BLK, code.shape[1]), 0)
    return jnp.sum(jnp.where(code == wanted, 1.0, 0.0), axis=1, keepdims=True)


def tile_places():
    return [(q, z, h, 2 * q + h) for q in range(2) for z in range(3 * q, 3 * q + 5) for h in range(2)]


def place_row(q, z, k):
    if 4 * q <= z < 4 * q + 4:
        return k * 256 + (z - 4 * q) * 64
    return 2304 + k // 3 * 256 + k % 3 * 64


def exact(a, selector):
    high = a.astype(BF16)
    rest = a - high.astype(F32)
    mid = rest.astype(BF16)
    low = (rest - mid.astype(F32)).astype(BF16)
    return nn(high, selector) + (nn(mid, selector) + nn(low, selector))


def y_face(dst, vel, eddy, high):
    for c in range(3):
        for i in range(2):
            lo = jnp.concatenate([vel[c, x, i : i + 1, :] for x in range(16)], axis=0)
            hi = jnp.concatenate([vel[c, x, 14 + i : 15 + i, :] for x in range(16)], axis=0)
            dst[(c * 2 + i) * 16 : (c * 2 + i + 1) * 16, :] = jnp.where(high, hi, lo)
    dst[96:104, :] = jnp.where(high, eddy[pl.ds(7, 8, stride=8), :], eddy[pl.ds(0, 8, stride=8), :]) * EDDY_SCALE


def diagonal():
    return iota((1, WIDE), 1) >> 6 == iota((SIDE, 1), 0)


def windows(ref, more, q):
    own = [
        ref[dx * SLAB : dx * SLAB + ROWS, j * 512 + q * 256 : j * 512 + (q + 1) * 256]
        for dx in range(3)
        for j in range(3)
    ]
    return jnp.concatenate(own + [more[q, dx * SLAB : dx * SLAB + ROWS, :] for dx in range(3)], axis=1)


def shifted_store(dst_ref, more, x, val):
    zero = jnp.zeros((1, BLK, WIDE), F32)
    lo, hi = (x + 1) * SLAB, (x + 2) * SLAB
    dst_ref[lo:hi, 0:512] = jnp.concatenate([zero, val[:-1]], axis=0).reshape(SLAB, WIDE).astype(BF16)
    dst_ref[lo:hi, 512:1024] = val.reshape(SLAB, WIDE).astype(BF16)
    dst_ref[lo:hi, 1024:1536] = jnp.concatenate([val[1:], zero], axis=0).reshape(SLAB, WIDE).astype(BF16)
    left = iota((SLAB, 128), 1) < 64
    zero = zero[:, :, :128]
    for q in range(2):
        part = val[:, :, 256:384] if q == 0 else val[:, :, 128:256]
        near = [jnp.concatenate([zero, part[:-1]], axis=0), part, jnp.concatenate([part[1:], zero], axis=0)]
        near = [v.reshape(SLAB, 128) for v in near]
        turn = (1,) if q == 0 else (0, 2)
        near = [pltpu.roll(v, 64, 1) if j in turn else v for j, v in enumerate(near)]
        more[q, lo:hi, 0:128] = jnp.where(left, near[0], near[1]).astype(BF16)
        more[q, lo:hi, 128:256] = jnp.where(left, near[2], 0.0).astype(BF16)


def clear_ends(ref, more):
    for at in (0, 9 * SLAB):
        ref[at : at + SLAB, :] = jnp.zeros((SLAB, 1536), BF16)
        for q in range(2):
            more[q, at : at + SLAB, :] = jnp.zeros((SLAB, 256), BF16)


def forward_kernel(
    vel_in, tgt_in, w1_in, w2_in, w3_in, own_in, blk_in,
    keep, send, eddy_out, loss_out, dl_out, ah_s, slope1_s, i1_s, dh_s, tb_s, vel, own, blk,
    pool_s, fp_s, a_s, tt_s, pre_s, slope2_s, dw_s, big_s, gh_s, w2_s,
    tgt, w1, w2, w3, sems, ea_s,
):
    pairs = ((w2_in, w2), (vel_in, vel), (tgt_in, tgt), (w1_in, w1), (w3_in, w3), (own_in, own), (blk_in, blk))
    copies = [pltpu.make_async_copy(src, dst, sems.at[n]) for n, (src, dst) in enumerate(pairs)]
    for copy in copies:
        copy.start()
    gx_at, gy_at, second = place()
    trainers = lax.axis_size("gx") * lax.axis_size("gy") * lax.axis_size("role")

    fp_s[...] = jnp.zeros(fp_s.shape, F32)
    clear_ends(a_s, ea_s)
    w2_s[:, 1664:1792] = jnp.zeros((64, 128), F32)
    zero_tile = jnp.zeros((64, 128), BF16)
    for q in range(2):
        for dx in range(3):
            for ref in (tt_s, tb_s):
                ref[q, 2304 + dx * 256 + 192 : 2304 + (dx + 1) * 256, :] = jnp.zeros((64, 256), BF16)
    for q, z, h, m in tile_places():
        for k in range(9):
            at, cols = place_row(q, z, k), slice(h * 128, (h + 1) * 128)
            if not -1 <= z - 2 * m <= 2:
                tt_s[q, at : at + 64, cols] = zero_tile
                tb_s[q, at : at + 64, cols] = zero_tile
    for copy in copies:
        copy.wait()

    for c in range(3):
        for x in range(SIDE):
            both = vel[c, 2 * x] + vel[c, 2 * x + 1]
            pool_s[c, x] = both
    rows = []
    for c in range(3):
        cols = []
        for x in range(SIDE):
            cols.append(pool_s[c, x, pl.ds(0, 8, stride=2), :] + pool_s[c, x, pl.ds(1, 8, stride=2), :])
        rows.append(jnp.concatenate(cols, axis=0))
    pooled = jnp.concatenate(rows, axis=0)
    zpool = jnp.where(iota((128, 1), 0) >> 1 == iota((1, 64), 1), 0.125, 0.0).astype(BF16)
    filt = exact(pooled, zpool).astype(BF16)
    tgt_rows = tgt[...].reshape(64, 64)
    zsel = jnp.concatenate([filt[0:64], filt[64:128], filt[128:192], tgt_rows], axis=1)
    spread = onehot(iota((ROWS, 1), 0) >> 3 == iota((1, 64), 1))
    by_block = nn(spread, zsel)
    mine = (iota((1, 256), 1) & 63) >> 3 == iota((ROWS, 1), 0) & 7
    by_block = jnp.where(mine, by_block, 0.0).astype(BF16)
    lane_in = iota((1, 256), 1)
    lane_off = lax.div(lane_in, 24)
    lane_cz = lane_in - lane_off * 24
    src = iota((256, 1), 0)
    pick = onehot(jnp.where(lane_in < 216, lane_cz, -1) == (src >> 6) * 8 + (src & 7))
    cells = nn(by_block, pick)
    pick_t = onehot(jnp.where(src >= 192, src & 7, -1) == iota((1, 24), 1) & 7)
    target = nn(by_block, pick_t)

    fp_s[1:9, 1:9] = cells.reshape(SIDE, SIDE, BLK, 256)
    group = lax.div(iota((1, 1, 1, 256), 3), 24)
    for x in range(SIDE):
        acc = jnp.zeros((1, SIDE, BLK, 256), F32)
        for k in range(9):
            part = fp_s[x + k // 3 : x + k // 3 + 1, k % 3 : k % 3 + SIDE]
            acc = jnp.where(group == k, part, acc)
        i1_s[x * SLAB : (x + 1) * SLAB, :] = acc.reshape(SLAB, 256).astype(BF16)

    j_at = iota((81, 1), 0)
    j_off, j_dz, j_c = lax.div(j_at, 9), lax.rem(lax.div(j_at, 3), 3) - 1, lax.rem(j_at, 3)
    lane_key = jnp.where(lane_in < 216, lane_off * 4 + (lane_cz >> 3), -1)
    same = lane_key == j_off * 4 + j_c
    w1v = w1[...]
    by_dz = [nn(w1v, onehot(jnp.where(same, j_dz, 9) == dz)) for dz in (-1, 0, 1)]
    z_in = jnp.broadcast_to(lane_in & 7, (CH, 256))
    t1 = []
    for z in range(SIDE):
        rows = jnp.where(z_in == z - 1, by_dz[0], jnp.where(z_in == z, by_dz[1], 0.0))
        t1.append(jnp.where(z_in == z + 1, by_dz[2], rows).astype(BF16))
    t1 = jnp.concatenate(t1, axis=0)
    pre_s[...] = nt(i1_s[...], t1)

    left = iota((64, 128), 1) < 64
    w2_s[:, 0:1728] = w2[...].astype(F32)
    w2t = jnp.concatenate(
        [
            jnp.transpose(jnp.concatenate([w2_s[:, t * 128 : (t + 1) * 128]] * 2, axis=0))
            for t in range(14)
        ],
        axis=0,
    )
    for k in range(9):
        base = (192 * k) // 128 * 128
        one, two = w2_s[:, base : base + 128], w2_s[:, base + 128 : base + 256]
        one_r, two_r = pltpu.roll(one, 64, 1), pltpu.roll(two, 64, 1)
        if k % 2 == 0:
            low, high = (one, one_r, two), (one_r, one, two_r)
        else:
            low, high = (one_r, two, two_r), (one, two_r, two)
        low, high = (0.0,) + low, high + (0.0,)
        tiles = {d: jnp.where(left, low[d + 2], high[d + 2]).astype(BF16) for d in (-2, -1, 0, 1)}
        kb = 8 - k
        turned = {dz: w2t[(3 * k + dz + 1) * 64 : (3 * k + dz + 2) * 64] for dz in (-1, 0, 1)}
        turned[-2] = turned[2] = jnp.zeros((64, 128), F32)
        forward = {d: jnp.where(left, turned[d], turned[d - 1]).astype(BF16) for d in (-1, 0, 1, 2)}
        for q, z, h, m in tile_places():
            at, cols = place_row(q, z, k), slice(h * 128, (h + 1) * 128)
            if z - 2 * m in forward:
                tt_s[q, at : at + 64, cols] = forward[z - 2 * m]
            d = 2 * m - z
            at = place_row(q, z, kb)
            if d in tiles:
                tb_s[q, at : at + 64, cols] = tiles[d]

    for x in range(SIDE):
        pre = pre_s[x * SLAB : (x + 1) * SLAB, :]
        sig = sigmoid(pre)
        slope1_s[x * SLAB : (x + 1) * SLAB, :] = sig * (1.0 + pre * (1.0 - sig))
        shifted_store(a_s, ea_s, x, (pre * sig).reshape(SIDE, BLK, WIDE))

    for q in range(2):
        pre_s[:, q * 256 : (q + 1) * 256] = nn(windows(a_s, ea_s, q), tt_s[q])
    for x in range(SIDE):
        pre = pre_s[x * SLAB : (x + 1) * SLAB, :]
        sig = sigmoid(pre)
        slope2_s[x * SLAB : (x + 1) * SLAB, :] = sig * (1.0 + pre * (1.0 - sig))
        ah_s[x * SLAB : (x + 1) * SLAB, :] = (pre * sig).astype(BF16)

    tile8 = onehot(iota((64, 1), 0) == iota((1, WIDE), 1) & 63)
    w3_wide = nn(w3[...], tile8)
    diag = diagonal()
    last = jnp.where(diag, w3_wide, 0.0).astype(BF16)
    last3 = jnp.concatenate([jnp.where(diag, w3_wide, 0.0)] * 3, axis=0).astype(BF16)
    logits = nt(ah_s[...], last3)
    eddy = 0.5 * (jnp.maximum(logits, 0.0) + jnp.log1p(jnp.exp(-jnp.abs(logits))))
    error = eddy - target
    lane24 = iota((1, 24), 1)
    squares = jnp.where(lane24 < SIDE, error * error, 0.0)
    losses = jnp.sum(jnp.sum(squares.reshape(64, BLK, 24), axis=0), axis=1, keepdims=True) / CELLS
    d_logit = (error * sigmoid(logits) / (trainers * CELLS)).astype(BF16)

    zrep = onehot(iota((24, 1), 0) & 7 == (iota((1, 128), 1) & 15) >> 1)
    e_high = eddy.astype(BF16).astype(F32)
    e_mid = (eddy - e_high).astype(BF16).astype(F32)
    e_parts = jnp.where(lane24 < 8, e_high, jnp.where(lane24 < 16, e_mid, eddy - e_high - e_mid))
    fine = nn(e_parts.astype(BF16), zrep)
    fine = jnp.where(iota((1, 128), 1) >> 4 == iota((ROWS, 1), 0) & 7, fine, 0.0)
    fine = jnp.sum(fine.reshape(64, BLK, 128), axis=1)
    eddy_out[...] = fine
    y_face(send.at[HIDDEN_TILES * 32 : HIDDEN_TILES * 32 + 104], vel, eddy_out, gy_at & 1 == 0)
    loss_out[...] = jnp.broadcast_to(losses, (BLK, 128))
    dl_out[...] = d_logit.astype(F32)[:, 0:SIDE]

    count = times_sampled(own, blk, gx_at)
    big_s[:, 0:512] = nn(d_logit, jnp.concatenate([last.astype(F32), jnp.zeros((16, WIDE), F32)], axis=0).astype(BF16))
    for x in range(SIDE):
        d_hid = big_s[x * SLAB : (x + 1) * SLAB, 0:512] * slope2_s[x * SLAB : (x + 1) * SLAB, :]
        d_hid = d_hid.astype(BF16)
        dh_s[x * SLAB : (x + 1) * SLAB, :] = d_hid
        d_hid = d_hid.astype(F32).reshape(SIDE, BLK, WIDE)
        dw_s[x * SLAB : (x + 1) * SLAB, :] = (d_hid * count[None]).reshape(SLAB, WIDE).astype(BF16)
    dwt = jnp.transpose(dw_s[...])

    sums = {}
    for p in range(4):
        first, last_z = max(2 * p - 1, 0), min(2 * p + 2, SIDE - 1)
        shifts = [
            a_s[dx * SLAB : dx * SLAB + ROWS, j * 512 + p * 128 : j * 512 + (p + 1) * 128]
            for dx in range(3)
            for j in range(3)
        ]
        found = nn(dwt[first * 64 : (last_z + 1) * 64], jnp.concatenate(shifts, axis=1))
        for z in range(first, last_z + 1):
            part = found[(z - first) * 64 : (z - first + 1) * 64]
            m = z - 2 * p
            sums[m] = part if m not in sums else sums[m] + part
    low_half = iota((64, 128), 1) < 64
    held = None
    for k in range(9):
        for dz in (-1, 0, 1):
            low, high = (sums[m][:, k * 128 : (k + 1) * 128] for m in (-dz, 1 - dz))
            at = (k * 3 + dz + 1) * 64
            if at % 128:
                gh_s[:, at - 64 : at + 64] = jnp.where(low_half, held, high + pltpu.roll(low, 64, 1))
            else:
                held = low + pltpu.roll(high, 64, 1)
    gh_s[:, 1664:1792] = jnp.where(low_half, held, 0.0)

    for t in range(HIDDEN_TILES):
        top, bottom = (gh_s[r : r + 32, t * 128 : (t + 1) * 128] for r in (0, 32))
        keep[t * 32 : (t + 1) * 32, :] = jnp.where(second, bottom, top)
        send[t * 32 : (t + 1) * 32, :] = jnp.where(second, top, bottom)


def backward_kernel(
    vel, own, blk, eddy, losses, dl_in, ah_s, slope1_s, i1_s, dh_s, tb_s,
    extra_out, halo1, halo2, halo3, halo4, hx_a, hx_b, hy_b, hz, d_s, pre_s, dw_s, ed_s,
):
    gx_at, gy_at, second = place()
    gx_odd, gy_odd = gx_at & 1 == 1, gy_at & 1 == 1
    dev = (gx_at * lax.axis_size("gy") + gy_at) * lax.axis_size("role") + lax.axis_index("role")
    count = times_sampled(own, blk, gx_at)

    clear_ends(d_s, ed_s)
    for x in range(SIDE):
        d_hid = dh_s[x * SLAB : (x + 1) * SLAB, :].astype(F32)
        shifted_store(d_s, ed_s, x, d_hid.reshape(SIDE, BLK, WIDE))

    for c in range(3):
        for i in range(2):
            lo, hi = vel[c, i], vel[c, 14 + i]
            at = (c * 2 + i) * 16
            hx_a[at : at + 16, :] = jnp.where(gx_odd, lo, hi)
            hx_b[at : at + 16, :] = jnp.where(gx_odd, hi, lo)
    fine = eddy[...]
    small = fine * EDDY_SCALE
    hx_a[96:104, :] = jnp.where(gx_odd, small[0:8], small[56:64])
    hx_b[96:104, :] = jnp.where(gx_odd, small[56:64], small[0:8])
    y_face(hy_b, vel, eddy, gy_odd)
    vt = jnp.transpose(vel[...].reshape(768, 128))
    et = jnp.transpose(jnp.concatenate([small, jnp.zeros((64, 128), F32)], axis=0))
    hz[...] = jnp.zeros(hz.shape, F32)
    for t in range(6):
        hz[t * 8 : t * 8 + 2, :] = vt[0:2, t * 128 : (t + 1) * 128]
        hz[t * 8 + 2 : t * 8 + 4, :] = vt[126:128, t * 128 : (t + 1) * 128]
    hz[48:49, :] = et[0:1]
    hz[49:50, :] = et[127:128]
    halo1[...] = jnp.where(second, hx_a[...], hy_b[...])
    halo2[...] = jnp.where(second, hy_b[...], hx_a[...])
    halo3[...] = jnp.where(second, hx_b[...], hz[...])
    halo4[...] = jnp.where(second, hz[...], hx_b[...])

    for q in range(2):
        pre_s[:, q * 256 : (q + 1) * 256] = nn(windows(d_s, ed_s, q), tb_s[q])
    for x in range(SIDE):
        rows = slice(x * SLAB, (x + 1) * SLAB)
        d_first = (pre_s[rows, :] * slope1_s[rows, :]).astype(BF16).astype(F32)
        dw_s[rows, :] = (d_first.reshape(SIDE, BLK, WIDE) * count[None]).reshape(SLAB, WIDE).astype(BF16)
    g1 = nn(jnp.transpose(dw_s[...]), i1_s[...])
    z_in = iota((1, 256), 1) & 7
    parts = []
    for dz in (-1, 0, 1):
        tot = jnp.zeros((64, 256), F32)
        for z in range(SIDE):
            if 0 <= z + dz < SIDE:
                tot = tot + jnp.where(z_in == z + dz, g1[z * 64 : (z + 1) * 64], 0.0)
        parts.append(tot)
    r_at = iota((768, 1), 0)
    c_at = iota((1, 128), 1)
    r_lane = r_at & 255
    r_off = lax.div(r_lane, 24)
    r_col = (r_off * 3 + (r_at >> 8)) * 3 + ((r_lane - r_off * 24) >> 3)
    fold = onehot(jnp.where(r_lane < 216, r_col, -1) == c_at)
    g_first = exact(jnp.concatenate(parts, axis=1), fold)

    count_rows = jnp.broadcast_to(count.reshape(1, BLK, 1), (64, BLK, 1)).reshape(ROWS, 1)
    dlw = dl_in[...] * count_rows
    dl_hi = dlw.astype(BF16)
    dl_lo = (dlw - dl_hi.astype(F32)).astype(BF16)
    ah = ah_s[...]
    gl = tn(dl_hi, ah) + tn(dl_lo, ah)
    gl = jnp.where(diagonal(), gl, 0.0)
    gl = jnp.sum(gl, axis=0, keepdims=True)
    gl = gl[:, 0:128] + gl[:, 128:256] + gl[:, 256:384] + gl[:, 384:512]
    at_lane = iota((1, 128), 1) & 63 == iota((64, 1), 0)
    g_last = jnp.sum(jnp.where(at_lane, gl, 0.0), axis=1, keepdims=True)

    lane8 = iota((BLK, 128), 1)
    loss_row = jnp.where(lane8 - (LOSS_COL + BLK * (dev >> 6)) == iota((BLK, 128), 0), losses[...], 0.0)
    loss_row = jnp.sum(loss_row, axis=0, keepdims=True)
    lane = iota((64, 128), 1)
    extra = jnp.where(lane == LAST_COL, g_last, g_first)
    extra = extra + jnp.where(iota((64, 128), 0) == dev & 63, loss_row, 0.0)

    extra_out[...] = extra


def vmem_spec():
    return pl.BlockSpec(memory_space=pltpu.VMEM)


def run_forward(*given):
    velocity, target, w1, w2, w3, own, blk = (pltpu.with_memory_space_constraint(a, pltpu.HBM) for a in given)
    half = pltpu.VMEM((HIDDEN_TILES * 32, 128), F32)
    return pl.pallas_call(
        forward_kernel,
        out_shape=(
            half,
            pltpu.VMEM((HIDDEN_TILES * 32 + 104, 128), F32),
            pltpu.VMEM((64, 128), F32),
            pltpu.VMEM((BLK, 128), F32),
            pltpu.VMEM((ROWS, SIDE), F32),
            pltpu.VMEM((ROWS, WIDE), BF16),
            pltpu.VMEM((ROWS, WIDE), F32),
            pltpu.VMEM((ROWS, 256), BF16),
            pltpu.VMEM((ROWS, WIDE), BF16),
            pltpu.VMEM((2, 3072, 256), BF16),
        )
        + tuple(pltpu.VMEM(a.shape, a.dtype) for a in (velocity, own, blk)),
        in_specs=[pl.BlockSpec(memory_space=pltpu.HBM)] * 7,
        out_specs=tuple(vmem_spec() for _ in range(13)),
        scratch_shapes=[
            pltpu.VMEM((3, SIDE, 16, 128), F32),
            pltpu.VMEM((10, 10, BLK, 256), F32),
            pltpu.VMEM((ROWS + 2 * SLAB, 1536), BF16),
            pltpu.VMEM((2, 3072, 256), BF16),
            pltpu.VMEM((ROWS, WIDE), F32),
            pltpu.VMEM((ROWS, WIDE), F32),
            pltpu.VMEM((ROWS, WIDE), BF16),
            pltpu.VMEM((ROWS, WIDE), F32),
            pltpu.VMEM((64, HIDDEN_TILES * 128), F32),
            pltpu.VMEM((64, 1792), F32),
        ]
        + [pltpu.VMEM(a.shape, a.dtype) for a in (target, w1, w2, w3)]
        + [pltpu.SemaphoreType.DMA((7,)), pltpu.VMEM((2, ROWS + 2 * SLAB, 256), BF16)],
        compiler_params=pltpu.CompilerParams(vmem_limit_bytes=40 * 1024 * 1024),
        name="forward",
    )(velocity, target, w1, w2, w3, own, blk)


def run_backward(velocity, own, blk, *kept):
    face = pltpu.VMEM((104, 128), F32)
    return pl.pallas_call(
        backward_kernel,
        out_shape=(pltpu.VMEM((64, 128), F32),) + (face,) * 4,
        in_specs=[vmem_spec()] * 11,
        out_specs=tuple(vmem_spec() for _ in range(5)),
        scratch_shapes=[face] * 4
        + [
            pltpu.VMEM((ROWS + 2 * SLAB, 1536), BF16),
            pltpu.VMEM((ROWS, WIDE), F32),
            pltpu.VMEM((ROWS, WIDE), BF16),
            pltpu.VMEM((2, ROWS + 2 * SLAB, 256), BF16),
        ],
        compiler_params=pltpu.CompilerParams(vmem_limit_bytes=40 * 1024 * 1024),
        name="backward",
    )(velocity, own, blk, *kept)


def flow_kernel(
    vel, eddy, got0, got1, got2, got3, got4, out, rx_a, rx_b, ry_a, ry_b, rz, vx_s, vy_s, visc_s, ez_s
):
    gx_at, gy_at = lax.axis_index("gx"), lax.axis_index("gy")
    gx_odd, gy_odd = gx_at & 1 == 1, gy_at & 1 == 1
    second = core_half(gy_at) == 1
    ry_a[...] = got0[...]
    ry_b[...] = jnp.where(second, got2[...], got1[...])
    rx_a[...] = jnp.where(second, got1[...], got2[...])
    rx_b[...] = jnp.where(second, got3[...], got4[...])
    rz[...] = jnp.where(second, got4[...], got3[...])
    lane = iota((1, 128), 1)

    def sides(odd, a, b, at, rows):
        one, two = a[at : at + rows, :], b[at : at + rows, :]
        return jnp.where(odd, one, two), jnp.where(odd, two, one)

    for c in range(3):
        for x in range(16):
            vy_s[(c * 16 + x) * 32 + 8 : (c * 16 + x) * 32 + 24, :] = vel[c, x]
        for i in range(2):
            below, above = sides(gy_odd, ry_a, ry_b, (c * 2 + i) * 16, 16)
            vy_s[pl.ds(c * 512 + 6 + i, 16, stride=32), :] = below
            vy_s[pl.ds(c * 512 + 24 + i, 16, stride=32), :] = above
            below, above = sides(gx_odd, rx_a, rx_b, (c * 2 + i) * 16, 16)
            vx_s[c, i] = below
            vx_s[c, 2 + i] = above

    zcols = jnp.concatenate([jnp.transpose(rz[t * 8 : t * 8 + 8, :]) for t in range(7)], axis=0)
    coarse = eddy[...]
    e_first, e_last = zcols[768:832, 0:1] / EDDY_SCALE, zcols[768:832, 1:2] / EDDY_SCALE
    ahead = jnp.where(lane == 127, e_first, pltpu.roll(coarse, 127, 1))
    behind = jnp.where(lane == 0, e_last, pltpu.roll(coarse, 1, 1))
    below_x, above_x = (v / EDDY_SCALE for v in sides(gx_odd, rx_a, rx_b, 96, 8))
    below_y, above_y = (v / EDDY_SCALE for v in sides(gy_odd, ry_a, ry_b, 96, 8))

    def put(dst, plane, val):
        dst[pl.ds(plane * 32 + 8, 8, stride=2), :] = val
        dst[pl.ds(plane * 32 + 9, 8, stride=2), :] = val

    put(visc_s, 0, base_visc + below_x)
    put(visc_s, 17, base_visc + above_x)
    for x in range(8):
        for r in range(2):
            plane = 2 * x + 1 + r
            put(visc_s, plane, base_visc + coarse[x * 8 : x * 8 + 8])
            visc_s[plane * 32 + 7 : plane * 32 + 8, :] = base_visc + below_y[x : x + 1]
            visc_s[plane * 32 + 24 : plane * 32 + 25, :] = base_visc + above_y[x : x + 1]
        put(ez_s, 2 * x, base_visc + ahead[x * 8 : x * 8 + 8])
        put(ez_s, 2 * x + 1, base_visc + behind[x * 8 : x * 8 + 8])

    def plane_of(c, x):
        if x < 0:
            return vx_s[c, x + 2]
        if x > 15:
            return vx_s[c, x - 14]
        return vel[c, x]

    for x in range(16):
        vat = (x + 1) * 32
        visc = visc_s[vat + 8 : vat + 24, :]
        faces = (
            (visc_s[vat + 40 : vat + 56, :], visc_s[vat - 24 : vat - 8, :]),
            (visc_s[vat + 9 : vat + 25, :], visc_s[vat + 7 : vat + 23, :]),
            (
                ez_s[(x // 2 * 2) * 32 + 8 : (x // 2 * 2) * 32 + 24, :],
                ez_s[(x // 2 * 2 + 1) * 32 + 8 : (x // 2 * 2 + 1) * 32 + 24, :],
            ),
        )
        faces = [(0.5 * (visc + a), 0.5 * (visc + b)) for a, b in faces]
        wind = [vel[a, x] for a in range(3)]
        for c in range(3):
            u = vel[c, x]
            at = (c * 16 + x) * 32
            zat = (c * 16 + x) * 16
            zc = zcols[zat : zat + 16]
            p1 = jnp.where(lane == 127, zc[:, 0:1], pltpu.roll(u, 127, 1))
            p2 = jnp.where(lane == 127, zc[:, 1:2], jnp.where(lane == 126, zc[:, 0:1], pltpu.roll(u, 126, 1)))
            m1 = jnp.where(lane == 0, zc[:, 3:4], pltpu.roll(u, 1, 1))
            m2 = jnp.where(lane == 0, zc[:, 2:3], jnp.where(lane == 1, zc[:, 3:4], pltpu.roll(u, 2, 1)))
            near = (
                (plane_of(c, x + 1), plane_of(c, x - 1), plane_of(c, x + 2), plane_of(c, x - 2)),
                (
                    vy_s[at + 9 : at + 25, :], vy_s[at + 7 : at + 23, :],
                    vy_s[at + 10 : at + 26, :], vy_s[at + 6 : at + 22, :],
                ),
                (p1, m1, p2, m2),
            )
            advect = None
            diffuse = None
            for a in range(3):
                q1, b1, q2, b2 = near[a]
                slope = (8.0 * (q1 - b1) - (q2 - b2)) * (1.0 / 12.0)
                term = wind[a] * slope
                advect = term if advect is None else advect + term
                flux = faces[a][0] * (q1 - u) - faces[a][1] * (u - b1)
                diffuse = flux if diffuse is None else diffuse + flux
            out[c, x] = u + time_step * (diffuse - advect)


def run_flow(velocity, eddy, *got):
    return pl.pallas_call(
        flow_kernel,
        out_shape=jax.ShapeDtypeStruct(velocity.shape, F32),
        in_specs=[vmem_spec()] * 7,
        out_specs=vmem_spec(),
        scratch_shapes=[
            pltpu.VMEM((104, 128), F32),
            pltpu.VMEM((104, 128), F32),
            pltpu.VMEM((104, 128), F32),
            pltpu.VMEM((104, 128), F32),
            pltpu.VMEM((104, 128), F32),
            pltpu.VMEM((3, 4, 16, 128), F32),
            pltpu.VMEM((3 * 16 * 32, 128), F32),
            pltpu.VMEM((18 * 32, 128), F32),
            pltpu.VMEM((16 * 32, 128), F32),
        ],
        compiler_params=pltpu.CompilerParams(vmem_limit_bytes=32 * 1024 * 1024),
        name="flow",
    )(velocity, eddy, *got)


def finish_kernel(own, blk, mine, other, loss_out, first_out, hidden_out, last_out):
    gx_at, gy_at = lax.axis_index("gx"), lax.axis_index("gy")
    n_z = lax.axis_size("role")
    in_group = gy_at * n_z + lax.axis_index("role")
    second = core_half(gy_at) == 1
    for t in range(HIDDEN_TILES):
        one, two = mine[t * 32 : (t + 1) * 32, :], other[t * 32 : (t + 1) * 32, :]
        top, bottom = jnp.where(second, two, one), jnp.where(second, one, two)
        width = min(128, 27 * CH - t * 128)
        hidden_out[0:32, t * 128 : t * 128 + width] = top[:, :width]
        hidden_out[32:64, t * 128 : t * 128 + width] = bottom[:, :width]
    extra = mine[HIDDEN_TILES * 32 :, :] + other[HIDDEN_TILES * 32 :, :]
    first_out[...] = extra[:, 0:81]
    turned = jnp.transpose(jnp.concatenate([extra, jnp.zeros((64, 128), F32)], axis=0))
    last_out[...] = turned[LAST_COL : LAST_COL + 1, 0:64]
    slots = loss_out.shape[1]
    dev = own[...] * (lax.axis_size("gy") * n_z) + in_group
    listed = dev.shape[1]
    pick = onehot(iota((64, listed), 0) == dev & 63, F32)
    rows = nn(turned[:, 0:64], pick, HIGH)
    rows = jnp.where(iota((128, listed), 0) == LOSS_COL + BLK * (dev >> 6) + blk[...], rows, 0.0)
    found = jnp.sum(rows, axis=0, keepdims=True)
    picked = jnp.zeros((1, slots), F32)
    for g in range(listed // slots):
        picked = jnp.where(gx_at == g, found[:, g * slots : (g + 1) * slots], picked)
    loss_out[...] = picked


def run_finish(own, blk, mine, other, slots):
    f = lambda *s: jax.ShapeDtypeStruct(s, F32)
    return pl.pallas_call(
        finish_kernel,
        out_shape=(f(1, slots), f(64, 81), f(64, 27 * CH), f(1, 64)),
        in_specs=[vmem_spec()] * 4,
        out_specs=tuple(vmem_spec() for _ in range(4)),
        compiler_params=pltpu.CompilerParams(vmem_limit_bytes=32 * 1024 * 1024),
        name="finish",
    )(own, blk, mine, other)


def on_device(velocity, target_visc, w_first, w_hidden, w_last, sample_owner, sample_block):
    n_x, n_y, n_z = lax.axis_size("gx"), lax.axis_size("gy"), lax.axis_size("role")
    trainers = n_x * n_y * n_z
    own = sample_owner.reshape(1, -1)
    blk = sample_block.reshape(1, -1)
    slots = own.shape[1] // n_x

    axes = ("gx", "gy", "role")

    def even_odd(i, count):
        return i ^ 1

    def odd_even(i, count):
        return (i - 1) % count if i % 2 == 0 else (i + 1) % count

    def partner(kind, i, j, r):
        if kind == "x":
            j = odd_even(j, n_y)
        elif kind == "y":
            r = r ^ 1
        elif kind == "z_a":
            i = even_odd(i, n_x)
        else:
            i = odd_even(i, n_x)
        return (i * n_y + j) * n_z + r

    def mixed(kinds):
        pairs = []
        for i in range(n_x):
            for j in range(n_y):
                for r in range(n_z):
                    pairs.append(((i * n_y + j) * n_z + r, partner(kinds[(j ^ (j >> 1)) & 1], i, j, r)))
        return pairs

    core_pairs = [(j, even_odd(j, n_y)) for j in range(n_y)]
    size = TILES * 32

    keep, send, eddy, *kept, velocity, own, blk = run_forward(
        velocity, target_visc, w_first, w_hidden, w_last.reshape(1, CH), own, blk
    )
    half = core_half(lax.axis_index("gy"))
    got = lax.ppermute(send, "gy", core_pairs)
    extra, *halos = run_backward(velocity, own, blk, eddy, *kept)
    total = jnp.concatenate([keep + got[: HIDDEN_TILES * 32], extra], axis=0)
    rims = [got[HIDDEN_TILES * 32 :]]
    halos = [h.astype(F16) for h in halos]

    def widen(values, exps):
        wide = values.astype(F32).reshape(TILES, 32, 128) * jnp.exp2(exps)[:, None, :]
        return wide.reshape(size, 128)

    top = jnp.max(jnp.abs(total.reshape(TILES, 32, 128)), axis=1)
    exps = jnp.clip(jnp.ceil(jnp.log2(jnp.maximum(top, 1e-30))) - 13.0, -110.0, 110.0)
    orders = (("x", "z_a", "y", "z_b"), ("z_a", "x", "z_b", "y"))
    for s in range(4):
        kinds = (orders[0][s], orders[1][s])
        scaled = total.reshape(TILES, 32, 128) * jnp.exp2(-exps)[:, None, :]
        pieces = [scaled.reshape(size, 128).astype(F16), exps.astype(F16)]
        message = jnp.concatenate(pieces + [halos[s]] if s < 3 else pieces, axis=0)
        message = lax.optimization_barrier(message)
        got = lax.ppermute(message, axes, mixed(kinds))
        if s == 1:
            far = lax.ppermute(halos[3], axes, mixed((orders[0][3], orders[1][3])))
        their_exps = got[size : size + TILES].astype(F32)
        mine, theirs = widen(message[:size], exps), widen(got[:size], their_exps)
        if n_x != 4 and "z_b" in kinds:
            theirs = jnp.where(half == kinds.index("z_b"), 0.0, theirs)
        total = mine + theirs
        exps = jnp.maximum(exps, their_exps) + 1.0
        if s < 3:
            rims.append(got[size + 16 :].astype(F32))
        if s == 1:
            total, far = lax.optimization_barrier((total, far))
        if s == 2:
            u_next = run_flow(velocity, eddy, *rims, far.astype(F32))
    total, u_next = lax.optimization_barrier((total, u_next))
    if n_x != 4:
        for bit in range(1, n_x.bit_length() - 1):
            total = total + lax.ppermute(total, "gx", [(i, i ^ (1 << bit)) for i in range(n_x)])
    other = lax.ppermute(total, "gy", core_pairs)

    losses, first, hidden, last = run_finish(own, blk, total, other, slots)
    return (u_next, losses.reshape(1, 1, slots), first, hidden, last.reshape(CH))


def solution(mesh):
    return jax.shard_map(
        on_device,
        mesh=mesh,
        in_specs=(
            P(None, "gx", "gy", "role"),
            P("gx", "gy", "role"),
            P(),
            P(),
            P(),
            P("gy", "role", None, None),
            P("gy", "role", None, None),
        ),
        out_specs=(P(None, "gx", "gy", "role"), P("gy", "role", "gx"), P(), P(), P()),
        check_vma=False,
    )
```

```python
import jax
import jax.numpy as jnp
from jax import lax
from jax.experimental import pallas as pl
from jax.experimental.pallas import tpu as pltpu
from jax.sharding import PartitionSpec as P

F32 = jnp.float32
BF16 = jnp.bfloat16
HIGH = lax.Precision.HIGHEST

SIDE = 8
CELLS = SIDE**3
CH = 64
BLK = 8
ROWS = SIDE * SIDE * BLK
WIDE = SIDE * CH
SLAB = SIDE * BLK
HIDDEN_TILES = 14
TILES = 16
LAST_COL = 81
LOSS_COL = 82

EDDY_SCALE = 2.0**-9
F16 = jnp.float16

base_visc = 0.02
time_step = 0.2


def iota(shape, dim):
    return lax.broadcasted_iota(jnp.int32, shape, dim)


def onehot(cond, dtype=BF16):
    return jnp.where(cond, 1.0, 0.0).astype(dtype)


def sigmoid(v):
    return 0.5 + 0.5 * jnp.tanh(0.5 * v)


def nt(a, b, precision=None):
    return lax.dot_general(a, b, (((1,), (1,)), ((), ())), preferred_element_type=F32, precision=precision)


def tn(a, b, precision=None):
    return lax.dot_general(a, b, (((0,), (0,)), ((), ())), preferred_element_type=F32, precision=precision)


def nn(a, b, precision=None):
    return lax.dot_general(a, b, (((1,), (0,)), ((), ())), preferred_element_type=F32, precision=precision)


def core_half(at):
    return (at ^ (at >> 1)) & 1


def place():
    gx_at, gy_at = lax.axis_index("gx"), lax.axis_index("gy")
    return gx_at, gy_at, core_half(gy_at) == 1


def times_sampled(own, blk, gx_at):
    code = own[...] * BLK + blk[...]
    wanted = gx_at * BLK + iota((BLK, code.shape[1]), 0)
    return jnp.sum(jnp.where(code == wanted, 1.0, 0.0), axis=1, keepdims=True)


def tile_places():
    return [(q, z, h, 2 * q + h) for q in range(2) for z in range(3 * q, 3 * q + 5) for h in range(2)]


def place_row(q, z, k):
    if 4 * q <= z < 4 * q + 4:
        return k * 256 + (z - 4 * q) * 64
    return 2304 + k // 3 * 256 + k % 3 * 64


def exact(a, selector):
    high = a.astype(BF16)
    rest = a - high.astype(F32)
    mid = rest.astype(BF16)
    low = (rest - mid.astype(F32)).astype(BF16)
    return nn(high, selector) + (nn(mid, selector) + nn(low, selector))


def y_face(dst, vel, eddy, high):
    for c in range(3):
        for i in range(2):
            lo = jnp.concatenate([vel[c, x, i : i + 1, :] for x in range(16)], axis=0)
            hi = jnp.concatenate([vel[c, x, 14 + i : 15 + i, :] for x in range(16)], axis=0)
            dst[(c * 2 + i) * 16 : (c * 2 + i + 1) * 16, :] = jnp.where(high, hi, lo)
    dst[96:104, :] = jnp.where(high, eddy[pl.ds(7, 8, stride=8), :], eddy[pl.ds(0, 8, stride=8), :]) * EDDY_SCALE


def diagonal():
    return iota((1, WIDE), 1) >> 6 == iota((SIDE, 1), 0)


def windows(ref, more, q):
    own = [
        ref[dx * SLAB : dx * SLAB + ROWS, j * 512 + q * 256 : j * 512 + (q + 1) * 256]
        for dx in range(3)
        for j in range(3)
    ]
    return jnp.concatenate(own + [more[q, dx * SLAB : dx * SLAB + ROWS, :] for dx in range(3)], axis=1)


def shifted_store(dst_ref, more, x, val):
    zero = jnp.zeros((1, BLK, WIDE), F32)
    lo, hi = (x + 1) * SLAB, (x + 2) * SLAB
    dst_ref[lo:hi, 0:512] = jnp.concatenate([zero, val[:-1]], axis=0).reshape(SLAB, WIDE).astype(BF16)
    dst_ref[lo:hi, 512:1024] = val.reshape(SLAB, WIDE).astype(BF16)
    dst_ref[lo:hi, 1024:1536] = jnp.concatenate([val[1:], zero], axis=0).reshape(SLAB, WIDE).astype(BF16)
    left = iota((SLAB, 128), 1) < 64
    zero = zero[:, :, :128]
    for q in range(2):
        part = val[:, :, 256:384] if q == 0 else val[:, :, 128:256]
        near = [jnp.concatenate([zero, part[:-1]], axis=0), part, jnp.concatenate([part[1:], zero], axis=0)]
        near = [v.reshape(SLAB, 128) for v in near]
        turn = (1,) if q == 0 else (0, 2)
        near = [pltpu.roll(v, 64, 1) if j in turn else v for j, v in enumerate(near)]
        more[q, lo:hi, 0:128] = jnp.where(left, near[0], near[1]).astype(BF16)
        more[q, lo:hi, 128:256] = jnp.where(left, near[2], 0.0).astype(BF16)


def clear_ends(ref, more):
    for at in (0, 9 * SLAB):
        ref[at : at + SLAB, :] = jnp.zeros((SLAB, 1536), BF16)
        for q in range(2):
            more[q, at : at + SLAB, :] = jnp.zeros((SLAB, 256), BF16)


def forward_kernel(
    vel_in, tgt_in, w1_in, w2_in, w3_in, own_in, blk_in,
    keep, send, eddy_out, loss_out, dl_out, ah_s, slope1_s, i1_s, dh_s, tb_s, vel, own, blk,
    pool_s, fp_s, a_s, tt_s, pre_s, slope2_s, dw_s, big_s, gh_s, w2_s,
    tgt, w1, w2, w3, sems, ea_s,
):
    pairs = ((w2_in, w2), (vel_in, vel), (tgt_in, tgt), (w1_in, w1), (w3_in, w3), (own_in, own), (blk_in, blk))
    copies = [pltpu.make_async_copy(src, dst, sems.at[n]) for n, (src, dst) in enumerate(pairs)]
    for copy in copies:
        copy.start()
    gx_at, gy_at, second = place()
    trainers = lax.axis_size("gx") * lax.axis_size("gy") * lax.axis_size("role")

    fp_s[...] = jnp.zeros(fp_s.shape, F32)
    clear_ends(a_s, ea_s)
    w2_s[:, 1664:1792] = jnp.zeros((64, 128), F32)
    zero_tile = jnp.zeros((64, 128), BF16)
    for q in range(2):
        for dx in range(3):
            for ref in (tt_s, tb_s):
                ref[q, 2304 + dx * 256 + 192 : 2304 + (dx + 1) * 256, :] = jnp.zeros((64, 256), BF16)
    for q, z, h, m in tile_places():
        for k in range(9):
            at, cols = place_row(q, z, k), slice(h * 128, (h + 1) * 128)
            if not -1 <= z - 2 * m <= 2:
                tt_s[q, at : at + 64, cols] = zero_tile
                tb_s[q, at : at + 64, cols] = zero_tile
    for copy in copies:
        copy.wait()

    for c in range(3):
        for x in range(SIDE):
            both = vel[c, 2 * x] + vel[c, 2 * x + 1]
            pool_s[c, x] = both
    rows = []
    for c in range(3):
        cols = []
        for x in range(SIDE):
            cols.append(pool_s[c, x, pl.ds(0, 8, stride=2), :] + pool_s[c, x, pl.ds(1, 8, stride=2), :])
        rows.append(jnp.concatenate(cols, axis=0))
    pooled = jnp.concatenate(rows, axis=0)
    zpool = jnp.where(iota((128, 1), 0) >> 1 == iota((1, 64), 1), 0.125, 0.0).astype(BF16)
    filt = exact(pooled, zpool).astype(BF16)
    tgt_rows = tgt[...].reshape(64, 64)
    zsel = jnp.concatenate([filt[0:64], filt[64:128], filt[128:192], tgt_rows], axis=1)
    spread = onehot(iota((ROWS, 1), 0) >> 3 == iota((1, 64), 1))
    by_block = nn(spread, zsel)
    mine = (iota((1, 256), 1) & 63) >> 3 == iota((ROWS, 1), 0) & 7
    by_block = jnp.where(mine, by_block, 0.0).astype(BF16)
    lane_in = iota((1, 256), 1)
    lane_off = lax.div(lane_in, 24)
    lane_cz = lane_in - lane_off * 24
    src = iota((256, 1), 0)
    pick = onehot(jnp.where(lane_in < 216, lane_cz, -1) == (src >> 6) * 8 + (src & 7))
    cells = nn(by_block, pick)
    pick_t = onehot(jnp.where(src >= 192, src & 7, -1) == iota((1, 24), 1) & 7)
    target = nn(by_block, pick_t)

    fp_s[1:9, 1:9] = cells.reshape(SIDE, SIDE, BLK, 256)
    for half, held in ((0, range(6)), (1, range(5, 9))):
        lanes = slice(half * 128, (half + 1) * 128)
        group = lax.div(iota((1, 1, 1, 128), 3) + half * 128, 24)
        for x in range(SIDE):
            acc = jnp.zeros((1, SIDE, BLK, 128), F32)
            for k in held:
                part = fp_s[x + k // 3 : x + k // 3 + 1, k % 3 : k % 3 + SIDE, :, lanes]
                acc = jnp.where(group == k, part, acc)
            i1_s[x * SLAB : (x + 1) * SLAB, lanes] = acc.reshape(SLAB, 128).astype(BF16)

    j_at = iota((81, 1), 0)
    j_off, j_dz, j_c = lax.div(j_at, 9), lax.rem(lax.div(j_at, 3), 3) - 1, lax.rem(j_at, 3)
    lane_key = jnp.where(lane_in < 216, lane_off * 4 + (lane_cz >> 3), -1)
    same = lane_key == j_off * 4 + j_c
    w1v = w1[...]
    by_dz = [nn(w1v, onehot(jnp.where(same, j_dz, 9) == dz)) for dz in (-1, 0, 1)]
    z_in = jnp.broadcast_to(lane_in & 7, (CH, 256))
    t1 = []
    for z in range(SIDE):
        rows = jnp.where(z_in == z - 1, by_dz[0], jnp.where(z_in == z, by_dz[1], 0.0))
        t1.append(jnp.where(z_in == z + 1, by_dz[2], rows).astype(BF16))
    t1 = jnp.concatenate(t1, axis=0)
    pre_s[...] = nt(i1_s[...], t1)

    left = iota((64, 128), 1) < 64
    w2_s[:, 0:1728] = w2[...].astype(F32)
    w2t = jnp.concatenate(
        [
            jnp.transpose(jnp.concatenate([w2_s[:, t * 128 : (t + 1) * 128]] * 2, axis=0))
            for t in range(14)
        ],
        axis=0,
    )
    for k in range(9):
        base = (192 * k) // 128 * 128
        one, two = w2_s[:, base : base + 128], w2_s[:, base + 128 : base + 256]
        one_r, two_r = pltpu.roll(one, 64, 1), pltpu.roll(two, 64, 1)
        if k % 2 == 0:
            low, high = (one, one_r, two), (one_r, one, two_r)
        else:
            low, high = (one_r, two, two_r), (one, two_r, two)
        low, high = (0.0,) + low, high + (0.0,)
        tiles = {d: jnp.where(left, low[d + 2], high[d + 2]).astype(BF16) for d in (-2, -1, 0, 1)}
        kb = 8 - k
        turned = {dz: w2t[(3 * k + dz + 1) * 64 : (3 * k + dz + 2) * 64] for dz in (-1, 0, 1)}
        turned[-2] = turned[2] = jnp.zeros((64, 128), F32)
        forward = {d: jnp.where(left, turned[d], turned[d - 1]).astype(BF16) for d in (-1, 0, 1, 2)}
        for q, z, h, m in tile_places():
            at, cols = place_row(q, z, k), slice(h * 128, (h + 1) * 128)
            if z - 2 * m in forward:
                tt_s[q, at : at + 64, cols] = forward[z - 2 * m]
            d = 2 * m - z
            at = place_row(q, z, kb)
            if d in tiles:
                tb_s[q, at : at + 64, cols] = tiles[d]

    for x in range(SIDE):
        pre = pre_s[x * SLAB : (x + 1) * SLAB, :]
        sig = sigmoid(pre)
        slope1_s[x * SLAB : (x + 1) * SLAB, :] = sig * (1.0 + pre * (1.0 - sig))
        shifted_store(a_s, ea_s, x, (pre * sig).reshape(SIDE, BLK, WIDE))

    for q in range(2):
        pre_s[:, q * 256 : (q + 1) * 256] = nn(windows(a_s, ea_s, q), tt_s[q])
    for x in range(SIDE):
        pre = pre_s[x * SLAB : (x + 1) * SLAB, :]
        sig = sigmoid(pre)
        slope2_s[x * SLAB : (x + 1) * SLAB, :] = sig * (1.0 + pre * (1.0 - sig))
        ah_s[x * SLAB : (x + 1) * SLAB, :] = (pre * sig).astype(BF16)

    tile8 = onehot(iota((64, 1), 0) == iota((1, WIDE), 1) & 63)
    w3_wide = nn(w3[...], tile8)
    diag = diagonal()
    last = jnp.where(diag, w3_wide, 0.0).astype(BF16)
    last3 = jnp.concatenate([jnp.where(diag, w3_wide, 0.0)] * 3, axis=0).astype(BF16)
    logits = nt(ah_s[...], last3)
    eddy = 0.5 * (jnp.maximum(logits, 0.0) + jnp.log1p(jnp.exp(-jnp.abs(logits))))
    error = eddy - target
    lane24 = iota((1, 24), 1)
    squares = jnp.where(lane24 < SIDE, error * error, 0.0)
    losses = jnp.sum(jnp.sum(squares.reshape(64, BLK, 24), axis=0), axis=1, keepdims=True) / CELLS
    d_logit = (error * sigmoid(logits) / (trainers * CELLS)).astype(BF16)

    zrep = onehot(iota((24, 1), 0) & 7 == (iota((1, 128), 1) & 15) >> 1)
    e_high = eddy.astype(BF16).astype(F32)
    e_mid = (eddy - e_high).astype(BF16).astype(F32)
    e_parts = jnp.where(lane24 < 8, e_high, jnp.where(lane24 < 16, e_mid, eddy - e_high - e_mid))
    fine = nn(e_parts.astype(BF16), zrep)
    fine = jnp.where(iota((1, 128), 1) >> 4 == iota((ROWS, 1), 0) & 7, fine, 0.0)
    fine = jnp.sum(fine.reshape(64, BLK, 128), axis=1)
    eddy_out[...] = fine
    y_face(send.at[HIDDEN_TILES * 32 : HIDDEN_TILES * 32 + 104], vel, eddy_out, gy_at & 1 == 0)
    loss_out[...] = jnp.broadcast_to(losses, (BLK, 128))
    dl_out[...] = d_logit.astype(F32)[:, 0:SIDE]

    count = times_sampled(own, blk, gx_at)
    big_s[:, 0:512] = nn(d_logit, jnp.concatenate([last.astype(F32), jnp.zeros((16, WIDE), F32)], axis=0).astype(BF16))
    for x in range(SIDE):
        d_hid = big_s[x * SLAB : (x + 1) * SLAB, 0:512] * slope2_s[x * SLAB : (x + 1) * SLAB, :]
        d_hid = d_hid.astype(BF16)
        dh_s[x * SLAB : (x + 1) * SLAB, :] = d_hid
        d_hid = d_hid.astype(F32).reshape(SIDE, BLK, WIDE)
        dw_s[x * SLAB : (x + 1) * SLAB, :] = (d_hid * count[None]).reshape(SLAB, WIDE).astype(BF16)
    dwt = jnp.transpose(dw_s[...])

    sums = {}
    for p in range(4):
        first, last_z = max(2 * p - 1, 0), min(2 * p + 2, SIDE - 1)
        shifts = [
            a_s[dx * SLAB : dx * SLAB + ROWS, j * 512 + p * 128 : j * 512 + (p + 1) * 128]
            for dx in range(3)
            for j in range(3)
        ]
        found = nn(dwt[first * 64 : (last_z + 1) * 64], jnp.concatenate(shifts, axis=1))
        for z in range(first, last_z + 1):
            part = found[(z - first) * 64 : (z - first + 1) * 64]
            m = z - 2 * p
            sums[m] = part if m not in sums else sums[m] + part
    low_half = iota((64, 128), 1) < 64
    held = None
    for k in range(9):
        for dz in (-1, 0, 1):
            low, high = (sums[m][:, k * 128 : (k + 1) * 128] for m in (-dz, 1 - dz))
            at = (k * 3 + dz + 1) * 64
            if at % 128:
                gh_s[:, at - 64 : at + 64] = jnp.where(low_half, held, high + pltpu.roll(low, 64, 1))
            else:
                held = low + pltpu.roll(high, 64, 1)
    gh_s[:, 1664:1792] = jnp.where(low_half, held, 0.0)

    for t in range(HIDDEN_TILES):
        top, bottom = (gh_s[r : r + 32, t * 128 : (t + 1) * 128] for r in (0, 32))
        keep[t * 32 : (t + 1) * 32, :] = jnp.where(second, bottom, top)
        send[t * 32 : (t + 1) * 32, :] = jnp.where(second, top, bottom)


def backward_kernel(
    vel, own, blk, eddy, losses, dl_in, ah_s, slope1_s, i1_s, dh_s, tb_s,
    extra_out, halo1, halo2, halo3, halo4, hx_a, hx_b, hy_b, hz, d_s, pre_s, dw_s, ed_s,
):
    gx_at, gy_at, second = place()
    gx_odd, gy_odd = gx_at & 1 == 1, gy_at & 1 == 1
    dev = (gx_at * lax.axis_size("gy") + gy_at) * lax.axis_size("role") + lax.axis_index("role")
    count = times_sampled(own, blk, gx_at)

    clear_ends(d_s, ed_s)
    for x in range(SIDE):
        d_hid = dh_s[x * SLAB : (x + 1) * SLAB, :].astype(F32)
        shifted_store(d_s, ed_s, x, d_hid.reshape(SIDE, BLK, WIDE))

    for c in range(3):
        for i in range(2):
            lo, hi = vel[c, i], vel[c, 14 + i]
            at = (c * 2 + i) * 16
            hx_a[at : at + 16, :] = jnp.where(gx_odd, lo, hi)
            hx_b[at : at + 16, :] = jnp.where(gx_odd, hi, lo)
    fine = eddy[...]
    small = fine * EDDY_SCALE
    hx_a[96:104, :] = jnp.where(gx_odd, small[0:8], small[56:64])
    hx_b[96:104, :] = jnp.where(gx_odd, small[56:64], small[0:8])
    y_face(hy_b, vel, eddy, gy_odd)
    vt = jnp.transpose(vel[...].reshape(768, 128))
    et = jnp.transpose(jnp.concatenate([small, jnp.zeros((64, 128), F32)], axis=0))
    hz[...] = jnp.zeros(hz.shape, F32)
    for t in range(6):
        hz[t * 8 : t * 8 + 2, :] = vt[0:2, t * 128 : (t + 1) * 128]
        hz[t * 8 + 2 : t * 8 + 4, :] = vt[126:128, t * 128 : (t + 1) * 128]
    hz[48:49, :] = et[0:1]
    hz[49:50, :] = et[127:128]
    halo1[...] = jnp.where(second, hx_a[...], hy_b[...])
    halo2[...] = jnp.where(second, hy_b[...], hx_a[...])
    halo3[...] = jnp.where(second, hx_b[...], hz[...])
    halo4[...] = jnp.where(second, hz[...], hx_b[...])

    for q in range(2):
        pre_s[:, q * 256 : (q + 1) * 256] = nn(windows(d_s, ed_s, q), tb_s[q])
    for x in range(SIDE):
        rows = slice(x * SLAB, (x + 1) * SLAB)
        d_first = (pre_s[rows, :] * slope1_s[rows, :]).astype(BF16).astype(F32)
        dw_s[rows, :] = (d_first.reshape(SIDE, BLK, WIDE) * count[None]).reshape(SLAB, WIDE).astype(BF16)
    g1 = nn(jnp.transpose(dw_s[...]), i1_s[...])
    z_in = iota((1, 256), 1) & 7
    parts = []
    for dz in (-1, 0, 1):
        tot = jnp.zeros((64, 256), F32)
        for z in range(SIDE):
            if 0 <= z + dz < SIDE:
                tot = tot + jnp.where(z_in == z + dz, g1[z * 64 : (z + 1) * 64], 0.0)
        parts.append(tot)
    r_at = iota((768, 1), 0)
    c_at = iota((1, 128), 1)
    r_lane = r_at & 255
    r_off = lax.div(r_lane, 24)
    r_col = (r_off * 3 + (r_at >> 8)) * 3 + ((r_lane - r_off * 24) >> 3)
    fold = onehot(jnp.where(r_lane < 216, r_col, -1) == c_at)
    g_first = exact(jnp.concatenate(parts, axis=1), fold)

    count_rows = jnp.broadcast_to(count.reshape(1, BLK, 1), (64, BLK, 1)).reshape(ROWS, 1)
    dlw = dl_in[...] * count_rows
    dl_hi = dlw.astype(BF16)
    dl_lo = (dlw - dl_hi.astype(F32)).astype(BF16)
    ah = ah_s[...]
    gl = tn(dl_hi, ah) + tn(dl_lo, ah)
    gl = jnp.where(diagonal(), gl, 0.0)
    gl = jnp.sum(gl, axis=0, keepdims=True)
    gl = gl[:, 0:128] + gl[:, 128:256] + gl[:, 256:384] + gl[:, 384:512]
    at_lane = iota((1, 128), 1) & 63 == iota((64, 1), 0)
    g_last = jnp.sum(jnp.where(at_lane, gl, 0.0), axis=1, keepdims=True)

    lane8 = iota((BLK, 128), 1)
    loss_row = jnp.where(lane8 - (LOSS_COL + BLK * (dev >> 6)) == iota((BLK, 128), 0), losses[...], 0.0)
    loss_row = jnp.sum(loss_row, axis=0, keepdims=True)
    lane = iota((64, 128), 1)
    extra = jnp.where(lane == LAST_COL, g_last, g_first)
    extra = extra + jnp.where(iota((64, 128), 0) == dev & 63, loss_row, 0.0)

    extra_out[...] = extra


def vmem_spec():
    return pl.BlockSpec(memory_space=pltpu.VMEM)


def run_forward(*given):
    velocity, target, w1, w2, w3, own, blk = (pltpu.with_memory_space_constraint(a, pltpu.HBM) for a in given)
    half = pltpu.VMEM((HIDDEN_TILES * 32, 128), F32)
    return pl.pallas_call(
        forward_kernel,
        out_shape=(
            half,
            pltpu.VMEM((HIDDEN_TILES * 32 + 104, 128), F32),
            pltpu.VMEM((64, 128), F32),
            pltpu.VMEM((BLK, 128), F32),
            pltpu.VMEM((ROWS, SIDE), F32),
            pltpu.VMEM((ROWS, WIDE), BF16),
            pltpu.VMEM((ROWS, WIDE), F32),
            pltpu.VMEM((ROWS, 256), BF16),
            pltpu.VMEM((ROWS, WIDE), BF16),
            pltpu.VMEM((2, 3072, 256), BF16),
        )
        + tuple(pltpu.VMEM(a.shape, a.dtype) for a in (velocity, own, blk)),
        in_specs=[pl.BlockSpec(memory_space=pltpu.HBM)] * 7,
        out_specs=tuple(vmem_spec() for _ in range(13)),
        scratch_shapes=[
            pltpu.VMEM((3, SIDE, 16, 128), F32),
            pltpu.VMEM((10, 10, BLK, 256), F32),
            pltpu.VMEM((ROWS + 2 * SLAB, 1536), BF16),
            pltpu.VMEM((2, 3072, 256), BF16),
            pltpu.VMEM((ROWS, WIDE), F32),
            pltpu.VMEM((ROWS, WIDE), F32),
            pltpu.VMEM((ROWS, WIDE), BF16),
            pltpu.VMEM((ROWS, WIDE), F32),
            pltpu.VMEM((64, HIDDEN_TILES * 128), F32),
            pltpu.VMEM((64, 1792), F32),
        ]
        + [pltpu.VMEM(a.shape, a.dtype) for a in (target, w1, w2, w3)]
        + [pltpu.SemaphoreType.DMA((7,)), pltpu.VMEM((2, ROWS + 2 * SLAB, 256), BF16)],
        compiler_params=pltpu.CompilerParams(vmem_limit_bytes=40 * 1024 * 1024),
        name="forward",
    )(velocity, target, w1, w2, w3, own, blk)


def run_backward(velocity, own, blk, *kept):
    face = pltpu.VMEM((104, 128), F32)
    return pl.pallas_call(
        backward_kernel,
        out_shape=(pltpu.VMEM((64, 128), F32),) + (face,) * 4,
        in_specs=[vmem_spec()] * 11,
        out_specs=tuple(vmem_spec() for _ in range(5)),
        scratch_shapes=[face] * 4
        + [
            pltpu.VMEM((ROWS + 2 * SLAB, 1536), BF16),
            pltpu.VMEM((ROWS, WIDE), F32),
            pltpu.VMEM((ROWS, WIDE), BF16),
            pltpu.VMEM((2, ROWS + 2 * SLAB, 256), BF16),
        ],
        compiler_params=pltpu.CompilerParams(vmem_limit_bytes=40 * 1024 * 1024),
        name="backward",
    )(velocity, own, blk, *kept)


def flow_kernel(
    vel, eddy, got0, got1, got2, got3, got4, out, rx_a, rx_b, ry_a, ry_b, rz, vx_s, vy_s, visc_s, ez_s
):
    gx_at, gy_at = lax.axis_index("gx"), lax.axis_index("gy")
    gx_odd, gy_odd = gx_at & 1 == 1, gy_at & 1 == 1
    second = core_half(gy_at) == 1
    ry_a[...] = got0[...]
    ry_b[...] = jnp.where(second, got2[...], got1[...])
    rx_a[...] = jnp.where(second, got1[...], got2[...])
    rx_b[...] = jnp.where(second, got3[...], got4[...])
    rz[...] = jnp.where(second, got4[...], got3[...])
    lane = iota((1, 128), 1)

    def sides(odd, a, b, at, rows):
        one, two = a[at : at + rows, :], b[at : at + rows, :]
        return jnp.where(odd, one, two), jnp.where(odd, two, one)

    for c in range(3):
        for x in range(16):
            vy_s[(c * 16 + x) * 32 + 8 : (c * 16 + x) * 32 + 24, :] = vel[c, x]
        for i in range(2):
            below, above = sides(gy_odd, ry_a, ry_b, (c * 2 + i) * 16, 16)
            vy_s[pl.ds(c * 512 + 6 + i, 16, stride=32), :] = below
            vy_s[pl.ds(c * 512 + 24 + i, 16, stride=32), :] = above
            below, above = sides(gx_odd, rx_a, rx_b, (c * 2 + i) * 16, 16)
            vx_s[c, i] = below
            vx_s[c, 2 + i] = above

    zcols = jnp.concatenate([jnp.transpose(rz[t * 8 : t * 8 + 8, :]) for t in range(7)], axis=0)
    coarse = eddy[...]
    e_first, e_last = zcols[768:832, 0:1] / EDDY_SCALE, zcols[768:832, 1:2] / EDDY_SCALE
    ahead = jnp.where(lane == 127, e_first, pltpu.roll(coarse, 127, 1))
    behind = jnp.where(lane == 0, e_last, pltpu.roll(coarse, 1, 1))
    below_x, above_x = (v / EDDY_SCALE for v in sides(gx_odd, rx_a, rx_b, 96, 8))
    below_y, above_y = (v / EDDY_SCALE for v in sides(gy_odd, ry_a, ry_b, 96, 8))

    def put(dst, plane, val):
        dst[pl.ds(plane * 32 + 8, 8, stride=2), :] = val
        dst[pl.ds(plane * 32 + 9, 8, stride=2), :] = val

    put(visc_s, 0, base_visc + below_x)
    put(visc_s, 17, base_visc + above_x)
    for x in range(8):
        for r in range(2):
            plane = 2 * x + 1 + r
            put(visc_s, plane, base_visc + coarse[x * 8 : x * 8 + 8])
            visc_s[plane * 32 + 7 : plane * 32 + 8, :] = base_visc + below_y[x : x + 1]
            visc_s[plane * 32 + 24 : plane * 32 + 25, :] = base_visc + above_y[x : x + 1]
        put(ez_s, 2 * x, base_visc + ahead[x * 8 : x * 8 + 8])
        put(ez_s, 2 * x + 1, base_visc + behind[x * 8 : x * 8 + 8])

    def plane_of(c, x):
        if x < 0:
            return vx_s[c, x + 2]
        if x > 15:
            return vx_s[c, x - 14]
        return vel[c, x]

    for x in range(16):
        vat = (x + 1) * 32
        visc = visc_s[vat + 8 : vat + 24, :]
        faces = (
            (visc_s[vat + 40 : vat + 56, :], visc_s[vat - 24 : vat - 8, :]),
            (visc_s[vat + 9 : vat + 25, :], visc_s[vat + 7 : vat + 23, :]),
            (
                ez_s[(x // 2 * 2) * 32 + 8 : (x // 2 * 2) * 32 + 24, :],
                ez_s[(x // 2 * 2 + 1) * 32 + 8 : (x // 2 * 2 + 1) * 32 + 24, :],
            ),
        )
        faces = [(0.5 * (visc + a), 0.5 * (visc + b)) for a, b in faces]
        wind = [vel[a, x] for a in range(3)]
        for c in range(3):
            u = vel[c, x]
            at = (c * 16 + x) * 32
            zat = (c * 16 + x) * 16
            zc = zcols[zat : zat + 16]
            p1 = jnp.where(lane == 127, zc[:, 0:1], pltpu.roll(u, 127, 1))
            p2 = jnp.where(lane == 127, zc[:, 1:2], jnp.where(lane == 126, zc[:, 0:1], pltpu.roll(u, 126, 1)))
            m1 = jnp.where(lane == 0, zc[:, 3:4], pltpu.roll(u, 1, 1))
            m2 = jnp.where(lane == 0, zc[:, 2:3], jnp.where(lane == 1, zc[:, 3:4], pltpu.roll(u, 2, 1)))
            near = (
                (plane_of(c, x + 1), plane_of(c, x - 1), plane_of(c, x + 2), plane_of(c, x - 2)),
                (
                    vy_s[at + 9 : at + 25, :], vy_s[at + 7 : at + 23, :],
                    vy_s[at + 10 : at + 26, :], vy_s[at + 6 : at + 22, :],
                ),
                (p1, m1, p2, m2),
            )
            advect = None
            diffuse = None
            for a in range(3):
                q1, b1, q2, b2 = near[a]
                slope = (8.0 * (q1 - b1) - (q2 - b2)) * (1.0 / 12.0)
                term = wind[a] * slope
                advect = term if advect is None else advect + term
                flux = faces[a][0] * (q1 - u) - faces[a][1] * (u - b1)
                diffuse = flux if diffuse is None else diffuse + flux
            out[c, x] = u + time_step * (diffuse - advect)


def run_flow(velocity, eddy, *got):
    return pl.pallas_call(
        flow_kernel,
        out_shape=jax.ShapeDtypeStruct(velocity.shape, F32),
        in_specs=[vmem_spec()] * 7,
        out_specs=vmem_spec(),
        scratch_shapes=[
            pltpu.VMEM((104, 128), F32),
            pltpu.VMEM((104, 128), F32),
            pltpu.VMEM((104, 128), F32),
            pltpu.VMEM((104, 128), F32),
            pltpu.VMEM((104, 128), F32),
            pltpu.VMEM((3, 4, 16, 128), F32),
            pltpu.VMEM((3 * 16 * 32, 128), F32),
            pltpu.VMEM((18 * 32, 128), F32),
            pltpu.VMEM((16 * 32, 128), F32),
        ],
        compiler_params=pltpu.CompilerParams(vmem_limit_bytes=32 * 1024 * 1024),
        name="flow",
    )(velocity, eddy, *got)


def finish_kernel(own, blk, mine, other, loss_out, first_out, hidden_out, last_out, hid_s, sem):
    gx_at, gy_at = lax.axis_index("gx"), lax.axis_index("gy")
    n_z = lax.axis_size("role")
    in_group = gy_at * n_z + lax.axis_index("role")
    second = core_half(gy_at) == 1
    for t in range(HIDDEN_TILES):
        one, two = mine[t * 32 : (t + 1) * 32, :], other[t * 32 : (t + 1) * 32, :]
        top, bottom = jnp.where(second, two, one), jnp.where(second, one, two)
        width = min(128, 27 * CH - t * 128)
        hid_s[0:32, t * 128 : t * 128 + width] = top[:, :width]
        hid_s[32:64, t * 128 : t * 128 + width] = bottom[:, :width]
    write = pltpu.make_async_copy(hid_s, hidden_out, sem)
    write.start()
    extra = mine[HIDDEN_TILES * 32 :, :] + other[HIDDEN_TILES * 32 :, :]
    first_out[...] = extra[:, 0:81]
    turned = jnp.transpose(jnp.concatenate([extra, jnp.zeros((64, 128), F32)], axis=0))
    last_out[...] = turned[LAST_COL : LAST_COL + 1, 0:64]
    slots = loss_out.shape[1]
    dev = own[...] * (lax.axis_size("gy") * n_z) + in_group
    listed = dev.shape[1]
    pick = onehot(iota((64, listed), 0) == dev & 63)
    rows = exact(turned[:, 0:64], pick)
    rows = jnp.where(iota((128, listed), 0) == LOSS_COL + BLK * (dev >> 6) + blk[...], rows, 0.0)
    found = jnp.sum(rows, axis=0, keepdims=True)
    picked = jnp.zeros((1, slots), F32)
    for g in range(listed // slots):
        picked = jnp.where(gx_at == g, found[:, g * slots : (g + 1) * slots], picked)
    loss_out[...] = picked
    write.wait()


def run_finish(own, blk, mine, other, slots):
    f = lambda *s: jax.ShapeDtypeStruct(s, F32)
    return pl.pallas_call(
        finish_kernel,
        out_shape=(f(1, slots), f(64, 81), f(64, 27 * CH), f(1, 64)),
        in_specs=[vmem_spec()] * 4,
        out_specs=(vmem_spec(), vmem_spec(), pl.BlockSpec(memory_space=pl.ANY), vmem_spec()),
        scratch_shapes=[pltpu.VMEM((64, 27 * CH), F32), pltpu.SemaphoreType.DMA],
        compiler_params=pltpu.CompilerParams(vmem_limit_bytes=32 * 1024 * 1024),
        name="finish",
    )(own, blk, mine, other)


def on_device(velocity, target_visc, w_first, w_hidden, w_last, sample_owner, sample_block):
    n_x, n_y, n_z = lax.axis_size("gx"), lax.axis_size("gy"), lax.axis_size("role")
    trainers = n_x * n_y * n_z
    own = sample_owner.reshape(1, -1)
    blk = sample_block.reshape(1, -1)
    slots = own.shape[1] // n_x

    axes = ("gx", "gy", "role")

    def even_odd(i, count):
        return i ^ 1

    def odd_even(i, count):
        return (i - 1) % count if i % 2 == 0 else (i + 1) % count

    def partner(kind, i, j, r):
        if kind == "x":
            j = odd_even(j, n_y)
        elif kind == "y":
            r = r ^ 1
        elif kind == "z_a":
            i = even_odd(i, n_x)
        else:
            i = odd_even(i, n_x)
        return (i * n_y + j) * n_z + r

    def mixed(kinds):
        pairs = []
        for i in range(n_x):
            for j in range(n_y):
                for r in range(n_z):
                    pairs.append(((i * n_y + j) * n_z + r, partner(kinds[(j ^ (j >> 1)) & 1], i, j, r)))
        return pairs

    core_pairs = [(j, even_odd(j, n_y)) for j in range(n_y)]
    size = TILES * 32

    keep, send, eddy, *kept, velocity, own, blk = run_forward(
        velocity, target_visc, w_first, w_hidden, w_last.reshape(1, CH), own, blk
    )
    half = core_half(lax.axis_index("gy"))
    got = lax.ppermute(send, "gy", core_pairs)
    extra, *halos = run_backward(velocity, own, blk, eddy, *kept)
    total = jnp.concatenate([keep + got[: HIDDEN_TILES * 32], extra], axis=0)
    rims = [got[HIDDEN_TILES * 32 :]]
    halos = [h.astype(F16) for h in halos]

    def widen(values, exps):
        wide = values.astype(F32).reshape(TILES, 32, 128) * jnp.exp2(exps)[:, None, :]
        return wide.reshape(size, 128)

    top = jnp.max(jnp.abs(total.reshape(TILES, 32, 128)), axis=1)
    exps = jnp.clip(jnp.ceil(jnp.log2(jnp.maximum(top, 1e-30))) - 13.0, -110.0, 110.0)
    orders = (("x", "z_a", "y", "z_b"), ("z_a", "x", "z_b", "y"))
    for s in range(4):
        kinds = (orders[0][s], orders[1][s])
        scaled = total.reshape(TILES, 32, 128) * jnp.exp2(-exps)[:, None, :]
        pieces = [scaled.reshape(size, 128).astype(F16), exps.astype(F16)]
        message = jnp.concatenate(pieces + [halos[s]] if s < 3 else pieces, axis=0)
        message = lax.optimization_barrier(message)
        got = lax.ppermute(message, axes, mixed(kinds))
        if s == 1:
            far = lax.ppermute(halos[3], axes, mixed((orders[0][3], orders[1][3])))
        their_exps = got[size : size + TILES].astype(F32)
        mine, theirs = widen(message[:size], exps), widen(got[:size], their_exps)
        if n_x != 4 and "z_b" in kinds:
            theirs = jnp.where(half == kinds.index("z_b"), 0.0, theirs)
        total = mine + theirs
        exps = jnp.maximum(exps, their_exps) + 1.0
        if s < 3:
            rims.append(got[size + 16 :].astype(F32))
        if s == 1:
            total, far = lax.optimization_barrier((total, far))
        if s == 2:
            u_next = run_flow(velocity, eddy, *rims, far.astype(F32))
    total, u_next = lax.optimization_barrier((total, u_next))
    if n_x != 4:
        for bit in range(1, n_x.bit_length() - 1):
            total = total + lax.ppermute(total, "gx", [(i, i ^ (1 << bit)) for i in range(n_x)])
    other = lax.ppermute(total, "gy", core_pairs)

    losses, first, hidden, last = run_finish(own, blk, total, other, slots)
    return (u_next, losses.reshape(1, 1, slots), first, hidden, last.reshape(CH))


def solution(mesh):
    return jax.shard_map(
        on_device,
        mesh=mesh,
        in_specs=(
            P(None, "gx", "gy", "role"),
            P("gx", "gy", "role"),
            P(),
            P(),
            P(),
            P("gy", "role", None, None),
            P("gy", "role", None, None),
        ),
        out_specs=(P(None, "gx", "gy", "role"), P("gy", "role", "gx"), P(), P(), P()),
        check_vma=False,
    )
```

```python
import jax
import jax.numpy as jnp
from jax import lax
from jax.experimental import pallas as pl
from jax.experimental.pallas import tpu as pltpu
from jax.sharding import PartitionSpec as P

F32 = jnp.float32
BF16 = jnp.bfloat16

SIDE = 8
CELLS = SIDE**3
CH = 64
BLK = 8
ROWS = SIDE * SIDE * BLK
WIDE = SIDE * CH
SLAB = SIDE * BLK
HIDDEN_TILES = 14
TILES = 16
LAST_COL = 81
LOSS_COL = 82

EDDY_SCALE = 2.0**-9
F16 = jnp.float16

base_visc = 0.02
time_step = 0.2


def iota(shape, dim):
    return lax.broadcasted_iota(jnp.int32, shape, dim)


def onehot(cond, dtype=BF16):
    return jnp.where(cond, 1.0, 0.0).astype(dtype)


def sigmoid(v):
    return 0.5 + 0.5 * jnp.tanh(0.5 * v)


def nt(a, b):
    return lax.dot_general(a, b, (((1,), (1,)), ((), ())), preferred_element_type=F32)


def tn(a, b):
    return lax.dot_general(a, b, (((0,), (0,)), ((), ())), preferred_element_type=F32)


def nn(a, b):
    return lax.dot_general(a, b, (((1,), (0,)), ((), ())), preferred_element_type=F32)


def core_half(at):
    return (at ^ (at >> 1)) & 1


def place():
    gx_at, gy_at = lax.axis_index("gx"), lax.axis_index("gy")
    return gx_at, gy_at, core_half(gy_at) == 1


def times_sampled(own, blk, gx_at):
    code = own[...] * BLK + blk[...]
    wanted = gx_at * BLK + iota((BLK, code.shape[1]), 0)
    return jnp.sum(jnp.where(code == wanted, 1.0, 0.0), axis=1, keepdims=True)


def tile_places():
    return [(q, z, h, 2 * q + h) for q in range(2) for z in range(3 * q, 3 * q + 5) for h in range(2)]


def place_row(q, z, k):
    if 4 * q <= z < 4 * q + 4:
        return k * 256 + (z - 4 * q) * 64
    return 2304 + k // 3 * 256 + k % 3 * 64


def exact(a, selector):
    high = a.astype(BF16)
    rest = a - high.astype(F32)
    mid = rest.astype(BF16)
    low = (rest - mid.astype(F32)).astype(BF16)
    return nn(high, selector) + (nn(mid, selector) + nn(low, selector))


def y_face(dst, vel, eddy, high):
    for c in range(3):
        for i in range(2):
            lo = jnp.concatenate([vel[c, x, i : i + 1, :] for x in range(16)], axis=0)
            hi = jnp.concatenate([vel[c, x, 14 + i : 15 + i, :] for x in range(16)], axis=0)
            dst[(c * 2 + i) * 16 : (c * 2 + i + 1) * 16, :] = jnp.where(high, hi, lo)
    dst[96:104, :] = jnp.where(high, eddy[pl.ds(7, 8, stride=8), :], eddy[pl.ds(0, 8, stride=8), :]) * EDDY_SCALE


def diagonal():
    return iota((1, WIDE), 1) >> 6 == iota((SIDE, 1), 0)


def windows(ref, more, q):
    own = [
        ref[dx * SLAB : dx * SLAB + ROWS, j * 512 + q * 256 : j * 512 + (q + 1) * 256]
        for dx in range(3)
        for j in range(3)
    ]
    return jnp.concatenate(own + [more[q, dx * SLAB : dx * SLAB + ROWS, :] for dx in range(3)], axis=1)


def shifted_store(dst_ref, more, x, q, val):
    zero = jnp.zeros((1, BLK, 256), F32)
    lo, hi = (x + 1) * SLAB, (x + 2) * SLAB
    near = [jnp.concatenate([zero, val[:-1]], axis=0), val, jnp.concatenate([val[1:], zero], axis=0)]
    near = [v.reshape(SLAB, 256) for v in near]
    for j in range(3):
        dst_ref[lo:hi, j * 512 + q * 256 : j * 512 + (q + 1) * 256] = near[j].astype(BF16)
    left = iota((SLAB, 128), 1) < 64
    turn = (0, 2) if q == 0 else (1,)
    near = [v[:, 128:256] if q == 0 else v[:, 0:128] for v in near]
    near = [pltpu.roll(v, 64, 1) if j in turn else v for j, v in enumerate(near)]
    more[1 - q, lo:hi, 0:128] = jnp.where(left, near[0], near[1]).astype(BF16)
    more[1 - q, lo:hi, 128:256] = jnp.where(left, near[2], 0.0).astype(BF16)


def clear_ends(ref, more):
    for at in (0, 9 * SLAB):
        ref[at : at + SLAB, :] = jnp.zeros((SLAB, 1536), BF16)
        for q in range(2):
            more[q, at : at + SLAB, :] = jnp.zeros((SLAB, 256), BF16)


def forward_kernel(
    vel_in, tgt_in, w1_in, w2_in, w3_in, own_in, blk_in,
    keep, send, eddy_out, loss_out, dl_out, ah_s, slope1_s, i1_s, dh_s, tb_s, vel, own, blk,
    pool_s, fp_s, a_s, tt_s, slope2_s, dw_s, big_s, gh_s, w2_s,
    tgt, w1, w2, w3, sems, ea_s,
):
    pairs = ((w2_in, w2), (vel_in, vel), (tgt_in, tgt), (w1_in, w1), (w3_in, w3), (own_in, own), (blk_in, blk))
    copies = [pltpu.make_async_copy(src, dst, sems.at[n]) for n, (src, dst) in enumerate(pairs)]
    for copy in copies:
        copy.start()
    gx_at, gy_at, second = place()
    trainers = lax.axis_size("gx") * lax.axis_size("gy") * lax.axis_size("role")

    fp_s[...] = jnp.zeros(fp_s.shape, F32)
    clear_ends(a_s, ea_s)
    w2_s[:, 1664:1792] = jnp.zeros((64, 128), F32)
    zero_tile = jnp.zeros((64, 128), BF16)
    for q in range(2):
        for dx in range(3):
            for ref in (tt_s, tb_s):
                ref[q, 2304 + dx * 256 + 192 : 2304 + (dx + 1) * 256, :] = jnp.zeros((64, 256), BF16)
    for q, z, h, m in tile_places():
        for k in range(9):
            at, cols = place_row(q, z, k), slice(h * 128, (h + 1) * 128)
            if not -1 <= z - 2 * m <= 2:
                tt_s[q, at : at + 64, cols] = zero_tile
                tb_s[q, at : at + 64, cols] = zero_tile
    for copy in copies:
        copy.wait()

    for c in range(3):
        for x in range(SIDE):
            both = vel[c, 2 * x] + vel[c, 2 * x + 1]
            pool_s[c, x] = both
    rows = []
    for c in range(3):
        cols = []
        for x in range(SIDE):
            cols.append(pool_s[c, x, pl.ds(0, 8, stride=2), :] + pool_s[c, x, pl.ds(1, 8, stride=2), :])
        rows.append(jnp.concatenate(cols, axis=0))
    pooled = jnp.concatenate(rows, axis=0)
    zpool = jnp.where(iota((128, 1), 0) >> 1 == iota((1, 64), 1), 0.125, 0.0).astype(BF16)
    filt = exact(pooled, zpool).astype(BF16)
    tgt_rows = tgt[...].reshape(64, 64)
    zsel = jnp.concatenate([filt[0:64], filt[64:128], filt[128:192], tgt_rows], axis=1)
    spread = onehot(iota((ROWS, 1), 0) >> 3 == iota((1, 64), 1))
    by_block = nn(spread, zsel)
    mine = (iota((1, 256), 1) & 63) >> 3 == iota((ROWS, 1), 0) & 7
    by_block = jnp.where(mine, by_block, 0.0).astype(BF16)
    lane_in = iota((1, 256), 1)
    lane_off = lax.div(lane_in, 24)
    lane_cz = lane_in - lane_off * 24
    src = iota((256, 1), 0)
    pick = onehot(jnp.where(lane_in < 216, lane_cz, -1) == (src >> 6) * 8 + (src & 7))
    cells = nn(by_block, pick)
    pick_t = onehot(jnp.where(src >= 192, src & 7, -1) == iota((1, 24), 1) & 7)
    target = nn(by_block, pick_t)

    fp_s[1:9, 1:9] = cells.reshape(SIDE, SIDE, BLK, 256)
    for half, held in ((0, range(6)), (1, range(5, 9))):
        lanes = slice(half * 128, (half + 1) * 128)
        group = lax.div(iota((1, 1, 1, 128), 3) + half * 128, 24)
        for x in range(SIDE):
            acc = jnp.zeros((1, SIDE, BLK, 128), F32)
            for k in held:
                part = fp_s[x + k // 3 : x + k // 3 + 1, k % 3 : k % 3 + SIDE, :, lanes]
                acc = jnp.where(group == k, part, acc)
            i1_s[x * SLAB : (x + 1) * SLAB, lanes] = acc.reshape(SLAB, 128).astype(BF16)

    j_at = iota((81, 1), 0)
    j_off, j_dz, j_c = lax.div(j_at, 9), lax.rem(lax.div(j_at, 3), 3) - 1, lax.rem(j_at, 3)
    lane_key = jnp.where(lane_in < 216, lane_off * 4 + (lane_cz >> 3), -1)
    same = lane_key == j_off * 4 + j_c
    w1v = w1[...]
    by_dz = [nn(w1v, onehot(jnp.where(same, j_dz, 9) == dz)) for dz in (-1, 0, 1)]
    z_in = jnp.broadcast_to(lane_in & 7, (CH, 256))
    t1 = []
    for z in range(SIDE):
        rows = jnp.where(z_in == z - 1, by_dz[0], jnp.where(z_in == z, by_dz[1], 0.0))
        t1.append(jnp.where(z_in == z + 1, by_dz[2], rows).astype(BF16))
    t1 = jnp.concatenate(t1, axis=0)

    left = iota((64, 128), 1) < 64
    w2_s[:, 0:1728] = w2[...].astype(F32)
    w2t = jnp.concatenate(
        [
            jnp.transpose(jnp.concatenate([w2_s[:, t * 128 : (t + 1) * 128]] * 2, axis=0))
            for t in range(14)
        ],
        axis=0,
    )
    for k in range(9):
        base = (192 * k) // 128 * 128
        one, two = w2_s[:, base : base + 128], w2_s[:, base + 128 : base + 256]
        one_r, two_r = pltpu.roll(one, 64, 1), pltpu.roll(two, 64, 1)
        if k % 2 == 0:
            low, high = (one, one_r, two), (one_r, one, two_r)
        else:
            low, high = (one_r, two, two_r), (one, two_r, two)
        low, high = (0.0,) + low, high + (0.0,)
        tiles = {d: jnp.where(left, low[d + 2], high[d + 2]).astype(BF16) for d in (-2, -1, 0, 1)}
        kb = 8 - k
        turned = {dz: w2t[(3 * k + dz + 1) * 64 : (3 * k + dz + 2) * 64] for dz in (-1, 0, 1)}
        turned[-2] = turned[2] = jnp.zeros((64, 128), F32)
        forward = {d: jnp.where(left, turned[d], turned[d - 1]).astype(BF16) for d in (-1, 0, 1, 2)}
        for q, z, h, m in tile_places():
            at, cols = place_row(q, z, k), slice(h * 128, (h + 1) * 128)
            if z - 2 * m in forward:
                tt_s[q, at : at + 64, cols] = forward[z - 2 * m]
            d = 2 * m - z
            at = place_row(q, z, kb)
            if d in tiles:
                tb_s[q, at : at + 64, cols] = tiles[d]

    for q in range(2):
        cols = slice(q * 256, (q + 1) * 256)
        pre_half = nt(i1_s[...], t1[q * 256 : (q + 1) * 256])
        for x in range(SIDE):
            rows = slice(x * SLAB, (x + 1) * SLAB)
            pre = pre_half[rows]
            sig = sigmoid(pre)
            slope1_s[rows, cols] = sig * (1.0 + pre * (1.0 - sig))
            shifted_store(a_s, ea_s, x, q, (pre * sig).reshape(SIDE, BLK, 256))

    for q in range(2):
        cols = slice(q * 256, (q + 1) * 256)
        pre_half = nn(windows(a_s, ea_s, q), tt_s[q])
        for x in range(SIDE):
            rows = slice(x * SLAB, (x + 1) * SLAB)
            pre = pre_half[rows]
            sig = sigmoid(pre)
            slope2_s[rows, cols] = sig * (1.0 + pre * (1.0 - sig))
            ah_s[rows, cols] = (pre * sig).astype(BF16)

    tile8 = onehot(iota((64, 1), 0) == iota((1, WIDE), 1) & 63)
    w3_wide = nn(w3[...], tile8)
    diag = diagonal()
    last = jnp.where(diag, w3_wide, 0.0).astype(BF16)
    last3 = jnp.concatenate([jnp.where(diag, w3_wide, 0.0)] * 3, axis=0).astype(BF16)
    logits = nt(ah_s[...], last3)
    eddy = 0.5 * (jnp.maximum(logits, 0.0) + jnp.log1p(jnp.exp(-jnp.abs(logits))))
    error = eddy - target
    lane24 = iota((1, 24), 1)
    squares = jnp.where(lane24 < SIDE, error * error, 0.0)
    losses = jnp.sum(jnp.sum(squares.reshape(64, BLK, 24), axis=0), axis=1, keepdims=True) / CELLS
    d_logit = (error * sigmoid(logits) / (trainers * CELLS)).astype(BF16)

    zrep = onehot(iota((24, 1), 0) & 7 == (iota((1, 128), 1) & 15) >> 1)
    e_high = eddy.astype(BF16).astype(F32)
    e_mid = (eddy - e_high).astype(BF16).astype(F32)
    e_parts = jnp.where(lane24 < 8, e_high, jnp.where(lane24 < 16, e_mid, eddy - e_high - e_mid))
    fine = nn(e_parts.astype(BF16), zrep)
    fine = jnp.where(iota((1, 128), 1) >> 4 == iota((ROWS, 1), 0) & 7, fine, 0.0)
    fine = jnp.sum(fine.reshape(64, BLK, 128), axis=1)
    eddy_out[...] = fine
    y_face(send.at[HIDDEN_TILES * 32 : HIDDEN_TILES * 32 + 104], vel, eddy_out, gy_at & 1 == 0)
    loss_out[...] = jnp.broadcast_to(losses, (BLK, 128))
    dl_out[...] = d_logit.astype(F32)[:, 0:SIDE]

    count = times_sampled(own, blk, gx_at)
    big_s[:, 0:512] = nn(d_logit, jnp.concatenate([last.astype(F32), jnp.zeros((16, WIDE), F32)], axis=0).astype(BF16))
    for x in range(SIDE):
        d_hid = big_s[x * SLAB : (x + 1) * SLAB, 0:512] * slope2_s[x * SLAB : (x + 1) * SLAB, :]
        d_hid = d_hid.astype(BF16)
        dh_s[x * SLAB : (x + 1) * SLAB, :] = d_hid
        d_hid = d_hid.astype(F32).reshape(SIDE, BLK, WIDE)
        dw_s[x * SLAB : (x + 1) * SLAB, :] = (d_hid * count[None]).reshape(SLAB, WIDE).astype(BF16)
    dwt = jnp.transpose(dw_s[...])

    sums = {}
    for p in range(4):
        first, last_z = max(2 * p - 1, 0), min(2 * p + 2, SIDE - 1)
        shifts = [
            a_s[dx * SLAB : dx * SLAB + ROWS, j * 512 + p * 128 : j * 512 + (p + 1) * 128]
            for dx in range(3)
            for j in range(3)
        ]
        found = nn(dwt[first * 64 : (last_z + 1) * 64], jnp.concatenate(shifts, axis=1))
        for z in range(first, last_z + 1):
            part = found[(z - first) * 64 : (z - first + 1) * 64]
            m = z - 2 * p
            sums[m] = part if m not in sums else sums[m] + part
    low_half = iota((64, 128), 1) < 64
    held = None
    for k in range(9):
        for dz in (-1, 0, 1):
            low, high = (sums[m][:, k * 128 : (k + 1) * 128] for m in (-dz, 1 - dz))
            at = (k * 3 + dz + 1) * 64
            if at % 128:
                gh_s[:, at - 64 : at + 64] = jnp.where(low_half, held, high + pltpu.roll(low, 64, 1))
            else:
                held = low + pltpu.roll(high, 64, 1)
    gh_s[:, 1664:1792] = jnp.where(low_half, held, 0.0)

    for t in range(HIDDEN_TILES):
        top, bottom = (gh_s[r : r + 32, t * 128 : (t + 1) * 128] for r in (0, 32))
        keep[t * 32 : (t + 1) * 32, :] = jnp.where(second, bottom, top)
        send[t * 32 : (t + 1) * 32, :] = jnp.where(second, top, bottom)


def backward_kernel(
    vel, own, blk, eddy, losses, dl_in, ah_s, slope1_s, i1_s, dh_s, tb_s,
    extra_out, halo1, halo2, halo3, halo4, hx_a, hx_b, hy_b, hz, d_s, dw_s, ed_s,
):
    gx_at, gy_at, second = place()
    gx_odd, gy_odd = gx_at & 1 == 1, gy_at & 1 == 1
    dev = (gx_at * lax.axis_size("gy") + gy_at) * lax.axis_size("role") + lax.axis_index("role")
    count = times_sampled(own, blk, gx_at)

    clear_ends(d_s, ed_s)
    for x in range(SIDE):
        d_hid = dh_s[x * SLAB : (x + 1) * SLAB, :].astype(F32)
        for q in range(2):
            shifted_store(d_s, ed_s, x, q, d_hid[:, q * 256 : (q + 1) * 256].reshape(SIDE, BLK, 256))

    for c in range(3):
        for i in range(2):
            lo, hi = vel[c, i], vel[c, 14 + i]
            at = (c * 2 + i) * 16
            hx_a[at : at + 16, :] = jnp.where(gx_odd, lo, hi)
            hx_b[at : at + 16, :] = jnp.where(gx_odd, hi, lo)
    fine = eddy[...]
    small = fine * EDDY_SCALE
    hx_a[96:104, :] = jnp.where(gx_odd, small[0:8], small[56:64])
    hx_b[96:104, :] = jnp.where(gx_odd, small[56:64], small[0:8])
    y_face(hy_b, vel, eddy, gy_odd)
    vt = jnp.transpose(vel[...].reshape(768, 128))
    et = jnp.transpose(jnp.concatenate([small, jnp.zeros((64, 128), F32)], axis=0))
    hz[...] = jnp.zeros(hz.shape, F32)
    for t in range(6):
        hz[t * 8 : t * 8 + 2, :] = vt[0:2, t * 128 : (t + 1) * 128]
        hz[t * 8 + 2 : t * 8 + 4, :] = vt[126:128, t * 128 : (t + 1) * 128]
    hz[48:49, :] = et[0:1]
    hz[49:50, :] = et[127:128]
    halo1[...] = jnp.where(second, hx_a[...], hy_b[...])
    halo2[...] = jnp.where(second, hy_b[...], hx_a[...])
    halo3[...] = jnp.where(second, hx_b[...], hz[...])
    halo4[...] = jnp.where(second, hz[...], hx_b[...])

    g1 = []
    for q in range(2):
        cols = slice(q * 256, (q + 1) * 256)
        d_act = nn(windows(d_s, ed_s, q), tb_s[q])
        for x in range(SIDE):
            rows = slice(x * SLAB, (x + 1) * SLAB)
            d_first = (d_act[rows] * slope1_s[rows, cols]).astype(BF16).astype(F32)
            dw_s[rows, cols] = (d_first.reshape(SIDE, BLK, 256) * count[None]).reshape(SLAB, 256).astype(BF16)
        g1.append(nn(jnp.transpose(dw_s[:, cols]), i1_s[...]))
    z_in = iota((1, 256), 1) & 7
    parts = []
    for dz in (-1, 0, 1):
        tot = jnp.zeros((64, 256), F32)
        for z in range(SIDE):
            if 0 <= z + dz < SIDE:
                tot = tot + jnp.where(z_in == z + dz, g1[z // 4][z % 4 * 64 : (z % 4 + 1) * 64], 0.0)
        parts.append(tot)
    r_at = iota((768, 1), 0)
    c_at = iota((1, 128), 1)
    r_lane = r_at & 255
    r_off = lax.div(r_lane, 24)
    r_col = (r_off * 3 + (r_at >> 8)) * 3 + ((r_lane - r_off * 24) >> 3)
    fold = onehot(jnp.where(r_lane < 216, r_col, -1) == c_at)
    g_first = exact(jnp.concatenate(parts, axis=1), fold)

    count_rows = jnp.broadcast_to(count.reshape(1, BLK, 1), (64, BLK, 1)).reshape(ROWS, 1)
    dlw = dl_in[...] * count_rows
    dl_hi = dlw.astype(BF16)
    dl_lo = (dlw - dl_hi.astype(F32)).astype(BF16)
    ah = ah_s[...]
    gl = tn(dl_hi, ah) + tn(dl_lo, ah)
    gl = jnp.where(diagonal(), gl, 0.0)
    gl = jnp.sum(gl, axis=0, keepdims=True)
    gl = gl[:, 0:128] + gl[:, 128:256] + gl[:, 256:384] + gl[:, 384:512]
    at_lane = iota((1, 128), 1) & 63 == iota((64, 1), 0)
    g_last = jnp.sum(jnp.where(at_lane, gl, 0.0), axis=1, keepdims=True)

    lane8 = iota((BLK, 128), 1)
    loss_row = jnp.where(lane8 - (LOSS_COL + BLK * (dev >> 6)) == iota((BLK, 128), 0), losses[...], 0.0)
    loss_row = jnp.sum(loss_row, axis=0, keepdims=True)
    lane = iota((64, 128), 1)
    extra = jnp.where(lane == LAST_COL, g_last, g_first)
    extra = extra + jnp.where(iota((64, 128), 0) == dev & 63, loss_row, 0.0)

    extra_out[...] = extra


def vmem_spec():
    return pl.BlockSpec(memory_space=pltpu.VMEM)


def run_forward(*given):
    velocity, target, w1, w2, w3, own, blk = (pltpu.with_memory_space_constraint(a, pltpu.HBM) for a in given)
    half = pltpu.VMEM((HIDDEN_TILES * 32, 128), F32)
    return pl.pallas_call(
        forward_kernel,
        out_shape=(
            half,
            pltpu.VMEM((HIDDEN_TILES * 32 + 104, 128), F32),
            pltpu.VMEM((64, 128), F32),
            pltpu.VMEM((BLK, 128), F32),
            pltpu.VMEM((ROWS, SIDE), F32),
            pltpu.VMEM((ROWS, WIDE), BF16),
            pltpu.VMEM((ROWS, WIDE), F32),
            pltpu.VMEM((ROWS, 256), BF16),
            pltpu.VMEM((ROWS, WIDE), BF16),
            pltpu.VMEM((2, 3072, 256), BF16),
        )
        + tuple(pltpu.VMEM(a.shape, a.dtype) for a in (velocity, own, blk)),
        in_specs=[pl.BlockSpec(memory_space=pltpu.HBM)] * 7,
        out_specs=tuple(vmem_spec() for _ in range(13)),
        scratch_shapes=[
            pltpu.VMEM((3, SIDE, 16, 128), F32),
            pltpu.VMEM((10, 10, BLK, 256), F32),
            pltpu.VMEM((ROWS + 2 * SLAB, 1536), BF16),
            pltpu.VMEM((2, 3072, 256), BF16),
            pltpu.VMEM((ROWS, WIDE), F32),
            pltpu.VMEM((ROWS, WIDE), BF16),
            pltpu.VMEM((ROWS, WIDE), F32),
            pltpu.VMEM((64, HIDDEN_TILES * 128), F32),
            pltpu.VMEM((64, 1792), F32),
        ]
        + [pltpu.VMEM(a.shape, a.dtype) for a in (target, w1, w2, w3)]
        + [pltpu.SemaphoreType.DMA((7,)), pltpu.VMEM((2, ROWS + 2 * SLAB, 256), BF16)],
        compiler_params=pltpu.CompilerParams(vmem_limit_bytes=40 * 1024 * 1024),
        name="forward",
    )(velocity, target, w1, w2, w3, own, blk)


def run_backward(velocity, own, blk, *kept):
    face = pltpu.VMEM((104, 128), F32)
    return pl.pallas_call(
        backward_kernel,
        out_shape=(pltpu.VMEM((64, 128), F32),) + (face,) * 4,
        in_specs=[vmem_spec()] * 11,
        out_specs=tuple(vmem_spec() for _ in range(5)),
        scratch_shapes=[face] * 4
        + [
            pltpu.VMEM((ROWS + 2 * SLAB, 1536), BF16),
            pltpu.VMEM((ROWS, WIDE), BF16),
            pltpu.VMEM((2, ROWS + 2 * SLAB, 256), BF16),
        ],
        compiler_params=pltpu.CompilerParams(vmem_limit_bytes=40 * 1024 * 1024),
        name="backward",
    )(velocity, own, blk, *kept)


def flow_kernel(
    vel, eddy, got0, got1, got2, got3, got4, out, rx_a, rx_b, ry_a, ry_b, rz, vx_s, vy_s, visc_s, ez_s
):
    gx_at, gy_at = lax.axis_index("gx"), lax.axis_index("gy")
    gx_odd, gy_odd = gx_at & 1 == 1, gy_at & 1 == 1
    second = core_half(gy_at) == 1
    ry_a[...] = got0[...]
    ry_b[...] = jnp.where(second, got2[...], got1[...])
    rx_a[...] = jnp.where(second, got1[...], got2[...])
    rx_b[...] = jnp.where(second, got3[...], got4[...])
    rz[...] = jnp.where(second, got4[...], got3[...])
    lane = iota((1, 128), 1)

    def sides(odd, a, b, at, rows):
        one, two = a[at : at + rows, :], b[at : at + rows, :]
        return jnp.where(odd, one, two), jnp.where(odd, two, one)

    for c in range(3):
        for x in range(16):
            vy_s[(c * 16 + x) * 32 + 8 : (c * 16 + x) * 32 + 24, :] = vel[c, x]
        for i in range(2):
            below, above = sides(gy_odd, ry_a, ry_b, (c * 2 + i) * 16, 16)
            vy_s[pl.ds(c * 512 + 6 + i, 16, stride=32), :] = below
            vy_s[pl.ds(c * 512 + 24 + i, 16, stride=32), :] = above
            below, above = sides(gx_odd, rx_a, rx_b, (c * 2 + i) * 16, 16)
            vx_s[c, i] = below
            vx_s[c, 2 + i] = above

    zcols = jnp.concatenate([jnp.transpose(rz[t * 8 : t * 8 + 8, :]) for t in range(7)], axis=0)
    coarse = eddy[...]
    e_first, e_last = zcols[768:832, 0:1] / EDDY_SCALE, zcols[768:832, 1:2] / EDDY_SCALE
    ahead = jnp.where(lane == 127, e_first, pltpu.roll(coarse, 127, 1))
    behind = jnp.where(lane == 0, e_last, pltpu.roll(coarse, 1, 1))
    below_x, above_x = (v / EDDY_SCALE for v in sides(gx_odd, rx_a, rx_b, 96, 8))
    below_y, above_y = (v / EDDY_SCALE for v in sides(gy_odd, ry_a, ry_b, 96, 8))

    def put(dst, plane, val):
        dst[pl.ds(plane * 32 + 8, 8, stride=2), :] = val
        dst[pl.ds(plane * 32 + 9, 8, stride=2), :] = val

    put(visc_s, 0, base_visc + below_x)
    put(visc_s, 17, base_visc + above_x)
    for x in range(8):
        for r in range(2):
            plane = 2 * x + 1 + r
            put(visc_s, plane, base_visc + coarse[x * 8 : x * 8 + 8])
            visc_s[plane * 32 + 7 : plane * 32 + 8, :] = base_visc + below_y[x : x + 1]
            visc_s[plane * 32 + 24 : plane * 32 + 25, :] = base_visc + above_y[x : x + 1]
        put(ez_s, 2 * x, base_visc + ahead[x * 8 : x * 8 + 8])
        put(ez_s, 2 * x + 1, base_visc + behind[x * 8 : x * 8 + 8])

    def plane_of(c, x):
        if x < 0:
            return vx_s[c, x + 2]
        if x > 15:
            return vx_s[c, x - 14]
        return vel[c, x]

    for x in range(16):
        vat = (x + 1) * 32
        visc = visc_s[vat + 8 : vat + 24, :]
        faces = (
            (visc_s[vat + 40 : vat + 56, :], visc_s[vat - 24 : vat - 8, :]),
            (visc_s[vat + 9 : vat + 25, :], visc_s[vat + 7 : vat + 23, :]),
            (
                ez_s[(x // 2 * 2) * 32 + 8 : (x // 2 * 2) * 32 + 24, :],
                ez_s[(x // 2 * 2 + 1) * 32 + 8 : (x // 2 * 2 + 1) * 32 + 24, :],
            ),
        )
        faces = [(0.5 * (visc + a), 0.5 * (visc + b)) for a, b in faces]
        wind = [vel[a, x] for a in range(3)]
        for c in range(3):
            u = vel[c, x]
            at = (c * 16 + x) * 32
            zat = (c * 16 + x) * 16
            zc = zcols[zat : zat + 16]
            p1 = jnp.where(lane == 127, zc[:, 0:1], pltpu.roll(u, 127, 1))
            p2 = jnp.where(lane == 127, zc[:, 1:2], jnp.where(lane == 126, zc[:, 0:1], pltpu.roll(u, 126, 1)))
            m1 = jnp.where(lane == 0, zc[:, 3:4], pltpu.roll(u, 1, 1))
            m2 = jnp.where(lane == 0, zc[:, 2:3], jnp.where(lane == 1, zc[:, 3:4], pltpu.roll(u, 2, 1)))
            near = (
                (plane_of(c, x + 1), plane_of(c, x - 1), plane_of(c, x + 2), plane_of(c, x - 2)),
                (
                    vy_s[at + 9 : at + 25, :], vy_s[at + 7 : at + 23, :],
                    vy_s[at + 10 : at + 26, :], vy_s[at + 6 : at + 22, :],
                ),
                (p1, m1, p2, m2),
            )
            advect = None
            diffuse = None
            for a in range(3):
                q1, b1, q2, b2 = near[a]
                slope = (8.0 * (q1 - b1) - (q2 - b2)) * (1.0 / 12.0)
                term = wind[a] * slope
                advect = term if advect is None else advect + term
                flux = faces[a][0] * (q1 - u) - faces[a][1] * (u - b1)
                diffuse = flux if diffuse is None else diffuse + flux
            out[c, x] = u + time_step * (diffuse - advect)


def run_flow(velocity, eddy, *got):
    return pl.pallas_call(
        flow_kernel,
        out_shape=jax.ShapeDtypeStruct(velocity.shape, F32),
        in_specs=[vmem_spec()] * 7,
        out_specs=vmem_spec(),
        scratch_shapes=[
            pltpu.VMEM((104, 128), F32),
            pltpu.VMEM((104, 128), F32),
            pltpu.VMEM((104, 128), F32),
            pltpu.VMEM((104, 128), F32),
            pltpu.VMEM((104, 128), F32),
            pltpu.VMEM((3, 4, 16, 128), F32),
            pltpu.VMEM((3 * 16 * 32, 128), F32),
            pltpu.VMEM((18 * 32, 128), F32),
            pltpu.VMEM((16 * 32, 128), F32),
        ],
        compiler_params=pltpu.CompilerParams(vmem_limit_bytes=32 * 1024 * 1024),
        name="flow",
    )(velocity, eddy, *got)


def finish_kernel(own, blk, mine, other, loss_out, first_out, hidden_out, last_out):
    gx_at, gy_at = lax.axis_index("gx"), lax.axis_index("gy")
    n_z = lax.axis_size("role")
    in_group = gy_at * n_z + lax.axis_index("role")
    second = core_half(gy_at) == 1
    for t in range(HIDDEN_TILES):
        one, two = mine[t * 32 : (t + 1) * 32, :], other[t * 32 : (t + 1) * 32, :]
        top, bottom = jnp.where(second, two, one), jnp.where(second, one, two)
        width = min(128, 27 * CH - t * 128)
        hidden_out[0:32, t * 128 : t * 128 + width] = top[:, :width]
        hidden_out[32:64, t * 128 : t * 128 + width] = bottom[:, :width]
    extra = mine[HIDDEN_TILES * 32 :, :] + other[HIDDEN_TILES * 32 :, :]
    first_out[...] = extra[:, 0:81]
    turned = jnp.transpose(jnp.concatenate([extra, jnp.zeros((64, 128), F32)], axis=0))
    last_out[...] = turned[LAST_COL : LAST_COL + 1, 0:64]
    slots = loss_out.shape[1]
    dev = own[...] * (lax.axis_size("gy") * n_z) + in_group
    listed = dev.shape[1]
    pick = onehot(iota((64, listed), 0) == dev & 63)
    rows = exact(turned[:, 0:64], pick)
    rows = jnp.where(iota((128, listed), 0) == LOSS_COL + BLK * (dev >> 6) + blk[...], rows, 0.0)
    found = jnp.sum(rows, axis=0, keepdims=True)
    picked = jnp.zeros((1, slots), F32)
    for g in range(listed // slots):
        picked = jnp.where(gx_at == g, found[:, g * slots : (g + 1) * slots], picked)
    loss_out[...] = picked


def run_finish(own, blk, mine, other, slots):
    f = lambda *s: jax.ShapeDtypeStruct(s, F32)
    return pl.pallas_call(
        finish_kernel,
        out_shape=(f(1, slots), f(64, 81), f(64, 27 * CH), f(1, 64)),
        in_specs=[vmem_spec()] * 4,
        out_specs=tuple(vmem_spec() for _ in range(4)),
        compiler_params=pltpu.CompilerParams(vmem_limit_bytes=32 * 1024 * 1024),
        name="finish",
    )(own, blk, mine, other)


def on_device(velocity, target_visc, w_first, w_hidden, w_last, sample_owner, sample_block):
    n_x, n_y, n_z = lax.axis_size("gx"), lax.axis_size("gy"), lax.axis_size("role")
    trainers = n_x * n_y * n_z
    own = sample_owner.reshape(1, -1)
    blk = sample_block.reshape(1, -1)
    slots = own.shape[1] // n_x

    axes = ("gx", "gy", "role")

    def even_odd(i, count):
        return i ^ 1

    def odd_even(i, count):
        return (i - 1) % count if i % 2 == 0 else (i + 1) % count

    def partner(kind, i, j, r):
        if kind == "x":
            j = odd_even(j, n_y)
        elif kind == "y":
            r = r ^ 1
        elif kind == "z_a":
            i = even_odd(i, n_x)
        else:
            i = odd_even(i, n_x)
        return (i * n_y + j) * n_z + r

    def mixed(kinds):
        pairs = []
        for i in range(n_x):
            for j in range(n_y):
                for r in range(n_z):
                    pairs.append(((i * n_y + j) * n_z + r, partner(kinds[(j ^ (j >> 1)) & 1], i, j, r)))
        return pairs

    core_pairs = [(j, even_odd(j, n_y)) for j in range(n_y)]
    size = TILES * 32

    keep, send, eddy, *kept, velocity, own, blk = run_forward(
        velocity, target_visc, w_first, w_hidden, w_last.reshape(1, CH), own, blk
    )
    half = core_half(lax.axis_index("gy"))
    got = lax.ppermute(send, "gy", core_pairs)
    extra, *halos = run_backward(velocity, own, blk, eddy, *kept)
    total = jnp.concatenate([keep + got[: HIDDEN_TILES * 32], extra], axis=0)
    rims = [got[HIDDEN_TILES * 32 :]]
    halos = [h.astype(F16) for h in halos]

    def widen(values, exps):
        wide = values.astype(F32).reshape(TILES, 32, 128) * jnp.exp2(exps)[:, None, :]
        return wide.reshape(size, 128)

    top = jnp.max(jnp.abs(total.reshape(TILES, 32, 128)), axis=1)
    exps = jnp.clip(jnp.ceil(jnp.log2(jnp.maximum(top, 1e-30))) - 13.0, -110.0, 110.0)
    orders = (("x", "z_a", "y", "z_b"), ("z_a", "x", "z_b", "y"))
    for s in range(4):
        kinds = (orders[0][s], orders[1][s])
        scaled = total.reshape(TILES, 32, 128) * jnp.exp2(-exps)[:, None, :]
        pieces = [scaled.reshape(size, 128).astype(F16), exps.astype(F16)]
        message = jnp.concatenate(pieces + [halos[s]] if s < 3 else pieces, axis=0)
        message = lax.optimization_barrier(message)
        got = lax.ppermute(message, axes, mixed(kinds))
        if s == 1:
            far = lax.ppermute(halos[3], axes, mixed((orders[0][3], orders[1][3])))
        their_exps = got[size : size + TILES].astype(F32)
        mine, theirs = widen(message[:size], exps), widen(got[:size], their_exps)
        if n_x != 4 and "z_b" in kinds:
            theirs = jnp.where(half == kinds.index("z_b"), 0.0, theirs)
        total = mine + theirs
        exps = jnp.maximum(exps, their_exps) + 1.0
        if s < 3:
            rims.append(got[size + 16 :].astype(F32))
        if s == 1:
            total, far = lax.optimization_barrier((total, far))
        if s == 2:
            u_next = run_flow(velocity, eddy, *rims, far.astype(F32))
    total, u_next = lax.optimization_barrier((total, u_next))
    if n_x != 4:
        for bit in range(1, n_x.bit_length() - 1):
            total = total + lax.ppermute(total, "gx", [(i, i ^ (1 << bit)) for i in range(n_x)])
    other = lax.ppermute(total, "gy", core_pairs)

    losses, first, hidden, last = run_finish(own, blk, total, other, slots)
    return (u_next, losses.reshape(1, 1, slots), first, hidden, last.reshape(CH))


def solution(mesh):
    return jax.shard_map(
        on_device,
        mesh=mesh,
        in_specs=(
            P(None, "gx", "gy", "role"),
            P("gx", "gy", "role"),
            P(),
            P(),
            P(),
            P("gy", "role", None, None),
            P("gy", "role", None, None),
        ),
        out_specs=(P(None, "gx", "gy", "role"), P("gy", "role", "gx"), P(), P(), P()),
        check_vma=False,
    )
```

```python
import jax
import jax.numpy as jnp
from jax import lax
from jax.experimental import pallas as pl
from jax.experimental.pallas import tpu as pltpu
from jax.sharding import PartitionSpec as P

F32 = jnp.float32
BF16 = jnp.bfloat16
HIGH = lax.Precision.HIGHEST

SIDE = 8
CELLS = SIDE**3
CH = 64
BLK = 8
ROWS = SIDE * SIDE * BLK
WIDE = SIDE * CH
SLAB = SIDE * BLK
HIDDEN_TILES = 14
TILES = 16
LAST_COL = 81
LOSS_COL = 82

EDDY_SCALE = 2.0**-9
F16 = jnp.float16

base_visc = 0.02
time_step = 0.2


def iota(shape, dim):
    return lax.broadcasted_iota(jnp.int32, shape, dim)


def onehot(cond, dtype=BF16):
    return jnp.where(cond, 1.0, 0.0).astype(dtype)


def sigmoid(v):
    return 0.5 + 0.5 * jnp.tanh(0.5 * v)


def nt(a, b, precision=None):
    return lax.dot_general(a, b, (((1,), (1,)), ((), ())), preferred_element_type=F32, precision=precision)


def tn(a, b, precision=None):
    return lax.dot_general(a, b, (((0,), (0,)), ((), ())), preferred_element_type=F32, precision=precision)


def nn(a, b, precision=None):
    return lax.dot_general(a, b, (((1,), (0,)), ((), ())), preferred_element_type=F32, precision=precision)


def core_half(at):
    return (at ^ (at >> 1)) & 1


def place():
    gx_at, gy_at = lax.axis_index("gx"), lax.axis_index("gy")
    return gx_at, gy_at, core_half(gy_at) == 1


def times_sampled(own, blk, gx_at):
    code = own[...] * BLK + blk[...]
    wanted = gx_at * BLK + iota((BLK, code.shape[1]), 0)
    return jnp.sum(jnp.where(code == wanted, 1.0, 0.0), axis=1, keepdims=True)


def tile_places():
    return [(q, z, h, 2 * q + h) for q in range(2) for z in range(3 * q, 3 * q + 5) for h in range(2)]


def place_row(q, z, k):
    if 4 * q <= z < 4 * q + 4:
        return k * 256 + (z - 4 * q) * 64
    return 2304 + k // 3 * 256 + k % 3 * 64


def exact(a, selector):
    high = a.astype(BF16)
    rest = a - high.astype(F32)
    mid = rest.astype(BF16)
    low = (rest - mid.astype(F32)).astype(BF16)
    return nn(high, selector) + (nn(mid, selector) + nn(low, selector))


def y_face(dst, vel, eddy, high):
    for c in range(3):
        for i in range(2):
            lo = jnp.concatenate([vel[c, x, i : i + 1, :] for x in range(16)], axis=0)
            hi = jnp.concatenate([vel[c, x, 14 + i : 15 + i, :] for x in range(16)], axis=0)
            dst[(c * 2 + i) * 16 : (c * 2 + i + 1) * 16, :] = jnp.where(high, hi, lo)
    dst[96:104, :] = jnp.where(high, eddy[pl.ds(7, 8, stride=8), :], eddy[pl.ds(0, 8, stride=8), :]) * EDDY_SCALE


def diagonal():
    return iota((1, WIDE), 1) >> 6 == iota((SIDE, 1), 0)


def windows(ref, more, q):
    own = [
        ref[dx * SLAB : dx * SLAB + ROWS, j * 512 + q * 256 : j * 512 + (q + 1) * 256]
        for dx in range(3)
        for j in range(3)
    ]
    return jnp.concatenate(own + [more[q, dx * SLAB : dx * SLAB + ROWS, :] for dx in range(3)], axis=1)


def shifted_store(dst_ref, more, x, val):
    zero = jnp.zeros((1, BLK, WIDE), F32)
    lo, hi = (x + 1) * SLAB, (x + 2) * SLAB
    dst_ref[lo:hi, 0:512] = jnp.concatenate([zero, val[:-1]], axis=0).reshape(SLAB, WIDE).astype(BF16)
    dst_ref[lo:hi, 512:1024] = val.reshape(SLAB, WIDE).astype(BF16)
    dst_ref[lo:hi, 1024:1536] = jnp.concatenate([val[1:], zero], axis=0).reshape(SLAB, WIDE).astype(BF16)
    left = iota((SLAB, 128), 1) < 64
    zero = zero[:, :, :128]
    for q in range(2):
        part = val[:, :, 256:384] if q == 0 else val[:, :, 128:256]
        near = [jnp.concatenate([zero, part[:-1]], axis=0), part, jnp.concatenate([part[1:], zero], axis=0)]
        near = [v.reshape(SLAB, 128) for v in near]
        turn = (1,) if q == 0 else (0, 2)
        near = [pltpu.roll(v, 64, 1) if j in turn else v for j, v in enumerate(near)]
        more[q, lo:hi, 0:128] = jnp.where(left, near[0], near[1]).astype(BF16)
        more[q, lo:hi, 128:256] = jnp.where(left, near[2], 0.0).astype(BF16)


def clear_ends(ref, more):
    for at in (0, 9 * SLAB):
        ref[at : at + SLAB, :] = jnp.zeros((SLAB, 1536), BF16)
        for q in range(2):
            more[q, at : at + SLAB, :] = jnp.zeros((SLAB, 256), BF16)


def forward_kernel(
    vel_in, tgt_in, w1_in, w2_in, w3_in, own_in, blk_in,
    keep, send, eddy_out, loss_out, dl_out, ah_s, slope1_s, i1_s, d_s, ed_s, tb_s, vel, own, blk,
    pool_s, fp_s, a_s, tt_s, pre_s, slope2_s, dw_s, big_s, gh_s, w2_s,
    tgt, w1, w2, w3, sems, ea_s,
):
    pairs = ((w2_in, w2), (vel_in, vel), (tgt_in, tgt), (w1_in, w1), (w3_in, w3), (own_in, own), (blk_in, blk))
    copies = [pltpu.make_async_copy(src, dst, sems.at[n]) for n, (src, dst) in enumerate(pairs)]
    for copy in copies:
        copy.start()
    gx_at, gy_at, second = place()
    trainers = lax.axis_size("gx") * lax.axis_size("gy") * lax.axis_size("role")

    fp_s[...] = jnp.zeros(fp_s.shape, F32)
    clear_ends(a_s, ea_s)
    clear_ends(d_s, ed_s)
    w2_s[:, 1664:1792] = jnp.zeros((64, 128), F32)
    zero_tile = jnp.zeros((64, 128), BF16)
    for q in range(2):
        for dx in range(3):
            for ref in (tt_s, tb_s):
                ref[q, 2304 + dx * 256 + 192 : 2304 + (dx + 1) * 256, :] = jnp.zeros((64, 256), BF16)
    for q, z, h, m in tile_places():
        for k in range(9):
            at, cols = place_row(q, z, k), slice(h * 128, (h + 1) * 128)
            if not -1 <= z - 2 * m <= 2:
                tt_s[q, at : at + 64, cols] = zero_tile
                tb_s[q, at : at + 64, cols] = zero_tile
    for copy in copies:
        copy.wait()

    for c in range(3):
        for x in range(SIDE):
            both = vel[c, 2 * x] + vel[c, 2 * x + 1]
            pool_s[c, x] = both
    rows = []
    for c in range(3):
        cols = []
        for x in range(SIDE):
            cols.append(pool_s[c, x, pl.ds(0, 8, stride=2), :] + pool_s[c, x, pl.ds(1, 8, stride=2), :])
        rows.append(jnp.concatenate(cols, axis=0))
    pooled = jnp.concatenate(rows, axis=0)
    zpool = jnp.where(iota((128, 1), 0) >> 1 == iota((1, 64), 1), 0.125, 0.0).astype(BF16)
    filt = exact(pooled, zpool).astype(BF16)
    tgt_rows = tgt[...].reshape(64, 64)
    zsel = jnp.concatenate([filt[0:64], filt[64:128], filt[128:192], tgt_rows], axis=1)
    spread = onehot(iota((ROWS, 1), 0) >> 3 == iota((1, 64), 1))
    by_block = nn(spread, zsel)
    mine = (iota((1, 256), 1) & 63) >> 3 == iota((ROWS, 1), 0) & 7
    by_block = jnp.where(mine, by_block, 0.0).astype(BF16)
    lane_in = iota((1, 256), 1)
    lane_off = lax.div(lane_in, 24)
    lane_cz = lane_in - lane_off * 24
    src = iota((256, 1), 0)
    pick = onehot(jnp.where(lane_in < 216, lane_cz, -1) == (src >> 6) * 8 + (src & 7))
    cells = nn(by_block, pick)
    pick_t = onehot(jnp.where(src >= 192, src & 7, -1) == iota((1, 24), 1) & 7)
    target = nn(by_block, pick_t)

    fp_s[1:9, 1:9] = cells.reshape(SIDE, SIDE, BLK, 256)
    for half, held in ((0, range(6)), (1, range(5, 9))):
        lanes = slice(half * 128, (half + 1) * 128)
        group = lax.div(iota((1, 1, 1, 128), 3) + half * 128, 24)
        for x in range(SIDE):
            acc = jnp.zeros((1, SIDE, BLK, 128), F32)
            for k in held:
                part = fp_s[x + k // 3 : x + k // 3 + 1, k % 3 : k % 3 + SIDE, :, lanes]
                acc = jnp.where(group == k, part, acc)
            i1_s[x * SLAB : (x + 1) * SLAB, lanes] = acc.reshape(SLAB, 128).astype(BF16)

    j_at = iota((81, 1), 0)
    j_off, j_dz, j_c = lax.div(j_at, 9), lax.rem(lax.div(j_at, 3), 3) - 1, lax.rem(j_at, 3)
    lane_key = jnp.where(lane_in < 216, lane_off * 4 + (lane_cz >> 3), -1)
    same = lane_key == j_off * 4 + j_c
    w1v = w1[...]
    by_dz = [nn(w1v, onehot(jnp.where(same, j_dz, 9) == dz)) for dz in (-1, 0, 1)]
    z_in = jnp.broadcast_to(lane_in & 7, (CH, 256))
    t1 = []
    for z in range(SIDE):
        rows = jnp.where(z_in == z - 1, by_dz[0], jnp.where(z_in == z, by_dz[1], 0.0))
        t1.append(jnp.where(z_in == z + 1, by_dz[2], rows).astype(BF16))
    t1 = jnp.concatenate(t1, axis=0)
    pre_s[...] = nt(i1_s[...], t1)

    left = iota((64, 128), 1) < 64
    w2_s[:, 0:1728] = w2[...].astype(F32)
    w2t = jnp.concatenate(
        [
            jnp.transpose(jnp.concatenate([w2_s[:, t * 128 : (t + 1) * 128]] * 2, axis=0))
            for t in range(14)
        ],
        axis=0,
    )
    for k in range(9):
        base = (192 * k) // 128 * 128
        one, two = w2_s[:, base : base + 128], w2_s[:, base + 128 : base + 256]
        one_r, two_r = pltpu.roll(one, 64, 1), pltpu.roll(two, 64, 1)
        if k % 2 == 0:
            low, high = (one, one_r, two), (one_r, one, two_r)
        else:
            low, high = (one_r, two, two_r), (one, two_r, two)
        low, high = (0.0,) + low, high + (0.0,)
        tiles = {d: jnp.where(left, low[d + 2], high[d + 2]).astype(BF16) for d in (-2, -1, 0, 1)}
        kb = 8 - k
        turned = {dz: w2t[(3 * k + dz + 1) * 64 : (3 * k + dz + 2) * 64] for dz in (-1, 0, 1)}
        turned[-2] = turned[2] = jnp.zeros((64, 128), F32)
        forward = {d: jnp.where(left, turned[d], turned[d - 1]).astype(BF16) for d in (-1, 0, 1, 2)}
        for q, z, h, m in tile_places():
            at, cols = place_row(q, z, k), slice(h * 128, (h + 1) * 128)
            if z - 2 * m in forward:
                tt_s[q, at : at + 64, cols] = forward[z - 2 * m]
            d = 2 * m - z
            at = place_row(q, z, kb)
            if d in tiles:
                tb_s[q, at : at + 64, cols] = tiles[d]

    for x in range(SIDE):
        pre = pre_s[x * SLAB : (x + 1) * SLAB, :]
        sig = sigmoid(pre)
        slope1_s[x * SLAB : (x + 1) * SLAB, :] = sig * (1.0 + pre * (1.0 - sig))
        shifted_store(a_s, ea_s, x, (pre * sig).reshape(SIDE, BLK, WIDE))

    for q in range(2):
        pre_s[:, q * 256 : (q + 1) * 256] = nn(windows(a_s, ea_s, q), tt_s[q])
    for x in range(SIDE):
        pre = pre_s[x * SLAB : (x + 1) * SLAB, :]
        sig = sigmoid(pre)
        slope2_s[x * SLAB : (x + 1) * SLAB, :] = sig * (1.0 + pre * (1.0 - sig))
        ah_s[x * SLAB : (x + 1) * SLAB, :] = (pre * sig).astype(BF16)

    tile8 = onehot(iota((64, 1), 0) == iota((1, WIDE), 1) & 63)
    w3_wide = nn(w3[...], tile8)
    diag = diagonal()
    last = jnp.where(diag, w3_wide, 0.0).astype(BF16)
    last3 = jnp.concatenate([jnp.where(diag, w3_wide, 0.0)] * 3, axis=0).astype(BF16)
    logits = nt(ah_s[...], last3)
    eddy = 0.5 * (jnp.maximum(logits, 0.0) + jnp.log1p(jnp.exp(-jnp.abs(logits))))
    error = eddy - target
    lane24 = iota((1, 24), 1)
    squares = jnp.where(lane24 < SIDE, error * error, 0.0)
    losses = jnp.sum(jnp.sum(squares.reshape(64, BLK, 24), axis=0), axis=1, keepdims=True) / CELLS
    d_logit = (error * sigmoid(logits) / (trainers * CELLS)).astype(BF16)

    zrep = onehot(iota((24, 1), 0) & 7 == (iota((1, 128), 1) & 15) >> 1)
    e_high = eddy.astype(BF16).astype(F32)
    e_mid = (eddy - e_high).astype(BF16).astype(F32)
    e_parts = jnp.where(lane24 < 8, e_high, jnp.where(lane24 < 16, e_mid, eddy - e_high - e_mid))
    fine = nn(e_parts.astype(BF16), zrep)
    fine = jnp.where(iota((1, 128), 1) >> 4 == iota((ROWS, 1), 0) & 7, fine, 0.0)
    fine = jnp.sum(fine.reshape(64, BLK, 128), axis=1)
    eddy_out[...] = fine
    y_face(send.at[HIDDEN_TILES * 32 : HIDDEN_TILES * 32 + 104], vel, eddy_out, gy_at & 1 == 0)
    loss_out[...] = jnp.broadcast_to(losses, (BLK, 128))
    dl_out[...] = d_logit.astype(F32)[:, 0:SIDE]

    count = times_sampled(own, blk, gx_at)
    big_s[:, 0:512] = nn(d_logit, jnp.concatenate([last.astype(F32), jnp.zeros((16, WIDE), F32)], axis=0).astype(BF16))
    for x in range(SIDE):
        d_hid = big_s[x * SLAB : (x + 1) * SLAB, 0:512] * slope2_s[x * SLAB : (x + 1) * SLAB, :]
        d_hid = d_hid.astype(BF16).astype(F32).reshape(SIDE, BLK, WIDE)
        shifted_store(d_s, ed_s, x, d_hid)
        dw_s[x * SLAB : (x + 1) * SLAB, :] = (d_hid * count[None]).reshape(SLAB, WIDE).astype(BF16)
    dwt = jnp.transpose(dw_s[...])

    sums = {}
    for p in range(4):
        first, last_z = max(2 * p - 1, 0), min(2 * p + 2, SIDE - 1)
        shifts = [
            a_s[dx * SLAB : dx * SLAB + ROWS, j * 512 + p * 128 : j * 512 + (p + 1) * 128]
            for dx in range(3)
            for j in range(3)
        ]
        found = nn(dwt[first * 64 : (last_z + 1) * 64], jnp.concatenate(shifts, axis=1))
        for z in range(first, last_z + 1):
            part = found[(z - first) * 64 : (z - first + 1) * 64]
            m = z - 2 * p
            sums[m] = part if m not in sums else sums[m] + part
    low_half = iota((64, 128), 1) < 64
    held = None
    for k in range(9):
        for dz in (-1, 0, 1):
            low, high = (sums[m][:, k * 128 : (k + 1) * 128] for m in (-dz, 1 - dz))
            at = (k * 3 + dz + 1) * 64
            if at % 128:
                gh_s[:, at - 64 : at + 64] = jnp.where(low_half, held, high + pltpu.roll(low, 64, 1))
            else:
                held = low + pltpu.roll(high, 64, 1)
    gh_s[:, 1664:1792] = jnp.where(low_half, held, 0.0)

    for t in range(HIDDEN_TILES):
        top, bottom = (gh_s[r : r + 32, t * 128 : (t + 1) * 128] for r in (0, 32))
        keep[t * 32 : (t + 1) * 32, :] = jnp.where(second, bottom, top)
        send[t * 32 : (t + 1) * 32, :] = jnp.where(second, top, bottom)


def backward_kernel(
    vel, own, blk, eddy, losses, dl_in, ah_s, slope1_s, i1_s, d_s, ed_s, tb_s,
    extra_out, halo1, halo2, halo3, halo4, hx_a, hx_b, hy_b, hz, pre_s, dw_s,
):
    gx_at, gy_at, second = place()
    gx_odd, gy_odd = gx_at & 1 == 1, gy_at & 1 == 1
    dev = (gx_at * lax.axis_size("gy") + gy_at) * lax.axis_size("role") + lax.axis_index("role")
    count = times_sampled(own, blk, gx_at)

    for c in range(3):
        for i in range(2):
            lo, hi = vel[c, i], vel[c, 14 + i]
            at = (c * 2 + i) * 16
            hx_a[at : at + 16, :] = jnp.where(gx_odd, lo, hi)
            hx_b[at : at + 16, :] = jnp.where(gx_odd, hi, lo)
    fine = eddy[...]
    small = fine * EDDY_SCALE
    hx_a[96:104, :] = jnp.where(gx_odd, small[0:8], small[56:64])
    hx_b[96:104, :] = jnp.where(gx_odd, small[56:64], small[0:8])
    y_face(hy_b, vel, eddy, gy_odd)
    vt = jnp.transpose(vel[...].reshape(768, 128))
    et = jnp.transpose(jnp.concatenate([small, jnp.zeros((64, 128), F32)], axis=0))
    hz[...] = jnp.zeros(hz.shape, F32)
    for t in range(6):
        hz[t * 8 : t * 8 + 2, :] = vt[0:2, t * 128 : (t + 1) * 128]
        hz[t * 8 + 2 : t * 8 + 4, :] = vt[126:128, t * 128 : (t + 1) * 128]
    hz[48:49, :] = et[0:1]
    hz[49:50, :] = et[127:128]
    halo1[...] = jnp.where(second, hx_a[...], hy_b[...])
    halo2[...] = jnp.where(second, hy_b[...], hx_a[...])
    halo3[...] = jnp.where(second, hx_b[...], hz[...])
    halo4[...] = jnp.where(second, hz[...], hx_b[...])

    for q in range(2):
        pre_s[:, q * 256 : (q + 1) * 256] = nn(windows(d_s, ed_s, q), tb_s[q])
    for x in range(SIDE):
        rows = slice(x * SLAB, (x + 1) * SLAB)
        d_first = (pre_s[rows, :] * slope1_s[rows, :]).astype(BF16).astype(F32)
        dw_s[rows, :] = (d_first.reshape(SIDE, BLK, WIDE) * count[None]).reshape(SLAB, WIDE).astype(BF16)
    g1 = nn(jnp.transpose(dw_s[...]), i1_s[...])
    z_in = iota((1, 256), 1) & 7
    parts = []
    for dz in (-1, 0, 1):
        tot = jnp.zeros((64, 256), F32)
        for z in range(SIDE):
            if 0 <= z + dz < SIDE:
                tot = tot + jnp.where(z_in == z + dz, g1[z * 64 : (z + 1) * 64], 0.0)
        parts.append(tot)
    r_at = iota((768, 1), 0)
    c_at = iota((1, 128), 1)
    r_lane = r_at & 255
    r_off = lax.div(r_lane, 24)
    r_col = (r_off * 3 + (r_at >> 8)) * 3 + ((r_lane - r_off * 24) >> 3)
    fold = onehot(jnp.where(r_lane < 216, r_col, -1) == c_at)
    g_first = exact(jnp.concatenate(parts, axis=1), fold)

    count_rows = jnp.broadcast_to(count.reshape(1, BLK, 1), (64, BLK, 1)).reshape(ROWS, 1)
    dlw = dl_in[...] * count_rows
    dl_hi = dlw.astype(BF16)
    dl_lo = (dlw - dl_hi.astype(F32)).astype(BF16)
    ah = ah_s[...]
    gl = tn(dl_hi, ah) + tn(dl_lo, ah)
    gl = jnp.where(diagonal(), gl, 0.0)
    gl = jnp.sum(gl, axis=0, keepdims=True)
    gl = gl[:, 0:128] + gl[:, 128:256] + gl[:, 256:384] + gl[:, 384:512]
    at_lane = iota((1, 128), 1) & 63 == iota((64, 1), 0)
    g_last = jnp.sum(jnp.where(at_lane, gl, 0.0), axis=1, keepdims=True)

    lane8 = iota((BLK, 128), 1)
    loss_row = jnp.where(lane8 - (LOSS_COL + BLK * (dev >> 6)) == iota((BLK, 128), 0), losses[...], 0.0)
    loss_row = jnp.sum(loss_row, axis=0, keepdims=True)
    lane = iota((64, 128), 1)
    extra = jnp.where(lane == LAST_COL, g_last, g_first)
    extra = extra + jnp.where(iota((64, 128), 0) == dev & 63, loss_row, 0.0)

    extra_out[...] = extra


def vmem_spec():
    return pl.BlockSpec(memory_space=pltpu.VMEM)


def run_forward(*given):
    velocity, target, w1, w2, w3, own, blk = (pltpu.with_memory_space_constraint(a, pltpu.HBM) for a in given)
    half = pltpu.VMEM((HIDDEN_TILES * 32, 128), F32)
    return pl.pallas_call(
        forward_kernel,
        out_shape=(
            half,
            pltpu.VMEM((HIDDEN_TILES * 32 + 104, 128), F32),
            pltpu.VMEM((64, 128), F32),
            pltpu.VMEM((BLK, 128), F32),
            pltpu.VMEM((ROWS, SIDE), F32),
            pltpu.VMEM((ROWS, WIDE), BF16),
            pltpu.VMEM((ROWS, WIDE), F32),
            pltpu.VMEM((ROWS, 256), BF16),
            pltpu.VMEM((ROWS + 2 * SLAB, 1536), BF16),
            pltpu.VMEM((2, ROWS + 2 * SLAB, 256), BF16),
            pltpu.VMEM((2, 3072, 256), BF16),
        )
        + tuple(pltpu.VMEM(a.shape, a.dtype) for a in (velocity, own, blk)),
        in_specs=[pl.BlockSpec(memory_space=pltpu.HBM)] * 7,
        out_specs=tuple(vmem_spec() for _ in range(14)),
        scratch_shapes=[
            pltpu.VMEM((3, SIDE, 16, 128), F32),
            pltpu.VMEM((10, 10, BLK, 256), F32),
            pltpu.VMEM((ROWS + 2 * SLAB, 1536), BF16),
            pltpu.VMEM((2, 3072, 256), BF16),
            pltpu.VMEM((ROWS, WIDE), F32),
            pltpu.VMEM((ROWS, WIDE), F32),
            pltpu.VMEM((ROWS, WIDE), BF16),
            pltpu.VMEM((ROWS, WIDE), F32),
            pltpu.VMEM((64, HIDDEN_TILES * 128), F32),
            pltpu.VMEM((64, 1792), F32),
        ]
        + [pltpu.VMEM(a.shape, a.dtype) for a in (target, w1, w2, w3)]
        + [pltpu.SemaphoreType.DMA((7,)), pltpu.VMEM((2, ROWS + 2 * SLAB, 256), BF16)],
        compiler_params=pltpu.CompilerParams(vmem_limit_bytes=40 * 1024 * 1024),
        name="forward",
    )(velocity, target, w1, w2, w3, own, blk)


def run_backward(velocity, own, blk, *kept):
    face = pltpu.VMEM((104, 128), F32)
    return pl.pallas_call(
        backward_kernel,
        out_shape=(pltpu.VMEM((64, 128), F32),) + (face,) * 4,
        in_specs=[vmem_spec()] * 12,
        out_specs=tuple(vmem_spec() for _ in range(5)),
        scratch_shapes=[face] * 4
        + [
            pltpu.VMEM((ROWS, WIDE), F32),
            pltpu.VMEM((ROWS, WIDE), BF16),
        ],
        compiler_params=pltpu.CompilerParams(vmem_limit_bytes=40 * 1024 * 1024),
        name="backward",
    )(velocity, own, blk, *kept)


def flow_kernel(
    vel, eddy, got0, got1, got2, got3, got4, out, rx_a, rx_b, ry_a, ry_b, rz, vx_s, vy_s, visc_s, ez_s
):
    gx_at, gy_at = lax.axis_index("gx"), lax.axis_index("gy")
    gx_odd, gy_odd = gx_at & 1 == 1, gy_at & 1 == 1
    second = core_half(gy_at) == 1
    ry_a[...] = got0[...]
    ry_b[...] = jnp.where(second, got2[...], got1[...])
    rx_a[...] = jnp.where(second, got1[...], got2[...])
    rx_b[...] = jnp.where(second, got3[...], got4[...])
    rz[...] = jnp.where(second, got4[...], got3[...])
    lane = iota((1, 128), 1)

    def sides(odd, a, b, at, rows):
        one, two = a[at : at + rows, :], b[at : at + rows, :]
        return jnp.where(odd, one, two), jnp.where(odd, two, one)

    for c in range(3):
        for x in range(16):
            vy_s[(c * 16 + x) * 32 + 8 : (c * 16 + x) * 32 + 24, :] = vel[c, x]
        for i in range(2):
            below, above = sides(gy_odd, ry_a, ry_b, (c * 2 + i) * 16, 16)
            vy_s[pl.ds(c * 512 + 6 + i, 16, stride=32), :] = below
            vy_s[pl.ds(c * 512 + 24 + i, 16, stride=32), :] = above
            below, above = sides(gx_odd, rx_a, rx_b, (c * 2 + i) * 16, 16)
            vx_s[c, i] = below
            vx_s[c, 2 + i] = above

    zcols = jnp.concatenate([jnp.transpose(rz[t * 8 : t * 8 + 8, :]) for t in range(7)], axis=0)
    coarse = eddy[...]
    e_first, e_last = zcols[768:832, 0:1] / EDDY_SCALE, zcols[768:832, 1:2] / EDDY_SCALE
    ahead = jnp.where(lane == 127, e_first, pltpu.roll(coarse, 127, 1))
    behind = jnp.where(lane == 0, e_last, pltpu.roll(coarse, 1, 1))
    below_x, above_x = (v / EDDY_SCALE for v in sides(gx_odd, rx_a, rx_b, 96, 8))
    below_y, above_y = (v / EDDY_SCALE for v in sides(gy_odd, ry_a, ry_b, 96, 8))

    def put(dst, plane, val):
        dst[pl.ds(plane * 32 + 8, 8, stride=2), :] = val
        dst[pl.ds(plane * 32 + 9, 8, stride=2), :] = val

    put(visc_s, 0, base_visc + below_x)
    put(visc_s, 17, base_visc + above_x)
    for x in range(8):
        for r in range(2):
            plane = 2 * x + 1 + r
            put(visc_s, plane, base_visc + coarse[x * 8 : x * 8 + 8])
            visc_s[plane * 32 + 7 : plane * 32 + 8, :] = base_visc + below_y[x : x + 1]
            visc_s[plane * 32 + 24 : plane * 32 + 25, :] = base_visc + above_y[x : x + 1]
        put(ez_s, 2 * x, base_visc + ahead[x * 8 : x * 8 + 8])
        put(ez_s, 2 * x + 1, base_visc + behind[x * 8 : x * 8 + 8])

    def plane_of(c, x):
        if x < 0:
            return vx_s[c, x + 2]
        if x > 15:
            return vx_s[c, x - 14]
        return vel[c, x]

    for x in range(16):
        vat = (x + 1) * 32
        visc = visc_s[vat + 8 : vat + 24, :]
        faces = (
            (visc_s[vat + 40 : vat + 56, :], visc_s[vat - 24 : vat - 8, :]),
            (visc_s[vat + 9 : vat + 25, :], visc_s[vat + 7 : vat + 23, :]),
            (
                ez_s[(x // 2 * 2) * 32 + 8 : (x // 2 * 2) * 32 + 24, :],
                ez_s[(x // 2 * 2 + 1) * 32 + 8 : (x // 2 * 2 + 1) * 32 + 24, :],
            ),
        )
        faces = [(0.5 * (visc + a), 0.5 * (visc + b)) for a, b in faces]
        wind = [vel[a, x] for a in range(3)]
        for c in range(3):
            u = vel[c, x]
            at = (c * 16 + x) * 32
            zat = (c * 16 + x) * 16
            zc = zcols[zat : zat + 16]
            p1 = jnp.where(lane == 127, zc[:, 0:1], pltpu.roll(u, 127, 1))
            p2 = jnp.where(lane == 127, zc[:, 1:2], jnp.where(lane == 126, zc[:, 0:1], pltpu.roll(u, 126, 1)))
            m1 = jnp.where(lane == 0, zc[:, 3:4], pltpu.roll(u, 1, 1))
            m2 = jnp.where(lane == 0, zc[:, 2:3], jnp.where(lane == 1, zc[:, 3:4], pltpu.roll(u, 2, 1)))
            near = (
                (plane_of(c, x + 1), plane_of(c, x - 1), plane_of(c, x + 2), plane_of(c, x - 2)),
                (
                    vy_s[at + 9 : at + 25, :], vy_s[at + 7 : at + 23, :],
                    vy_s[at + 10 : at + 26, :], vy_s[at + 6 : at + 22, :],
                ),
                (p1, m1, p2, m2),
            )
            advect = None
            diffuse = None
            for a in range(3):
                q1, b1, q2, b2 = near[a]
                slope = (8.0 * (q1 - b1) - (q2 - b2)) * (1.0 / 12.0)
                term = wind[a] * slope
                advect = term if advect is None else advect + term
                flux = faces[a][0] * (q1 - u) - faces[a][1] * (u - b1)
                diffuse = flux if diffuse is None else diffuse + flux
            out[c, x] = u + time_step * (diffuse - advect)


def run_flow(velocity, eddy, *got):
    return pl.pallas_call(
        flow_kernel,
        out_shape=jax.ShapeDtypeStruct(velocity.shape, F32),
        in_specs=[vmem_spec()] * 7,
        out_specs=vmem_spec(),
        scratch_shapes=[
            pltpu.VMEM((104, 128), F32),
            pltpu.VMEM((104, 128), F32),
            pltpu.VMEM((104, 128), F32),
            pltpu.VMEM((104, 128), F32),
            pltpu.VMEM((104, 128), F32),
            pltpu.VMEM((3, 4, 16, 128), F32),
            pltpu.VMEM((3 * 16 * 32, 128), F32),
            pltpu.VMEM((18 * 32, 128), F32),
            pltpu.VMEM((16 * 32, 128), F32),
        ],
        compiler_params=pltpu.CompilerParams(vmem_limit_bytes=32 * 1024 * 1024),
        name="flow",
    )(velocity, eddy, *got)


def finish_kernel(own, blk, mine, other, loss_out, first_out, hidden_out, last_out):
    gx_at, gy_at = lax.axis_index("gx"), lax.axis_index("gy")
    n_z = lax.axis_size("role")
    in_group = gy_at * n_z + lax.axis_index("role")
    second = core_half(gy_at) == 1
    for t in range(HIDDEN_TILES):
        one, two = mine[t * 32 : (t + 1) * 32, :], other[t * 32 : (t + 1) * 32, :]
        top, bottom = jnp.where(second, two, one), jnp.where(second, one, two)
        width = min(128, 27 * CH - t * 128)
        hidden_out[0:32, t * 128 : t * 128 + width] = top[:, :width]
        hidden_out[32:64, t * 128 : t * 128 + width] = bottom[:, :width]
    extra = mine[HIDDEN_TILES * 32 :, :] + other[HIDDEN_TILES * 32 :, :]
    first_out[...] = extra[:, 0:81]
    turned = jnp.transpose(jnp.concatenate([extra, jnp.zeros((64, 128), F32)], axis=0))
    last_out[...] = turned[LAST_COL : LAST_COL + 1, 0:64]
    slots = loss_out.shape[1]
    dev = own[...] * (lax.axis_size("gy") * n_z) + in_group
    listed = dev.shape[1]
    pick = onehot(iota((64, listed), 0) == dev & 63, F32)
    rows = nn(turned[:, 0:64], pick, HIGH)
    rows = jnp.where(iota((128, listed), 0) == LOSS_COL + BLK * (dev >> 6) + blk[...], rows, 0.0)
    found = jnp.sum(rows, axis=0, keepdims=True)
    picked = jnp.zeros((1, slots), F32)
    for g in range(listed // slots):
        picked = jnp.where(gx_at == g, found[:, g * slots : (g + 1) * slots], picked)
    loss_out[...] = picked


def run_finish(own, blk, mine, other, slots):
    f = lambda *s: jax.ShapeDtypeStruct(s, F32)
    return pl.pallas_call(
        finish_kernel,
        out_shape=(f(1, slots), f(64, 81), f(64, 27 * CH), f(1, 64)),
        in_specs=[vmem_spec()] * 4,
        out_specs=tuple(vmem_spec() for _ in range(4)),
        compiler_params=pltpu.CompilerParams(vmem_limit_bytes=32 * 1024 * 1024),
        name="finish",
    )(own, blk, mine, other)


def on_device(velocity, target_visc, w_first, w_hidden, w_last, sample_owner, sample_block):
    n_x, n_y, n_z = lax.axis_size("gx"), lax.axis_size("gy"), lax.axis_size("role")
    trainers = n_x * n_y * n_z
    own = sample_owner.reshape(1, -1)
    blk = sample_block.reshape(1, -1)
    slots = own.shape[1] // n_x

    axes = ("gx", "gy", "role")

    def even_odd(i, count):
        return i ^ 1

    def odd_even(i, count):
        return (i - 1) % count if i % 2 == 0 else (i + 1) % count

    def partner(kind, i, j, r):
        if kind == "x":
            j = odd_even(j, n_y)
        elif kind == "y":
            r = r ^ 1
        elif kind == "z_a":
            i = even_odd(i, n_x)
        else:
            i = odd_even(i, n_x)
        return (i * n_y + j) * n_z + r

    def mixed(kinds):
        pairs = []
        for i in range(n_x):
            for j in range(n_y):
                for r in range(n_z):
                    pairs.append(((i * n_y + j) * n_z + r, partner(kinds[(j ^ (j >> 1)) & 1], i, j, r)))
        return pairs

    core_pairs = [(j, even_odd(j, n_y)) for j in range(n_y)]
    size = TILES * 32

    keep, send, eddy, *kept, velocity, own, blk = run_forward(
        velocity, target_visc, w_first, w_hidden, w_last.reshape(1, CH), own, blk
    )
    half = core_half(lax.axis_index("gy"))
    got = lax.ppermute(send, "gy", core_pairs)
    extra, *halos = run_backward(velocity, own, blk, eddy, *kept)
    total = jnp.concatenate([keep + got[: HIDDEN_TILES * 32], extra], axis=0)
    rims = [got[HIDDEN_TILES * 32 :]]
    halos = [h.astype(F16) for h in halos]

    def widen(values, exps):
        wide = values.astype(F32).reshape(TILES, 32, 128) * jnp.exp2(exps)[:, None, :]
        return wide.reshape(size, 128)

    top = jnp.max(jnp.abs(total.reshape(TILES, 32, 128)), axis=1)
    exps = jnp.clip(jnp.ceil(jnp.log2(jnp.maximum(top, 1e-30))) - 13.0, -110.0, 110.0)
    orders = (("x", "z_a", "y", "z_b"), ("z_a", "x", "z_b", "y"))
    for s in range(4):
        kinds = (orders[0][s], orders[1][s])
        scaled = total.reshape(TILES, 32, 128) * jnp.exp2(-exps)[:, None, :]
        pieces = [scaled.reshape(size, 128).astype(F16), exps.astype(F16)]
        message = jnp.concatenate(pieces + [halos[s]] if s < 3 else pieces, axis=0)
        message = lax.optimization_barrier(message)
        got = lax.ppermute(message, axes, mixed(kinds))
        if s == 1:
            far = lax.ppermute(halos[3], axes, mixed((orders[0][3], orders[1][3])))
        their_exps = got[size : size + TILES].astype(F32)
        mine, theirs = widen(message[:size], exps), widen(got[:size], their_exps)
        if n_x != 4 and "z_b" in kinds:
            theirs = jnp.where(half == kinds.index("z_b"), 0.0, theirs)
        total = mine + theirs
        exps = jnp.maximum(exps, their_exps) + 1.0
        if s < 3:
            rims.append(got[size + 16 :].astype(F32))
        if s == 1:
            total, far = lax.optimization_barrier((total, far))
        if s == 2:
            u_next = run_flow(velocity, eddy, *rims, far.astype(F32))
    total, u_next = lax.optimization_barrier((total, u_next))
    if n_x != 4:
        for bit in range(1, n_x.bit_length() - 1):
            total = total + lax.ppermute(total, "gx", [(i, i ^ (1 << bit)) for i in range(n_x)])
    other = lax.ppermute(total, "gy", core_pairs)

    losses, first, hidden, last = run_finish(own, blk, total, other, slots)
    return (u_next, losses.reshape(1, 1, slots), first, hidden, last.reshape(CH))


def solution(mesh):
    return jax.shard_map(
        on_device,
        mesh=mesh,
        in_specs=(
            P(None, "gx", "gy", "role"),
            P("gx", "gy", "role"),
            P(),
            P(),
            P(),
            P("gy", "role", None, None),
            P("gy", "role", None, None),
        ),
        out_specs=(P(None, "gx", "gy", "role"), P("gy", "role", "gx"), P(), P(), P()),
        check_vma=False,
    )
```

```python
import jax
import jax.numpy as jnp
from jax import lax
from jax.experimental import pallas as pl
from jax.experimental.pallas import tpu as pltpu
from jax.sharding import PartitionSpec as P

F32 = jnp.float32
BF16 = jnp.bfloat16
HIGH = lax.Precision.HIGHEST

SIDE = 8
CELLS = SIDE**3
CH = 64
BLK = 8
ROWS = SIDE * SIDE * BLK
WIDE = SIDE * CH
SLAB = SIDE * BLK
HIDDEN_TILES = 14
TILES = 16
LAST_COL = 81
LOSS_COL = 82

EDDY_SCALE = 2.0**-9
F16 = jnp.float16

base_visc = 0.02
time_step = 0.2


def iota(shape, dim):
    return lax.broadcasted_iota(jnp.int32, shape, dim)


def onehot(cond, dtype=BF16):
    return jnp.where(cond, 1.0, 0.0).astype(dtype)


def sigmoid(v):
    return 0.5 + 0.5 * jnp.tanh(0.5 * v)


def nt(a, b, precision=None):
    return lax.dot_general(a, b, (((1,), (1,)), ((), ())), preferred_element_type=F32, precision=precision)


def tn(a, b, precision=None):
    return lax.dot_general(a, b, (((0,), (0,)), ((), ())), preferred_element_type=F32, precision=precision)


def nn(a, b, precision=None):
    return lax.dot_general(a, b, (((1,), (0,)), ((), ())), preferred_element_type=F32, precision=precision)


def core_half(at):
    return (at ^ (at >> 1)) & 1


def place():
    gx_at, gy_at = lax.axis_index("gx"), lax.axis_index("gy")
    return gx_at, gy_at, core_half(gy_at) == 1


def times_sampled(own, blk, gx_at):
    code = own[...] * BLK + blk[...]
    wanted = gx_at * BLK + iota((BLK, code.shape[1]), 0)
    return jnp.sum(jnp.where(code == wanted, 1.0, 0.0), axis=1, keepdims=True)


def tile_places():
    return [(q, z, h, 2 * q + h) for q in range(2) for z in range(3 * q, 3 * q + 5) for h in range(2)]


def place_row(q, z, k):
    if 4 * q <= z < 4 * q + 4:
        return k * 256 + (z - 4 * q) * 64
    return 2304 + k // 3 * 256 + k % 3 * 64


def exact(a, selector):
    high = a.astype(BF16)
    rest = a - high.astype(F32)
    mid = rest.astype(BF16)
    low = (rest - mid.astype(F32)).astype(BF16)
    return nn(high, selector) + (nn(mid, selector) + nn(low, selector))


def y_face(dst, vel, eddy, high):
    for c in range(3):
        for i in range(2):
            lo = jnp.concatenate([vel[c, x, i : i + 1, :] for x in range(16)], axis=0)
            hi = jnp.concatenate([vel[c, x, 14 + i : 15 + i, :] for x in range(16)], axis=0)
            dst[(c * 2 + i) * 16 : (c * 2 + i + 1) * 16, :] = jnp.where(high, hi, lo)
    dst[96:104, :] = jnp.where(high, eddy[pl.ds(7, 8, stride=8), :], eddy[pl.ds(0, 8, stride=8), :]) * EDDY_SCALE


def diagonal():
    return iota((1, WIDE), 1) >> 6 == iota((SIDE, 1), 0)


def windows(ref, more, q):
    own = [
        ref[dx * SLAB : dx * SLAB + ROWS, j * 512 + q * 256 : j * 512 + (q + 1) * 256]
        for dx in range(3)
        for j in range(3)
    ]
    return jnp.concatenate(own + [more[q, dx * SLAB : dx * SLAB + ROWS, :] for dx in range(3)], axis=1)


def shifted_store(dst_ref, more, x, val):
    zero = jnp.zeros((1, BLK, WIDE), F32)
    lo, hi = (x + 1) * SLAB, (x + 2) * SLAB
    dst_ref[lo:hi, 0:512] = jnp.concatenate([zero, val[:-1]], axis=0).reshape(SLAB, WIDE).astype(BF16)
    dst_ref[lo:hi, 512:1024] = val.reshape(SLAB, WIDE).astype(BF16)
    dst_ref[lo:hi, 1024:1536] = jnp.concatenate([val[1:], zero], axis=0).reshape(SLAB, WIDE).astype(BF16)
    left = iota((SLAB, 128), 1) < 64
    zero = zero[:, :, :128]
    for q in range(2):
        part = val[:, :, 256:384] if q == 0 else val[:, :, 128:256]
        near = [jnp.concatenate([zero, part[:-1]], axis=0), part, jnp.concatenate([part[1:], zero], axis=0)]
        near = [v.reshape(SLAB, 128) for v in near]
        turn = (1,) if q == 0 else (0, 2)
        near = [pltpu.roll(v, 64, 1) if j in turn else v for j, v in enumerate(near)]
        more[q, lo:hi, 0:128] = jnp.where(left, near[0], near[1]).astype(BF16)
        more[q, lo:hi, 128:256] = jnp.where(left, near[2], 0.0).astype(BF16)


def clear_ends(ref, more):
    for at in (0, 9 * SLAB):
        ref[at : at + SLAB, :] = jnp.zeros((SLAB, 1536), BF16)
        for q in range(2):
            more[q, at : at + SLAB, :] = jnp.zeros((SLAB, 256), BF16)


def forward_kernel(
    vel_in, tgt_in, w1_in, w2_in, w3_in, own_in, blk_in,
    keep, send, eddy_out, loss_out, dl_out, ah_s, slope1_s, i1_s, d_s, ed_s, tb_s, vel, own, blk,
    pool_s, fp_s, a_s, tt_s, pre_s, slope2_s, dw_s, big_s, gh_s, w2_s,
    tgt, w1, w2, w3, sems, ea_s,
):
    pairs = ((w2_in, w2), (vel_in, vel), (tgt_in, tgt), (w1_in, w1), (w3_in, w3), (own_in, own), (blk_in, blk))
    copies = [pltpu.make_async_copy(src, dst, sems.at[n]) for n, (src, dst) in enumerate(pairs)]
    for copy in copies:
        copy.start()
    gx_at, gy_at, second = place()
    trainers = lax.axis_size("gx") * lax.axis_size("gy") * lax.axis_size("role")

    fp_s[...] = jnp.zeros(fp_s.shape, F32)
    clear_ends(a_s, ea_s)
    clear_ends(d_s, ed_s)
    w2_s[:, 1664:1792] = jnp.zeros((64, 128), F32)
    zero_tile = jnp.zeros((64, 128), BF16)
    for q in range(2):
        for dx in range(3):
            for ref in (tt_s, tb_s):
                ref[q, 2304 + dx * 256 + 192 : 2304 + (dx + 1) * 256, :] = jnp.zeros((64, 256), BF16)
    for q, z, h, m in tile_places():
        for k in range(9):
            at, cols = place_row(q, z, k), slice(h * 128, (h + 1) * 128)
            if not -1 <= z - 2 * m <= 2:
                tt_s[q, at : at + 64, cols] = zero_tile
                tb_s[q, at : at + 64, cols] = zero_tile
    for copy in copies:
        copy.wait()

    for c in range(3):
        for x in range(SIDE):
            both = vel[c, 2 * x] + vel[c, 2 * x + 1]
            pool_s[c, x, 0:16] = both
    rows = []
    for c in range(3):
        cols = []
        for x in range(SIDE):
            cols.append(pool_s[c, x, pl.ds(0, 8, stride=2), :] + pool_s[c, x, pl.ds(1, 8, stride=2), :])
        rows.append(jnp.concatenate(cols, axis=0))
    pooled = jnp.concatenate(rows, axis=0)
    zpool = jnp.where(iota((128, 1), 0) >> 1 == iota((1, 64), 1), 0.125, 0.0).astype(BF16)
    filt = exact(pooled, zpool).astype(BF16)
    tgt_rows = tgt[...].reshape(64, 64)
    zsel = jnp.concatenate([filt[0:64], filt[64:128], filt[128:192], tgt_rows], axis=1)
    spread = onehot(iota((ROWS, 1), 0) >> 3 == iota((1, 64), 1))
    by_block = nn(spread, zsel)
    mine = (iota((1, 256), 1) & 63) >> 3 == iota((ROWS, 1), 0) & 7
    by_block = jnp.where(mine, by_block, 0.0).astype(BF16)
    lane_in = iota((1, 256), 1)
    lane_off = lax.div(lane_in, 24)
    lane_cz = lane_in - lane_off * 24
    src = iota((256, 1), 0)
    pick = onehot(jnp.where(lane_in < 216, lane_cz, -1) == (src >> 6) * 8 + (src & 7))
    cells = nn(by_block, pick)
    pick_t = onehot(jnp.where(src >= 192, src & 7, -1) == iota((1, 24), 1) & 7)
    target = nn(by_block, pick_t)

    fp_s[1:9, 1:9] = cells.reshape(SIDE, SIDE, BLK, 256)
    for half, held in ((0, range(6)), (1, range(5, 9))):
        lanes = slice(half * 128, (half + 1) * 128)
        group = lax.div(iota((1, 1, 1, 128), 3) + half * 128, 24)
        for x in range(SIDE):
            acc = jnp.zeros((1, SIDE, BLK, 128), F32)
            for k in held:
                part = fp_s[x + k // 3 : x + k // 3 + 1, k % 3 : k % 3 + SIDE, :, lanes]
                acc = jnp.where(group == k, part, acc)
            i1_s[x * SLAB : (x + 1) * SLAB, lanes] = acc.reshape(SLAB, 128).astype(BF16)

    j_at = iota((81, 1), 0)
    j_off, j_dz, j_c = lax.div(j_at, 9), lax.rem(lax.div(j_at, 3), 3) - 1, lax.rem(j_at, 3)
    lane_key = jnp.where(lane_in < 216, lane_off * 4 + (lane_cz >> 3), -1)
    same = lane_key == j_off * 4 + j_c
    w1v = w1[...]
    by_dz = [nn(w1v, onehot(jnp.where(same, j_dz, 9) == dz)) for dz in (-1, 0, 1)]
    z_in = jnp.broadcast_to(lane_in & 7, (CH, 256))
    t1 = []
    for z in range(SIDE):
        rows = jnp.where(z_in == z - 1, by_dz[0], jnp.where(z_in == z, by_dz[1], 0.0))
        t1.append(jnp.where(z_in == z + 1, by_dz[2], rows).astype(BF16))
    t1 = jnp.concatenate(t1, axis=0)
    pre_s[...] = nt(i1_s[...], t1)

    left = iota((64, 128), 1) < 64
    w2_s[:, 0:1728] = w2[...].astype(F32)
    w2t = jnp.concatenate(
        [
            jnp.transpose(jnp.concatenate([w2_s[:, t * 128 : (t + 1) * 128]] * 2, axis=0))
            for t in range(14)
        ],
        axis=0,
    )
    for k in range(9):
        base = (192 * k) // 128 * 128
        one, two = w2_s[:, base : base + 128], w2_s[:, base + 128 : base + 256]
        one_r, two_r = pltpu.roll(one, 64, 1), pltpu.roll(two, 64, 1)
        if k % 2 == 0:
            low, high = (one, one_r, two), (one_r, one, two_r)
        else:
            low, high = (one_r, two, two_r), (one, two_r, two)
        low, high = (0.0,) + low, high + (0.0,)
        tiles = {d: jnp.where(left, low[d + 2], high[d + 2]).astype(BF16) for d in (-2, -1, 0, 1)}
        kb = 8 - k
        turned = {dz: w2t[(3 * k + dz + 1) * 64 : (3 * k + dz + 2) * 64] for dz in (-1, 0, 1)}
        turned[-2] = turned[2] = jnp.zeros((64, 128), F32)
        forward = {d: jnp.where(left, turned[d], turned[d - 1]).astype(BF16) for d in (-1, 0, 1, 2)}
        for q, z, h, m in tile_places():
            at, cols = place_row(q, z, k), slice(h * 128, (h + 1) * 128)
            if z - 2 * m in forward:
                tt_s[q, at : at + 64, cols] = forward[z - 2 * m]
            d = 2 * m - z
            at = place_row(q, z, kb)
            if d in tiles:
                tb_s[q, at : at + 64, cols] = tiles[d]

    for x in range(SIDE):
        pre = pre_s[x * SLAB : (x + 1) * SLAB, :]
        sig = sigmoid(pre)
        slope1_s[x * SLAB : (x + 1) * SLAB, :] = sig * (1.0 + pre * (1.0 - sig))
        shifted_store(a_s, ea_s, x, (pre * sig).reshape(SIDE, BLK, WIDE))

    for q in range(2):
        pre_s[:, q * 256 : (q + 1) * 256] = nn(windows(a_s, ea_s, q), tt_s[q])
    for x in range(SIDE):
        pre = pre_s[x * SLAB : (x + 1) * SLAB, :]
        sig = sigmoid(pre)
        slope2_s[x * SLAB : (x + 1) * SLAB, :] = sig * (1.0 + pre * (1.0 - sig))
        ah_s[x * SLAB : (x + 1) * SLAB, :] = (pre * sig).astype(BF16)

    tile8 = onehot(iota((64, 1), 0) == iota((1, WIDE), 1) & 63)
    w3_wide = nn(w3[...], tile8)
    diag = diagonal()
    last = jnp.where(diag, w3_wide, 0.0).astype(BF16)
    last3 = jnp.concatenate([jnp.where(diag, w3_wide, 0.0)] * 3, axis=0).astype(BF16)
    logits = nt(ah_s[...], last3)
    eddy = 0.5 * (jnp.maximum(logits, 0.0) + jnp.log1p(jnp.exp(-jnp.abs(logits))))
    error = eddy - target
    lane24 = iota((1, 24), 1)
    squares = jnp.where(lane24 < SIDE, error * error, 0.0)
    losses = jnp.sum(jnp.sum(squares.reshape(64, BLK, 24), axis=0), axis=1, keepdims=True) / CELLS
    d_logit = (error * sigmoid(logits) / (trainers * CELLS)).astype(BF16)

    zrep = onehot(iota((24, 1), 0) & 7 == (iota((1, 128), 1) & 15) >> 1)
    e_high = eddy.astype(BF16).astype(F32)
    e_mid = (eddy - e_high).astype(BF16).astype(F32)
    e_parts = jnp.where(lane24 < 8, e_high, jnp.where(lane24 < 16, e_mid, eddy - e_high - e_mid))
    fine = nn(e_parts.astype(BF16), zrep)
    fine = jnp.where(iota((1, 128), 1) >> 4 == iota((ROWS, 1), 0) & 7, fine, 0.0)
    fine = jnp.sum(fine.reshape(64, BLK, 128), axis=1)
    eddy_out[0:64, :] = fine
    eddy_out[64:72, :] = jnp.zeros((8, 128), F32)
    y_face(send.at[HIDDEN_TILES * 32 : HIDDEN_TILES * 32 + 104], vel, eddy_out, gy_at & 1 == 0)
    loss_out[...] = jnp.broadcast_to(losses, (BLK, 128))
    dl_out[...] = d_logit.astype(F32)[:, 0:SIDE]

    count = times_sampled(own, blk, gx_at)
    big_s[:, 0:512] = nn(d_logit, jnp.concatenate([last.astype(F32), jnp.zeros((16, WIDE), F32)], axis=0).astype(BF16))
    for x in range(SIDE):
        d_hid = big_s[x * SLAB : (x + 1) * SLAB, 0:512] * slope2_s[x * SLAB : (x + 1) * SLAB, :]
        d_hid = d_hid.astype(BF16).astype(F32).reshape(SIDE, BLK, WIDE)
        shifted_store(d_s, ed_s, x, d_hid)
        dw_s[x * SLAB : (x + 1) * SLAB, :] = (d_hid * count[None]).reshape(SLAB, WIDE).astype(BF16)
    dwt = jnp.transpose(dw_s[...])

    sums = {}
    for p in range(4):
        first, last_z = max(2 * p - 1, 0), min(2 * p + 2, SIDE - 1)
        shifts = [
            a_s[dx * SLAB : dx * SLAB + ROWS, j * 512 + p * 128 : j * 512 + (p + 1) * 128]
            for dx in range(3)
            for j in range(3)
        ]
        found = nn(dwt[first * 64 : (last_z + 1) * 64], jnp.concatenate(shifts, axis=1))
        for z in range(first, last_z + 1):
            part = found[(z - first) * 64 : (z - first + 1) * 64]
            m = z - 2 * p
            sums[m] = part if m not in sums else sums[m] + part
    low_half = iota((64, 128), 1) < 64
    held = None
    for k in range(9):
        for dz in (-1, 0, 1):
            low, high = (sums[m][:, k * 128 : (k + 1) * 128] for m in (-dz, 1 - dz))
            at = (k * 3 + dz + 1) * 64
            if at % 128:
                gh_s[:, at - 64 : at + 64] = jnp.where(low_half, held, high + pltpu.roll(low, 64, 1))
            else:
                held = low + pltpu.roll(high, 64, 1)
    gh_s[:, 1664:1792] = jnp.where(low_half, held, 0.0)

    for t in range(HIDDEN_TILES):
        top, bottom = (gh_s[r : r + 32, t * 128 : (t + 1) * 128] for r in (0, 32))
        keep[t * 32 : (t + 1) * 32, :] = jnp.where(second, bottom, top)
        send[t * 32 : (t + 1) * 32, :] = jnp.where(second, top, bottom)


def backward_kernel(
    vel, own, blk, eddy, losses, dl_in, ah_s, slope1_s, i1_s, d_s, ed_s, tb_s,
    extra_out, halo1, halo2, halo3, halo4, hx_a, hx_b, hy_b, hz, pre_s, dw_s,
):
    gx_at, gy_at, second = place()
    gx_odd, gy_odd = gx_at & 1 == 1, gy_at & 1 == 1
    dev = (gx_at * lax.axis_size("gy") + gy_at) * lax.axis_size("role") + lax.axis_index("role")
    count = times_sampled(own, blk, gx_at)

    for c in range(3):
        for i in range(2):
            lo, hi = vel[c, i], vel[c, 14 + i]
            at = (c * 2 + i) * 16
            hx_a[at : at + 16, :] = jnp.where(gx_odd, lo, hi)
            hx_b[at : at + 16, :] = jnp.where(gx_odd, hi, lo)
    fine = eddy[0:64, :]
    small = fine * EDDY_SCALE
    hx_a[96:104, :] = jnp.where(gx_odd, small[0:8], small[56:64])
    hx_b[96:104, :] = jnp.where(gx_odd, small[56:64], small[0:8])
    y_face(hy_b, vel, eddy, gy_odd)
    vt = jnp.transpose(vel[...].reshape(768, 128))
    et = jnp.transpose(jnp.concatenate([small, jnp.zeros((64, 128), F32)], axis=0))
    hz[...] = jnp.zeros(hz.shape, F32)
    for t in range(6):
        hz[t * 8 : t * 8 + 2, :] = vt[0:2, t * 128 : (t + 1) * 128]
        hz[t * 8 + 2 : t * 8 + 4, :] = vt[126:128, t * 128 : (t + 1) * 128]
    hz[48:49, :] = et[0:1]
    hz[49:50, :] = et[127:128]
    halo1[...] = jnp.where(second, hx_a[...], hy_b[...])
    halo2[...] = jnp.where(second, hy_b[...], hx_a[...])
    halo3[...] = jnp.where(second, hx_b[...], hz[...])
    halo4[...] = jnp.where(second, hz[...], hx_b[...])

    for q in range(2):
        pre_s[:, q * 256 : (q + 1) * 256] = nn(windows(d_s, ed_s, q), tb_s[q])
    for x in range(SIDE):
        rows = slice(x * SLAB, (x + 1) * SLAB)
        d_first = (pre_s[rows, :] * slope1_s[rows, :]).astype(BF16).astype(F32)
        dw_s[rows, :] = (d_first.reshape(SIDE, BLK, WIDE) * count[None]).reshape(SLAB, WIDE).astype(BF16)
    g1 = nn(jnp.transpose(dw_s[...]), i1_s[...])
    z_in = iota((1, 256), 1) & 7
    parts = []
    for dz in (-1, 0, 1):
        tot = jnp.zeros((64, 256), F32)
        for z in range(SIDE):
            if 0 <= z + dz < SIDE:
                tot = tot + jnp.where(z_in == z + dz, g1[z * 64 : (z + 1) * 64], 0.0)
        parts.append(tot)
    r_at = iota((768, 1), 0)
    c_at = iota((1, 128), 1)
    r_lane = r_at & 255
    r_off = lax.div(r_lane, 24)
    r_col = (r_off * 3 + (r_at >> 8)) * 3 + ((r_lane - r_off * 24) >> 3)
    fold = onehot(jnp.where(r_lane < 216, r_col, -1) == c_at)
    g_first = exact(jnp.concatenate(parts, axis=1), fold)

    count_rows = jnp.broadcast_to(count.reshape(1, BLK, 1), (64, BLK, 1)).reshape(ROWS, 1)
    dlw = dl_in[...] * count_rows
    dl_hi = dlw.astype(BF16)
    dl_lo = (dlw - dl_hi.astype(F32)).astype(BF16)
    ah = ah_s[...]
    gl = tn(dl_hi, ah) + tn(dl_lo, ah)
    gl = jnp.where(diagonal(), gl, 0.0)
    gl = jnp.sum(gl, axis=0, keepdims=True)
    gl = gl[:, 0:128] + gl[:, 128:256] + gl[:, 256:384] + gl[:, 384:512]
    at_lane = iota((1, 128), 1) & 63 == iota((64, 1), 0)
    g_last = jnp.sum(jnp.where(at_lane, gl, 0.0), axis=1, keepdims=True)

    lane8 = iota((BLK, 128), 1)
    loss_row = jnp.where(lane8 - (LOSS_COL + BLK * (dev >> 6)) == iota((BLK, 128), 0), losses[...], 0.0)
    loss_row = jnp.sum(loss_row, axis=0, keepdims=True)
    lane = iota((64, 128), 1)
    extra = jnp.where(lane == LAST_COL, g_last, g_first)
    extra = extra + jnp.where(iota((64, 128), 0) == dev & 63, loss_row, 0.0)

    extra_out[...] = extra


def vmem_spec():
    return pl.BlockSpec(memory_space=pltpu.VMEM)


def run_forward(*given):
    velocity, target, w1, w2, w3, own, blk = (pltpu.with_memory_space_constraint(a, pltpu.HBM) for a in given)
    half = pltpu.VMEM((HIDDEN_TILES * 32, 128), F32)
    return pl.pallas_call(
        forward_kernel,
        out_shape=(
            half,
            pltpu.VMEM((HIDDEN_TILES * 32 + 104, 128), F32),
            pltpu.VMEM((72, 128), F32),
            pltpu.VMEM((BLK, 128), F32),
            pltpu.VMEM((ROWS, SIDE), F32),
            pltpu.VMEM((ROWS, WIDE), BF16),
            pltpu.VMEM((ROWS, WIDE), F32),
            pltpu.VMEM((ROWS, 256), BF16),
            pltpu.VMEM((ROWS + 2 * SLAB, 1536), BF16),
            pltpu.VMEM((2, ROWS + 2 * SLAB, 256), BF16),
            pltpu.VMEM((2, 3072, 256), BF16),
        )
        + tuple(pltpu.VMEM(a.shape, a.dtype) for a in (velocity, own, blk)),
        in_specs=[pl.BlockSpec(memory_space=pltpu.HBM)] * 7,
        out_specs=tuple(vmem_spec() for _ in range(14)),
        scratch_shapes=[
            pltpu.VMEM((3, SIDE, 24, 128), F32),
            pltpu.VMEM((10, 10, BLK, 256), F32),
            pltpu.VMEM((ROWS + 2 * SLAB, 1536), BF16),
            pltpu.VMEM((2, 3072, 256), BF16),
            pltpu.VMEM((ROWS, WIDE), F32),
            pltpu.VMEM((ROWS, WIDE), F32),
            pltpu.VMEM((ROWS, WIDE), BF16),
            pltpu.VMEM((ROWS, WIDE), F32),
            pltpu.VMEM((64, HIDDEN_TILES * 128), F32),
            pltpu.VMEM((64, 1792), F32),
        ]
        + [pltpu.VMEM(a.shape, a.dtype) for a in (target, w1, w2, w3)]
        + [pltpu.SemaphoreType.DMA((7,)), pltpu.VMEM((2, ROWS + 2 * SLAB, 256), BF16)],
        compiler_params=pltpu.CompilerParams(vmem_limit_bytes=40 * 1024 * 1024),
        name="forward",
    )(velocity, target, w1, w2, w3, own, blk)


def run_backward(velocity, own, blk, *kept):
    face = pltpu.VMEM((104, 128), F32)
    return pl.pallas_call(
        backward_kernel,
        out_shape=(pltpu.VMEM((64, 128), F32),) + (face,) * 4,
        in_specs=[vmem_spec()] * 12,
        out_specs=tuple(vmem_spec() for _ in range(5)),
        scratch_shapes=[face] * 4
        + [
            pltpu.VMEM((ROWS, WIDE), F32),
            pltpu.VMEM((ROWS, WIDE), BF16),
        ],
        compiler_params=pltpu.CompilerParams(vmem_limit_bytes=40 * 1024 * 1024),
        name="backward",
    )(velocity, own, blk, *kept)


def flow_kernel(
    vel, eddy, got0, got1, got2, got3, got4, out, rx_a, rx_b, ry_a, ry_b, rz, vx_s, vy_s, visc_s, ez_s
):
    gx_at, gy_at = lax.axis_index("gx"), lax.axis_index("gy")
    gx_odd, gy_odd = gx_at & 1 == 1, gy_at & 1 == 1
    second = core_half(gy_at) == 1
    ry_a[...] = got0[...]
    ry_b[...] = jnp.where(second, got2[...], got1[...])
    rx_a[...] = jnp.where(second, got1[...], got2[...])
    rx_b[...] = jnp.where(second, got3[...], got4[...])
    rz[...] = jnp.where(second, got4[...], got3[...])
    lane = iota((1, 128), 1)

    def sides(odd, a, b, at, rows):
        one, two = a[at : at + rows, :], b[at : at + rows, :]
        return jnp.where(odd, one, two), jnp.where(odd, two, one)

    for c in range(3):
        for x in range(16):
            vy_s[(c * 16 + x) * 32 + 8 : (c * 16 + x) * 32 + 24, :] = vel[c, x]
        for i in range(2):
            below, above = sides(gy_odd, ry_a, ry_b, (c * 2 + i) * 16, 16)
            vy_s[pl.ds(c * 512 + 6 + i, 16, stride=32), :] = below
            vy_s[pl.ds(c * 512 + 24 + i, 16, stride=32), :] = above
            below, above = sides(gx_odd, rx_a, rx_b, (c * 2 + i) * 16, 16)
            vx_s[c, i] = below
            vx_s[c, 2 + i] = above

    zcols = jnp.concatenate([jnp.transpose(rz[t * 8 : t * 8 + 8, :]) for t in range(7)], axis=0)
    coarse = eddy[0:64, :]
    e_first, e_last = zcols[768:832, 0:1] / EDDY_SCALE, zcols[768:832, 1:2] / EDDY_SCALE
    ahead = jnp.where(lane == 127, e_first, pltpu.roll(coarse, 127, 1))
    behind = jnp.where(lane == 0, e_last, pltpu.roll(coarse, 1, 1))
    below_x, above_x = (v / EDDY_SCALE for v in sides(gx_odd, rx_a, rx_b, 96, 8))
    below_y, above_y = (v / EDDY_SCALE for v in sides(gy_odd, ry_a, ry_b, 96, 8))

    def put(dst, plane, val):
        dst[pl.ds(plane * 32 + 8, 8, stride=2), :] = val
        dst[pl.ds(plane * 32 + 9, 8, stride=2), :] = val

    put(visc_s, 0, base_visc + below_x)
    put(visc_s, 17, base_visc + above_x)
    for x in range(8):
        for r in range(2):
            plane = 2 * x + 1 + r
            put(visc_s, plane, base_visc + coarse[x * 8 : x * 8 + 8])
            visc_s[plane * 32 + 7 : plane * 32 + 8, :] = base_visc + below_y[x : x + 1]
            visc_s[plane * 32 + 24 : plane * 32 + 25, :] = base_visc + above_y[x : x + 1]
        put(ez_s, 2 * x, base_visc + ahead[x * 8 : x * 8 + 8])
        put(ez_s, 2 * x + 1, base_visc + behind[x * 8 : x * 8 + 8])

    def plane_of(c, x):
        if x < 0:
            return vx_s[c, x + 2]
        if x > 15:
            return vx_s[c, x - 14]
        return vel[c, x]

    for x in range(16):
        vat = (x + 1) * 32
        visc = visc_s[vat + 8 : vat + 24, :]
        faces = (
            (visc_s[vat + 40 : vat + 56, :], visc_s[vat - 24 : vat - 8, :]),
            (visc_s[vat + 9 : vat + 25, :], visc_s[vat + 7 : vat + 23, :]),
            (
                ez_s[(x // 2 * 2) * 32 + 8 : (x // 2 * 2) * 32 + 24, :],
                ez_s[(x // 2 * 2 + 1) * 32 + 8 : (x // 2 * 2 + 1) * 32 + 24, :],
            ),
        )
        faces = [(0.5 * (visc + a), 0.5 * (visc + b)) for a, b in faces]
        wind = [vel[a, x] for a in range(3)]
        for c in range(3):
            u = vel[c, x]
            at = (c * 16 + x) * 32
            zat = (c * 16 + x) * 16
            zc = zcols[zat : zat + 16]
            p1 = jnp.where(lane == 127, zc[:, 0:1], pltpu.roll(u, 127, 1))
            p2 = jnp.where(lane == 127, zc[:, 1:2], jnp.where(lane == 126, zc[:, 0:1], pltpu.roll(u, 126, 1)))
            m1 = jnp.where(lane == 0, zc[:, 3:4], pltpu.roll(u, 1, 1))
            m2 = jnp.where(lane == 0, zc[:, 2:3], jnp.where(lane == 1, zc[:, 3:4], pltpu.roll(u, 2, 1)))
            near = (
                (plane_of(c, x + 1), plane_of(c, x - 1), plane_of(c, x + 2), plane_of(c, x - 2)),
                (
                    vy_s[at + 9 : at + 25, :], vy_s[at + 7 : at + 23, :],
                    vy_s[at + 10 : at + 26, :], vy_s[at + 6 : at + 22, :],
                ),
                (p1, m1, p2, m2),
            )
            advect = None
            diffuse = None
            for a in range(3):
                q1, b1, q2, b2 = near[a]
                slope = (8.0 * (q1 - b1) - (q2 - b2)) * (1.0 / 12.0)
                term = wind[a] * slope
                advect = term if advect is None else advect + term
                flux = faces[a][0] * (q1 - u) - faces[a][1] * (u - b1)
                diffuse = flux if diffuse is None else diffuse + flux
            out[c, x] = u + time_step * (diffuse - advect)


def run_flow(velocity, eddy, *got):
    return pl.pallas_call(
        flow_kernel,
        out_shape=jax.ShapeDtypeStruct(velocity.shape, F32),
        in_specs=[vmem_spec()] * 7,
        out_specs=vmem_spec(),
        scratch_shapes=[
            pltpu.VMEM((104, 128), F32),
            pltpu.VMEM((104, 128), F32),
            pltpu.VMEM((104, 128), F32),
            pltpu.VMEM((104, 128), F32),
            pltpu.VMEM((104, 128), F32),
            pltpu.VMEM((3, 4, 16, 128), F32),
            pltpu.VMEM((3 * 16 * 32 + 32, 128), F32),
            pltpu.VMEM((18 * 32, 128), F32),
            pltpu.VMEM((16 * 32, 128), F32),
        ],
        compiler_params=pltpu.CompilerParams(vmem_limit_bytes=32 * 1024 * 1024),
        name="flow",
    )(velocity, eddy, *got)


def finish_kernel(own, blk, mine, other, loss_out, first_out, hidden_out, last_out):
    gx_at, gy_at = lax.axis_index("gx"), lax.axis_index("gy")
    n_z = lax.axis_size("role")
    in_group = gy_at * n_z + lax.axis_index("role")
    second = core_half(gy_at) == 1
    for t in range(HIDDEN_TILES):
        one, two = mine[t * 32 : (t + 1) * 32, :], other[t * 32 : (t + 1) * 32, :]
        top, bottom = jnp.where(second, two, one), jnp.where(second, one, two)
        width = min(128, 27 * CH - t * 128)
        hidden_out[0:32, t * 128 : t * 128 + width] = top[:, :width]
        hidden_out[32:64, t * 128 : t * 128 + width] = bottom[:, :width]
    extra = mine[HIDDEN_TILES * 32 :, :] + other[HIDDEN_TILES * 32 :, :]
    first_out[...] = extra[:, 0:81]
    turned = jnp.transpose(jnp.concatenate([extra, jnp.zeros((64, 128), F32)], axis=0))
    last_out[...] = turned[LAST_COL : LAST_COL + 1, 0:64]
    slots = loss_out.shape[1]
    dev = own[...] * (lax.axis_size("gy") * n_z) + in_group
    listed = dev.shape[1]
    pick = onehot(iota((64, listed), 0) == dev & 63, F32)
    rows = nn(turned[:, 0:64], pick, HIGH)
    rows = jnp.where(iota((128, listed), 0) == LOSS_COL + BLK * (dev >> 6) + blk[...], rows, 0.0)
    found = jnp.sum(rows, axis=0, keepdims=True)
    picked = jnp.zeros((1, slots), F32)
    for g in range(listed // slots):
        picked = jnp.where(gx_at == g, found[:, g * slots : (g + 1) * slots], picked)
    loss_out[...] = picked


def run_finish(own, blk, mine, other, slots):
    f = lambda *s: jax.ShapeDtypeStruct(s, F32)
    return pl.pallas_call(
        finish_kernel,
        out_shape=(f(1, slots), f(64, 81), f(64, 27 * CH), f(1, 64)),
        in_specs=[vmem_spec()] * 4,
        out_specs=tuple(vmem_spec() for _ in range(4)),
        compiler_params=pltpu.CompilerParams(vmem_limit_bytes=32 * 1024 * 1024),
        name="finish",
    )(own, blk, mine, other)


def on_device(velocity, target_visc, w_first, w_hidden, w_last, sample_owner, sample_block):
    n_x, n_y, n_z = lax.axis_size("gx"), lax.axis_size("gy"), lax.axis_size("role")
    trainers = n_x * n_y * n_z
    own = sample_owner.reshape(1, -1)
    blk = sample_block.reshape(1, -1)
    slots = own.shape[1] // n_x

    axes = ("gx", "gy", "role")

    def even_odd(i, count):
        return i ^ 1

    def odd_even(i, count):
        return (i - 1) % count if i % 2 == 0 else (i + 1) % count

    def partner(kind, i, j, r):
        if kind == "x":
            j = odd_even(j, n_y)
        elif kind == "y":
            r = r ^ 1
        elif kind == "z_a":
            i = even_odd(i, n_x)
        else:
            i = odd_even(i, n_x)
        return (i * n_y + j) * n_z + r

    def mixed(kinds):
        pairs = []
        for i in range(n_x):
            for j in range(n_y):
                for r in range(n_z):
                    pairs.append(((i * n_y + j) * n_z + r, partner(kinds[(j ^ (j >> 1)) & 1], i, j, r)))
        return pairs

    core_pairs = [(j, even_odd(j, n_y)) for j in range(n_y)]
    size = TILES * 32

    keep, send, eddy, *kept, velocity, own, blk = run_forward(
        velocity, target_visc, w_first, w_hidden, w_last.reshape(1, CH), own, blk
    )
    half = core_half(lax.axis_index("gy"))
    got = lax.ppermute(send, "gy", core_pairs)
    extra, *halos = run_backward(velocity, own, blk, eddy, *kept)
    total = jnp.concatenate([keep + got[: HIDDEN_TILES * 32], extra], axis=0)
    rims = [got[HIDDEN_TILES * 32 :]]
    halos = [h.astype(F16) for h in halos]

    def widen(values, exps):
        wide = values.astype(F32).reshape(TILES, 32, 128) * jnp.exp2(exps)[:, None, :]
        return wide.reshape(size, 128)

    top = jnp.max(jnp.abs(total.reshape(TILES, 32, 128)), axis=1)
    exps = jnp.clip(jnp.ceil(jnp.log2(jnp.maximum(top, 1e-30))) - 13.0, -110.0, 110.0)
    orders = (("x", "z_a", "y", "z_b"), ("z_a", "x", "z_b", "y"))
    for s in range(4):
        kinds = (orders[0][s], orders[1][s])
        scaled = total.reshape(TILES, 32, 128) * jnp.exp2(-exps)[:, None, :]
        pieces = [scaled.reshape(size, 128).astype(F16), exps.astype(F16)]
        message = jnp.concatenate(pieces + [halos[s]] if s < 3 else pieces, axis=0)
        message = lax.optimization_barrier(message)
        got = lax.ppermute(message, axes, mixed(kinds))
        if s == 1:
            far = lax.ppermute(halos[3], axes, mixed((orders[0][3], orders[1][3])))
        their_exps = got[size : size + TILES].astype(F32)
        mine, theirs = widen(message[:size], exps), widen(got[:size], their_exps)
        if n_x != 4 and "z_b" in kinds:
            theirs = jnp.where(half == kinds.index("z_b"), 0.0, theirs)
        total = mine + theirs
        exps = jnp.maximum(exps, their_exps) + 1.0
        if s < 3:
            rims.append(got[size + 16 :].astype(F32))
        if s == 1:
            total, far = lax.optimization_barrier((total, far))
        if s == 2:
            u_next = run_flow(velocity, eddy, *rims, far.astype(F32))
    total, u_next = lax.optimization_barrier((total, u_next))
    if n_x != 4:
        for bit in range(1, n_x.bit_length() - 1):
            total = total + lax.ppermute(total, "gx", [(i, i ^ (1 << bit)) for i in range(n_x)])
    other = lax.ppermute(total, "gy", core_pairs)

    losses, first, hidden, last = run_finish(own, blk, total, other, slots)
    return (u_next, losses.reshape(1, 1, slots), first, hidden, last.reshape(CH))


def solution(mesh):
    return jax.shard_map(
        on_device,
        mesh=mesh,
        in_specs=(
            P(None, "gx", "gy", "role"),
            P("gx", "gy", "role"),
            P(),
            P(),
            P(),
            P("gy", "role", None, None),
            P("gy", "role", None, None),
        ),
        out_specs=(P(None, "gx", "gy", "role"), P("gy", "role", "gx"), P(), P(), P()),
        check_vma=False,
    )
```
